32 devices in a mesh: dp: 4 (over y, core), mp: 8 (over z, x).
Axes of the slice: x: 2, y: 2, z: 4, core: 2. Of those that a mesh axis runs over, the one named last changes fastest.
Arguments:
- tokens: int32 [4, 8, 256], P('dp'), may hold values from 0 to 3839
- lengths: int32 [4, 8], P('dp'), may hold values from 1 to 256, as said below
- places: int32 [4, 8, 25], P('dp', 'mp'), may hold values from 0 to 255, as said below
- targets: int32 [4, 8, 25], P('dp'), may hold values from 0 to 3839
- ramp: int32 [2, 3072], replicated, may hold values from 0 to 8
- attn: float32 [2, 4, 768, 768], P(None, None, 'mp'), may hold values from -0.21875 to 0.21875
- attn_m: float32 [2, 4, 768, 768], P(None, None, 'mp'), may hold values from -0.00036621094 to 0.00036621094
- attn_v: float32 [2, 4, 768, 768], P(None, None, 'mp'), may hold values from 4.9846235e-11 to 1.9938494e-10
- ffn: float32 [2, 2, 3072, 768], P(None, None, 'mp'), may hold values from -0.21875 to 0.21875
- ffn_m: float32 [2, 2, 3072, 768], P(None, None, 'mp'), may hold values from -0.00036621094 to 0.00036621094
- ffn_v: float32 [2, 2, 3072, 768], P(None, None, 'mp'), may hold values from 4.9846235e-11 to 1.9938494e-10
- table: float32 [3840, 768], P(None, 'mp'), may hold values from -0.625 to 0.625
- table_m: float32 [3840, 768], P(None, 'mp'), may hold values from -2.2888184e-05 to 2.2888184e-05
- table_v: float32 [3840, 768], P(None, 'mp'), may hold values from 2.0769264e-13 to 8.3077057e-13
- out_table: float32 [3840, 768], P('mp'), may hold values from -0.5412659 to 0.5412659
- out_m: float32 [3840, 768], P('mp'), may hold values from -0.00036621094 to 0.00036621094
- out_v: float32 [3840, 768], P('mp'), may hold values from 4.9846235e-11 to 1.9938494e-10
- gains: float32 [5, 2, 768], replicated, may hold values from -1 to 2
- gains_m: float32 [5, 2, 768], replicated, may hold values from -0.0012207031 to 0.0012207031
- gains_v: float32 [5, 2, 768], replicated, may hold values from 4.984623e-10 to 1.9938493e-09
Outputs:
- loss: float32 [2], replicated
- grad_norm: float32 [1], replicated
- attn_m_new: float32 [2, 4, 768, 768], P(None, None, 'mp')
- attn_v_new: float32 [2, 4, 768, 768], P(None, None, 'mp')
- attn_new: float32 [2, 4, 768, 768], P(None, None, 'mp')
- ffn_m_new: float32 [2, 2, 3072, 768], P(None, None, 'mp')
- ffn_v_new: float32 [2, 2, 3072, 768], P(None, None, 'mp')
- ffn_new: float32 [2, 2, 3072, 768], P(None, None, 'mp')
- table_m_new: float32 [3840, 768], P(None, 'mp')
- table_v_new: float32 [3840, 768], P(None, 'mp')
- table_new: float32 [3840, 768], P(None, 'mp')
- out_m_new: float32 [3840, 768], P('mp')
- out_v_new: float32 [3840, 768], P('mp')
- out_new: float32 [3840, 768], P('mp')
- gains_m_new: float32 [5, 2, 768], replicated
- gains_v_new: float32 [5, 2, 768], replicated
- gains_new: float32 [5, 2, 768], replicated
The draws below stay inside these ranges and needn't reach their ends.
Inputs may be any that keep to these rules, and one draw needn't show every extreme that they name: `lengths`: each group of 8 sequences along dp holds one sequence of exactly 256 tokens. `places`: each slot lies below its sequence's length.
All inputs are finite; a program needn't handle non-finite values.
Results may differ from the reference program's by a relative error of at most 0.0075.
The reference program's roundings to bfloat16 on the way count: a program that leaves them out, or rounds other values in their place, can miss the bound.
Values may be sent and summed in bfloat16 or wider, within the bound.
A program may use at most 320 MiB of HBM per device.

```python
import math
import jax
import jax.numpy as jnp
import numpy as np
from jax import lax

D = 768
HEADS = 12
HD = 64
FF = 3072
LAYERS = 2
STEP = 10
RAMP = 4
TOK_DEV = 256
PRED = 25
VOCAB = 3840
SEQS = 32
NPARAM = 20061696
N_DP = 4
N_MP = 8


def ragged_lengths(key):
    mp_rank = jnp.arange(N_MP, dtype=jnp.int32)[None, :]
    dp_rank = jnp.arange(N_DP, dtype=jnp.int32)[:, None]
    upper = TOK_DEV * (N_MP - 1 + mp_rank) * (N_DP - 1 + dp_rank) // (4 * (N_MP - 1) * (N_DP - 1))
    upper = jnp.maximum(upper, 1)
    lower = jnp.maximum(upper * 4 // 5, 1)
    drawn = jax.random.randint(jax.random.fold_in(key, 101), (N_DP, N_MP), lower, upper + 1)
    longest = jax.random.randint(jax.random.fold_in(key, 102), (N_DP, 1), 0, N_MP)
    return jnp.where(mp_rank == longest, TOK_DEV, drawn).astype(jnp.int32)


def draw_lengths(key, part):
    shared = ragged_lengths(key)
    return shared


def draw_places(key, part):
    shared = ragged_lengths(key)
    key = jax.random.fold_in(key, 5)
    drawn = jax.random.randint(key, (N_DP, N_MP, PRED), 0, shared[:, :, None])
    first = jnp.arange(PRED)[None, None, :] == 0
    return jnp.where(first, shared[:, :, None] - 1, drawn).astype(jnp.int32)


def draw_out_table(key, part):
    key = jax.random.fold_in(key, 11)
    ramp = jnp.arange(VOCAB, dtype=jnp.float32)[:, None] / (VOCAB - 1)
    base = jnp.clip(jax.random.normal(key, (VOCAB, D), jnp.float32), -5.0, 5.0)
    return base * (1.0 + 2.0 * ramp) / math.sqrt(D)


def draw_gains(key, part):
    key = jax.random.fold_in(key, 7)
    scale_key, shift_key = jax.random.split(key)
    ramp = jnp.arange(D, dtype=jnp.float32) / (D - 1)
    factor = jax.random.uniform(scale_key, (1 + 2 * LAYERS, 1, D), jnp.float32, 0.85, 1.15)
    shift = jnp.clip(0.2 * jax.random.normal(shift_key, (1 + 2 * LAYERS, 1, D), jnp.float32), -0.8, 0.8)
    return jnp.concatenate([(0.5 + ramp) * factor, shift], axis=1)


def with_ends(values, rng, low, top_value):
    place = [jax.random.randint(jax.random.fold_in(rng, axis), (), 0, length) for axis, length in enumerate(values.shape)]
    widest = values.shape.index(max(values.shape))
    next_to = place[:widest] + [(place[widest] + 1) % values.shape[widest]] + place[widest + 1:]
    return values.at[tuple(place)].set(low).at[tuple(next_to)].set(top_value)


def steps_of(own_key, extent, cuts, smallest, largest):
    factor_of = 1.0
    for dim, blocks in cuts:
        steps = jax.random.uniform(jax.random.fold_in(jax.random.fold_in(own_key, 6), dim), (blocks,), jnp.float32, smallest / len(cuts), largest / len(cuts))
        factor_of = factor_of * jnp.repeat(jnp.exp(steps), extent[dim] // blocks).reshape((-1,) + (1,) * (len(extent) - 1 - dim))
    return factor_of


def rank_table(number_of, skew):
    portions = [(1 << 20) // math.isqrt(rank ** skew) + 1 for rank in range(1, number_of + 1)]
    deviation = 1 + sum(portions) // (1 << 30)
    return np.cumsum(np.array([max(1, weight // deviation) for weight in portions]))


def skewed_ids(key, dims, count, lean):
    grid = rank_table(count, lean)
    ticket = jax.random.randint(jax.random.fold_in(key, 1), dims, 0, int(grid[count - 1]))
    standing = jnp.searchsorted(jnp.asarray(grid, jnp.int32), ticket, side="right")
    return jax.random.permutation(jax.random.fold_in(key, 2), count)[standing].astype(jnp.int32)


def normal_values(stream_key, shape, scale, most, cuts=(), kind=jnp.bfloat16):
    array = jax.random.normal(stream_key, shape, jnp.float32) * scale
    if len(cuts) > 0:
        array = steps_of(stream_key, shape, cuts, -0.22, 0.18) * array
    return jnp.clip(array, min=-most, max=most).astype(kind)


def setup_inputs(seed: int = 0) -> dict:
    splits = jax.random.split(jax.random.key(seed), 21)
    tokens = with_ends(skewed_ids(splits[0], (N_DP, N_MP, TOK_DEV), VOCAB, 2), jax.random.fold_in(splits[0], 3), 0, VOCAB - 1).astype(jnp.int32)
    lengths = draw_lengths(jax.random.fold_in(splits[20], 71), 0)
    places = draw_places(jax.random.fold_in(splits[20], 71), 0)
    targets = with_ends(skewed_ids(splits[3], (N_DP, N_MP, PRED), VOCAB, 2), jax.random.fold_in(splits[3], 3), 0, VOCAB - 1).astype(jnp.int32)
    ramp = with_ends(jax.random.randint(splits[4], (LAYERS, FF), 0, RAMP + 5), jax.random.fold_in(splits[4], 1), 0, (RAMP + 5) - 1).astype(jnp.int32)
    attn = normal_values(splits[5], (LAYERS, 4, D, D), D ** -0.5, 0.21875, ((2, 8),), jnp.float32)
    attn_m = normal_values(splits[6], (LAYERS, 4, D, D), (0.11 / NPARAM ** 0.5), 0.00036621094, ((2, 8),), jnp.float32)
    attn_v = jnp.clip(jnp.exp(math.log(1.9938493911464406e-10) - 1.3862944 * jax.random.uniform(splits[7], (LAYERS, 4, D, D), jnp.float32) ** steps_of(splits[7], (LAYERS, 4, D, D), ((2, 8),), -0.2, 0.2)), 4.9846234778661014e-11, 1.9938493911464406e-10)
    ffn = normal_values(splits[8], (LAYERS, 2, FF, D), D ** -0.5, 0.21875, ((2, 8),), jnp.float32)
    ffn_m = normal_values(splits[9], (LAYERS, 2, FF, D), (0.11 / NPARAM ** 0.5), 0.00036621094, ((2, 8),), jnp.float32)
    ffn_v = jnp.clip(jnp.exp(math.log(1.9938493911464406e-10) - 1.3862944 * jax.random.uniform(splits[10], (LAYERS, 2, FF, D), jnp.float32) ** steps_of(splits[10], (LAYERS, 2, FF, D), ((2, 8),), -0.2, 0.2)), 4.9846234778661014e-11, 1.9938493911464406e-10)
    table = normal_values(splits[11], (VOCAB, D), 0.04, 0.625, ((1, 8),), jnp.float32)
    table_m = normal_values(splits[12], (VOCAB, D), (0.44 / (NPARAM * VOCAB) ** 0.5), 2.288818359375e-05, ((1, 8),), jnp.float32)
    table_v = jnp.clip(jnp.exp(math.log(8.307705651883213e-13) - 1.3862944 * jax.random.uniform(splits[13], (VOCAB, D), jnp.float32) ** steps_of(splits[13], (VOCAB, D), ((1, 8),), -0.2, 0.2)), 2.0769264129708032e-13, 8.307705651883213e-13)
    out_table = draw_out_table(jax.random.fold_in(splits[20], 71), 0)
    out_m = normal_values(splits[15], (VOCAB, D), (0.11 / NPARAM ** 0.5), 0.00036621094, ((0, 8),), jnp.float32)
    out_v = jnp.clip(jnp.exp(math.log(1.9938493911464406e-10) - 1.3862944 * jax.random.uniform(splits[16], (VOCAB, D), jnp.float32) ** steps_of(splits[16], (VOCAB, D), ((0, 8),), -0.2, 0.2)), 4.9846234778661014e-11, 1.9938493911464406e-10)
    gains = draw_gains(jax.random.fold_in(splits[20], 71), 0)
    gains_m = normal_values(splits[18], (1 + 2 * LAYERS, 2, D), (0.35 / NPARAM ** 0.5), 0.0012207031, (), jnp.float32)
    gains_v = jnp.clip(jnp.exp(jax.random.uniform(splits[19], (1 + 2 * LAYERS, 2, D), jnp.float32, math.log(4.984623269699284e-10), math.log(1.9938493078797137e-09))), 4.984623269699284e-10, 1.9938493078797137e-09)
    return {"tokens": tokens, "lengths": lengths, "places": places, "targets": targets, "ramp": ramp, "attn": attn, "attn_m": attn_m, "attn_v": attn_v, "ffn": ffn, "ffn_m": ffn_m, "ffn_v": ffn_v, "table": table, "table_m": table_m, "table_v": table_v, "out_table": out_table, "out_m": out_m, "out_v": out_v, "gains": gains, "gains_m": gains_m, "gains_v": gains_v}


norm_eps = 1e-05
beta_one = 0.9
beta_two = 0.999
learn_rate = 0.02
gain_rate = 0.3
weight_decay = 0.01
adam_eps = 1e-08
clip_limit = 1.0
masked_score = -1000000000.0
highest = lax.Precision.HIGHEST

@jax.custom_vjp
def low(v):
    return lax.optimization_barrier(v.astype(jnp.bfloat16)).astype(jnp.float32)

@jax.custom_vjp
def low_back(v):
    return v

def low_keep(v):
    return (low(v), None)

def low_pass(kept, grad):
    return (grad,)

def back_keep(v):
    return (v, None)

def back_low(kept, grad):
    return (low(grad),)
low.defvjp(low_keep, low_pass)
low_back.defvjp(back_keep, back_low)

def sinusoid(count, width):
    places = jnp.arange(count, dtype=jnp.float32)[:, None]
    freqs = jnp.exp(jnp.arange(width // 2, dtype=jnp.float32) * (-2.0 * math.log(10000.0) / width))
    angles = places * freqs[None, :]
    return jnp.concatenate([jnp.sin(angles), jnp.cos(angles)], axis=1)

def layer_norm(values, gain, shift):
    centre = lax.optimization_barrier(jnp.mean(values, axis=-1, keepdims=True))
    offset = values - centre
    spread = lax.optimization_barrier(jnp.mean(offset * offset, axis=-1, keepdims=True))
    return offset * lax.rsqrt(spread + norm_eps) * gain + shift

def matmul(left, right):
    return jnp.dot(left, right, precision=highest, preferred_element_type=jnp.float32)

def encoder_layer(states, attn_w, ffn_w, pair, length, unit_mask):
    count = states.shape[0]
    inputs = low(states)
    projected = [low(low_back(matmul(inputs, attn_w[which]))) for which in range(3)]
    query, keyed, valued = [item.reshape(count, HEADS, HD).transpose(1, 0, 2) for item in projected]
    scores = jnp.einsum('hqe,hke->hqk', query, keyed, precision=highest) * HD ** (-0.5)
    scores = low_back(scores)
    visible = jnp.arange(count) < length
    scores = jnp.where(visible[None, None, :], scores, masked_score)
    weights = low(jax.nn.softmax(scores, axis=-1))
    mixed = jnp.einsum('hqk,hke->hqe', weights, valued, precision=highest)
    mixed = low(low_back(mixed.transpose(1, 0, 2).reshape(count, HEADS * HD)))
    branch = low_back(matmul(mixed, attn_w[3]))
    middle = layer_norm(states + branch, pair[0, 0], pair[0, 1])
    hidden = low_back(jnp.einsum('td,fd->tf', low(middle), ffn_w[0], precision=highest))
    active = low(jax.nn.gelu(hidden, approximate=False) * unit_mask[None, :])
    output = low_back(jnp.einsum('tf,fd->td', active, ffn_w[1], precision=highest))
    return layer_norm(middle + output, pair[1, 0], pair[1, 1])

def sequence_loss(ids, length, spots, labels, params, masks):
    attn_b, ffn_b, table, out_b, gains = params
    states = table[ids] + sinusoid(TOK_DEV, D)
    states = layer_norm(states, gains[0, 0], gains[0, 1])
    for depth in range(LAYERS):
        states = encoder_layer(states, attn_b[depth], ffn_b[depth], gains[1 + 2 * depth:3 + 2 * depth], length, masks[depth])
    picked = low(states[spots])
    logits = low_back(jnp.einsum('rd,vd->rv', picked, out_b, precision=highest))
    totals = jax.nn.logsumexp(logits, axis=-1)
    target_logit = jnp.take_along_axis(logits, labels[:, None], axis=1)[:, 0]
    counted = jnp.maximum(1, length * PRED // TOK_DEV)
    valid = jnp.arange(PRED) < counted
    return jnp.sum(jnp.where(valid, totals - target_logit, 0.0))

def total_loss(params, tokens, lengths, places, targets, masks):
    attn, ffn, table, out_table, gains = params
    lowered = (low(attn), low(ffn), table, low(out_table), gains)
    block = min(SEQS, max(1, 4096 // TOK_DEV))
    pieces = (tokens.reshape(-1, block, TOK_DEV), lengths.reshape(-1, block), places.reshape(-1, block, PRED), targets.reshape(-1, block, PRED))

    def one_block(carry, group):
        losses = jax.vmap(lambda ids, length, spots, labels: sequence_loss(ids, length, spots, labels, lowered, masks))(*group)
        return (carry + jnp.sum(losses), None)
    total, unused = lax.scan(jax.checkpoint(one_block), jnp.zeros((), jnp.float32), pieces)
    return total

def adamw(weight, moment_one, moment_two, grad, decay, rate):
    moment_one = beta_one * moment_one + (1.0 - beta_one) * grad
    moment_two = beta_two * moment_two + (1.0 - beta_two) * grad * grad
    fixed_one = moment_one / (1.0 - beta_one ** STEP)
    fixed_two = moment_two / (1.0 - beta_two ** STEP)
    weight = weight - rate * (fixed_one / (jnp.sqrt(fixed_two) + adam_eps) + decay * weight)
    return (moment_one, moment_two, weight)

def reference(tokens, lengths, places, targets, ramp, attn, attn_m, attn_v, ffn, ffn_m, ffn_v, table, table_m, table_v, out_table, out_m, out_v, gains, gains_m, gains_v):
    masks = jnp.minimum(ramp, RAMP).astype(jnp.float32) / RAMP
    params = (attn, ffn, table, out_table, gains)
    loss_sum, pullback = jax.vjp(lambda values: total_loss(values, tokens, lengths, places, targets, masks), params)
    grads = pullback(jnp.ones((), jnp.float32))[0]
    squares = jnp.zeros((), jnp.float32)
    for grad in grads:
        squares = squares + jnp.sum(grad * grad)
    grad_norm = jnp.sqrt(squares)
    factor = clip_limit / jnp.maximum(grad_norm, clip_limit)
    counted = jnp.sum(jnp.maximum(1, lengths * PRED // TOK_DEV)).astype(jnp.float32)
    attn_m_new, attn_v_new, attn_new = adamw(attn, attn_m, attn_v, grads[0] * factor, weight_decay, learn_rate)
    ffn_m_new, ffn_v_new, ffn_new = adamw(ffn, ffn_m, ffn_v, grads[1] * factor, weight_decay, learn_rate)
    table_m_new, table_v_new, table_new = adamw(table, table_m, table_v, grads[2] * factor, weight_decay, learn_rate)
    out_m_new, out_v_new, out_new = adamw(out_table, out_m, out_v, grads[3] * factor, weight_decay, learn_rate)
    gains_m_new, gains_v_new, gains_new = adamw(gains, gains_m, gains_v, grads[4] * factor, 0.0, gain_rate)
    return (jnp.stack([loss_sum, counted]), grad_norm.reshape(1), attn_m_new, attn_v_new, attn_new, ffn_m_new, ffn_v_new, ffn_new, table_m_new, table_v_new, table_new, out_m_new, out_v_new, out_new, gains_m_new, gains_v_new, gains_new)
```

```python
import functools
import math

import jax
import jax.numpy as jnp
from jax import lax
from jax.experimental import pallas as pl
from jax.experimental.pallas import tpu as pltpu
from jax.sharding import PartitionSpec as P

HEADS = 12
LAYERS = 2
STEP = 10
RAMP = 4


norm_eps = 1e-05
beta_one = 0.9
beta_two = 0.999
learn_rate = 0.02
gain_rate = 0.3
weight_decay = 0.01
adam_eps = 1e-08
clip_limit = 1.0
masked_score = -1000000000.0


MESH = pl.DeviceIdType.MESH
VMEM_LIMIT = 60 * 1024 * 1024


def dot_nn(left, right):
    return lax.dot_general(
        left, right, (((1,), (0,)), ((), ())), preferred_element_type=jnp.float32
    )


def dot_nt(left, right):
    return lax.dot_general(
        left, right, (((1,), (1,)), ((), ())), preferred_element_type=jnp.float32
    )


def dot_tn(left, right):
    return lax.dot_general(
        left, right, (((0,), (0,)), ((), ())), preferred_element_type=jnp.float32
    )


def ring_index(place, n):
    late = place // (n // 2)
    return (1 - late) * 2 * place + late * (2 * (n - 1 - place) + 1)


def ring_place(index, n):
    odd = index % 2
    return (1 - odd) * (index // 2) + odd * (n - 1 - index // 2)


class Spot:
    def __init__(self, n):
        self.n = n
        self.dp = lax.axis_index("dp")
        self.mp = lax.axis_index("mp")
        self.core = self.dp % 2
        self.place = ring_place(self.mp, n)
        self.partner = (self.dp + 1 - 2 * self.core, self.mp)
        self.across = ((self.dp + 2) % 4, self.mp)
        self.ring = (
            (self.dp, ring_index((self.place + 1) % n, n)),
            (self.dp, ring_index((self.place + n - 1) % n, n)),
        )

    def shard(self, offset):
        return ring_index((self.place + offset + self.n) % self.n, self.n)


def greet(devices):
    barrier = pltpu.get_barrier_semaphore()
    for device in devices:
        pl.semaphore_signal(barrier, inc=1, device_id=device, device_id_type=MESH)
    pl.semaphore_wait(barrier, len(devices))


def last_step(n, way, part):
    return n // 2 if way == part else n // 2 - 1


WAYS = ((0, 0), (1, 1), (0, 1), (1, 0))


def normed_of(values):
    centre = jnp.mean(values, axis=-1, keepdims=True)
    offset = values - centre
    spread = jnp.mean(offset * offset, axis=-1, keepdims=True)
    inverse = lax.rsqrt(spread + norm_eps)
    return offset * inverse, inverse


def forward_kernel(
    n,
    visible_ref,
    states_ref,
    gains_ref,
    mask_ref,
    attn_sh,
    ffn_sh,
    attn_full,
    ffn_full,
    final_ref,
    inputs_ref,
    proj_ref,
    mixed_ref,
    pre_ref,
    mid_ref,
    slope_ref,
    act_ref,
    wa,
    wf,
    state,
    own_sem,
    out_sem,
    ring_send,
    ring_recv,
    core_send,
    core_recv,
):
    spot = Spot(n)
    core = spot.core
    rows_a = attn_sh.shape[2]
    rows_f = ffn_sh.shape[2]
    part_f = rows_f // 2
    width = attn_sh.shape[3]
    steps = n // 2

    def rows_at(shard, rows):
        return pl.ds(pl.multiple_of(shard * rows, 16), rows)

    def chunk(piece, shard, part):
        kind, depth = piece % 2, piece // 2
        if kind == 0:
            return wa.at[depth, 2 * core + part, rows_at(shard, rows_a), :]
        start = pl.multiple_of(shard * rows_f + part * part_f, 16)
        return wf.at[depth, core, pl.ds(start, part_f), :]

    def chunk_other(piece, shard, part):
        kind, depth = piece % 2, piece // 2
        if kind == 0:
            return wa.at[depth, 2 * (1 - core) + part, rows_at(shard, rows_a), :]
        start = pl.multiple_of(shard * rows_f + part * part_f, 16)
        return wf.at[depth, 1 - core, pl.ds(start, part_f), :]

    def chunk_own(piece, part):
        kind, depth = piece % 2, piece // 2
        if kind == 0:
            return attn_sh.at[depth, 2 * core + part]
        return ffn_sh.at[depth, core, pl.ds(part * part_f, part_f), :]

    def sign(way):
        return -1 if way == 0 else 1

    def ring_out(piece, way, part, step):
        target = chunk(piece, spot.shard(sign(way) * (step - 1)), part)
        return pltpu.make_async_remote_copy(
            src_ref=chunk_own(piece, part) if step == 1 else target,
            dst_ref=target,
            send_sem=ring_send.at[piece, way, part, step - 1],
            recv_sem=ring_recv.at[piece, way, part, step - 1],
            device_id=spot.ring[way],
            device_id_type=MESH,
        )

    def ring_in(piece, way, part, step):
        target = chunk(piece, spot.shard(sign(way) * step), part)
        return pltpu.make_async_remote_copy(
            src_ref=target,
            dst_ref=target,
            send_sem=ring_send.at[piece, way, part, step - 1],
            recv_sem=ring_recv.at[piece, way, part, step - 1],
            device_id=spot.ring[way],
            device_id_type=MESH,
        )

    def core_out(piece, way, part, step):
        target = chunk(piece, spot.shard(sign(way) * step), part)
        return pltpu.make_async_remote_copy(
            src_ref=target,
            dst_ref=target,
            send_sem=core_send.at[piece, way, part, step - 1],
            recv_sem=core_recv.at[piece, way, part, step - 1],
            device_id=spot.partner,
            device_id_type=MESH,
        )

    def core_in(piece, way, part, step):
        target = chunk_other(piece, spot.shard(sign(way) * step), part)
        return pltpu.make_async_remote_copy(
            src_ref=target,
            dst_ref=target,
            send_sem=core_send.at[piece, way, part, step - 1],
            recv_sem=core_recv.at[piece, way, part, step - 1],
            device_id=spot.partner,
            device_id_type=MESH,
        )

    own_copies = []
    for depth in range(LAYERS):
        for which in range(4):
            own_copies.append(
                pltpu.make_async_copy(
                    attn_sh.at[depth, which],
                    wa.at[depth, which, rows_at(spot.mp, rows_a), :],
                    own_sem.at[2 * depth, which],
                )
            )
        for which in range(2):
            own_copies.append(
                pltpu.make_async_copy(
                    ffn_sh.at[depth, which],
                    wf.at[depth, which, rows_at(spot.mp, rows_f), :],
                    own_sem.at[2 * depth + 1, which],
                )
            )
    greet((spot.ring[0], spot.ring[1], spot.partner))

    def launch(piece):
        for way, part in WAYS:
            ring_out(piece, way, part, 1).start()

    def pass_on(piece, step):
        for way, part in WAYS:
            if step <= last_step(n, way, part):
                ring_in(piece, way, part, step).wait_recv()
                if step < last_step(n, way, part):
                    ring_out(piece, way, part, step + 1).start()
                core_out(piece, way, part, step).start()

    def settle(piece, step):
        for way, part in WAYS:
            if step <= last_step(n, way, part):
                core_in(piece, way, part, step).wait_recv()

    launch(0)
    for copy in own_copies:
        copy.start()
    state[...] = states_ref[...]
    for copy in own_copies:
        copy.wait()

    lanes = lax.broadcasted_iota(jnp.int32, (1, 128), 1) < 64
    visible = visible_ref[...] > 0.0

    def head_pair(depth, pair):
        columns = pl.ds(pl.multiple_of(pair * 128, 128), 128)
        query = proj_ref[depth, 0, :, columns]
        keyed = proj_ref[depth, 1, :, columns]
        valued = proj_ref[depth, 2, :, columns]
        outs = []
        for side in range(2):
            mine = lanes if side == 0 else jnp.logical_not(lanes)
            scores = dot_nt(jnp.where(mine, query, jnp.zeros_like(query)), keyed) * 0.125
            scores = jnp.where(visible, scores, masked_score)
            expo = jnp.exp(scores - jnp.max(scores, axis=-1, keepdims=True))
            total = jnp.sum(expo, axis=-1, keepdims=True)
            outs.append(dot_nn((expo / total).astype(jnp.bfloat16), valued))
        mixed_ref[depth, :, columns] = jnp.where(lanes, outs[0], outs[1]).astype(jnp.bfloat16)

    def ffn_shard(depth, offset):
        shard = spot.shard(offset)
        rows = rows_at(shard, rows_f)
        hidden = dot_nt(mid_ref[depth], wf[depth, 0, rows, :])
        spread = 0.5 * (1.0 + lax.erf(hidden * (0.5**0.5)))
        mask = mask_ref[depth : depth + 1, pl.ds(pl.multiple_of(shard * rows_f, 128), rows_f)]
        bell = jnp.exp(hidden * hidden * -0.5) * (1.0 / math.sqrt(2.0 * math.pi))
        slope_ref[depth, shard] = (spread + hidden * bell) * mask
        active = (hidden * spread * mask).astype(jnp.bfloat16)
        act_ref[depth, shard] = active
        pre_ref[depth, 1] += dot_nn(active, wf[depth, 1, rows, :])

    out_copies = []
    for depth in range(LAYERS):
        piece_a, piece_f = 2 * depth, 2 * depth + 1
        for step in range(1, steps + 1):
            pass_on(piece_a, step)
            if step == steps - 1:
                launch(piece_f)
        for step in range(1, steps + 1):
            settle(piece_a, step)
        copy = pltpu.make_async_copy(wa.at[depth], attn_full.at[depth], out_sem.at[piece_a])
        copy.start()
        out_copies.append(copy)
        inputs = state[...].astype(jnp.bfloat16)
        inputs_ref[depth] = inputs
        for which in range(3):
            proj_ref[depth, which] = dot_nn(inputs, wa[depth, which]).astype(jnp.bfloat16)
        pass_on(piece_f, 1)

        @pl.loop(0, HEADS // 2)
        def _(pair):
            head_pair(depth, pair)

        pre_ref[depth, 0] = state[...] + dot_nn(mixed_ref[depth], wa[depth, 3])
        normed, _ = normed_of(pre_ref[depth, 0])
        middle = (
            normed * gains_ref[1 + 2 * depth, 0:1, :] + gains_ref[1 + 2 * depth, 1:2, :]
        )
        mid_ref[depth] = middle.astype(jnp.bfloat16)
        pre_ref[depth, 1] = middle
        ffn_shard(depth, 0)
        pass_on(piece_f, 2)
        settle(piece_f, 1)
        ffn_shard(depth, -1)
        ffn_shard(depth, 1)
        pass_on(piece_f, 3)
        if depth + 1 < LAYERS:
            launch(piece_a + 2)
        settle(piece_f, 2)
        ffn_shard(depth, -2)
        ffn_shard(depth, 2)
        settle(piece_f, 3)
        ffn_shard(depth, -3)
        ffn_shard(depth, 3)
        pass_on(piece_f, 4)
        settle(piece_f, 4)
        ffn_shard(depth, 4)
        copy = pltpu.make_async_copy(wf.at[depth], ffn_full.at[depth], out_sem.at[piece_f])
        copy.start()
        out_copies.append(copy)
        normed, _ = normed_of(pre_ref[depth, 1])
        state[...] = normed * gains_ref[2 + 2 * depth, 0:1, :] + gains_ref[2 + 2 * depth, 1:2, :]
    final_ref[...] = state[...]
    for piece in range(2 * LAYERS):
        for way, part in WAYS:
            for step in range(1, last_step(n, way, part) + 1):
                ring_out(piece, way, part, step).wait_send()
                core_out(piece, way, part, step).wait_send()
    for copy in out_copies:
        copy.wait()


def forward_call(n, visible, states, gains, masks, attn_b, ffn_b):
    count, width = states.shape
    rows_f = ffn_b.shape[2]
    f32, bf16 = jnp.float32, jnp.bfloat16
    vmem = pl.BlockSpec(memory_space=pltpu.VMEM)
    anywhere = pl.BlockSpec(memory_space=pl.ANY)
    shape = jax.ShapeDtypeStruct
    sems = pltpu.SemaphoreType.DMA((2 * LAYERS, 2, 2, n // 2))
    return pl.pallas_call(
        functools.partial(forward_kernel, n),
        out_shape=(
            shape((LAYERS, 4, width, width), bf16),
            shape((LAYERS, 2, rows_f * n, width), bf16),
            shape((count, width), f32),
            shape((LAYERS, count, width), bf16),
            shape((LAYERS, 3, count, width), bf16),
            shape((LAYERS, count, width), bf16),
            shape((LAYERS, 2, count, width), f32),
            shape((LAYERS, count, width), bf16),
            shape((LAYERS, n, count, rows_f), f32),
            shape((LAYERS, n, count, rows_f), bf16),
        ),
        in_specs=[vmem, vmem, vmem, vmem, anywhere, anywhere],
        out_specs=(anywhere, anywhere) + (vmem,) * 8,
        scratch_shapes=[
            pltpu.VMEM((LAYERS, 4, width, width), bf16),
            pltpu.VMEM((LAYERS, 2, rows_f * n, width), bf16),
            pltpu.VMEM((count, width), f32),
            pltpu.SemaphoreType.DMA((2 * LAYERS, 4)),
            pltpu.SemaphoreType.DMA((2 * LAYERS,)),
            sems,
            sems,
            sems,
            sems,
        ],
        compiler_params=pltpu.CompilerParams(
            collective_id=1, has_side_effects=True, vmem_limit_bytes=VMEM_LIMIT
        ),
        name="forward_layers",
    )(visible, states, gains, masks, attn_b, ffn_b)


def merged(value, axis, join):
    pieces = jax.tree.map(lambda part: lax.all_gather(part, axis), value)
    head = jax.tree.map(lambda part: part[0], pieces)
    tail = jax.tree.map(lambda part: part[1:], pieces)
    total, _ = lax.scan(lambda total, section: (join(total, section), None), head, tail)
    return total


def sinusoid(count, width):
    places = jnp.arange(count, dtype=jnp.float32)[:, None]
    freqs = jnp.exp(jnp.arange(width // 2, dtype=jnp.float32) * (-2.0 * math.log(10000.0) / width))
    angles = places * freqs[None, :]
    return jnp.concatenate([jnp.sin(angles), jnp.cos(angles)], axis=1)


def layer_norm(values, gain, shift):
    centre = jnp.mean(values, axis=-1, keepdims=True)
    offset = values - centre
    spread = jnp.mean(offset * offset, axis=-1, keepdims=True)
    inverse = lax.rsqrt(spread + norm_eps)
    normed = offset * inverse
    return (normed * gain + shift, (normed, inverse))


def norm_backward(grad, saved, gain):
    normed, inverse = saved
    scaled = grad * gain
    centred = scaled - jnp.mean(scaled, axis=-1, keepdims=True)
    result = inverse * (centred - normed * jnp.mean(scaled * normed, axis=-1, keepdims=True))
    return (result, jnp.stack([jnp.sum(grad * normed, axis=0), jnp.sum(grad, axis=0)]))


def gelu_exact(values):
    return jax.nn.gelu(values, approximate=False)


def gelu_back(hidden, grad):
    unused, pullback = jax.vjp(gelu_exact, hidden)
    return pullback(grad)[0]


def masked_scores(query, keyed, length):
    scale = query.shape[-1] ** (-0.5)
    scores = jnp.einsum("hqe,hke->hqk", query, keyed, preferred_element_type=jnp.float32) * scale
    visible = jnp.arange(keyed.shape[1]) < length
    return jnp.where(visible[None, None, :], scores, masked_score)


def fetch_forward(attn_part, ffn_part):
    return (
        lax.all_gather(attn_part, "mp", axis=1, tiled=True),
        lax.all_gather(ffn_part, "mp", axis=1, tiled=True),
    )


def fetch_backward(attn_part, ffn_part):
    return (
        lax.all_gather(attn_part, "mp", axis=1, tiled=True),
        lax.all_gather(ffn_part, "mp", axis=1, tiled=True),
    )


def reduce_layer(attn_grad, ffn_grad):
    return (
        lax.psum_scatter(attn_grad, "mp", scatter_dimension=1, tiled=True),
        lax.psum_scatter(ffn_grad, "mp", scatter_dimension=1, tiled=True),
    )


def ffn_forward(middle_b, ffn_w, unit_mask):
    hidden = jnp.einsum("td,fd->tf", middle_b, ffn_w[0], preferred_element_type=jnp.float32)
    active = (gelu_exact(hidden) * unit_mask[None, :]).astype(jnp.bfloat16)
    output = jnp.einsum("tf,fd->td", active, ffn_w[1], preferred_element_type=jnp.float32)
    return (hidden, active, output)


def ffn_backward(grad_out, middle_b, hidden, active, ffn_w, unit_mask):
    grad_active = jnp.einsum("td,fd->tf", grad_out, ffn_w[1], preferred_element_type=jnp.float32)
    grad_hidden = gelu_back(hidden, grad_active * unit_mask[None, :]).astype(jnp.bfloat16)
    up_grad = jnp.einsum("tf,td->fd", grad_hidden, middle_b, preferred_element_type=jnp.float32)
    down_grad = jnp.einsum("tf,td->fd", active, grad_out, preferred_element_type=jnp.float32)
    from_ffn = jnp.einsum("tf,fd->td", grad_hidden, ffn_w[0], preferred_element_type=jnp.float32)
    return (jnp.stack([up_grad, down_grad]), from_ffn)


def layer_forward(states, attn_w, ffn_w, pair, length, unit_mask):
    count = states.shape[0]
    inputs = states.astype(jnp.bfloat16)
    projected = jnp.einsum(
        "td,kde->kte", inputs, attn_w[:3], preferred_element_type=jnp.float32
    ).astype(jnp.bfloat16)
    heads = projected.reshape(3, count, HEADS, -1).transpose(0, 2, 1, 3)
    scores = masked_scores(heads[0], heads[1], length)
    peak = jnp.max(scores, axis=-1, keepdims=True)
    expo = jnp.exp(scores - peak)
    total = jnp.sum(expo, axis=-1, keepdims=True)
    log_total = peak + jnp.log(total)
    probs = (expo / total).astype(jnp.bfloat16)
    mixed = jnp.einsum("hqk,hke->hqe", probs, heads[2], preferred_element_type=jnp.float32)
    mixed = mixed.transpose(1, 0, 2).reshape(count, -1).astype(jnp.bfloat16)
    branch = jnp.dot(mixed, attn_w[3], preferred_element_type=jnp.float32)
    middle, norm_one = layer_norm(states + branch, pair[0, 0], pair[0, 1])
    middle_b = middle.astype(jnp.bfloat16)
    hidden, active, output = ffn_forward(middle_b, ffn_w, unit_mask)
    result, norm_two = layer_norm(middle + output, pair[1, 0], pair[1, 1])
    return (result, (inputs, heads, log_total, mixed, norm_one, middle_b, hidden, active, norm_two))


def layer_backward(grad, attn_w, ffn_w, pair, length, unit_mask, kept):
    inputs, heads, log_total, mixed, norm_one, middle_b, hidden, active, norm_two = kept
    count = inputs.shape[0]
    grad_two, pair_two = norm_backward(grad, norm_two, pair[1, 0])
    ffn_grad, from_ffn = ffn_backward(
        grad_two.astype(jnp.bfloat16), middle_b, hidden, active, ffn_w, unit_mask
    )
    grad_one, pair_one = norm_backward(grad_two + from_ffn, norm_one, pair[0, 0])
    grad_branch = grad_one.astype(jnp.bfloat16)
    output_grad = jnp.einsum("td,te->de", mixed, grad_branch, preferred_element_type=jnp.float32)
    grad_mixed = jnp.einsum("te,de->td", grad_branch, attn_w[3], preferred_element_type=jnp.float32)
    grad_mixed = grad_mixed.astype(jnp.bfloat16).reshape(count, HEADS, -1).transpose(1, 0, 2)
    scale = heads.shape[-1] ** (-0.5)
    probs = jnp.exp(masked_scores(heads[0], heads[1], length) - log_total)
    grad_values = jnp.einsum(
        "hqk,hqe->hke", probs.astype(jnp.bfloat16), grad_mixed, preferred_element_type=jnp.float32
    )
    grad_probs = jnp.einsum(
        "hqe,hke->hqk", grad_mixed, heads[2], preferred_element_type=jnp.float32
    )
    grad_scores = probs * (grad_probs - jnp.sum(grad_probs * probs, axis=-1, keepdims=True))
    grad_scores = grad_scores.astype(jnp.bfloat16)
    grad_query = (
        jnp.einsum("hqk,hke->hqe", grad_scores, heads[1], preferred_element_type=jnp.float32)
        * scale
    )
    grad_key = (
        jnp.einsum("hqk,hqe->hke", grad_scores, heads[0], preferred_element_type=jnp.float32)
        * scale
    )
    stacked = (
        jnp.stack([grad_query, grad_key, grad_values]).transpose(0, 2, 1, 3).reshape(3, count, -1)
    )
    stacked = stacked.astype(jnp.bfloat16)
    input_grad = jnp.einsum("td,kte->kde", inputs, stacked, preferred_element_type=jnp.float32)
    from_attn = jnp.einsum("kte,kde->td", stacked, attn_w[:3], preferred_element_type=jnp.float32)
    attn_grad = jnp.concatenate([input_grad, output_grad[None]], axis=0)
    return (grad_one + from_attn, attn_grad, ffn_grad, jnp.stack([pair_one, pair_two]))


def adamw(weight, moment_one, moment_two, grad, decay, rate):
    moment_one = beta_one * moment_one + (1.0 - beta_one) * grad
    moment_two = beta_two * moment_two + (1.0 - beta_two) * grad * grad
    fixed_one = moment_one / (1.0 - beta_one**STEP)
    fixed_two = moment_two / (1.0 - beta_two**STEP)
    weight = weight - rate * (fixed_one / (jnp.sqrt(fixed_two) + adam_eps) + decay * weight)
    return (moment_one, moment_two, weight)


def combine_vocab(first, second):
    peak = jnp.maximum(first[0], second[0])
    total = first[1] * jnp.exp(first[0] - peak) + second[1] * jnp.exp(second[0] - peak)
    return (peak, total, first[2] + second[2])


def ffn_backward_kept(grad_out, middle_b, hidden, active, ffn_w, unit_mask):
    grad_active = jnp.einsum("td,fd->tf", grad_out, ffn_w[1], preferred_element_type=jnp.float32)
    grad_hidden = (hidden * grad_active).astype(jnp.bfloat16)
    up_grad = jnp.einsum("tf,td->fd", grad_hidden, middle_b, preferred_element_type=jnp.float32)
    down_grad = jnp.einsum("tf,td->fd", active, grad_out, preferred_element_type=jnp.float32)
    from_ffn = jnp.einsum("tf,fd->td", grad_hidden, ffn_w[0], preferred_element_type=jnp.float32)
    return (jnp.stack([up_grad, down_grad]), from_ffn)


def layer_backward_kept(grad, attn_w, ffn_w, pair, length, unit_mask, kept):
    inputs, heads, log_total, mixed, norm_one, middle_b, hidden, active, norm_two = kept
    count = inputs.shape[0]
    grad_two, pair_two = norm_backward(grad, norm_two, pair[1, 0])
    ffn_grad, from_ffn = ffn_backward_kept(
        grad_two.astype(jnp.bfloat16), middle_b, hidden, active, ffn_w, unit_mask
    )
    grad_one, pair_one = norm_backward(grad_two + from_ffn, norm_one, pair[0, 0])
    grad_branch = grad_one.astype(jnp.bfloat16)
    output_grad = jnp.einsum("td,te->de", mixed, grad_branch, preferred_element_type=jnp.float32)
    grad_mixed = jnp.einsum("te,de->td", grad_branch, attn_w[3], preferred_element_type=jnp.float32)
    grad_mixed = grad_mixed.astype(jnp.bfloat16).reshape(count, HEADS, -1).transpose(1, 0, 2)
    scale = heads.shape[-1] ** (-0.5)
    probs = jnp.exp(masked_scores(heads[0], heads[1], length) - log_total)
    grad_values = jnp.einsum(
        "hqk,hqe->hke", probs.astype(jnp.bfloat16), grad_mixed, preferred_element_type=jnp.float32
    )
    grad_probs = jnp.einsum(
        "hqe,hke->hqk", grad_mixed, heads[2], preferred_element_type=jnp.float32
    )
    grad_scores = probs * (grad_probs - jnp.sum(grad_probs * probs, axis=-1, keepdims=True))
    grad_scores = grad_scores.astype(jnp.bfloat16)
    grad_query = (
        jnp.einsum("hqk,hke->hqe", grad_scores, heads[1], preferred_element_type=jnp.float32)
        * scale
    )
    grad_key = (
        jnp.einsum("hqk,hqe->hke", grad_scores, heads[0], preferred_element_type=jnp.float32)
        * scale
    )
    stacked = (
        jnp.stack([grad_query, grad_key, grad_values]).transpose(0, 2, 1, 3).reshape(3, count, -1)
    )
    stacked = stacked.astype(jnp.bfloat16)
    input_grad = jnp.einsum("td,kte->kde", inputs, stacked, preferred_element_type=jnp.float32)
    from_attn = jnp.einsum("kte,kde->td", stacked, attn_w[:3], preferred_element_type=jnp.float32)
    attn_grad = jnp.concatenate([input_grad, output_grad[None]], axis=0)
    return (grad_one + from_attn, attn_grad, ffn_grad, jnp.stack([pair_one, pair_two]))


def local_general(
    tokens,
    lengths,
    places,
    targets,
    ramp,
    attn,
    attn_m,
    attn_v,
    ffn,
    ffn_m,
    ffn_v,
    table,
    table_m,
    table_v,
    out_table,
    out_m,
    out_v,
    gains,
    gains_m,
    gains_v,
):
    rank = lax.axis_index("mp")
    count = tokens.shape[2]
    flat_ids = tokens.reshape(-1)
    all_lengths = lengths.reshape(-1)
    length = lax.dynamic_index_in_dim(all_lengths, rank, keepdims=False)
    masks = jnp.minimum(ramp, RAMP).astype(jnp.float32) / RAMP
    unit_masks = [masks[depth] for depth in range(LAYERS)]
    looked = jnp.take(table, flat_ids, axis=0)
    embedded = lax.all_to_all(looked, "mp", split_axis=0, concat_axis=1, tiled=True)
    states, norm_zero = layer_norm(
        embedded + sinusoid(count, embedded.shape[1]), gains[0, 0], gains[0, 1]
    )
    kept_all = []
    weights_all = []
    for depth in range(LAYERS):
        attn_w, ffn_w = fetch_forward(
            attn[depth].astype(jnp.bfloat16), ffn[depth].astype(jnp.bfloat16)
        )
        states, kept = layer_forward(
            states, attn_w, ffn_w, gains[1 + 2 * depth : 3 + 2 * depth], length, unit_masks[depth]
        )
        kept_all.append(kept)
        weights_all.append(None)
    spots = places.reshape(-1)
    picked = jnp.take(states, spots, axis=0).astype(jnp.bfloat16)
    picked_all = lax.all_gather(picked, "mp", axis=0, tiled=True)
    out_b = out_table.astype(jnp.bfloat16)
    logits = jnp.einsum("rd,vd->rv", picked_all, out_b, preferred_element_type=jnp.float32)
    labels = targets.reshape(-1)
    columns = rank * out_table.shape[0] + jnp.arange(out_table.shape[0])
    hits = (labels[:, None] == columns[None, :]).astype(jnp.float32)
    peak = jnp.max(logits, axis=1)
    expsum = jnp.sum(jnp.exp(logits - peak[:, None]), axis=1)
    target_part = jnp.sum(hits * logits, axis=1)
    peak_all, expsum_all, target_all = merged((peak, expsum, target_part), "mp", combine_vocab)
    log_total = peak_all + jnp.log(expsum_all)
    slot_count = targets.shape[2]
    counted = jnp.maximum(1, all_lengths * slot_count // count)
    valid = (jnp.arange(slot_count)[None, :] < counted[:, None]).reshape(-1)
    loss_pair = jnp.stack(
        [
            jnp.sum(jnp.where(valid, log_total - target_all, 0.0)),
            jnp.sum(counted).astype(jnp.float32),
        ]
    )
    grad_logits = jnp.where(
        valid[:, None], jnp.exp(logits - log_total[:, None]) - hits, 0.0
    ).astype(jnp.bfloat16)
    out_grad = jnp.einsum("rv,rd->vd", grad_logits, picked_all, preferred_element_type=jnp.float32)
    picked_grad = lax.psum_scatter(
        jnp.dot(grad_logits, out_b, preferred_element_type=jnp.float32),
        "mp",
        scatter_dimension=0,
        tiled=True,
    )
    grad = jnp.zeros_like(states).at[spots].add(picked_grad)
    attn_parts = [None] * LAYERS
    ffn_parts = [None] * LAYERS
    pair_grads = [None] * LAYERS
    for depth in reversed(range(LAYERS)):
        attn_w, ffn_w = fetch_backward(
            attn[depth].astype(jnp.bfloat16), ffn[depth].astype(jnp.bfloat16)
        )
        grad, attn_grad, ffn_grad, pair_grad = layer_backward(
            grad,
            attn_w,
            ffn_w,
            gains[1 + 2 * depth : 3 + 2 * depth],
            length,
            unit_masks[depth],
            kept_all[depth],
        )
        attn_parts[depth], ffn_parts[depth] = reduce_layer(attn_grad, ffn_grad)
        pair_grads[depth] = pair_grad
    grad_sum, zero_grad = norm_backward(grad, norm_zero, gains[0, 0])
    returned = lax.all_to_all(grad_sum, "mp", split_axis=1, concat_axis=0, tiled=True)
    table_grad = jnp.zeros_like(table).at[flat_ids].add(returned)
    gains_grad = jnp.concatenate([zero_grad[None]] + pair_grads, axis=0)
    attn_sum, ffn_sum, table_sum, out_sum, gains_part, loss = lax.psum(
        (jnp.stack(attn_parts), jnp.stack(ffn_parts), table_grad, out_grad, gains_grad, loss_pair),
        "dp",
    )
    shard_squares = (
        jnp.sum(attn_sum * attn_sum)
        + jnp.sum(ffn_sum * ffn_sum)
        + jnp.sum(table_sum * table_sum)
        + jnp.sum(out_sum * out_sum)
    )
    square_total, gains_sum = lax.psum((shard_squares, gains_part), "mp")
    grad_norm = jnp.sqrt(square_total + jnp.sum(gains_sum * gains_sum))
    factor = clip_limit / jnp.maximum(grad_norm, clip_limit)
    attn_m_new, attn_v_new, attn_new = adamw(
        attn, attn_m, attn_v, attn_sum * factor, weight_decay, learn_rate
    )
    ffn_m_new, ffn_v_new, ffn_new = adamw(
        ffn, ffn_m, ffn_v, ffn_sum * factor, weight_decay, learn_rate
    )
    table_m_new, table_v_new, table_new = adamw(
        table, table_m, table_v, table_sum * factor, weight_decay, learn_rate
    )
    out_m_new, out_v_new, out_new = adamw(
        out_table, out_m, out_v, out_sum * factor, weight_decay, learn_rate
    )
    gains_m_new, gains_v_new, gains_new = adamw(
        gains, gains_m, gains_v, gains_sum * factor, 0.0, gain_rate
    )
    return (
        loss,
        grad_norm.reshape(1),
        attn_m_new,
        attn_v_new,
        attn_new,
        ffn_m_new,
        ffn_v_new,
        ffn_new,
        table_m_new,
        table_v_new,
        table_new,
        out_m_new,
        out_v_new,
        out_new,
        gains_m_new,
        gains_v_new,
        gains_new,
    )


def local(
    tokens,
    lengths,
    places,
    targets,
    ramp,
    attn,
    attn_m,
    attn_v,
    ffn,
    ffn_m,
    ffn_v,
    table,
    table_m,
    table_v,
    out_table,
    out_m,
    out_v,
    gains,
    gains_m,
    gains_v,
):
    rank = lax.axis_index("mp")
    count = tokens.shape[2]
    flat_ids = tokens.reshape(-1)
    all_lengths = lengths.reshape(-1)
    length = lax.dynamic_index_in_dim(all_lengths, rank, keepdims=False)
    masks = jnp.minimum(ramp, RAMP).astype(jnp.float32) / RAMP
    unit_masks = [masks[depth] for depth in range(LAYERS)]
    looked = jnp.take(table, flat_ids, axis=0)
    embedded = lax.all_to_all(looked, "mp", split_axis=0, concat_axis=1, tiled=True)
    states, norm_zero = layer_norm(
        embedded + sinusoid(count, embedded.shape[1]), gains[0, 0], gains[0, 1]
    )
    n = attn.shape[3] // attn.shape[2]
    visible = (jnp.arange(count) < length).astype(jnp.float32)[None, :]
    (
        attn_full, ffn_full, states, inputs_all, proj_all, mixed_all, pre_all, mid_all, slope_all, act_all,
    ) = forward_call(
        n, visible, states, gains, masks, attn.astype(jnp.bfloat16), ffn.astype(jnp.bfloat16)
    )
    kept_all = []
    for depth in range(LAYERS):
        heads = proj_all[depth].reshape(3, count, HEADS, -1).transpose(0, 2, 1, 3)
        scores = masked_scores(heads[0], heads[1], length)
        log_total = jax.nn.logsumexp(scores, axis=-1, keepdims=True)
        slope = slope_all[depth].transpose(1, 0, 2).reshape(count, -1)
        act = act_all[depth].transpose(1, 0, 2).reshape(count, -1)
        kept_all.append((inputs_all[depth], heads, log_total, mixed_all[depth], normed_of(pre_all[depth, 0]),
           mid_all[depth], slope, act, normed_of(pre_all[depth, 1])))
    spots = places.reshape(-1)
    picked = jnp.take(states, spots, axis=0).astype(jnp.bfloat16)
    picked_all = lax.all_gather(picked, "mp", axis=0, tiled=True)
    out_b = out_table.astype(jnp.bfloat16)
    logits = jnp.einsum("rd,vd->rv", picked_all, out_b, preferred_element_type=jnp.float32)
    labels = targets.reshape(-1)
    columns = rank * out_table.shape[0] + jnp.arange(out_table.shape[0])
    hits = (labels[:, None] == columns[None, :]).astype(jnp.float32)
    peak = jnp.max(logits, axis=1)
    expsum = jnp.sum(jnp.exp(logits - peak[:, None]), axis=1)
    target_part = jnp.sum(hits * logits, axis=1)
    peak_all, expsum_all, target_all = merged((peak, expsum, target_part), "mp", combine_vocab)
    log_total = peak_all + jnp.log(expsum_all)
    slot_count = targets.shape[2]
    counted = jnp.maximum(1, all_lengths * slot_count // count)
    valid = (jnp.arange(slot_count)[None, :] < counted[:, None]).reshape(-1)
    loss_pair = jnp.stack(
        [
            jnp.sum(jnp.where(valid, log_total - target_all, 0.0)),
            jnp.sum(counted).astype(jnp.float32),
        ]
    )
    grad_logits = jnp.where(
        valid[:, None], jnp.exp(logits - log_total[:, None]) - hits, 0.0
    ).astype(jnp.bfloat16)
    out_grad = jnp.einsum("rv,rd->vd", grad_logits, picked_all, preferred_element_type=jnp.float32)
    picked_grad = lax.psum_scatter(
        jnp.dot(grad_logits, out_b, preferred_element_type=jnp.float32),
        "mp",
        scatter_dimension=0,
        tiled=True,
    )
    grad = jnp.zeros_like(states).at[spots].add(picked_grad)
    attn_parts = [None] * LAYERS
    ffn_parts = [None] * LAYERS
    pair_grads = [None] * LAYERS
    for depth in reversed(range(LAYERS)):
        attn_w, ffn_w = attn_full[depth], ffn_full[depth]
        grad, attn_grad, ffn_grad, pair_grad = layer_backward_kept(
            grad,
            attn_w,
            ffn_w,
            gains[1 + 2 * depth : 3 + 2 * depth],
            length,
            unit_masks[depth],
            kept_all[depth],
        )
        attn_parts[depth], ffn_parts[depth] = reduce_layer(attn_grad, ffn_grad)
        pair_grads[depth] = pair_grad
    grad_sum, zero_grad = norm_backward(grad, norm_zero, gains[0, 0])
    returned = lax.all_to_all(grad_sum, "mp", split_axis=1, concat_axis=0, tiled=True)
    table_grad = jnp.zeros_like(table).at[flat_ids].add(returned)
    gains_grad = jnp.concatenate([zero_grad[None]] + pair_grads, axis=0)
    attn_sum, ffn_sum, table_sum, out_sum, gains_part, loss = lax.psum(
        (jnp.stack(attn_parts), jnp.stack(ffn_parts), table_grad, out_grad, gains_grad, loss_pair),
        "dp",
    )
    shard_squares = (
        jnp.sum(attn_sum * attn_sum)
        + jnp.sum(ffn_sum * ffn_sum)
        + jnp.sum(table_sum * table_sum)
        + jnp.sum(out_sum * out_sum)
    )
    square_total, gains_sum = lax.psum((shard_squares, gains_part), "mp")
    grad_norm = jnp.sqrt(square_total + jnp.sum(gains_sum * gains_sum))
    factor = clip_limit / jnp.maximum(grad_norm, clip_limit)
    attn_m_new, attn_v_new, attn_new = adamw(
        attn, attn_m, attn_v, attn_sum * factor, weight_decay, learn_rate
    )
    ffn_m_new, ffn_v_new, ffn_new = adamw(
        ffn, ffn_m, ffn_v, ffn_sum * factor, weight_decay, learn_rate
    )
    table_m_new, table_v_new, table_new = adamw(
        table, table_m, table_v, table_sum * factor, weight_decay, learn_rate
    )
    out_m_new, out_v_new, out_new = adamw(
        out_table, out_m, out_v, out_sum * factor, weight_decay, learn_rate
    )
    gains_m_new, gains_v_new, gains_new = adamw(
        gains, gains_m, gains_v, gains_sum * factor, 0.0, gain_rate
    )
    return (
        loss,
        grad_norm.reshape(1),
        attn_m_new,
        attn_v_new,
        attn_new,
        ffn_m_new,
        ffn_v_new,
        ffn_new,
        table_m_new,
        table_v_new,
        table_new,
        out_m_new,
        out_v_new,
        out_new,
        gains_m_new,
        gains_v_new,
        gains_new,
    )


def solution(mesh):
    in_specs = (
        P("dp", None, None),
        P("dp", None),
        P("dp", "mp", None),
        P("dp", None, None),
        P(),
        P(None, None, "mp", None),
        P(None, None, "mp", None),
        P(None, None, "mp", None),
        P(None, None, "mp", None),
        P(None, None, "mp", None),
        P(None, None, "mp", None),
        P(None, "mp"),
        P(None, "mp"),
        P(None, "mp"),
        P("mp", None),
        P("mp", None),
        P("mp", None),
        P(),
        P(),
        P(),
    )
    out_specs = (
        P(),
        P(),
        P(None, None, "mp", None),
        P(None, None, "mp", None),
        P(None, None, "mp", None),
        P(None, None, "mp", None),
        P(None, None, "mp", None),
        P(None, None, "mp", None),
        P(None, "mp"),
        P(None, "mp"),
        P(None, "mp"),
        P("mp", None),
        P("mp", None),
        P("mp", None),
        P(),
        P(),
        P(),
    )
    rows_attn, rows_ffn = 768 // mesh.shape['mp'], 3072 // mesh.shape['mp']
    fits = mesh.shape['mp'] == 8
    chosen = local if fits else local_general
    return jax.shard_map(chosen, mesh=mesh, in_specs=in_specs, out_specs=out_specs, check_vma=False)
```

```python
import functools
import math

import jax
import jax.numpy as jnp
from jax import lax
from jax.experimental import pallas as pl
from jax.experimental.pallas import tpu as pltpu
from jax.sharding import PartitionSpec as P

HEADS = 12
LAYERS = 2
STEP = 10
RAMP = 4


norm_eps = 1e-05
beta_one = 0.9
beta_two = 0.999
learn_rate = 0.02
gain_rate = 0.3
weight_decay = 0.01
adam_eps = 1e-08
clip_limit = 1.0
masked_score = -1000000000.0


MESH = pl.DeviceIdType.MESH
VMEM_LIMIT = 60 * 1024 * 1024


def dot_nn(left, right):
    return lax.dot_general(
        left, right, (((1,), (0,)), ((), ())), preferred_element_type=jnp.float32
    )


def dot_nt(left, right):
    return lax.dot_general(
        left, right, (((1,), (1,)), ((), ())), preferred_element_type=jnp.float32
    )


def dot_tn(left, right):
    return lax.dot_general(
        left, right, (((0,), (0,)), ((), ())), preferred_element_type=jnp.float32
    )


def ring_index(place, n):
    late = place // (n // 2)
    return (1 - late) * 2 * place + late * (2 * (n - 1 - place) + 1)


def ring_place(index, n):
    odd = index % 2
    return (1 - odd) * (index // 2) + odd * (n - 1 - index // 2)


class Spot:
    def __init__(self, n):
        self.n = n
        self.dp = lax.axis_index("dp")
        self.mp = lax.axis_index("mp")
        self.core = self.dp % 2
        self.place = ring_place(self.mp, n)
        self.partner = (self.dp + 1 - 2 * self.core, self.mp)
        self.across = ((self.dp + 2) % 4, self.mp)
        self.ring = (
            (self.dp, ring_index((self.place + 1) % n, n)),
            (self.dp, ring_index((self.place + n - 1) % n, n)),
        )

    def shard(self, offset):
        return ring_index((self.place + offset + self.n) % self.n, self.n)


def greet(devices):
    barrier = pltpu.get_barrier_semaphore()
    for device in devices:
        pl.semaphore_signal(barrier, inc=1, device_id=device, device_id_type=MESH)
    pl.semaphore_wait(barrier, len(devices))


def last_step(n, way, part):
    return n // 2 if way == part else n // 2 - 1


WAYS = ((0, 0), (1, 1), (0, 1), (1, 0))


def normed_of(values):
    centre = jnp.mean(values, axis=-1, keepdims=True)
    offset = values - centre
    spread = jnp.mean(offset * offset, axis=-1, keepdims=True)
    inverse = lax.rsqrt(spread + norm_eps)
    return offset * inverse, inverse


def forward_kernel(
    n,
    visible_ref,
    states_ref,
    gains_ref,
    mask_ref,
    attn_sh,
    ffn_sh,
    attn_full,
    ffn_full,
    final_ref,
    inputs_ref,
    proj_ref,
    mixed_ref,
    pre_ref,
    mid_ref,
    slope_ref,
    act_ref,
    wa,
    wf,
    state,
    own_sem,
    out_sem,
    ring_send,
    ring_recv,
    core_send,
    core_recv,
):
    spot = Spot(n)
    core = spot.core
    rows_a = attn_sh.shape[2]
    rows_f = ffn_sh.shape[2]
    part_f = rows_f // 2
    width = attn_sh.shape[3]
    steps = n // 2

    def rows_at(shard, rows):
        return pl.ds(pl.multiple_of(shard * rows, 16), rows)

    def chunk(piece, shard, part):
        kind, depth = piece % 2, piece // 2
        if kind == 0:
            return wa.at[depth, 2 * core + part, rows_at(shard, rows_a), :]
        start = pl.multiple_of(shard * rows_f + part * part_f, 16)
        return wf.at[depth, core, pl.ds(start, part_f), :]

    def chunk_other(piece, shard, part):
        kind, depth = piece % 2, piece // 2
        if kind == 0:
            return wa.at[depth, 2 * (1 - core) + part, rows_at(shard, rows_a), :]
        start = pl.multiple_of(shard * rows_f + part * part_f, 16)
        return wf.at[depth, 1 - core, pl.ds(start, part_f), :]

    def chunk_own(piece, part):
        kind, depth = piece % 2, piece // 2
        if kind == 0:
            return attn_sh.at[depth, 2 * core + part]
        return ffn_sh.at[depth, core, pl.ds(part * part_f, part_f), :]

    def sign(way):
        return -1 if way == 0 else 1

    def ring_out(piece, way, part, step):
        target = chunk(piece, spot.shard(sign(way) * (step - 1)), part)
        return pltpu.make_async_remote_copy(
            src_ref=chunk_own(piece, part) if step == 1 else target,
            dst_ref=target,
            send_sem=ring_send.at[piece, way, part, step - 1],
            recv_sem=ring_recv.at[piece, way, part, step - 1],
            device_id=spot.ring[way],
            device_id_type=MESH,
        )

    def ring_in(piece, way, part, step):
        target = chunk(piece, spot.shard(sign(way) * step), part)
        return pltpu.make_async_remote_copy(
            src_ref=target,
            dst_ref=target,
            send_sem=ring_send.at[piece, way, part, step - 1],
            recv_sem=ring_recv.at[piece, way, part, step - 1],
            device_id=spot.ring[way],
            device_id_type=MESH,
        )

    def core_out(piece, way, part, step):
        target = chunk(piece, spot.shard(sign(way) * step), part)
        return pltpu.make_async_remote_copy(
            src_ref=target,
            dst_ref=target,
            send_sem=core_send.at[piece, way, part, step - 1],
            recv_sem=core_recv.at[piece, way, part, step - 1],
            device_id=spot.partner,
            device_id_type=MESH,
        )

    def core_in(piece, way, part, step):
        target = chunk_other(piece, spot.shard(sign(way) * step), part)
        return pltpu.make_async_remote_copy(
            src_ref=target,
            dst_ref=target,
            send_sem=core_send.at[piece, way, part, step - 1],
            recv_sem=core_recv.at[piece, way, part, step - 1],
            device_id=spot.partner,
            device_id_type=MESH,
        )

    own_copies = []
    for depth in range(LAYERS):
        for which in range(4):
            own_copies.append(
                pltpu.make_async_copy(
                    attn_sh.at[depth, which],
                    wa.at[depth, which, rows_at(spot.mp, rows_a), :],
                    own_sem.at[2 * depth, which],
                )
            )
        for which in range(2):
            own_copies.append(
                pltpu.make_async_copy(
                    ffn_sh.at[depth, which],
                    wf.at[depth, which, rows_at(spot.mp, rows_f), :],
                    own_sem.at[2 * depth + 1, which],
                )
            )
    greet((spot.ring[0], spot.ring[1], spot.partner))

    def launch(piece):
        for way, part in WAYS:
            ring_out(piece, way, part, 1).start()

    def pass_on(piece, step):
        for way, part in WAYS:
            if step <= last_step(n, way, part):
                ring_in(piece, way, part, step).wait_recv()
                if step < last_step(n, way, part):
                    ring_out(piece, way, part, step + 1).start()
                core_out(piece, way, part, step).start()

    def settle(piece, step):
        for way, part in WAYS:
            if step <= last_step(n, way, part):
                core_in(piece, way, part, step).wait_recv()

    launch(0)
    for copy in own_copies:
        copy.start()
    state[...] = states_ref[...]
    for copy in own_copies:
        copy.wait()

    lanes = lax.broadcasted_iota(jnp.int32, (1, 128), 1) < 64
    visible = visible_ref[...] > 0.0

    def head_pair(depth, pair):
        columns = pl.ds(pl.multiple_of(pair * 128, 128), 128)
        query = proj_ref[depth, 0, :, columns]
        keyed = proj_ref[depth, 1, :, columns]
        valued = proj_ref[depth, 2, :, columns]
        outs = []
        for side in range(2):
            mine = lanes if side == 0 else jnp.logical_not(lanes)
            scores = dot_nt(jnp.where(mine, query, jnp.zeros_like(query)), keyed) * 0.125
            scores = jnp.where(visible, scores, masked_score)
            expo = jnp.exp(scores - jnp.max(scores, axis=-1, keepdims=True))
            total = jnp.sum(expo, axis=-1, keepdims=True)
            outs.append(dot_nn((expo / total).astype(jnp.bfloat16), valued))
        mixed_ref[depth, :, columns] = jnp.where(lanes, outs[0], outs[1]).astype(jnp.bfloat16)

    def ffn_shard(depth, offset):
        shard = spot.shard(offset)
        rows = rows_at(shard, rows_f)
        hidden = dot_nt(mid_ref[depth], wf[depth, 0, rows, :])
        spread = 0.5 * (1.0 + lax.erf(hidden * (0.5**0.5)))
        mask = mask_ref[depth : depth + 1, pl.ds(pl.multiple_of(shard * rows_f, 128), rows_f)]
        bell = jnp.exp(hidden * hidden * -0.5) * (1.0 / math.sqrt(2.0 * math.pi))
        slope_ref[depth, shard] = (spread + hidden * bell) * mask
        active = (hidden * spread * mask).astype(jnp.bfloat16)
        act_ref[depth, shard] = active
        pre_ref[depth, 1] += dot_nn(active, wf[depth, 1, rows, :])

    out_copies = []
    for depth in range(LAYERS):
        piece_a, piece_f = 2 * depth, 2 * depth + 1
        for step in range(1, steps + 1):
            pass_on(piece_a, step)
            if step == steps - 1:
                launch(piece_f)
        for step in range(1, steps + 1):
            settle(piece_a, step)
        copy = pltpu.make_async_copy(wa.at[depth], attn_full.at[depth], out_sem.at[piece_a])
        copy.start()
        out_copies.append(copy)
        inputs = state[...].astype(jnp.bfloat16)
        inputs_ref[depth] = inputs
        for which in range(3):
            proj_ref[depth, which] = dot_nn(inputs, wa[depth, which]).astype(jnp.bfloat16)
        pass_on(piece_f, 1)

        @pl.loop(0, HEADS // 2)
        def _(pair):
            head_pair(depth, pair)

        pre_ref[depth, 0] = state[...] + dot_nn(mixed_ref[depth], wa[depth, 3])
        normed, _ = normed_of(pre_ref[depth, 0])
        middle = (
            normed * gains_ref[1 + 2 * depth, 0:1, :] + gains_ref[1 + 2 * depth, 1:2, :]
        )
        mid_ref[depth] = middle.astype(jnp.bfloat16)
        pre_ref[depth, 1] = middle
        ffn_shard(depth, 0)
        pass_on(piece_f, 2)
        settle(piece_f, 1)
        ffn_shard(depth, -1)
        ffn_shard(depth, 1)
        pass_on(piece_f, 3)
        if depth + 1 < LAYERS:
            launch(piece_a + 2)
        settle(piece_f, 2)
        ffn_shard(depth, -2)
        ffn_shard(depth, 2)
        settle(piece_f, 3)
        ffn_shard(depth, -3)
        ffn_shard(depth, 3)
        pass_on(piece_f, 4)
        settle(piece_f, 4)
        ffn_shard(depth, 4)
        copy = pltpu.make_async_copy(wf.at[depth], ffn_full.at[depth], out_sem.at[piece_f])
        copy.start()
        out_copies.append(copy)
        normed, _ = normed_of(pre_ref[depth, 1])
        state[...] = normed * gains_ref[2 + 2 * depth, 0:1, :] + gains_ref[2 + 2 * depth, 1:2, :]
    final_ref[...] = state[...]
    for piece in range(2 * LAYERS):
        for way, part in WAYS:
            for step in range(1, last_step(n, way, part) + 1):
                ring_out(piece, way, part, step).wait_send()
                core_out(piece, way, part, step).wait_send()
    for copy in out_copies:
        copy.wait()


def forward_call(n, visible, states, gains, masks, attn_b, ffn_b):
    count, width = states.shape
    rows_f = ffn_b.shape[2]
    f32, bf16 = jnp.float32, jnp.bfloat16
    vmem = pl.BlockSpec(memory_space=pltpu.VMEM)
    anywhere = pl.BlockSpec(memory_space=pl.ANY)
    shape = jax.ShapeDtypeStruct
    sems = pltpu.SemaphoreType.DMA((2 * LAYERS, 2, 2, n // 2))
    return pl.pallas_call(
        functools.partial(forward_kernel, n),
        out_shape=(
            shape((LAYERS, 4, width, width), bf16),
            shape((LAYERS, 2, rows_f * n, width), bf16),
            shape((count, width), f32),
            shape((LAYERS, count, width), bf16),
            shape((LAYERS, 3, count, width), bf16),
            shape((LAYERS, count, width), bf16),
            shape((LAYERS, 2, count, width), f32),
            shape((LAYERS, count, width), bf16),
            shape((LAYERS, n, count, rows_f), f32),
            shape((LAYERS, n, count, rows_f), bf16),
        ),
        in_specs=[vmem, vmem, vmem, vmem, anywhere, anywhere],
        out_specs=(anywhere, anywhere) + (vmem,) * 8,
        scratch_shapes=[
            pltpu.VMEM((LAYERS, 4, width, width), bf16),
            pltpu.VMEM((LAYERS, 2, rows_f * n, width), bf16),
            pltpu.VMEM((count, width), f32),
            pltpu.SemaphoreType.DMA((2 * LAYERS, 4)),
            pltpu.SemaphoreType.DMA((2 * LAYERS,)),
            sems,
            sems,
            sems,
            sems,
        ],
        compiler_params=pltpu.CompilerParams(
            collective_id=1, has_side_effects=True, vmem_limit_bytes=VMEM_LIMIT
        ),
        name="forward_layers",
    )(visible, states, gains, masks, attn_b, ffn_b)


def norm_back(grad, values, gain):
    normed, inverse = normed_of(values)
    scaled = grad * gain
    centred = scaled - jnp.mean(scaled, axis=-1, keepdims=True)
    result = inverse * (centred - normed * jnp.mean(scaled * normed, axis=-1, keepdims=True))
    return (
        result,
        jnp.sum(grad * normed, axis=0, keepdims=True),
        jnp.sum(grad, axis=0, keepdims=True),
    )


SLOTS = 3


def backward_kernel(
    n,
    visible_ref,
    grad_ref,
    first_ref,
    gains_ref,
    inputs_ref,
    proj_ref,
    mixed_ref,
    pre_ref,
    mid_ref,
    attn_full,
    ffn_full,
    slope_all,
    act_all,
    attn_sum,
    ffn_sum,
    grad_out,
    pair_out,
    wa,
    wf,
    slope,
    act,
    sum_a,
    sum_f,
    theirs_f,
    land_f,
    theirs_a,
    land_a,
    ring_a,
    ring_f,
    state,
    grad_rows,
    left_a,
    left_f,
    right_f,
    spread_a,
    spread_f,
    done_a,
    done_f,
    wa_sem,
    load_sem,
    core_send,
    core_recv,
    core_free,
    swap_send,
    swap_recv,
    swap_free,
    ring_send,
    ring_recv,
    ring_free,
    across_send,
    across_recv,
    out_sem,
    last_send,
    last_recv,
):
    spot = Spot(n)
    core = spot.core
    other = 1 - core
    rows_a = attn_sum.shape[2]
    rows_f = ffn_sum.shape[2]
    part_f = rows_f // 2
    order = (4, 3, -3, 2, -2, 1, -1, 0)
    total = LAYERS * n

    def rows_at(shard, rows):
        return pl.ds(pl.multiple_of(shard * rows, 16), rows)

    def remote(source, target, send, recv, device):
        return pltpu.make_async_remote_copy(
            src_ref=source,
            dst_ref=target,
            send_sem=send,
            recv_sem=recv,
            device_id=device,
            device_id_type=MESH,
        )

    def turn_of(turn):
        return LAYERS - 1 - turn // n, spot.shard(order[turn % n])

    def loads(turn):
        depth, shard = turn_of(turn)
        slot = turn % SLOTS
        return (
            pltpu.make_async_copy(
                ffn_full.at[depth, :, rows_at(shard, rows_f), :], wf.at[slot], load_sem.at[0, slot]
            ),
            pltpu.make_async_copy(slope_all.at[depth, shard], slope.at[slot], load_sem.at[1, slot]),
            pltpu.make_async_copy(act_all.at[depth, shard], act.at[slot], load_sem.at[2, slot]),
        )

    def load_attn(depth):
        return pltpu.make_async_copy(attn_full.at[depth], wa, wa_sem.at[0])

    def core_copy(turn):
        slot = turn % SLOTS
        return remote(
            theirs_f.at[slot],
            land_f.at[slot],
            core_send.at[turn],
            core_recv.at[turn],
            spot.partner,
        )

    def fold(turn):
        depth, shard = turn_of(turn)
        core_copy(turn).wait_recv()
        sum_f[depth, shard] = (
            sum_f[depth, shard].astype(jnp.float32)
            + land_f[turn % SLOTS].astype(jnp.float32)
        ).astype(jnp.bfloat16)
        if turn + SLOTS < total:
            pl.semaphore_signal(
                core_free.at[0], inc=1, device_id=spot.partner, device_id_type=MESH
            )

    def swap_copy(depth, part):
        return remote(
            theirs_a.at[part],
            land_a.at[part],
            swap_send.at[depth, part],
            swap_recv.at[depth, part],
            spot.partner,
        )

    def summed(piece, shard, part):
        kind, depth = piece % 2, piece // 2
        if kind == 0:
            return sum_a.at[depth, part, rows_at(shard, rows_a), :]
        return sum_f.at[depth, shard, pl.ds(part * part_f, part_f), :]

    def landed(piece, way, part, step):
        return (ring_a if piece % 2 == 0 else ring_f).at[way, part, step - 1]

    def ring_copy(piece, way, part, step):
        offset = last_step(n, way, part) - step + 1
        shard = spot.shard(offset if way == 0 else -offset)
        return remote(
            summed(piece, shard, part),
            landed(piece, way, part, step),
            ring_send.at[piece, way, part, step - 1],
            ring_recv.at[piece, way, part, step - 1],
            spot.ring[way],
        )

    def launch(piece, long):
        for way, part in WAYS:
            if (way == part) == long:
                if piece // 2 < LAYERS - 1:
                    pl.semaphore_wait(ring_free.at[piece % 2, way, part], 1)
                ring_copy(piece, way, part, 1).start()

    def relay(piece, step):
        for way, part in WAYS:
            last = last_step(n, way, part)
            if step < last:
                ring_copy(piece, way, part, step).wait_recv()
                shard = spot.shard(last - step if way == 0 else step - last)
                into = summed(piece, shard, part)
                into[...] = (
                    into[...].astype(jnp.float32)
                    + landed(piece, way, part, step)[...].astype(jnp.float32)
                ).astype(jnp.bfloat16)
                ring_copy(piece, way, part, step + 1).start()

    def across_copy(piece):
        kind, depth = piece % 2, piece // 2
        buffer = spread_a if kind == 0 else spread_f
        return remote(
            buffer.at[depth, 0],
            buffer.at[depth, 1],
            across_send.at[piece],
            across_recv.at[piece],
            spot.across,
        )

    def finish(piece):
        kind, depth = piece % 2, piece // 2
        for part in range(2):
            value = summed(piece, spot.mp, part)[...].astype(jnp.float32)
            for way in range(2):
                step = last_step(n, way, part)
                ring_copy(piece, way, part, step).wait_recv()
                value = value + landed(piece, way, part, step)[...].astype(jnp.float32)
            value = value.astype(jnp.bfloat16)
            if kind == 0:
                spread_a[depth, 0, part] = value
            else:
                spread_f[depth, 0, pl.ds(part * part_f, part_f), :] = value
            if depth > 0:
                for way in range(2):
                    pl.semaphore_signal(
                        ring_free.at[kind, way, part],
                        inc=1,
                        device_id=spot.ring[1 - way],
                        device_id_type=MESH,
                    )
        across_copy(piece).start()

    def out_copies(piece):
        kind, depth = piece % 2, piece // 2
        if kind == 0:
            source, target = done_a, attn_sum.at[depth, pl.ds(2 * core, 2)]
        else:
            source, target = done_f, ffn_sum.at[depth, core]
        return (
            pltpu.make_async_copy(source, target, out_sem.at[piece]),
            remote(source, target, last_send.at[piece], last_recv.at[piece], spot.partner),
        )

    def conclude(piece):
        kind, depth = piece % 2, piece // 2
        across_copy(piece).wait_recv()
        if depth < LAYERS - 1:
            local, away = out_copies(piece + 2)
            local.wait()
            away.wait_send()
        if kind == 0:
            done_a[...] = spread_a[depth, 0].astype(jnp.float32) + spread_a[depth, 1].astype(
                jnp.float32
            )
        else:
            done_f[...] = spread_f[depth, 0].astype(jnp.float32) + spread_f[depth, 1].astype(
                jnp.float32
            )
        for copy in out_copies(piece):
            copy.start()

    load_attn(LAYERS - 1).start()
    for turn in range(SLOTS):
        for copy in loads(turn):
            copy.start()
    greet((spot.ring[0], spot.ring[1], spot.partner, spot.across))
    state[...] = grad_ref[...]
    lanes = lax.broadcasted_iota(jnp.int32, (1, 128), 1) < 64
    visible = visible_ref[...] > 0.0

    def ffn_turn(turn):
        depth, shard = turn_of(turn)
        slot = turn % SLOTS
        for copy in loads(turn):
            copy.wait()
        grad_active = dot_nt(right_f[1], wf[slot, 1])
        left_f[0] = (grad_active * slope[slot]).astype(jnp.bfloat16)
        left_f[1] = act[slot]
        sum_f[depth, shard] = dot_tn(left_f[core], right_f[core]).astype(jnp.bfloat16)
        if turn >= SLOTS:
            core_copy(turn - SLOTS).wait_send()
        theirs_f[slot] = dot_tn(left_f[other], right_f[other]).astype(jnp.bfloat16)
        if turn >= SLOTS:
            pl.semaphore_wait(core_free.at[0], 1)
        core_copy(turn).start()
        state[...] += dot_nn(left_f[0], wf[slot, 0])
        if turn + SLOTS < total:
            for copy in loads(turn + SLOTS):
                copy.start()

    def head_pair(depth, pair):
        columns = pl.ds(pl.multiple_of(pair * 128, 128), 128)
        query = proj_ref[depth, 0, :, columns]
        keyed = proj_ref[depth, 1, :, columns]
        valued = proj_ref[depth, 2, :, columns]
        grad_mixed = grad_rows[4, :, columns]
        outs = []
        for side in range(2):
            mine = lanes if side == 0 else jnp.logical_not(lanes)
            scores = dot_nt(jnp.where(mine, query, jnp.zeros_like(query)), keyed) * 0.125
            scores = jnp.where(visible, scores, masked_score)
            expo = jnp.exp(scores - jnp.max(scores, axis=-1, keepdims=True))
            probs = expo / jnp.sum(expo, axis=-1, keepdims=True)
            grad_probs = dot_nt(jnp.where(mine, grad_mixed, jnp.zeros_like(query)), valued)
            inner = jnp.sum(grad_probs * probs, axis=-1, keepdims=True)
            grad_scores = (probs * (grad_probs - inner)).astype(jnp.bfloat16)
            outs.append(
                (
                    dot_nn(grad_scores, keyed) * 0.125,
                    dot_tn(grad_scores, query) * 0.125,
                    dot_tn(probs.astype(jnp.bfloat16), grad_mixed),
                )
            )
        for which in range(3):
            grad_rows[which, :, columns] = jnp.where(
                lanes, outs[0][which], outs[1][which]
            ).astype(jnp.bfloat16)

    def layer(depth, hooks):
        base = (LAYERS - 1 - depth) * n
        piece_a, piece_f = 2 * depth, 2 * depth + 1
        grad_two, pair_out[2 + 2 * depth, 0:1, :], pair_out[2 + 2 * depth, 1:2, :] = norm_back(
            state[...], pre_ref[depth, 1], gains_ref[2 + 2 * depth, 0:1, :]
        )
        state[...] = grad_two
        right_f[0] = mid_ref[depth]
        right_f[1] = grad_two.astype(jnp.bfloat16)
        for step in range(n):
            ffn_turn(base + step)
            if step >= 1:
                fold(base + step - 1)
            if step == 1:
                launch(piece_f, True)
            if step == 3:
                launch(piece_f, False)
            hooks.get(("ffn", step), lambda: None)()
        fold(base + n - 1)
        hooks.get("middle", lambda: None)()
        grad_one, pair_out[1 + 2 * depth, 0:1, :], pair_out[1 + 2 * depth, 1:2, :] = norm_back(
            state[...], pre_ref[depth, 0], gains_ref[1 + 2 * depth, 0:1, :]
        )
        state[...] = grad_one
        grad_rows[3] = grad_one.astype(jnp.bfloat16)
        load_attn(depth).wait()
        grad_rows[4] = dot_nt(grad_rows[3], wa[3]).astype(jnp.bfloat16)

        @pl.loop(0, HEADS // 2)
        def _(pair):
            head_pair(depth, pair)

        hooks.get("heads", lambda: None)()
        left_a[0] = inputs_ref[depth]
        left_a[1] = mixed_ref[depth]
        for part in range(2):
            if depth < LAYERS - 1:
                swap_copy(depth + 1, part).wait_send()
            left = 0 if part == 0 else other
            theirs_a[part] = dot_tn(left_a[left], grad_rows[2 * other + part]).astype(jnp.bfloat16)
            if depth < LAYERS - 1:
                pl.semaphore_wait(swap_free.at[part], 1)
            swap_copy(depth, part).start()
        for part in range(2):
            left = 0 if part == 0 else core
            sum_a[depth, part] = dot_tn(left_a[left], grad_rows[2 * core + part]).astype(
                jnp.bfloat16
            )
        hooks.get("mats", lambda: None)()
        for part in range(2):
            swap_copy(depth, part).wait_recv()

            @pl.loop(0, n)
            def _(block):
                rows = rows_at(block, rows_a)
                sum_a[depth, part, rows, :] = (
                    sum_a[depth, part, rows, :].astype(jnp.float32)
                    + land_a[part, rows, :].astype(jnp.float32)
                ).astype(jnp.bfloat16)

            if depth > 0:
                pl.semaphore_signal(
                    swap_free.at[part], inc=1, device_id=spot.partner, device_id_type=MESH
                )
        launch(piece_a, True)
        launch(piece_a, False)
        for which in range(3):
            state[...] += dot_nt(grad_rows[which], wa[which])
        if depth > 0:
            load_attn(depth - 1).start()

    layer(
        1,
        {
            "middle": lambda: relay(3, 1),
            "heads": lambda: relay(3, 2),
        },
    )
    relay(3, 3)
    finish(3)
    layer(
        0,
        {
            ("ffn", 3): lambda: relay(2, 1),
            ("ffn", 5): lambda: conclude(3),
            "middle": lambda: relay(2, 2),
            "heads": lambda: relay(1, 1),
            "mats": lambda: (relay(2, 3), finish(2)),
        },
    )
    grad_sum, pair_out[0, 0:1, :], pair_out[0, 1:2, :] = norm_back(
        state[...], first_ref[...], gains_ref[0, 0:1, :]
    )
    grad_out[...] = grad_sum
    relay(1, 2)
    conclude(2)
    relay(0, 1)
    relay(1, 3)
    relay(0, 2)
    finish(1)
    relay(0, 3)
    conclude(1)
    finish(0)
    conclude(0)
    for turn in range(total - SLOTS, total):
        core_copy(turn).wait_send()
    for part in range(2):
        swap_copy(0, part).wait_send()
    for piece in range(2 * LAYERS):
        for way, part in WAYS:
            for step in range(1, last_step(n, way, part) + 1):
                ring_copy(piece, way, part, step).wait_send()
        across_copy(piece).wait_send()
        local, away = out_copies(piece)
        if piece < 2:
            local.wait()
            away.wait_send()
        away.wait_recv()


def backward_call(n, visible, grad, first, gains, kept, attn_full, ffn_full, slope, act):
    count, width = grad.shape
    rows_f = ffn_full.shape[2] // n
    rows_a = attn_full.shape[2] // n
    f32, bf16 = jnp.float32, jnp.bfloat16
    vmem = pl.BlockSpec(memory_space=pltpu.VMEM)
    anywhere = pl.BlockSpec(memory_space=pl.ANY)
    shape = jax.ShapeDtypeStruct
    dma = pltpu.SemaphoreType.DMA
    regular = pltpu.SemaphoreType.REGULAR
    ring_sems = dma((2 * LAYERS, 2, 2, n // 2))
    return pl.pallas_call(
        functools.partial(backward_kernel, n),
        out_shape=(
            shape((LAYERS, 4, rows_a, width), f32),
            shape((LAYERS, 2, rows_f, width), f32),
            shape((count, width), f32),
            shape(gains.shape, f32),
        ),
        in_specs=[vmem] * 9 + [anywhere] * 4,
        out_specs=(anywhere, anywhere, vmem, vmem),
        scratch_shapes=[
            pltpu.VMEM((4, width, width), bf16),
            pltpu.VMEM((SLOTS, 2, rows_f, width), bf16),
            pltpu.VMEM((SLOTS, count, rows_f), f32),
            pltpu.VMEM((SLOTS, count, rows_f), bf16),
            pltpu.VMEM((LAYERS, 2, width, width), bf16),
            pltpu.VMEM((LAYERS, n, rows_f, width), bf16),
            pltpu.VMEM((SLOTS, rows_f, width), bf16),
            pltpu.VMEM((SLOTS, rows_f, width), bf16),
            pltpu.VMEM((2, width, width), bf16),
            pltpu.VMEM((2, width, width), bf16),
            pltpu.VMEM((2, 2, n // 2, rows_a, width), bf16),
            pltpu.VMEM((2, 2, n // 2, rows_f // 2, width), bf16),
            pltpu.VMEM((count, width), f32),
            pltpu.VMEM((5, count, width), bf16),
            pltpu.VMEM((2, count, width), bf16),
            pltpu.VMEM((2, count, rows_f), bf16),
            pltpu.VMEM((2, count, width), bf16),
            pltpu.VMEM((LAYERS, 2, 2, rows_a, width), bf16),
            pltpu.VMEM((LAYERS, 2, rows_f, width), bf16),
            pltpu.VMEM((2, rows_a, width), f32),
            pltpu.VMEM((rows_f, width), f32),
            dma((1,)),
            dma((3, SLOTS)),
            dma((LAYERS * n,)),
            dma((LAYERS * n,)),
            regular((1,)),
            dma((LAYERS, 2)),
            dma((LAYERS, 2)),
            regular((2,)),
            ring_sems,
            ring_sems,
            regular((2, 2, 2)),
            dma((2 * LAYERS,)),
            dma((2 * LAYERS,)),
            dma((2 * LAYERS,)),
            dma((2 * LAYERS,)),
            dma((2 * LAYERS,)),
        ],
        compiler_params=pltpu.CompilerParams(
            collective_id=2, has_side_effects=True, vmem_limit_bytes=VMEM_LIMIT
        ),
        name="backward_layers",
    )(visible, grad, first, gains, *kept, attn_full, ffn_full, slope, act)


def merged(value, axis, join):
    pieces = jax.tree.map(lambda part: lax.all_gather(part, axis), value)
    head = jax.tree.map(lambda part: part[0], pieces)
    tail = jax.tree.map(lambda part: part[1:], pieces)
    total, _ = lax.scan(lambda total, section: (join(total, section), None), head, tail)
    return total


def sinusoid(count, width):
    places = jnp.arange(count, dtype=jnp.float32)[:, None]
    freqs = jnp.exp(jnp.arange(width // 2, dtype=jnp.float32) * (-2.0 * math.log(10000.0) / width))
    angles = places * freqs[None, :]
    return jnp.concatenate([jnp.sin(angles), jnp.cos(angles)], axis=1)


def layer_norm(values, gain, shift):
    centre = jnp.mean(values, axis=-1, keepdims=True)
    offset = values - centre
    spread = jnp.mean(offset * offset, axis=-1, keepdims=True)
    inverse = lax.rsqrt(spread + norm_eps)
    normed = offset * inverse
    return (normed * gain + shift, (normed, inverse))


def norm_backward(grad, saved, gain):
    normed, inverse = saved
    scaled = grad * gain
    centred = scaled - jnp.mean(scaled, axis=-1, keepdims=True)
    result = inverse * (centred - normed * jnp.mean(scaled * normed, axis=-1, keepdims=True))
    return (result, jnp.stack([jnp.sum(grad * normed, axis=0), jnp.sum(grad, axis=0)]))


def gelu_exact(values):
    return jax.nn.gelu(values, approximate=False)


def gelu_back(hidden, grad):
    unused, pullback = jax.vjp(gelu_exact, hidden)
    return pullback(grad)[0]


def masked_scores(query, keyed, length):
    scale = query.shape[-1] ** (-0.5)
    scores = jnp.einsum("hqe,hke->hqk", query, keyed, preferred_element_type=jnp.float32) * scale
    visible = jnp.arange(keyed.shape[1]) < length
    return jnp.where(visible[None, None, :], scores, masked_score)


def fetch_forward(attn_part, ffn_part):
    return (
        lax.all_gather(attn_part, "mp", axis=1, tiled=True),
        lax.all_gather(ffn_part, "mp", axis=1, tiled=True),
    )


def fetch_backward(attn_part, ffn_part):
    return (
        lax.all_gather(attn_part, "mp", axis=1, tiled=True),
        lax.all_gather(ffn_part, "mp", axis=1, tiled=True),
    )


def reduce_layer(attn_grad, ffn_grad):
    return (
        lax.psum_scatter(attn_grad, "mp", scatter_dimension=1, tiled=True),
        lax.psum_scatter(ffn_grad, "mp", scatter_dimension=1, tiled=True),
    )


def ffn_forward(middle_b, ffn_w, unit_mask):
    hidden = jnp.einsum("td,fd->tf", middle_b, ffn_w[0], preferred_element_type=jnp.float32)
    active = (gelu_exact(hidden) * unit_mask[None, :]).astype(jnp.bfloat16)
    output = jnp.einsum("tf,fd->td", active, ffn_w[1], preferred_element_type=jnp.float32)
    return (hidden, active, output)


def ffn_backward(grad_out, middle_b, hidden, active, ffn_w, unit_mask):
    grad_active = jnp.einsum("td,fd->tf", grad_out, ffn_w[1], preferred_element_type=jnp.float32)
    grad_hidden = gelu_back(hidden, grad_active * unit_mask[None, :]).astype(jnp.bfloat16)
    up_grad = jnp.einsum("tf,td->fd", grad_hidden, middle_b, preferred_element_type=jnp.float32)
    down_grad = jnp.einsum("tf,td->fd", active, grad_out, preferred_element_type=jnp.float32)
    from_ffn = jnp.einsum("tf,fd->td", grad_hidden, ffn_w[0], preferred_element_type=jnp.float32)
    return (jnp.stack([up_grad, down_grad]), from_ffn)


def layer_forward(states, attn_w, ffn_w, pair, length, unit_mask):
    count = states.shape[0]
    inputs = states.astype(jnp.bfloat16)
    projected = jnp.einsum(
        "td,kde->kte", inputs, attn_w[:3], preferred_element_type=jnp.float32
    ).astype(jnp.bfloat16)
    heads = projected.reshape(3, count, HEADS, -1).transpose(0, 2, 1, 3)
    scores = masked_scores(heads[0], heads[1], length)
    peak = jnp.max(scores, axis=-1, keepdims=True)
    expo = jnp.exp(scores - peak)
    total = jnp.sum(expo, axis=-1, keepdims=True)
    log_total = peak + jnp.log(total)
    probs = (expo / total).astype(jnp.bfloat16)
    mixed = jnp.einsum("hqk,hke->hqe", probs, heads[2], preferred_element_type=jnp.float32)
    mixed = mixed.transpose(1, 0, 2).reshape(count, -1).astype(jnp.bfloat16)
    branch = jnp.dot(mixed, attn_w[3], preferred_element_type=jnp.float32)
    middle, norm_one = layer_norm(states + branch, pair[0, 0], pair[0, 1])
    middle_b = middle.astype(jnp.bfloat16)
    hidden, active, output = ffn_forward(middle_b, ffn_w, unit_mask)
    result, norm_two = layer_norm(middle + output, pair[1, 0], pair[1, 1])
    return (result, (inputs, heads, log_total, mixed, norm_one, middle_b, hidden, active, norm_two))


def layer_backward(grad, attn_w, ffn_w, pair, length, unit_mask, kept):
    inputs, heads, log_total, mixed, norm_one, middle_b, hidden, active, norm_two = kept
    count = inputs.shape[0]
    grad_two, pair_two = norm_backward(grad, norm_two, pair[1, 0])
    ffn_grad, from_ffn = ffn_backward(
        grad_two.astype(jnp.bfloat16), middle_b, hidden, active, ffn_w, unit_mask
    )
    grad_one, pair_one = norm_backward(grad_two + from_ffn, norm_one, pair[0, 0])
    grad_branch = grad_one.astype(jnp.bfloat16)
    output_grad = jnp.einsum("td,te->de", mixed, grad_branch, preferred_element_type=jnp.float32)
    grad_mixed = jnp.einsum("te,de->td", grad_branch, attn_w[3], preferred_element_type=jnp.float32)
    grad_mixed = grad_mixed.astype(jnp.bfloat16).reshape(count, HEADS, -1).transpose(1, 0, 2)
    scale = heads.shape[-1] ** (-0.5)
    probs = jnp.exp(masked_scores(heads[0], heads[1], length) - log_total)
    grad_values = jnp.einsum(
        "hqk,hqe->hke", probs.astype(jnp.bfloat16), grad_mixed, preferred_element_type=jnp.float32
    )
    grad_probs = jnp.einsum(
        "hqe,hke->hqk", grad_mixed, heads[2], preferred_element_type=jnp.float32
    )
    grad_scores = probs * (grad_probs - jnp.sum(grad_probs * probs, axis=-1, keepdims=True))
    grad_scores = grad_scores.astype(jnp.bfloat16)
    grad_query = (
        jnp.einsum("hqk,hke->hqe", grad_scores, heads[1], preferred_element_type=jnp.float32)
        * scale
    )
    grad_key = (
        jnp.einsum("hqk,hqe->hke", grad_scores, heads[0], preferred_element_type=jnp.float32)
        * scale
    )
    stacked = (
        jnp.stack([grad_query, grad_key, grad_values]).transpose(0, 2, 1, 3).reshape(3, count, -1)
    )
    stacked = stacked.astype(jnp.bfloat16)
    input_grad = jnp.einsum("td,kte->kde", inputs, stacked, preferred_element_type=jnp.float32)
    from_attn = jnp.einsum("kte,kde->td", stacked, attn_w[:3], preferred_element_type=jnp.float32)
    attn_grad = jnp.concatenate([input_grad, output_grad[None]], axis=0)
    return (grad_one + from_attn, attn_grad, ffn_grad, jnp.stack([pair_one, pair_two]))


def adamw(weight, moment_one, moment_two, grad, decay, rate):
    moment_one = beta_one * moment_one + (1.0 - beta_one) * grad
    moment_two = beta_two * moment_two + (1.0 - beta_two) * grad * grad
    fixed_one = moment_one / (1.0 - beta_one**STEP)
    fixed_two = moment_two / (1.0 - beta_two**STEP)
    weight = weight - rate * (fixed_one / (jnp.sqrt(fixed_two) + adam_eps) + decay * weight)
    return (moment_one, moment_two, weight)


def combine_vocab(first, second):
    peak = jnp.maximum(first[0], second[0])
    total = first[1] * jnp.exp(first[0] - peak) + second[1] * jnp.exp(second[0] - peak)
    return (peak, total, first[2] + second[2])


def local_general(
    tokens,
    lengths,
    places,
    targets,
    ramp,
    attn,
    attn_m,
    attn_v,
    ffn,
    ffn_m,
    ffn_v,
    table,
    table_m,
    table_v,
    out_table,
    out_m,
    out_v,
    gains,
    gains_m,
    gains_v,
):
    rank = lax.axis_index("mp")
    count = tokens.shape[2]
    flat_ids = tokens.reshape(-1)
    all_lengths = lengths.reshape(-1)
    length = lax.dynamic_index_in_dim(all_lengths, rank, keepdims=False)
    masks = jnp.minimum(ramp, RAMP).astype(jnp.float32) / RAMP
    unit_masks = [masks[depth] for depth in range(LAYERS)]
    looked = jnp.take(table, flat_ids, axis=0)
    embedded = lax.all_to_all(looked, "mp", split_axis=0, concat_axis=1, tiled=True)
    states, norm_zero = layer_norm(
        embedded + sinusoid(count, embedded.shape[1]), gains[0, 0], gains[0, 1]
    )
    kept_all = []
    weights_all = []
    for depth in range(LAYERS):
        attn_w, ffn_w = fetch_forward(
            attn[depth].astype(jnp.bfloat16), ffn[depth].astype(jnp.bfloat16)
        )
        states, kept = layer_forward(
            states, attn_w, ffn_w, gains[1 + 2 * depth : 3 + 2 * depth], length, unit_masks[depth]
        )
        kept_all.append(kept)
        weights_all.append(None)
    spots = places.reshape(-1)
    picked = jnp.take(states, spots, axis=0).astype(jnp.bfloat16)
    picked_all = lax.all_gather(picked, "mp", axis=0, tiled=True)
    out_b = out_table.astype(jnp.bfloat16)
    logits = jnp.einsum("rd,vd->rv", picked_all, out_b, preferred_element_type=jnp.float32)
    labels = targets.reshape(-1)
    columns = rank * out_table.shape[0] + jnp.arange(out_table.shape[0])
    hits = (labels[:, None] == columns[None, :]).astype(jnp.float32)
    peak = jnp.max(logits, axis=1)
    expsum = jnp.sum(jnp.exp(logits - peak[:, None]), axis=1)
    target_part = jnp.sum(hits * logits, axis=1)
    peak_all, expsum_all, target_all = merged((peak, expsum, target_part), "mp", combine_vocab)
    log_total = peak_all + jnp.log(expsum_all)
    slot_count = targets.shape[2]
    counted = jnp.maximum(1, all_lengths * slot_count // count)
    valid = (jnp.arange(slot_count)[None, :] < counted[:, None]).reshape(-1)
    loss_pair = jnp.stack(
        [
            jnp.sum(jnp.where(valid, log_total - target_all, 0.0)),
            jnp.sum(counted).astype(jnp.float32),
        ]
    )
    grad_logits = jnp.where(
        valid[:, None], jnp.exp(logits - log_total[:, None]) - hits, 0.0
    ).astype(jnp.bfloat16)
    out_grad = jnp.einsum("rv,rd->vd", grad_logits, picked_all, preferred_element_type=jnp.float32)
    picked_grad = lax.psum_scatter(
        jnp.dot(grad_logits, out_b, preferred_element_type=jnp.float32),
        "mp",
        scatter_dimension=0,
        tiled=True,
    )
    grad = jnp.zeros_like(states).at[spots].add(picked_grad)
    attn_parts = [None] * LAYERS
    ffn_parts = [None] * LAYERS
    pair_grads = [None] * LAYERS
    for depth in reversed(range(LAYERS)):
        attn_w, ffn_w = fetch_backward(
            attn[depth].astype(jnp.bfloat16), ffn[depth].astype(jnp.bfloat16)
        )
        grad, attn_grad, ffn_grad, pair_grad = layer_backward(
            grad,
            attn_w,
            ffn_w,
            gains[1 + 2 * depth : 3 + 2 * depth],
            length,
            unit_masks[depth],
            kept_all[depth],
        )
        attn_parts[depth], ffn_parts[depth] = reduce_layer(attn_grad, ffn_grad)
        pair_grads[depth] = pair_grad
    grad_sum, zero_grad = norm_backward(grad, norm_zero, gains[0, 0])
    returned = lax.all_to_all(grad_sum, "mp", split_axis=1, concat_axis=0, tiled=True)
    table_grad = jnp.zeros_like(table).at[flat_ids].add(returned)
    gains_grad = jnp.concatenate([zero_grad[None]] + pair_grads, axis=0)
    attn_sum, ffn_sum, table_sum, out_sum, gains_part, loss = lax.psum(
        (jnp.stack(attn_parts), jnp.stack(ffn_parts), table_grad, out_grad, gains_grad, loss_pair),
        "dp",
    )
    shard_squares = (
        jnp.sum(attn_sum * attn_sum)
        + jnp.sum(ffn_sum * ffn_sum)
        + jnp.sum(table_sum * table_sum)
        + jnp.sum(out_sum * out_sum)
    )
    square_total, gains_sum = lax.psum((shard_squares, gains_part), "mp")
    grad_norm = jnp.sqrt(square_total + jnp.sum(gains_sum * gains_sum))
    factor = clip_limit / jnp.maximum(grad_norm, clip_limit)
    attn_m_new, attn_v_new, attn_new = adamw(
        attn, attn_m, attn_v, attn_sum * factor, weight_decay, learn_rate
    )
    ffn_m_new, ffn_v_new, ffn_new = adamw(
        ffn, ffn_m, ffn_v, ffn_sum * factor, weight_decay, learn_rate
    )
    table_m_new, table_v_new, table_new = adamw(
        table, table_m, table_v, table_sum * factor, weight_decay, learn_rate
    )
    out_m_new, out_v_new, out_new = adamw(
        out_table, out_m, out_v, out_sum * factor, weight_decay, learn_rate
    )
    gains_m_new, gains_v_new, gains_new = adamw(
        gains, gains_m, gains_v, gains_sum * factor, 0.0, gain_rate
    )
    return (
        loss,
        grad_norm.reshape(1),
        attn_m_new,
        attn_v_new,
        attn_new,
        ffn_m_new,
        ffn_v_new,
        ffn_new,
        table_m_new,
        table_v_new,
        table_new,
        out_m_new,
        out_v_new,
        out_new,
        gains_m_new,
        gains_v_new,
        gains_new,
    )


def local(
    tokens,
    lengths,
    places,
    targets,
    ramp,
    attn,
    attn_m,
    attn_v,
    ffn,
    ffn_m,
    ffn_v,
    table,
    table_m,
    table_v,
    out_table,
    out_m,
    out_v,
    gains,
    gains_m,
    gains_v,
):
    rank = lax.axis_index("mp")
    count = tokens.shape[2]
    flat_ids = tokens.reshape(-1)
    all_lengths = lengths.reshape(-1)
    length = lax.dynamic_index_in_dim(all_lengths, rank, keepdims=False)
    masks = jnp.minimum(ramp, RAMP).astype(jnp.float32) / RAMP
    looked = jnp.take(table, flat_ids, axis=0)
    embedded = lax.all_to_all(looked, "mp", split_axis=0, concat_axis=1, tiled=True)
    first = embedded + sinusoid(count, embedded.shape[1])
    states, _ = layer_norm(first, gains[0, 0], gains[0, 1])
    n = attn.shape[3] // attn.shape[2]
    visible = (jnp.arange(count) < length).astype(jnp.float32)[None, :]
    attn_full, ffn_full, states, *kept, slope, act = forward_call(
        n, visible, states, gains, masks, attn.astype(jnp.bfloat16), ffn.astype(jnp.bfloat16)
    )
    spots = places.reshape(-1)
    picked = jnp.take(states, spots, axis=0).astype(jnp.bfloat16)
    picked_all = lax.all_gather(picked, "mp", axis=0, tiled=True)
    out_b = out_table.astype(jnp.bfloat16)
    logits = jnp.einsum("rd,vd->rv", picked_all, out_b, preferred_element_type=jnp.float32)
    labels = targets.reshape(-1)
    columns = rank * out_table.shape[0] + jnp.arange(out_table.shape[0])
    hits = (labels[:, None] == columns[None, :]).astype(jnp.float32)
    peak = jnp.max(logits, axis=1)
    expsum = jnp.sum(jnp.exp(logits - peak[:, None]), axis=1)
    target_part = jnp.sum(hits * logits, axis=1)
    peak_all, expsum_all, target_all = merged((peak, expsum, target_part), "mp", combine_vocab)
    log_total = peak_all + jnp.log(expsum_all)
    slot_count = targets.shape[2]
    counted = jnp.maximum(1, all_lengths * slot_count // count)
    valid = (jnp.arange(slot_count)[None, :] < counted[:, None]).reshape(-1)
    loss_pair = jnp.stack(
        [
            jnp.sum(jnp.where(valid, log_total - target_all, 0.0)),
            jnp.sum(counted).astype(jnp.float32),
        ]
    )
    grad_logits = jnp.where(
        valid[:, None], jnp.exp(logits - log_total[:, None]) - hits, 0.0
    ).astype(jnp.bfloat16)
    out_grad = jnp.einsum("rv,rd->vd", grad_logits, picked_all, preferred_element_type=jnp.float32)
    picked_grad = lax.psum_scatter(
        jnp.dot(grad_logits, out_b, preferred_element_type=jnp.float32),
        "mp",
        scatter_dimension=0,
        tiled=True,
    )
    grad = jnp.zeros_like(states).at[spots].add(picked_grad)
    attn_sum, ffn_sum, grad_sum, gains_grad = backward_call(
        n, visible, grad, first, gains, kept, attn_full, ffn_full, slope, act
    )
    returned = lax.all_to_all(grad_sum, "mp", split_axis=1, concat_axis=0, tiled=True)
    table_grad = jnp.zeros_like(table).at[flat_ids].add(returned)
    table_sum, out_sum, gains_part, loss = lax.psum(
        (table_grad, out_grad, gains_grad, loss_pair),
        "dp",
    )
    shard_squares = (
        jnp.sum(attn_sum * attn_sum)
        + jnp.sum(ffn_sum * ffn_sum)
        + jnp.sum(table_sum * table_sum)
        + jnp.sum(out_sum * out_sum)
    )
    square_total, gains_sum = lax.psum((shard_squares, gains_part), "mp")
    grad_norm = jnp.sqrt(square_total + jnp.sum(gains_sum * gains_sum))
    factor = clip_limit / jnp.maximum(grad_norm, clip_limit)
    attn_m_new, attn_v_new, attn_new = adamw(
        attn, attn_m, attn_v, attn_sum * factor, weight_decay, learn_rate
    )
    ffn_m_new, ffn_v_new, ffn_new = adamw(
        ffn, ffn_m, ffn_v, ffn_sum * factor, weight_decay, learn_rate
    )
    table_m_new, table_v_new, table_new = adamw(
        table, table_m, table_v, table_sum * factor, weight_decay, learn_rate
    )
    out_m_new, out_v_new, out_new = adamw(
        out_table, out_m, out_v, out_sum * factor, weight_decay, learn_rate
    )
    gains_m_new, gains_v_new, gains_new = adamw(
        gains, gains_m, gains_v, gains_sum * factor, 0.0, gain_rate
    )
    return (
        loss,
        grad_norm.reshape(1),
        attn_m_new,
        attn_v_new,
        attn_new,
        ffn_m_new,
        ffn_v_new,
        ffn_new,
        table_m_new,
        table_v_new,
        table_new,
        out_m_new,
        out_v_new,
        out_new,
        gains_m_new,
        gains_v_new,
        gains_new,
    )


def solution(mesh):
    in_specs = (
        P("dp", None, None),
        P("dp", None),
        P("dp", "mp", None),
        P("dp", None, None),
        P(),
        P(None, None, "mp", None),
        P(None, None, "mp", None),
        P(None, None, "mp", None),
        P(None, None, "mp", None),
        P(None, None, "mp", None),
        P(None, None, "mp", None),
        P(None, "mp"),
        P(None, "mp"),
        P(None, "mp"),
        P("mp", None),
        P("mp", None),
        P("mp", None),
        P(),
        P(),
        P(),
    )
    out_specs = (
        P(),
        P(),
        P(None, None, "mp", None),
        P(None, None, "mp", None),
        P(None, None, "mp", None),
        P(None, None, "mp", None),
        P(None, None, "mp", None),
        P(None, None, "mp", None),
        P(None, "mp"),
        P(None, "mp"),
        P(None, "mp"),
        P("mp", None),
        P("mp", None),
        P("mp", None),
        P(),
        P(),
        P(),
    )
    fits = mesh.shape['mp'] == 8 and mesh.shape['dp'] == 4
    chosen = local if fits else local_general
    return jax.shard_map(chosen, mesh=mesh, in_specs=in_specs, out_specs=out_specs, check_vma=False)
```

```python
import functools
import math

import jax
import jax.numpy as jnp
from jax import lax
from jax.experimental import pallas as pl
from jax.experimental.pallas import tpu as pltpu
from jax.sharding import PartitionSpec as P

HEADS = 12
LAYERS = 2
STEP = 10
RAMP = 4


norm_eps = 1e-05
beta_one = 0.9
beta_two = 0.999
learn_rate = 0.02
gain_rate = 0.3
weight_decay = 0.01
adam_eps = 1e-08
clip_limit = 1.0
masked_score = -1000000000.0


MESH = pl.DeviceIdType.MESH
VMEM_LIMIT = 60 * 1024 * 1024
SLOTS = 3


def dot_nn(left, right):
    return lax.dot_general(
        left, right, (((1,), (0,)), ((), ())), preferred_element_type=jnp.float32
    )


def dot_nt(left, right):
    return lax.dot_general(
        left, right, (((1,), (1,)), ((), ())), preferred_element_type=jnp.float32
    )


def dot_tn(left, right):
    return lax.dot_general(
        left, right, (((0,), (0,)), ((), ())), preferred_element_type=jnp.float32
    )


def ring_index(place, n):
    late = place // (n // 2)
    return (1 - late) * 2 * place + late * (2 * (n - 1 - place) + 1)


def ring_place(index, n):
    odd = index % 2
    return (1 - odd) * (index // 2) + odd * (n - 1 - index // 2)


class Spot:
    def __init__(self, n):
        self.n = n
        self.dp = lax.axis_index("dp")
        self.mp = lax.axis_index("mp")
        self.core = self.dp % 2
        self.place = ring_place(self.mp, n)
        self.partner = (self.dp + 1 - 2 * self.core, self.mp)
        self.across = ((self.dp + 2) % 4, self.mp)
        self.ring = (
            (self.dp, ring_index((self.place + 1) % n, n)),
            (self.dp, ring_index((self.place + n - 1) % n, n)),
        )

    def shard(self, offset):
        return ring_index((self.place + offset + self.n) % self.n, self.n)


def greet(devices):
    barrier = pltpu.get_barrier_semaphore()
    for device in devices:
        pl.semaphore_signal(barrier, inc=1, device_id=device, device_id_type=MESH)
    pl.semaphore_wait(barrier, len(devices))


def last_step(n, way, part):
    return n // 2 if way == part else n // 2 - 1


WAYS = ((0, 0), (1, 1), (0, 1), (1, 0))


def normed_of(values):
    centre = jnp.mean(values, axis=-1, keepdims=True)
    offset = values - centre
    spread = jnp.mean(offset * offset, axis=-1, keepdims=True)
    inverse = lax.rsqrt(spread + norm_eps)
    return offset * inverse, inverse


def forward_kernel(
    n,
    ids_ref,
    table_ref,
    where_ref,
    visible_ref,
    gains_ref,
    mask_ref,
    places_ref,
    labels_ref,
    valid_ref,
    out_ref,
    attn_sh,
    ffn_sh,
    attn_full,
    ffn_full,
    first_ref,
    inputs_ref,
    proj_ref,
    mixed_ref,
    pre_ref,
    mid_ref,
    slope_ref,
    act_ref,
    grad_ref,
    out_grad_ref,
    loss_ref,
    wa,
    wf,
    raw_a,
    raw_f,
    slope,
    act,
    state,
    row_out,
    row_in,
    picked,
    stats,
    back_out,
    back_in,
    raw_sem,
    out_sem,
    kept_sem,
    ring_send,
    ring_recv,
    core_send,
    core_recv,
    fan_send,
    fan_recv,
):
    spot = Spot(n)
    core = spot.core
    rows_a = attn_sh.shape[2]
    rows_f = ffn_sh.shape[2]
    part_f = rows_f // 2
    steps = n // 2
    count = first_ref.shape[0]
    columns_own = table_ref.shape[1]
    slots = places_ref.shape[0]

    def rows_at(shard, rows):
        return pl.ds(pl.multiple_of(shard * rows, 16), rows)

    def remote(source, target, send, recv, device):
        return pltpu.make_async_remote_copy(
            src_ref=source,
            dst_ref=target,
            send_sem=send,
            recv_sem=recv,
            device_id=device,
            device_id_type=MESH,
        )

    def chunk(piece, shard, part, side):
        kind, depth = piece % 2, piece // 2
        if kind == 0:
            return wa.at[depth, 2 * side + part, rows_at(shard, rows_a), :]
        start = pl.multiple_of(shard * rows_f + part * part_f, 16)
        return wf.at[depth, side, pl.ds(start, part_f), :]

    def sign(way):
        return -1 if way == 0 else 1

    def ring_copy(piece, way, part, step, arriving):
        target = chunk(piece, spot.shard(sign(way) * (step - 1 + arriving)), part, core)
        return remote(
            target,
            target,
            ring_send.at[piece, way, part, step - 1],
            ring_recv.at[piece, way, part, step - 1],
            spot.ring[way],
        )

    def core_copy(piece, way, part, step, side):
        target = chunk(piece, spot.shard(sign(way) * step), part, side)
        return remote(
            target,
            target,
            core_send.at[piece, way, part, step - 1],
            core_recv.at[piece, way, part, step - 1],
            spot.partner,
        )

    def peer(offset):
        return (spot.mp + offset + n) % n

    def fan_copy(which, offset, source, target):
        return remote(
            source,
            target,
            fan_send.at[which, offset - 1],
            fan_recv.at[which, offset - 1],
            (spot.dp, peer(offset)),
        )

    def share(which, buffer, offset):
        return fan_copy(which, offset, buffer.at[spot.mp], buffer.at[spot.mp])

    def arrived(which, buffer, offset):
        return fan_copy(which, offset, buffer.at[peer(-offset)], buffer.at[peer(-offset)])

    def deal(which, source, target, offset):
        return fan_copy(which, offset, source.at[peer(offset)], target.at[spot.mp])

    def raw_copy(piece):
        kind, depth = piece % 2, piece // 2
        if kind == 0:
            return pltpu.make_async_copy(attn_sh.at[depth], raw_a.at[depth], raw_sem.at[piece])
        return pltpu.make_async_copy(ffn_sh.at[depth], raw_f.at[depth], raw_sem.at[piece])

    def take_own(piece):
        kind, depth = piece % 2, piece // 2
        raw_copy(piece).wait()
        if kind == 0:
            for which in range(4):
                wa[depth, which, rows_at(spot.mp, rows_a), :] = raw_a[depth, which].astype(
                    jnp.bfloat16
                )
        else:
            for which in range(2):
                wf[depth, which, rows_at(spot.mp, rows_f), :] = raw_f[depth, which].astype(
                    jnp.bfloat16
                )

    def launch(piece):
        for way, part in WAYS:
            ring_copy(piece, way, part, 1, 0).start()

    def pass_on(piece, step):
        for way, part in WAYS:
            if step <= last_step(n, way, part):
                ring_copy(piece, way, part, step, 1).wait_recv()
                if step < last_step(n, way, part):
                    ring_copy(piece, way, part, step + 1, 0).start()
                core_copy(piece, way, part, step, core).start()

    def settle(piece, step):
        for way, part in WAYS:
            if step <= last_step(n, way, part):
                core_copy(piece, way, part, step, 1 - core).wait_recv()

    def look_up(offset):
        whose = peer(offset)

        @pl.loop(0, count // 8)
        def _(group):
            for step in range(8):
                row = group * 8 + step
                token = ids_ref[whose, row]
                row_out[whose, pl.ds(row, 1), :] = table_ref[pl.ds(token, 1), :]

        if offset > 0:
            deal(0, row_out, row_in, offset).start()

    for piece in range(2 * LAYERS):
        raw_copy(piece).start()
    greet([spot.partner] + [(spot.dp, peer(offset)) for offset in range(1, n)])
    take_own(0)
    launch(0)
    for offset in range(1, 4):
        look_up(offset)
    pass_on(0, 1)
    for offset in range(4, 7):
        look_up(offset)
    pass_on(0, 2)
    take_own(1)
    launch(1)
    look_up(7)
    look_up(0)
    row_in[spot.mp] = row_out[spot.mp]
    pass_on(0, 3)
    for offset in range(1, n):
        arrived(0, row_in, offset).wait_recv()
    for whose in range(n):
        first_ref[:, whose * columns_own : (whose + 1) * columns_own] = row_in[whose]
    first_ref[...] += where_ref[...]
    normed, _ = normed_of(first_ref[...])
    state[...] = normed * gains_ref[0, 0:1, :] + gains_ref[0, 1:2, :]
    take_own(2)
    take_own(3)
    pass_on(0, 4)

    lanes = lax.broadcasted_iota(jnp.int32, (1, 128), 1) < 64
    visible = visible_ref[...] > 0.0

    def head_pair(depth, pair):
        columns = pl.ds(pl.multiple_of(pair * 128, 128), 128)
        query = proj_ref[depth, 0, :, columns]
        keyed = proj_ref[depth, 1, :, columns]
        valued = proj_ref[depth, 2, :, columns]
        outs = []
        for side in range(2):
            mine = lanes if side == 0 else jnp.logical_not(lanes)
            scores = dot_nt(jnp.where(mine, query, jnp.zeros_like(query)), keyed) * 0.125
            scores = jnp.where(visible, scores, masked_score)
            expo = jnp.exp(scores - jnp.max(scores, axis=-1, keepdims=True))
            total = jnp.sum(expo, axis=-1, keepdims=True)
            outs.append(dot_nn((expo / total).astype(jnp.bfloat16), valued))
        mixed_ref[depth, :, columns] = jnp.where(lanes, outs[0], outs[1]).astype(jnp.bfloat16)

    def kept_copies(turn, depth, shard):
        slot = turn % SLOTS
        return (
            pltpu.make_async_copy(slope.at[slot], slope_ref.at[depth, shard], kept_sem.at[0, slot]),
            pltpu.make_async_copy(act.at[slot], act_ref.at[depth, shard], kept_sem.at[1, slot]),
        )

    turns = []

    def ffn_shard(depth, offset):
        shard = spot.shard(offset)
        turn = len(turns)
        turns.append((depth, shard))
        if turn >= SLOTS:
            for copy in kept_copies(turn, *turns[turn - SLOTS]):
                copy.wait()
        rows = rows_at(shard, rows_f)
        hidden = dot_nt(mid_ref[depth], wf[depth, 0, rows, :])
        spread = 0.5 * (1.0 + lax.erf(hidden * (0.5**0.5)))
        mask = mask_ref[depth : depth + 1, pl.ds(pl.multiple_of(shard * rows_f, 128), rows_f)]
        bell = jnp.exp(hidden * hidden * -0.5) * (1.0 / math.sqrt(2.0 * math.pi))
        slope[turn % SLOTS] = (spread + hidden * bell) * mask
        active = (hidden * spread * mask).astype(jnp.bfloat16)
        act[turn % SLOTS] = active
        for copy in kept_copies(turn, depth, shard):
            copy.start()
        pre_ref[depth, 1] += dot_nn(active, wf[depth, 1, rows, :])

    out_copies = []
    for depth in range(LAYERS):
        piece_a, piece_f = 2 * depth, 2 * depth + 1
        if depth > 0:
            for step in range(1, steps + 1):
                pass_on(piece_a, step)
                if step == steps - 1:
                    launch(piece_f)
        for step in range(1, steps + 1):
            settle(piece_a, step)
        copy = pltpu.make_async_copy(wa.at[depth], attn_full.at[depth], out_sem.at[piece_a])
        copy.start()
        out_copies.append(copy)
        inputs = state[...].astype(jnp.bfloat16)
        inputs_ref[depth] = inputs
        for which in range(3):
            proj_ref[depth, which] = dot_nn(inputs, wa[depth, which]).astype(jnp.bfloat16)
        pass_on(piece_f, 1)

        @pl.loop(0, HEADS // 2)
        def _(pair):
            head_pair(depth, pair)

        pre_ref[depth, 0] = state[...] + dot_nn(mixed_ref[depth], wa[depth, 3])
        normed, _ = normed_of(pre_ref[depth, 0])
        middle = (
            normed * gains_ref[1 + 2 * depth, 0:1, :] + gains_ref[1 + 2 * depth, 1:2, :]
        )
        mid_ref[depth] = middle.astype(jnp.bfloat16)
        pre_ref[depth, 1] = middle
        ffn_shard(depth, 0)
        pass_on(piece_f, 2)
        settle(piece_f, 1)
        ffn_shard(depth, -1)
        ffn_shard(depth, 1)
        pass_on(piece_f, 3)
        if depth + 1 < LAYERS:
            launch(piece_a + 2)
        settle(piece_f, 2)
        ffn_shard(depth, -2)
        ffn_shard(depth, 2)
        settle(piece_f, 3)
        ffn_shard(depth, -3)
        ffn_shard(depth, 3)
        pass_on(piece_f, 4)
        settle(piece_f, 4)
        ffn_shard(depth, 4)
        copy = pltpu.make_async_copy(wf.at[depth], ffn_full.at[depth], out_sem.at[piece_f])
        copy.start()
        out_copies.append(copy)
        normed, _ = normed_of(pre_ref[depth, 1])
        state[...] = normed * gains_ref[2 + 2 * depth, 0:1, :] + gains_ref[2 + 2 * depth, 1:2, :]

    spots = (
        lax.broadcasted_iota(jnp.int32, (slots, count), 1) == places_ref[...]
    ).astype(jnp.bfloat16)
    picked[spot.mp] = dot_nn(spots, state[...].astype(jnp.bfloat16)).astype(jnp.bfloat16)
    for offset in range(1, n):
        share(1, picked, offset).start()
    out_b = out_ref[...].astype(jnp.bfloat16)
    rows_v = out_ref.shape[0]
    hits = (
        labels_ref[...] == spot.mp * rows_v + lax.broadcasted_iota(jnp.int32, (rows_v, 1), 0)
    ).astype(jnp.float32)
    for offset in range(1, n):
        arrived(1, picked, offset).wait_recv()
    picked_all = picked[...].reshape(n * slots, -1)
    logits = dot_nt(out_b, picked_all)
    peak = jnp.max(logits, axis=0, keepdims=True)
    expsum = jnp.sum(jnp.exp(logits - peak), axis=0, keepdims=True)
    stats[spot.mp, 0:1, :] = peak
    stats[spot.mp, 1:2, :] = expsum
    stats[spot.mp, 2:3, :] = jnp.sum(hits * logits, axis=0, keepdims=True)
    for offset in range(1, n):
        share(2, stats, offset).start()
    for offset in range(1, n):
        arrived(2, stats, offset).wait_recv()
    peak = stats[0, 0:1, :]
    for whose in range(1, n):
        peak = jnp.maximum(peak, stats[whose, 0:1, :])
    expsum = stats[0, 1:2, :] * jnp.exp(stats[0, 0:1, :] - peak)
    target = stats[0, 2:3, :]
    for whose in range(1, n):
        expsum = expsum + stats[whose, 1:2, :] * jnp.exp(stats[whose, 0:1, :] - peak)
        target = target + stats[whose, 2:3, :]
    log_total = peak + jnp.log(expsum)
    valid = valid_ref[...] > 0.0
    loss_ref[...] = jnp.where(valid, log_total - target, 0.0)
    grad_logits = jnp.where(valid, jnp.exp(logits - log_total) - hits, 0.0).astype(jnp.bfloat16)
    picked_grad = dot_tn(grad_logits, out_b).astype(jnp.bfloat16)
    for whose in range(n):
        back_out[whose] = picked_grad[whose * slots : (whose + 1) * slots, :]
    for offset in range(1, n):
        deal(3, back_out, back_in, offset).start()
    back_in[spot.mp] = back_out[spot.mp]
    out_grad_ref[...] = dot_nn(grad_logits, picked_all)
    for offset in range(1, n):
        arrived(3, back_in, offset).wait_recv()
    summed = back_in[0].astype(jnp.float32)
    for whose in range(1, n):
        summed = summed + back_in[whose].astype(jnp.float32)
    high = summed.astype(jnp.bfloat16)
    low = (summed - high.astype(jnp.float32)).astype(jnp.bfloat16)
    grad_ref[...] = dot_tn(spots, high) + dot_tn(spots, low)

    for piece in range(2 * LAYERS):
        for way, part in WAYS:
            for step in range(1, last_step(n, way, part) + 1):
                ring_copy(piece, way, part, step, 0).wait_send()
                core_copy(piece, way, part, step, core).wait_send()
    for offset in range(1, n):
        deal(0, row_out, row_in, offset).wait_send()
        share(1, picked, offset).wait_send()
        share(2, stats, offset).wait_send()
        deal(3, back_out, back_in, offset).wait_send()
    for turn in range(len(turns) - SLOTS, len(turns)):
        for copy in kept_copies(turn, *turns[turn]):
            copy.wait()
    for copy in out_copies:
        copy.wait()


def forward_call(
    n, ids, table, where, visible, gains, masks, places, labels, valid, out_table, attn, ffn
):
    count, width = where.shape
    rows_f = ffn.shape[2]
    slots = places.shape[0]
    f32, bf16 = jnp.float32, jnp.bfloat16
    vmem = pl.BlockSpec(memory_space=pltpu.VMEM)
    smem = pl.BlockSpec(memory_space=pltpu.SMEM)
    anywhere = pl.BlockSpec(memory_space=pl.ANY)
    shape = jax.ShapeDtypeStruct
    dma = pltpu.SemaphoreType.DMA
    sems = dma((2 * LAYERS, 2, 2, n // 2))
    return pl.pallas_call(
        functools.partial(forward_kernel, n),
        out_shape=(
            shape((LAYERS, 4, width, width), bf16),
            shape((LAYERS, 2, rows_f * n, width), bf16),
            shape((count, width), f32),
            shape((LAYERS, count, width), bf16),
            shape((LAYERS, 3, count, width), bf16),
            shape((LAYERS, count, width), bf16),
            shape((LAYERS, 2, count, width), f32),
            shape((LAYERS, count, width), bf16),
            shape((LAYERS, n, count, rows_f), f32),
            shape((LAYERS, n, count, rows_f), bf16),
            shape((count, width), f32),
            shape(out_table.shape, f32),
            shape((1, n * slots), f32),
        ),
        in_specs=[smem] + [vmem] * 9 + [anywhere] * 2,
        out_specs=(anywhere,) * 2 + (vmem,) * 6 + (anywhere,) * 2 + (vmem,) * 3,
        scratch_shapes=[
            pltpu.VMEM((LAYERS, 4, width, width), bf16),
            pltpu.VMEM((LAYERS, 2, rows_f * n, width), bf16),
            pltpu.VMEM(attn.shape, f32),
            pltpu.VMEM(ffn.shape, f32),
            pltpu.VMEM((SLOTS, count, rows_f), f32),
            pltpu.VMEM((SLOTS, count, rows_f), bf16),
            pltpu.VMEM((count, width), f32),
            pltpu.VMEM((n, count, table.shape[1]), f32),
            pltpu.VMEM((n, count, table.shape[1]), f32),
            pltpu.VMEM((n, slots, width), bf16),
            pltpu.VMEM((n, 8, n * slots), f32),
            pltpu.VMEM((n, slots, width), bf16),
            pltpu.VMEM((n, slots, width), bf16),
            dma((2 * LAYERS,)),
            dma((2 * LAYERS,)),
            dma((2, SLOTS)),
            sems,
            sems,
            sems,
            sems,
            dma((4, n - 1)),
            dma((4, n - 1)),
        ],
        compiler_params=pltpu.CompilerParams(
            collective_id=1, has_side_effects=True, vmem_limit_bytes=VMEM_LIMIT
        ),
        name="forward_layers",
    )(ids, table, where, visible, gains, masks, places, labels, valid, out_table, attn, ffn)


def norm_back(grad, values, gain):
    normed, inverse = normed_of(values)
    scaled = grad * gain
    centred = scaled - jnp.mean(scaled, axis=-1, keepdims=True)
    result = inverse * (centred - normed * jnp.mean(scaled * normed, axis=-1, keepdims=True))
    return (
        result,
        jnp.sum(grad * normed, axis=0, keepdims=True),
        jnp.sum(grad, axis=0, keepdims=True),
    )


def backward_kernel(
    n,
    visible_ref,
    grad_ref,
    first_ref,
    gains_ref,
    inputs_ref,
    proj_ref,
    mixed_ref,
    pre_ref,
    mid_ref,
    attn_full,
    ffn_full,
    slope_all,
    act_all,
    attn_sum,
    ffn_sum,
    grad_out,
    pair_out,
    wa,
    wf,
    slope,
    act,
    sum_a,
    sum_f,
    theirs_f,
    land_f,
    theirs_a,
    land_a,
    ring_a,
    ring_f,
    state,
    grad_rows,
    left_a,
    left_f,
    right_f,
    spread_a,
    spread_f,
    done_a,
    done_f,
    wa_sem,
    load_sem,
    core_send,
    core_recv,
    core_free,
    swap_send,
    swap_recv,
    swap_free,
    ring_send,
    ring_recv,
    ring_free,
    across_send,
    across_recv,
    out_sem,
    last_send,
    last_recv,
):
    spot = Spot(n)
    core = spot.core
    other = 1 - core
    rows_a = attn_sum.shape[2]
    rows_f = ffn_sum.shape[2]
    part_f = rows_f // 2
    order = (4, 3, -3, 2, -2, 1, -1, 0)
    total = LAYERS * n

    def rows_at(shard, rows):
        return pl.ds(pl.multiple_of(shard * rows, 16), rows)

    def remote(source, target, send, recv, device):
        return pltpu.make_async_remote_copy(
            src_ref=source,
            dst_ref=target,
            send_sem=send,
            recv_sem=recv,
            device_id=device,
            device_id_type=MESH,
        )

    def turn_of(turn):
        return LAYERS - 1 - turn // n, spot.shard(order[turn % n])

    def loads(turn):
        depth, shard = turn_of(turn)
        slot = turn % SLOTS
        return (
            pltpu.make_async_copy(
                ffn_full.at[depth, :, rows_at(shard, rows_f), :], wf.at[slot], load_sem.at[0, slot]
            ),
            pltpu.make_async_copy(slope_all.at[depth, shard], slope.at[slot], load_sem.at[1, slot]),
            pltpu.make_async_copy(act_all.at[depth, shard], act.at[slot], load_sem.at[2, slot]),
        )

    def load_attn(depth):
        return pltpu.make_async_copy(attn_full.at[depth], wa, wa_sem.at[0])

    def core_copy(turn):
        slot = turn % SLOTS
        return remote(
            theirs_f.at[slot],
            land_f.at[slot],
            core_send.at[turn],
            core_recv.at[turn],
            spot.partner,
        )

    def fold(turn):
        depth, shard = turn_of(turn)
        core_copy(turn).wait_recv()
        sum_f[depth, shard] = (
            sum_f[depth, shard].astype(jnp.float32)
            + land_f[turn % SLOTS].astype(jnp.float32)
        ).astype(jnp.bfloat16)
        if turn + SLOTS < total:
            pl.semaphore_signal(
                core_free.at[0], inc=1, device_id=spot.partner, device_id_type=MESH
            )

    def swap_copy(depth, part):
        return remote(
            theirs_a.at[part],
            land_a.at[part],
            swap_send.at[depth, part],
            swap_recv.at[depth, part],
            spot.partner,
        )

    def summed(piece, shard, part):
        kind, depth = piece % 2, piece // 2
        if kind == 0:
            return sum_a.at[depth, part, rows_at(shard, rows_a), :]
        return sum_f.at[depth, shard, pl.ds(part * part_f, part_f), :]

    def landed(piece, way, part, step):
        return (ring_a if piece % 2 == 0 else ring_f).at[way, part, step - 1]

    def ring_copy(piece, way, part, step):
        offset = last_step(n, way, part) - step + 1
        shard = spot.shard(offset if way == 0 else -offset)
        return remote(
            summed(piece, shard, part),
            landed(piece, way, part, step),
            ring_send.at[piece, way, part, step - 1],
            ring_recv.at[piece, way, part, step - 1],
            spot.ring[way],
        )

    def launch(piece, long):
        for way, part in WAYS:
            if (way == part) == long:
                if piece // 2 < LAYERS - 1:
                    pl.semaphore_wait(ring_free.at[piece % 2, way, part], 1)
                ring_copy(piece, way, part, 1).start()

    def relay(piece, step):
        for way, part in WAYS:
            last = last_step(n, way, part)
            if step < last:
                ring_copy(piece, way, part, step).wait_recv()
                shard = spot.shard(last - step if way == 0 else step - last)
                into = summed(piece, shard, part)
                into[...] = (
                    into[...].astype(jnp.float32)
                    + landed(piece, way, part, step)[...].astype(jnp.float32)
                ).astype(jnp.bfloat16)
                ring_copy(piece, way, part, step + 1).start()

    def across_copy(piece):
        kind, depth = piece % 2, piece // 2
        buffer = spread_a if kind == 0 else spread_f
        return remote(
            buffer.at[depth, 0],
            buffer.at[depth, 1],
            across_send.at[piece],
            across_recv.at[piece],
            spot.across,
        )

    def finish(piece):
        kind, depth = piece % 2, piece // 2
        for part in range(2):
            value = summed(piece, spot.mp, part)[...].astype(jnp.float32)
            for way in range(2):
                step = last_step(n, way, part)
                ring_copy(piece, way, part, step).wait_recv()
                value = value + landed(piece, way, part, step)[...].astype(jnp.float32)
            value = value.astype(jnp.bfloat16)
            if kind == 0:
                spread_a[depth, 0, part] = value
            else:
                spread_f[depth, 0, pl.ds(part * part_f, part_f), :] = value
            if depth > 0:
                for way in range(2):
                    pl.semaphore_signal(
                        ring_free.at[kind, way, part],
                        inc=1,
                        device_id=spot.ring[1 - way],
                        device_id_type=MESH,
                    )
        across_copy(piece).start()

    def out_copies(piece):
        kind, depth = piece % 2, piece // 2
        if kind == 0:
            source, target = done_a, attn_sum.at[depth, pl.ds(2 * core, 2)]
        else:
            source, target = done_f, ffn_sum.at[depth, core]
        return (
            pltpu.make_async_copy(source, target, out_sem.at[piece]),
            remote(source, target, last_send.at[piece], last_recv.at[piece], spot.partner),
        )

    def conclude(piece):
        kind, depth = piece % 2, piece // 2
        across_copy(piece).wait_recv()
        if depth < LAYERS - 1:
            local, away = out_copies(piece + 2)
            local.wait()
            away.wait_send()
        if kind == 0:
            done_a[...] = spread_a[depth, 0].astype(jnp.float32) + spread_a[depth, 1].astype(
                jnp.float32
            )
        else:
            done_f[...] = spread_f[depth, 0].astype(jnp.float32) + spread_f[depth, 1].astype(
                jnp.float32
            )
        for copy in out_copies(piece):
            copy.start()

    load_attn(LAYERS - 1).start()
    for turn in range(SLOTS):
        for copy in loads(turn):
            copy.start()
    greet((spot.ring[0], spot.ring[1], spot.partner, spot.across))
    state[...] = grad_ref[...]
    lanes = lax.broadcasted_iota(jnp.int32, (1, 128), 1) < 64
    visible = visible_ref[...] > 0.0

    def ffn_turn(turn):
        depth, shard = turn_of(turn)
        slot = turn % SLOTS
        for copy in loads(turn):
            copy.wait()
        grad_active = dot_nt(right_f[1], wf[slot, 1])
        left_f[0] = (grad_active * slope[slot]).astype(jnp.bfloat16)
        left_f[1] = act[slot]
        sum_f[depth, shard] = dot_tn(left_f[core], right_f[core]).astype(jnp.bfloat16)
        if turn >= SLOTS:
            core_copy(turn - SLOTS).wait_send()
        theirs_f[slot] = dot_tn(left_f[other], right_f[other]).astype(jnp.bfloat16)
        if turn >= SLOTS:
            pl.semaphore_wait(core_free.at[0], 1)
        core_copy(turn).start()
        state[...] += dot_nn(left_f[0], wf[slot, 0])
        if turn + SLOTS < total:
            for copy in loads(turn + SLOTS):
                copy.start()

    def head_pair(depth, pair):
        columns = pl.ds(pl.multiple_of(pair * 128, 128), 128)
        query = proj_ref[depth, 0, :, columns]
        keyed = proj_ref[depth, 1, :, columns]
        valued = proj_ref[depth, 2, :, columns]
        grad_mixed = grad_rows[4, :, columns]
        outs = []
        for side in range(2):
            mine = lanes if side == 0 else jnp.logical_not(lanes)
            scores = dot_nt(jnp.where(mine, query, jnp.zeros_like(query)), keyed) * 0.125
            scores = jnp.where(visible, scores, masked_score)
            expo = jnp.exp(scores - jnp.max(scores, axis=-1, keepdims=True))
            probs = expo / jnp.sum(expo, axis=-1, keepdims=True)
            grad_probs = dot_nt(jnp.where(mine, grad_mixed, jnp.zeros_like(query)), valued)
            inner = jnp.sum(grad_probs * probs, axis=-1, keepdims=True)
            grad_scores = (probs * (grad_probs - inner)).astype(jnp.bfloat16)
            outs.append(
                (
                    dot_nn(grad_scores, keyed) * 0.125,
                    dot_tn(grad_scores, query) * 0.125,
                    dot_tn(probs.astype(jnp.bfloat16), grad_mixed),
                )
            )
        for which in range(3):
            grad_rows[which, :, columns] = jnp.where(
                lanes, outs[0][which], outs[1][which]
            ).astype(jnp.bfloat16)

    def layer(depth, hooks):
        base = (LAYERS - 1 - depth) * n
        piece_a, piece_f = 2 * depth, 2 * depth + 1
        grad_two, pair_out[2 + 2 * depth, 0:1, :], pair_out[2 + 2 * depth, 1:2, :] = norm_back(
            state[...], pre_ref[depth, 1], gains_ref[2 + 2 * depth, 0:1, :]
        )
        state[...] = grad_two
        right_f[0] = mid_ref[depth]
        right_f[1] = grad_two.astype(jnp.bfloat16)
        for step in range(n):
            ffn_turn(base + step)
            if step >= 1:
                fold(base + step - 1)
            if step == 1:
                launch(piece_f, True)
            if step == 3:
                launch(piece_f, False)
            hooks.get(("ffn", step), lambda: None)()
        fold(base + n - 1)
        hooks.get("middle", lambda: None)()
        grad_one, pair_out[1 + 2 * depth, 0:1, :], pair_out[1 + 2 * depth, 1:2, :] = norm_back(
            state[...], pre_ref[depth, 0], gains_ref[1 + 2 * depth, 0:1, :]
        )
        state[...] = grad_one
        grad_rows[3] = grad_one.astype(jnp.bfloat16)
        load_attn(depth).wait()
        grad_rows[4] = dot_nt(grad_rows[3], wa[3]).astype(jnp.bfloat16)

        @pl.loop(0, HEADS // 2)
        def _(pair):
            head_pair(depth, pair)

        hooks.get("heads", lambda: None)()
        left_a[0] = inputs_ref[depth]
        left_a[1] = mixed_ref[depth]
        for part in range(2):
            if depth < LAYERS - 1:
                swap_copy(depth + 1, part).wait_send()
            left = 0 if part == 0 else other
            theirs_a[part] = dot_tn(left_a[left], grad_rows[2 * other + part]).astype(jnp.bfloat16)
            if depth < LAYERS - 1:
                pl.semaphore_wait(swap_free.at[part], 1)
            swap_copy(depth, part).start()
        for part in range(2):
            left = 0 if part == 0 else core
            sum_a[depth, part] = dot_tn(left_a[left], grad_rows[2 * core + part]).astype(
                jnp.bfloat16
            )
        hooks.get("mats", lambda: None)()
        for part in range(2):
            swap_copy(depth, part).wait_recv()

            @pl.loop(0, n)
            def _(block):
                rows = rows_at(block, rows_a)
                sum_a[depth, part, rows, :] = (
                    sum_a[depth, part, rows, :].astype(jnp.float32)
                    + land_a[part, rows, :].astype(jnp.float32)
                ).astype(jnp.bfloat16)

            if depth > 0:
                pl.semaphore_signal(
                    swap_free.at[part], inc=1, device_id=spot.partner, device_id_type=MESH
                )
        launch(piece_a, True)
        launch(piece_a, False)
        for which in range(3):
            state[...] += dot_nt(grad_rows[which], wa[which])
        if depth > 0:
            load_attn(depth - 1).start()

    layer(
        1,
        {
            "middle": lambda: relay(3, 1),
            "heads": lambda: relay(3, 2),
        },
    )
    relay(3, 3)
    finish(3)
    layer(
        0,
        {
            ("ffn", 3): lambda: relay(2, 1),
            ("ffn", 5): lambda: conclude(3),
            "middle": lambda: relay(2, 2),
            "heads": lambda: relay(1, 1),
            "mats": lambda: (relay(2, 3), finish(2)),
        },
    )
    grad_sum, pair_out[0, 0:1, :], pair_out[0, 1:2, :] = norm_back(
        state[...], first_ref[...], gains_ref[0, 0:1, :]
    )
    grad_out[...] = grad_sum
    relay(1, 2)
    conclude(2)
    relay(0, 1)
    relay(1, 3)
    relay(0, 2)
    finish(1)
    relay(0, 3)
    conclude(1)
    finish(0)
    conclude(0)
    for turn in range(total - SLOTS, total):
        core_copy(turn).wait_send()
    for part in range(2):
        swap_copy(0, part).wait_send()
    for piece in range(2 * LAYERS):
        for way, part in WAYS:
            for step in range(1, last_step(n, way, part) + 1):
                ring_copy(piece, way, part, step).wait_send()
        across_copy(piece).wait_send()
        local, away = out_copies(piece)
        if piece < 2:
            local.wait()
            away.wait_send()
        away.wait_recv()


def backward_call(n, visible, grad, first, gains, kept, attn_full, ffn_full, slope, act):
    count, width = grad.shape
    rows_f = ffn_full.shape[2] // n
    rows_a = attn_full.shape[2] // n
    f32, bf16 = jnp.float32, jnp.bfloat16
    vmem = pl.BlockSpec(memory_space=pltpu.VMEM)
    anywhere = pl.BlockSpec(memory_space=pl.ANY)
    shape = jax.ShapeDtypeStruct
    dma = pltpu.SemaphoreType.DMA
    regular = pltpu.SemaphoreType.REGULAR
    ring_sems = dma((2 * LAYERS, 2, 2, n // 2))
    return pl.pallas_call(
        functools.partial(backward_kernel, n),
        out_shape=(
            shape((LAYERS, 4, rows_a, width), f32),
            shape((LAYERS, 2, rows_f, width), f32),
            shape((count, width), f32),
            shape(gains.shape, f32),
        ),
        in_specs=[vmem] * 9 + [anywhere] * 4,
        out_specs=(anywhere, anywhere, vmem, vmem),
        scratch_shapes=[
            pltpu.VMEM((4, width, width), bf16),
            pltpu.VMEM((SLOTS, 2, rows_f, width), bf16),
            pltpu.VMEM((SLOTS, count, rows_f), f32),
            pltpu.VMEM((SLOTS, count, rows_f), bf16),
            pltpu.VMEM((LAYERS, 2, width, width), bf16),
            pltpu.VMEM((LAYERS, n, rows_f, width), bf16),
            pltpu.VMEM((SLOTS, rows_f, width), bf16),
            pltpu.VMEM((SLOTS, rows_f, width), bf16),
            pltpu.VMEM((2, width, width), bf16),
            pltpu.VMEM((2, width, width), bf16),
            pltpu.VMEM((2, 2, n // 2, rows_a, width), bf16),
            pltpu.VMEM((2, 2, n // 2, rows_f // 2, width), bf16),
            pltpu.VMEM((count, width), f32),
            pltpu.VMEM((5, count, width), bf16),
            pltpu.VMEM((2, count, width), bf16),
            pltpu.VMEM((2, count, rows_f), bf16),
            pltpu.VMEM((2, count, width), bf16),
            pltpu.VMEM((LAYERS, 2, 2, rows_a, width), bf16),
            pltpu.VMEM((LAYERS, 2, rows_f, width), bf16),
            pltpu.VMEM((2, rows_a, width), f32),
            pltpu.VMEM((rows_f, width), f32),
            dma((1,)),
            dma((3, SLOTS)),
            dma((LAYERS * n,)),
            dma((LAYERS * n,)),
            regular((1,)),
            dma((LAYERS, 2)),
            dma((LAYERS, 2)),
            regular((2,)),
            ring_sems,
            ring_sems,
            regular((2, 2, 2)),
            dma((2 * LAYERS,)),
            dma((2 * LAYERS,)),
            dma((2 * LAYERS,)),
            dma((2 * LAYERS,)),
            dma((2 * LAYERS,)),
        ],
        compiler_params=pltpu.CompilerParams(
            collective_id=2, has_side_effects=True, vmem_limit_bytes=VMEM_LIMIT
        ),
        name="backward_layers",
    )(visible, grad, first, gains, *kept, attn_full, ffn_full, slope, act)


def merged(value, axis, join):
    pieces = jax.tree.map(lambda part: lax.all_gather(part, axis), value)
    head = jax.tree.map(lambda part: part[0], pieces)
    tail = jax.tree.map(lambda part: part[1:], pieces)
    total, _ = lax.scan(lambda total, section: (join(total, section), None), head, tail)
    return total


def sinusoid(count, width):
    places = jnp.arange(count, dtype=jnp.float32)[:, None]
    freqs = jnp.exp(jnp.arange(width // 2, dtype=jnp.float32) * (-2.0 * math.log(10000.0) / width))
    angles = places * freqs[None, :]
    return jnp.concatenate([jnp.sin(angles), jnp.cos(angles)], axis=1)


def layer_norm(values, gain, shift):
    centre = jnp.mean(values, axis=-1, keepdims=True)
    offset = values - centre
    spread = jnp.mean(offset * offset, axis=-1, keepdims=True)
    inverse = lax.rsqrt(spread + norm_eps)
    normed = offset * inverse
    return (normed * gain + shift, (normed, inverse))


def norm_backward(grad, saved, gain):
    normed, inverse = saved
    scaled = grad * gain
    centred = scaled - jnp.mean(scaled, axis=-1, keepdims=True)
    result = inverse * (centred - normed * jnp.mean(scaled * normed, axis=-1, keepdims=True))
    return (result, jnp.stack([jnp.sum(grad * normed, axis=0), jnp.sum(grad, axis=0)]))


def gelu_exact(values):
    return jax.nn.gelu(values, approximate=False)


def gelu_back(hidden, grad):
    unused, pullback = jax.vjp(gelu_exact, hidden)
    return pullback(grad)[0]


def masked_scores(query, keyed, length):
    scale = query.shape[-1] ** (-0.5)
    scores = jnp.einsum("hqe,hke->hqk", query, keyed, preferred_element_type=jnp.float32) * scale
    visible = jnp.arange(keyed.shape[1]) < length
    return jnp.where(visible[None, None, :], scores, masked_score)


def fetch_forward(attn_part, ffn_part):
    return (
        lax.all_gather(attn_part, "mp", axis=1, tiled=True),
        lax.all_gather(ffn_part, "mp", axis=1, tiled=True),
    )


def fetch_backward(attn_part, ffn_part):
    return (
        lax.all_gather(attn_part, "mp", axis=1, tiled=True),
        lax.all_gather(ffn_part, "mp", axis=1, tiled=True),
    )


def reduce_layer(attn_grad, ffn_grad):
    return (
        lax.psum_scatter(attn_grad, "mp", scatter_dimension=1, tiled=True),
        lax.psum_scatter(ffn_grad, "mp", scatter_dimension=1, tiled=True),
    )


def ffn_forward(middle_b, ffn_w, unit_mask):
    hidden = jnp.einsum("td,fd->tf", middle_b, ffn_w[0], preferred_element_type=jnp.float32)
    active = (gelu_exact(hidden) * unit_mask[None, :]).astype(jnp.bfloat16)
    output = jnp.einsum("tf,fd->td", active, ffn_w[1], preferred_element_type=jnp.float32)
    return (hidden, active, output)


def ffn_backward(grad_out, middle_b, hidden, active, ffn_w, unit_mask):
    grad_active = jnp.einsum("td,fd->tf", grad_out, ffn_w[1], preferred_element_type=jnp.float32)
    grad_hidden = gelu_back(hidden, grad_active * unit_mask[None, :]).astype(jnp.bfloat16)
    up_grad = jnp.einsum("tf,td->fd", grad_hidden, middle_b, preferred_element_type=jnp.float32)
    down_grad = jnp.einsum("tf,td->fd", active, grad_out, preferred_element_type=jnp.float32)
    from_ffn = jnp.einsum("tf,fd->td", grad_hidden, ffn_w[0], preferred_element_type=jnp.float32)
    return (jnp.stack([up_grad, down_grad]), from_ffn)


def layer_forward(states, attn_w, ffn_w, pair, length, unit_mask):
    count = states.shape[0]
    inputs = states.astype(jnp.bfloat16)
    projected = jnp.einsum(
        "td,kde->kte", inputs, attn_w[:3], preferred_element_type=jnp.float32
    ).astype(jnp.bfloat16)
    heads = projected.reshape(3, count, HEADS, -1).transpose(0, 2, 1, 3)
    scores = masked_scores(heads[0], heads[1], length)
    peak = jnp.max(scores, axis=-1, keepdims=True)
    expo = jnp.exp(scores - peak)
    total = jnp.sum(expo, axis=-1, keepdims=True)
    log_total = peak + jnp.log(total)
    probs = (expo / total).astype(jnp.bfloat16)
    mixed = jnp.einsum("hqk,hke->hqe", probs, heads[2], preferred_element_type=jnp.float32)
    mixed = mixed.transpose(1, 0, 2).reshape(count, -1).astype(jnp.bfloat16)
    branch = jnp.dot(mixed, attn_w[3], preferred_element_type=jnp.float32)
    middle, norm_one = layer_norm(states + branch, pair[0, 0], pair[0, 1])
    middle_b = middle.astype(jnp.bfloat16)
    hidden, active, output = ffn_forward(middle_b, ffn_w, unit_mask)
    result, norm_two = layer_norm(middle + output, pair[1, 0], pair[1, 1])
    return (result, (inputs, heads, log_total, mixed, norm_one, middle_b, hidden, active, norm_two))


def layer_backward(grad, attn_w, ffn_w, pair, length, unit_mask, kept):
    inputs, heads, log_total, mixed, norm_one, middle_b, hidden, active, norm_two = kept
    count = inputs.shape[0]
    grad_two, pair_two = norm_backward(grad, norm_two, pair[1, 0])
    ffn_grad, from_ffn = ffn_backward(
        grad_two.astype(jnp.bfloat16), middle_b, hidden, active, ffn_w, unit_mask
    )
    grad_one, pair_one = norm_backward(grad_two + from_ffn, norm_one, pair[0, 0])
    grad_branch = grad_one.astype(jnp.bfloat16)
    output_grad = jnp.einsum("td,te->de", mixed, grad_branch, preferred_element_type=jnp.float32)
    grad_mixed = jnp.einsum("te,de->td", grad_branch, attn_w[3], preferred_element_type=jnp.float32)
    grad_mixed = grad_mixed.astype(jnp.bfloat16).reshape(count, HEADS, -1).transpose(1, 0, 2)
    scale = heads.shape[-1] ** (-0.5)
    probs = jnp.exp(masked_scores(heads[0], heads[1], length) - log_total)
    grad_values = jnp.einsum(
        "hqk,hqe->hke", probs.astype(jnp.bfloat16), grad_mixed, preferred_element_type=jnp.float32
    )
    grad_probs = jnp.einsum(
        "hqe,hke->hqk", grad_mixed, heads[2], preferred_element_type=jnp.float32
    )
    grad_scores = probs * (grad_probs - jnp.sum(grad_probs * probs, axis=-1, keepdims=True))
    grad_scores = grad_scores.astype(jnp.bfloat16)
    grad_query = (
        jnp.einsum("hqk,hke->hqe", grad_scores, heads[1], preferred_element_type=jnp.float32)
        * scale
    )
    grad_key = (
        jnp.einsum("hqk,hqe->hke", grad_scores, heads[0], preferred_element_type=jnp.float32)
        * scale
    )
    stacked = (
        jnp.stack([grad_query, grad_key, grad_values]).transpose(0, 2, 1, 3).reshape(3, count, -1)
    )
    stacked = stacked.astype(jnp.bfloat16)
    input_grad = jnp.einsum("td,kte->kde", inputs, stacked, preferred_element_type=jnp.float32)
    from_attn = jnp.einsum("kte,kde->td", stacked, attn_w[:3], preferred_element_type=jnp.float32)
    attn_grad = jnp.concatenate([input_grad, output_grad[None]], axis=0)
    return (grad_one + from_attn, attn_grad, ffn_grad, jnp.stack([pair_one, pair_two]))


def adamw(weight, moment_one, moment_two, grad, decay, rate):
    moment_one = beta_one * moment_one + (1.0 - beta_one) * grad
    moment_two = beta_two * moment_two + (1.0 - beta_two) * grad * grad
    fixed_one = moment_one / (1.0 - beta_one**STEP)
    fixed_two = moment_two / (1.0 - beta_two**STEP)
    weight = weight - rate * (fixed_one / (jnp.sqrt(fixed_two) + adam_eps) + decay * weight)
    return (moment_one, moment_two, weight)


def combine_vocab(first, second):
    peak = jnp.maximum(first[0], second[0])
    total = first[1] * jnp.exp(first[0] - peak) + second[1] * jnp.exp(second[0] - peak)
    return (peak, total, first[2] + second[2])


def local_general(
    tokens,
    lengths,
    places,
    targets,
    ramp,
    attn,
    attn_m,
    attn_v,
    ffn,
    ffn_m,
    ffn_v,
    table,
    table_m,
    table_v,
    out_table,
    out_m,
    out_v,
    gains,
    gains_m,
    gains_v,
):
    rank = lax.axis_index("mp")
    count = tokens.shape[2]
    flat_ids = tokens.reshape(-1)
    all_lengths = lengths.reshape(-1)
    length = lax.dynamic_index_in_dim(all_lengths, rank, keepdims=False)
    masks = jnp.minimum(ramp, RAMP).astype(jnp.float32) / RAMP
    unit_masks = [masks[depth] for depth in range(LAYERS)]
    looked = jnp.take(table, flat_ids, axis=0)
    embedded = lax.all_to_all(looked, "mp", split_axis=0, concat_axis=1, tiled=True)
    states, norm_zero = layer_norm(
        embedded + sinusoid(count, embedded.shape[1]), gains[0, 0], gains[0, 1]
    )
    kept_all = []
    weights_all = []
    for depth in range(LAYERS):
        attn_w, ffn_w = fetch_forward(
            attn[depth].astype(jnp.bfloat16), ffn[depth].astype(jnp.bfloat16)
        )
        states, kept = layer_forward(
            states, attn_w, ffn_w, gains[1 + 2 * depth : 3 + 2 * depth], length, unit_masks[depth]
        )
        kept_all.append(kept)
        weights_all.append(None)
    spots = places.reshape(-1)
    picked = jnp.take(states, spots, axis=0).astype(jnp.bfloat16)
    picked_all = lax.all_gather(picked, "mp", axis=0, tiled=True)
    out_b = out_table.astype(jnp.bfloat16)
    logits = jnp.einsum("rd,vd->rv", picked_all, out_b, preferred_element_type=jnp.float32)
    labels = targets.reshape(-1)
    columns = rank * out_table.shape[0] + jnp.arange(out_table.shape[0])
    hits = (labels[:, None] == columns[None, :]).astype(jnp.float32)
    peak = jnp.max(logits, axis=1)
    expsum = jnp.sum(jnp.exp(logits - peak[:, None]), axis=1)
    target_part = jnp.sum(hits * logits, axis=1)
    peak_all, expsum_all, target_all = merged((peak, expsum, target_part), "mp", combine_vocab)
    log_total = peak_all + jnp.log(expsum_all)
    slot_count = targets.shape[2]
    counted = jnp.maximum(1, all_lengths * slot_count // count)
    valid = (jnp.arange(slot_count)[None, :] < counted[:, None]).reshape(-1)
    loss_pair = jnp.stack(
        [
            jnp.sum(jnp.where(valid, log_total - target_all, 0.0)),
            jnp.sum(counted).astype(jnp.float32),
        ]
    )
    grad_logits = jnp.where(
        valid[:, None], jnp.exp(logits - log_total[:, None]) - hits, 0.0
    ).astype(jnp.bfloat16)
    out_grad = jnp.einsum("rv,rd->vd", grad_logits, picked_all, preferred_element_type=jnp.float32)
    picked_grad = lax.psum_scatter(
        jnp.dot(grad_logits, out_b, preferred_element_type=jnp.float32),
        "mp",
        scatter_dimension=0,
        tiled=True,
    )
    grad = jnp.zeros_like(states).at[spots].add(picked_grad)
    attn_parts = [None] * LAYERS
    ffn_parts = [None] * LAYERS
    pair_grads = [None] * LAYERS
    for depth in reversed(range(LAYERS)):
        attn_w, ffn_w = fetch_backward(
            attn[depth].astype(jnp.bfloat16), ffn[depth].astype(jnp.bfloat16)
        )
        grad, attn_grad, ffn_grad, pair_grad = layer_backward(
            grad,
            attn_w,
            ffn_w,
            gains[1 + 2 * depth : 3 + 2 * depth],
            length,
            unit_masks[depth],
            kept_all[depth],
        )
        attn_parts[depth], ffn_parts[depth] = reduce_layer(attn_grad, ffn_grad)
        pair_grads[depth] = pair_grad
    grad_sum, zero_grad = norm_backward(grad, norm_zero, gains[0, 0])
    returned = lax.all_to_all(grad_sum, "mp", split_axis=1, concat_axis=0, tiled=True)
    table_grad = jnp.zeros_like(table).at[flat_ids].add(returned)
    gains_grad = jnp.concatenate([zero_grad[None]] + pair_grads, axis=0)
    attn_sum, ffn_sum, table_sum, out_sum, gains_part, loss = lax.psum(
        (jnp.stack(attn_parts), jnp.stack(ffn_parts), table_grad, out_grad, gains_grad, loss_pair),
        "dp",
    )
    shard_squares = (
        jnp.sum(attn_sum * attn_sum)
        + jnp.sum(ffn_sum * ffn_sum)
        + jnp.sum(table_sum * table_sum)
        + jnp.sum(out_sum * out_sum)
    )
    square_total, gains_sum = lax.psum((shard_squares, gains_part), "mp")
    grad_norm = jnp.sqrt(square_total + jnp.sum(gains_sum * gains_sum))
    factor = clip_limit / jnp.maximum(grad_norm, clip_limit)
    attn_m_new, attn_v_new, attn_new = adamw(
        attn, attn_m, attn_v, attn_sum * factor, weight_decay, learn_rate
    )
    ffn_m_new, ffn_v_new, ffn_new = adamw(
        ffn, ffn_m, ffn_v, ffn_sum * factor, weight_decay, learn_rate
    )
    table_m_new, table_v_new, table_new = adamw(
        table, table_m, table_v, table_sum * factor, weight_decay, learn_rate
    )
    out_m_new, out_v_new, out_new = adamw(
        out_table, out_m, out_v, out_sum * factor, weight_decay, learn_rate
    )
    gains_m_new, gains_v_new, gains_new = adamw(
        gains, gains_m, gains_v, gains_sum * factor, 0.0, gain_rate
    )
    return (
        loss,
        grad_norm.reshape(1),
        attn_m_new,
        attn_v_new,
        attn_new,
        ffn_m_new,
        ffn_v_new,
        ffn_new,
        table_m_new,
        table_v_new,
        table_new,
        out_m_new,
        out_v_new,
        out_new,
        gains_m_new,
        gains_v_new,
        gains_new,
    )


def local(
    tokens,
    lengths,
    places,
    targets,
    ramp,
    attn,
    attn_m,
    attn_v,
    ffn,
    ffn_m,
    ffn_v,
    table,
    table_m,
    table_v,
    out_table,
    out_m,
    out_v,
    gains,
    gains_m,
    gains_v,
):
    rank = lax.axis_index("mp")
    n = tokens.shape[1]
    count, width = tokens.shape[2], gains.shape[2]
    flat_ids = tokens.reshape(-1)
    all_lengths = lengths.reshape(-1)
    length = lax.dynamic_index_in_dim(all_lengths, rank, keepdims=False)
    masks = jnp.minimum(ramp, RAMP).astype(jnp.float32) / RAMP
    visible = (jnp.arange(count) < length).astype(jnp.float32)[None, :]
    slot_count = targets.shape[2]
    slots = 32 * -(-slot_count // 32)
    counted = jnp.maximum(1, all_lengths * slot_count // count)
    valid = (jnp.arange(slots)[None, :] < counted[:, None]).astype(jnp.float32).reshape(1, -1)
    extra = slots - slot_count
    spots = jnp.pad(places.reshape(-1), (0, extra), constant_values=-1)[:, None]
    labels = jnp.pad(targets[0], ((0, 0), (0, extra)), constant_values=-1).reshape(1, -1)
    where = sinusoid(count, width)
    attn_full, ffn_full, first, *kept, slope, act, grad, out_grad, losses = forward_call(
        n, tokens[0], table, where, visible, gains, masks, spots, labels, valid, out_table, attn, ffn
    )
    loss_pair = jnp.stack([jnp.sum(losses), jnp.sum(counted).astype(jnp.float32)])
    attn_sum, ffn_sum, grad_sum, gains_grad = backward_call(
        n, visible, grad, first, gains, kept, attn_full, ffn_full, slope, act
    )
    returned = lax.all_to_all(grad_sum, "mp", split_axis=1, concat_axis=0, tiled=True)
    table_grad = jnp.zeros_like(table).at[flat_ids].add(returned)
    table_sum, out_sum, gains_part, loss = lax.psum(
        (table_grad, out_grad, gains_grad, loss_pair),
        "dp",
    )
    shard_squares = (
        jnp.sum(attn_sum * attn_sum)
        + jnp.sum(ffn_sum * ffn_sum)
        + jnp.sum(table_sum * table_sum)
        + jnp.sum(out_sum * out_sum)
    )
    square_total, gains_sum = lax.psum((shard_squares, gains_part), "mp")
    grad_norm = jnp.sqrt(square_total + jnp.sum(gains_sum * gains_sum))
    factor = clip_limit / jnp.maximum(grad_norm, clip_limit)
    attn_m_new, attn_v_new, attn_new = adamw(
        attn, attn_m, attn_v, attn_sum * factor, weight_decay, learn_rate
    )
    ffn_m_new, ffn_v_new, ffn_new = adamw(
        ffn, ffn_m, ffn_v, ffn_sum * factor, weight_decay, learn_rate
    )
    table_m_new, table_v_new, table_new = adamw(
        table, table_m, table_v, table_sum * factor, weight_decay, learn_rate
    )
    out_m_new, out_v_new, out_new = adamw(
        out_table, out_m, out_v, out_sum * factor, weight_decay, learn_rate
    )
    gains_m_new, gains_v_new, gains_new = adamw(
        gains, gains_m, gains_v, gains_sum * factor, 0.0, gain_rate
    )
    return (
        loss,
        grad_norm.reshape(1),
        attn_m_new,
        attn_v_new,
        attn_new,
        ffn_m_new,
        ffn_v_new,
        ffn_new,
        table_m_new,
        table_v_new,
        table_new,
        out_m_new,
        out_v_new,
        out_new,
        gains_m_new,
        gains_v_new,
        gains_new,
    )


def solution(mesh):
    in_specs = (
        P("dp", None, None),
        P("dp", None),
        P("dp", "mp", None),
        P("dp", None, None),
        P(),
        P(None, None, "mp", None),
        P(None, None, "mp", None),
        P(None, None, "mp", None),
        P(None, None, "mp", None),
        P(None, None, "mp", None),
        P(None, None, "mp", None),
        P(None, "mp"),
        P(None, "mp"),
        P(None, "mp"),
        P("mp", None),
        P("mp", None),
        P("mp", None),
        P(),
        P(),
        P(),
    )
    out_specs = (
        P(),
        P(),
        P(None, None, "mp", None),
        P(None, None, "mp", None),
        P(None, None, "mp", None),
        P(None, None, "mp", None),
        P(None, None, "mp", None),
        P(None, None, "mp", None),
        P(None, "mp"),
        P(None, "mp"),
        P(None, "mp"),
        P("mp", None),
        P("mp", None),
        P("mp", None),
        P(),
        P(),
        P(),
    )
    fits = mesh.shape['mp'] == 8 and mesh.shape['dp'] == 4
    chosen = local if fits else local_general
    return jax.shard_map(chosen, mesh=mesh, in_specs=in_specs, out_specs=out_specs, check_vma=False)
```

```python
import functools
import math

import jax
import jax.numpy as jnp
from jax import lax
from jax.experimental import pallas as pl
from jax.experimental.pallas import tpu as pltpu
from jax.sharding import PartitionSpec as P

HEADS = 12
LAYERS = 2
STEP = 10
RAMP = 4


norm_eps = 1e-05
beta_one = 0.9
beta_two = 0.999
learn_rate = 0.02
gain_rate = 0.3
weight_decay = 0.01
adam_eps = 1e-08
clip_limit = 1.0
masked_score = -1000000000.0


MESH = pl.DeviceIdType.MESH
VMEM_LIMIT = 62 * 1024 * 1024
SLOTS = 3


def dot_nn(left, right):
    return lax.dot_general(
        left, right, (((1,), (0,)), ((), ())), preferred_element_type=jnp.float32
    )


def dot_nt(left, right):
    return lax.dot_general(
        left, right, (((1,), (1,)), ((), ())), preferred_element_type=jnp.float32
    )


def dot_tn(left, right):
    return lax.dot_general(
        left, right, (((0,), (0,)), ((), ())), preferred_element_type=jnp.float32
    )


def ring_index(place, n):
    late = place // (n // 2)
    return (1 - late) * 2 * place + late * (2 * (n - 1 - place) + 1)


def ring_place(index, n):
    odd = index % 2
    return (1 - odd) * (index // 2) + odd * (n - 1 - index // 2)


class Spot:
    def __init__(self, n):
        self.n = n
        self.dp = lax.axis_index("dp")
        self.mp = lax.axis_index("mp")
        self.core = self.dp % 2
        self.place = ring_place(self.mp, n)
        self.partner = (self.dp + 1 - 2 * self.core, self.mp)
        self.across = ((self.dp + 2) % 4, self.mp)
        self.ring = (
            (self.dp, ring_index((self.place + 1) % n, n)),
            (self.dp, ring_index((self.place + n - 1) % n, n)),
        )

    def shard(self, offset):
        return ring_index((self.place + offset + self.n) % self.n, self.n)


def greet(devices):
    barrier = pltpu.get_barrier_semaphore()
    for device in devices:
        pl.semaphore_signal(barrier, inc=1, device_id=device, device_id_type=MESH)
    pl.semaphore_wait(barrier, len(devices))


def last_step(n, way, part):
    return n // 2 if way == part else n // 2 - 1


WAYS = ((0, 0), (1, 1), (0, 1), (1, 0))


def normed_of(values):
    centre = jnp.mean(values, axis=-1, keepdims=True)
    offset = values - centre
    spread = jnp.mean(offset * offset, axis=-1, keepdims=True)
    inverse = lax.rsqrt(spread + norm_eps)
    return offset * inverse, inverse


def forward_kernel(
    n,
    ids_ref,
    table_ref,
    where_ref,
    visible_ref,
    gains_ref,
    mask_ref,
    places_ref,
    labels_ref,
    valid_ref,
    out_ref,
    attn_sh,
    ffn_sh,
    attn_full,
    ffn_full,
    first_ref,
    inputs_ref,
    proj_ref,
    mixed_ref,
    pre_ref,
    mid_ref,
    slope_ref,
    act_ref,
    grad_ref,
    out_grad_ref,
    loss_ref,
    wa,
    wf,
    raw_a,
    raw_f,
    slope,
    act,
    state,
    row_out,
    row_in,
    picked,
    stats,
    back_out,
    back_in,
    raw_sem,
    out_sem,
    kept_sem,
    ring_send,
    ring_recv,
    core_send,
    core_recv,
    fan_send,
    fan_recv,
):
    spot = Spot(n)
    core = spot.core
    rows_a = attn_sh.shape[2]
    rows_f = ffn_sh.shape[2]
    part_f = rows_f // 2
    steps = n // 2
    count = first_ref.shape[0]
    columns_own = table_ref.shape[1]
    slots = places_ref.shape[0]

    def rows_at(shard, rows):
        return pl.ds(pl.multiple_of(shard * rows, 16), rows)

    def remote(source, target, send, recv, device):
        return pltpu.make_async_remote_copy(
            src_ref=source,
            dst_ref=target,
            send_sem=send,
            recv_sem=recv,
            device_id=device,
            device_id_type=MESH,
        )

    def chunk(piece, shard, part, side):
        kind, depth = piece % 2, piece // 2
        if kind == 0:
            return wa.at[depth, 2 * side + part, rows_at(shard, rows_a), :]
        start = pl.multiple_of(shard * rows_f + part * part_f, 16)
        return wf.at[depth, side, pl.ds(start, part_f), :]

    def sign(way):
        return -1 if way == 0 else 1

    def ring_copy(piece, way, part, step, arriving):
        target = chunk(piece, spot.shard(sign(way) * (step - 1 + arriving)), part, core)
        return remote(
            target,
            target,
            ring_send.at[piece, way, part, step - 1],
            ring_recv.at[piece, way, part, step - 1],
            spot.ring[way],
        )

    def core_copy(piece, way, part, step, side):
        target = chunk(piece, spot.shard(sign(way) * step), part, side)
        return remote(
            target,
            target,
            core_send.at[piece, way, part, step - 1],
            core_recv.at[piece, way, part, step - 1],
            spot.partner,
        )

    def peer(offset):
        return (spot.mp + offset + n) % n

    def fan_copy(which, offset, source, target):
        return remote(
            source,
            target,
            fan_send.at[which, offset - 1],
            fan_recv.at[which, offset - 1],
            (spot.dp, peer(offset)),
        )

    def share(which, buffer, offset):
        return fan_copy(which, offset, buffer.at[spot.mp], buffer.at[spot.mp])

    def arrived(which, buffer, offset):
        return fan_copy(which, offset, buffer.at[peer(-offset)], buffer.at[peer(-offset)])

    def deal(which, source, target, offset):
        return fan_copy(which, offset, source.at[peer(offset)], target.at[spot.mp])

    def raw_copy(piece):
        kind, depth = piece % 2, piece // 2
        if kind == 0:
            return pltpu.make_async_copy(attn_sh.at[depth], raw_a.at[depth], raw_sem.at[piece])
        return pltpu.make_async_copy(ffn_sh.at[depth], raw_f.at[depth], raw_sem.at[piece])

    def take_own(piece):
        kind, depth = piece % 2, piece // 2
        raw_copy(piece).wait()
        if kind == 0:
            for which in range(4):
                wa[depth, which, rows_at(spot.mp, rows_a), :] = raw_a[depth, which].astype(
                    jnp.bfloat16
                )
        else:
            for which in range(2):
                wf[depth, which, rows_at(spot.mp, rows_f), :] = raw_f[depth, which].astype(
                    jnp.bfloat16
                )

    def launch(piece):
        for way, part in WAYS:
            ring_copy(piece, way, part, 1, 0).start()

    def pass_on(piece, step):
        for way, part in WAYS:
            if step <= last_step(n, way, part):
                ring_copy(piece, way, part, step, 1).wait_recv()
                if step < last_step(n, way, part):
                    ring_copy(piece, way, part, step + 1, 0).start()
                core_copy(piece, way, part, step, core).start()

    def settle(piece, step):
        for way, part in WAYS:
            if step <= last_step(n, way, part):
                core_copy(piece, way, part, step, 1 - core).wait_recv()

    def look_up(offset):
        whose = peer(offset)

        @pl.loop(0, count // 8)
        def _(group):
            for step in range(8):
                row = group * 8 + step
                token = ids_ref[whose, row]
                row_out[whose, pl.ds(row, 1), :] = table_ref[pl.ds(token, 1), :]

        if offset > 0:
            deal(0, row_out, row_in, offset).start()

    for piece in range(2 * LAYERS):
        raw_copy(piece).start()
    greet([spot.partner] + [(spot.dp, peer(offset)) for offset in range(1, n)])
    take_own(0)
    launch(0)
    for offset in range(1, 4):
        look_up(offset)
    pass_on(0, 1)
    for offset in range(4, 7):
        look_up(offset)
    pass_on(0, 2)
    take_own(1)
    launch(1)
    look_up(7)
    look_up(0)
    row_in[spot.mp] = row_out[spot.mp]
    pass_on(0, 3)
    for offset in range(1, n):
        arrived(0, row_in, offset).wait_recv()
    for whose in range(n):
        first_ref[:, whose * columns_own : (whose + 1) * columns_own] = row_in[whose]
    first_ref[...] += where_ref[...]
    normed, _ = normed_of(first_ref[...])
    state[...] = normed * gains_ref[0, 0:1, :] + gains_ref[0, 1:2, :]
    take_own(2)
    take_own(3)
    pass_on(0, 4)

    lanes = lax.broadcasted_iota(jnp.int32, (1, 128), 1) < 64
    visible = visible_ref[...] > 0.0

    def head_pair(depth, pair):
        columns = pl.ds(pl.multiple_of(pair * 128, 128), 128)
        query = proj_ref[depth, 0, :, columns]
        keyed = proj_ref[depth, 1, :, columns]
        valued = proj_ref[depth, 2, :, columns]
        outs = []
        for side in range(2):
            mine = lanes if side == 0 else jnp.logical_not(lanes)
            scores = dot_nt(jnp.where(mine, query, jnp.zeros_like(query)), keyed) * 0.125
            scores = jnp.where(visible, scores, masked_score)
            expo = jnp.exp(scores - jnp.max(scores, axis=-1, keepdims=True))
            total = jnp.sum(expo, axis=-1, keepdims=True)
            outs.append(dot_nn((expo / total).astype(jnp.bfloat16), valued))
        mixed_ref[depth, :, columns] = jnp.where(lanes, outs[0], outs[1]).astype(jnp.bfloat16)

    def kept_copies(turn, depth, shard):
        slot = turn % SLOTS
        return (
            pltpu.make_async_copy(slope.at[slot], slope_ref.at[depth, shard], kept_sem.at[0, slot]),
            pltpu.make_async_copy(act.at[slot], act_ref.at[depth, shard], kept_sem.at[1, slot]),
        )

    turns = []

    def ffn_shard(depth, offset):
        shard = spot.shard(offset)
        turn = len(turns)
        turns.append((depth, shard))
        if turn >= SLOTS:
            for copy in kept_copies(turn, *turns[turn - SLOTS]):
                copy.wait()
        rows = rows_at(shard, rows_f)
        hidden = dot_nt(mid_ref[depth], wf[depth, 0, rows, :])
        spread = 0.5 * (1.0 + lax.erf(hidden * (0.5**0.5)))
        mask = mask_ref[depth : depth + 1, pl.ds(pl.multiple_of(shard * rows_f, 128), rows_f)]
        bell = jnp.exp(hidden * hidden * -0.5) * (1.0 / math.sqrt(2.0 * math.pi))
        slope[turn % SLOTS] = (spread + hidden * bell) * mask
        active = (hidden * spread * mask).astype(jnp.bfloat16)
        act[turn % SLOTS] = active
        for copy in kept_copies(turn, depth, shard):
            copy.start()
        pre_ref[depth, 1] += dot_nn(active, wf[depth, 1, rows, :])

    out_copies = []
    for depth in range(LAYERS):
        piece_a, piece_f = 2 * depth, 2 * depth + 1
        if depth > 0:
            for step in range(1, steps + 1):
                pass_on(piece_a, step)
                if step == steps - 1:
                    launch(piece_f)
        for step in range(1, steps + 1):
            settle(piece_a, step)
        copy = pltpu.make_async_copy(wa.at[depth], attn_full.at[depth], out_sem.at[piece_a])
        copy.start()
        out_copies.append(copy)
        inputs = state[...].astype(jnp.bfloat16)
        inputs_ref[depth] = inputs
        for which in range(3):
            proj_ref[depth, which] = dot_nn(inputs, wa[depth, which]).astype(jnp.bfloat16)
        pass_on(piece_f, 1)

        @pl.loop(0, HEADS // 2)
        def _(pair):
            head_pair(depth, pair)

        pre_ref[depth, 0] = state[...] + dot_nn(mixed_ref[depth], wa[depth, 3])
        normed, _ = normed_of(pre_ref[depth, 0])
        middle = (
            normed * gains_ref[1 + 2 * depth, 0:1, :] + gains_ref[1 + 2 * depth, 1:2, :]
        )
        mid_ref[depth] = middle.astype(jnp.bfloat16)
        pre_ref[depth, 1] = middle
        ffn_shard(depth, 0)
        pass_on(piece_f, 2)
        settle(piece_f, 1)
        ffn_shard(depth, -1)
        ffn_shard(depth, 1)
        pass_on(piece_f, 3)
        if depth + 1 < LAYERS:
            launch(piece_a + 2)
        settle(piece_f, 2)
        ffn_shard(depth, -2)
        ffn_shard(depth, 2)
        settle(piece_f, 3)
        ffn_shard(depth, -3)
        ffn_shard(depth, 3)
        pass_on(piece_f, 4)
        settle(piece_f, 4)
        ffn_shard(depth, 4)
        copy = pltpu.make_async_copy(wf.at[depth], ffn_full.at[depth], out_sem.at[piece_f])
        copy.start()
        out_copies.append(copy)
        normed, _ = normed_of(pre_ref[depth, 1])
        state[...] = normed * gains_ref[2 + 2 * depth, 0:1, :] + gains_ref[2 + 2 * depth, 1:2, :]

    spots = (
        lax.broadcasted_iota(jnp.int32, (slots, count), 1) == places_ref[...]
    ).astype(jnp.bfloat16)
    picked[spot.mp] = dot_nn(spots, state[...].astype(jnp.bfloat16)).astype(jnp.bfloat16)
    for offset in range(1, n):
        share(1, picked, offset).start()
    out_b = out_ref[...].astype(jnp.bfloat16)
    rows_v = out_ref.shape[0]
    hits = (
        labels_ref[...] == spot.mp * rows_v + lax.broadcasted_iota(jnp.int32, (rows_v, 1), 0)
    ).astype(jnp.float32)
    for offset in range(1, n):
        arrived(1, picked, offset).wait_recv()
    picked_all = picked[...].reshape(n * slots, -1)
    logits = dot_nt(out_b, picked_all)
    peak = jnp.max(logits, axis=0, keepdims=True)
    expsum = jnp.sum(jnp.exp(logits - peak), axis=0, keepdims=True)
    stats[spot.mp, 0:1, :] = peak
    stats[spot.mp, 1:2, :] = expsum
    stats[spot.mp, 2:3, :] = jnp.sum(hits * logits, axis=0, keepdims=True)
    for offset in range(1, n):
        share(2, stats, offset).start()
    for offset in range(1, n):
        arrived(2, stats, offset).wait_recv()
    peak = stats[0, 0:1, :]
    for whose in range(1, n):
        peak = jnp.maximum(peak, stats[whose, 0:1, :])
    expsum = stats[0, 1:2, :] * jnp.exp(stats[0, 0:1, :] - peak)
    target = stats[0, 2:3, :]
    for whose in range(1, n):
        expsum = expsum + stats[whose, 1:2, :] * jnp.exp(stats[whose, 0:1, :] - peak)
        target = target + stats[whose, 2:3, :]
    log_total = peak + jnp.log(expsum)
    valid = valid_ref[...] > 0.0
    loss_ref[...] = jnp.where(valid, log_total - target, 0.0)
    grad_logits = jnp.where(valid, jnp.exp(logits - log_total) - hits, 0.0).astype(jnp.bfloat16)
    picked_grad = dot_tn(grad_logits, out_b).astype(jnp.bfloat16)
    for whose in range(n):
        back_out[whose] = picked_grad[whose * slots : (whose + 1) * slots, :]
    for offset in range(1, n):
        deal(3, back_out, back_in, offset).start()
    back_in[spot.mp] = back_out[spot.mp]
    out_grad_ref[...] = dot_nn(grad_logits, picked_all)
    for offset in range(1, n):
        arrived(3, back_in, offset).wait_recv()
    summed = back_in[0].astype(jnp.float32)
    for whose in range(1, n):
        summed = summed + back_in[whose].astype(jnp.float32)
    high = summed.astype(jnp.bfloat16)
    low = (summed - high.astype(jnp.float32)).astype(jnp.bfloat16)
    grad_ref[...] = dot_tn(spots, high) + dot_tn(spots, low)

    for piece in range(2 * LAYERS):
        for way, part in WAYS:
            for step in range(1, last_step(n, way, part) + 1):
                ring_copy(piece, way, part, step, 0).wait_send()
                core_copy(piece, way, part, step, core).wait_send()
    for offset in range(1, n):
        deal(0, row_out, row_in, offset).wait_send()
        share(1, picked, offset).wait_send()
        share(2, stats, offset).wait_send()
        deal(3, back_out, back_in, offset).wait_send()
    for turn in range(len(turns) - SLOTS, len(turns)):
        for copy in kept_copies(turn, *turns[turn]):
            copy.wait()
    for copy in out_copies:
        copy.wait()


def forward_call(
    n, ids, table, where, visible, gains, masks, places, labels, valid, out_table, attn, ffn
):
    count, width = where.shape
    rows_f = ffn.shape[2]
    slots = places.shape[0]
    f32, bf16 = jnp.float32, jnp.bfloat16
    vmem = pl.BlockSpec(memory_space=pltpu.VMEM)
    smem = pl.BlockSpec(memory_space=pltpu.SMEM)
    anywhere = pl.BlockSpec(memory_space=pl.ANY)
    shape = jax.ShapeDtypeStruct
    dma = pltpu.SemaphoreType.DMA
    sems = dma((2 * LAYERS, 2, 2, n // 2))
    return pl.pallas_call(
        functools.partial(forward_kernel, n),
        out_shape=(
            shape((LAYERS, 4, width, width), bf16),
            shape((LAYERS, 2, rows_f * n, width), bf16),
            shape((count, width), f32),
            shape((LAYERS, count, width), bf16),
            shape((LAYERS, 3, count, width), bf16),
            shape((LAYERS, count, width), bf16),
            shape((LAYERS, 2, count, width), f32),
            shape((LAYERS, count, width), bf16),
            shape((LAYERS, n, count, rows_f), f32),
            shape((LAYERS, n, count, rows_f), bf16),
            shape((count, width), f32),
            shape(out_table.shape, f32),
            shape((1, n * slots), f32),
        ),
        in_specs=[smem] + [vmem] * 9 + [anywhere] * 2,
        out_specs=(anywhere,) * 2 + (vmem,) * 6 + (anywhere,) * 2 + (vmem,) * 3,
        scratch_shapes=[
            pltpu.VMEM((LAYERS, 4, width, width), bf16),
            pltpu.VMEM((LAYERS, 2, rows_f * n, width), bf16),
            pltpu.VMEM(attn.shape, f32),
            pltpu.VMEM(ffn.shape, f32),
            pltpu.VMEM((SLOTS, count, rows_f), f32),
            pltpu.VMEM((SLOTS, count, rows_f), bf16),
            pltpu.VMEM((count, width), f32),
            pltpu.VMEM((n, count, table.shape[1]), f32),
            pltpu.VMEM((n, count, table.shape[1]), f32),
            pltpu.VMEM((n, slots, width), bf16),
            pltpu.VMEM((n, 8, n * slots), f32),
            pltpu.VMEM((n, slots, width), bf16),
            pltpu.VMEM((n, slots, width), bf16),
            dma((2 * LAYERS,)),
            dma((2 * LAYERS,)),
            dma((2, SLOTS)),
            sems,
            sems,
            sems,
            sems,
            dma((4, n - 1)),
            dma((4, n - 1)),
        ],
        compiler_params=pltpu.CompilerParams(
            collective_id=1, has_side_effects=True, vmem_limit_bytes=VMEM_LIMIT
        ),
        name="forward_layers",
    )(ids, table, where, visible, gains, masks, places, labels, valid, out_table, attn, ffn)


def norm_back(grad, values, gain):
    normed, inverse = normed_of(values)
    scaled = grad * gain
    centred = scaled - jnp.mean(scaled, axis=-1, keepdims=True)
    result = inverse * (centred - normed * jnp.mean(scaled * normed, axis=-1, keepdims=True))
    return (
        result,
        jnp.sum(grad * normed, axis=0, keepdims=True),
        jnp.sum(grad, axis=0, keepdims=True),
    )


def backward_kernel(
    n,
    ids_ref,
    counted_ref,
    losses_ref,
    visible_ref,
    grad_ref,
    first_ref,
    gains_ref,
    out_grad_ref,
    inputs_ref,
    mixed_ref,
    mid_ref,
    proj_all,
    pre_all,
    attn_full,
    ffn_full,
    slope_all,
    act_all,
    attn_sum,
    ffn_sum,
    table_sum,
    out_sum,
    small_out,
    square_out,
    proj,
    pre,
    wa,
    wf,
    slope,
    act,
    sum_a,
    sum_f,
    theirs_f,
    land_f,
    land_a,
    ring_a,
    ring_f,
    state,
    grad_rows,
    left_a,
    left_f,
    right_f,
    spread_a,
    spread_f,
    done_a,
    done_f,
    wa_sem,
    load_sem,
    core_send,
    core_recv,
    core_free,
    swap_send,
    swap_recv,
    swap_free,
    ring_send,
    ring_recv,
    ring_free,
    across_send,
    across_recv,
    out_sem,
    last_send,
    last_recv,
    small,
    small_in,
    columns_out,
    columns_in,
    table_grad,
    table_half,
    out_half,
    out_done,
    squares,
    square_parts,
    proj_sem,
    small_send,
    small_recv,
    deal_send,
    deal_recv,
    half_send,
    half_recv,
    half_sem,
    norm_send,
    norm_recv,
):
    spot = Spot(n)
    core = spot.core
    other = 1 - core
    rows_a = attn_sum.shape[2]
    rows_f = ffn_sum.shape[2]
    part_f = rows_f // 2
    order = (4, 3, -3, 2, -2, 1, -1, 0)
    total = LAYERS * n

    def rows_at(shard, rows):
        return pl.ds(pl.multiple_of(shard * rows, 16), rows)

    def peer(offset):
        return (spot.mp + offset + n) % n

    def remote(source, target, send, recv, device):
        return pltpu.make_async_remote_copy(
            src_ref=source,
            dst_ref=target,
            send_sem=send,
            recv_sem=recv,
            device_id=device,
            device_id_type=MESH,
        )

    def turn_of(turn):
        return LAYERS - 1 - turn // n, spot.shard(order[turn % n])

    def loads(turn):
        depth, shard = turn_of(turn)
        slot = turn % SLOTS
        return (
            pltpu.make_async_copy(
                ffn_full.at[depth, :, rows_at(shard, rows_f), :], wf.at[slot], load_sem.at[0, slot]
            ),
            pltpu.make_async_copy(slope_all.at[depth, shard], slope.at[slot], load_sem.at[1, slot]),
            pltpu.make_async_copy(act_all.at[depth, shard], act.at[slot], load_sem.at[2, slot]),
        )

    def load_pre(depth):
        return pltpu.make_async_copy(pre_all.at[depth], pre, proj_sem.at[0])

    def load_proj(depth):
        return pltpu.make_async_copy(proj_all.at[depth], proj, proj_sem.at[1])

    def load_attn(depth):
        return pltpu.make_async_copy(attn_full.at[depth], wa, wa_sem.at[0])

    def core_copy(turn):
        slot = turn % SLOTS
        return remote(
            theirs_f.at[slot],
            land_f.at[slot],
            core_send.at[turn],
            core_recv.at[turn],
            spot.partner,
        )

    def fold(turn):
        depth, shard = turn_of(turn)
        core_copy(turn).wait_recv()
        sum_f[depth, shard] = (
            sum_f[depth, shard].astype(jnp.float32)
            + land_f[turn % SLOTS].astype(jnp.float32)
        ).astype(jnp.bfloat16)
        if turn + SLOTS < total:
            pl.semaphore_signal(
                core_free.at[0], inc=1, device_id=spot.partner, device_id_type=MESH
            )

    def swap_copy(depth, part):
        return remote(
            wa.at[part],
            land_a.at[part],
            swap_send.at[depth, part],
            swap_recv.at[depth, part],
            spot.partner,
        )

    def summed(piece, shard, part):
        kind, depth = piece % 2, piece // 2
        if kind == 0:
            return sum_a.at[depth, part, rows_at(shard, rows_a), :]
        return sum_f.at[depth, shard, pl.ds(part * part_f, part_f), :]

    def landed(piece, way, part, step):
        return (ring_a if piece % 2 == 0 else ring_f).at[way, part, step - 1]

    def ring_copy(piece, way, part, step):
        offset = last_step(n, way, part) - step + 1
        shard = spot.shard(offset if way == 0 else -offset)
        return remote(
            summed(piece, shard, part),
            landed(piece, way, part, step),
            ring_send.at[piece, way, part, step - 1],
            ring_recv.at[piece, way, part, step - 1],
            spot.ring[way],
        )

    def launch(piece, long):
        for way, part in WAYS:
            if (way == part) == long:
                if piece // 2 < LAYERS - 1:
                    pl.semaphore_wait(ring_free.at[piece % 2, way, part], 1)
                ring_copy(piece, way, part, 1).start()

    def relay(piece, step):
        for way, part in WAYS:
            last = last_step(n, way, part)
            if step < last:
                ring_copy(piece, way, part, step).wait_recv()
                shard = spot.shard(last - step if way == 0 else step - last)
                into = summed(piece, shard, part)
                into[...] = (
                    into[...].astype(jnp.float32)
                    + landed(piece, way, part, step)[...].astype(jnp.float32)
                ).astype(jnp.bfloat16)
                ring_copy(piece, way, part, step + 1).start()

    def across_copy(piece):
        kind, depth = piece % 2, piece // 2
        buffer = spread_a if kind == 0 else spread_f
        return remote(
            buffer.at[depth, 0],
            buffer.at[depth, 1],
            across_send.at[piece],
            across_recv.at[piece],
            spot.across,
        )

    def finish(piece):
        kind, depth = piece % 2, piece // 2
        for part in range(2):
            value = summed(piece, spot.mp, part)[...].astype(jnp.float32)
            for way in range(2):
                step = last_step(n, way, part)
                ring_copy(piece, way, part, step).wait_recv()
                value = value + landed(piece, way, part, step)[...].astype(jnp.float32)
            value = value.astype(jnp.bfloat16)
            if kind == 0:
                spread_a[depth, 0, part] = value
            else:
                spread_f[depth, 0, pl.ds(part * part_f, part_f), :] = value
            if depth > 0:
                for way in range(2):
                    pl.semaphore_signal(
                        ring_free.at[kind, way, part],
                        inc=1,
                        device_id=spot.ring[1 - way],
                        device_id_type=MESH,
                    )
        across_copy(piece).start()

    def out_copies(piece):
        kind, depth = piece % 2, piece // 2
        if kind == 0:
            source, target = done_a, attn_sum.at[depth, pl.ds(2 * core, 2)]
        else:
            source, target = done_f, ffn_sum.at[depth, core]
        return (
            pltpu.make_async_copy(source, target, out_sem.at[piece]),
            remote(source, target, last_send.at[piece], last_recv.at[piece], spot.partner),
        )

    def conclude(piece):
        kind, depth = piece % 2, piece // 2
        across_copy(piece).wait_recv()
        if depth < LAYERS - 1:
            local, away = out_copies(piece + 2)
            local.wait()
            away.wait_send()
        if kind == 0:
            for part in range(2):
                value = spread_a[depth, 0, part].astype(jnp.float32) + spread_a[
                    depth, 1, part
                ].astype(jnp.float32)
                done_a[part] = value
                add_squares(value)
        else:
            value = spread_f[depth, 0].astype(jnp.float32) + spread_f[depth, 1].astype(
                jnp.float32
            )
            done_f[...] = value
            add_squares(value)
        for copy in out_copies(piece):
            copy.start()

    load_pre(LAYERS - 1).start()
    for turn in range(SLOTS):
        for copy in loads(turn):
            copy.start()
    load_attn(LAYERS - 1).start()
    load_proj(LAYERS - 1).start()
    greet([spot.partner, spot.across] + [(spot.dp, peer(offset)) for offset in range(1, n)])
    state[...] = grad_ref[...]
    lanes = lax.broadcasted_iota(jnp.int32, (1, 128), 1) < 64
    visible = visible_ref[...] > 0.0

    def ffn_turn(turn):
        depth, shard = turn_of(turn)
        slot = turn % SLOTS
        for copy in loads(turn):
            copy.wait()
        grad_active = dot_nt(right_f[1], wf[slot, 1])
        left_f[0] = (grad_active * slope[slot]).astype(jnp.bfloat16)
        left_f[1] = act[slot]
        sum_f[depth, shard] = dot_tn(left_f[core], right_f[core]).astype(jnp.bfloat16)
        if turn >= SLOTS:
            core_copy(turn - SLOTS).wait_send()
        theirs_f[slot] = dot_tn(left_f[other], right_f[other]).astype(jnp.bfloat16)
        if turn >= SLOTS:
            pl.semaphore_wait(core_free.at[0], 1)
        core_copy(turn).start()
        state[...] += dot_nn(left_f[0], wf[slot, 0])
        if turn + SLOTS < total:
            for copy in loads(turn + SLOTS):
                copy.start()

    def head_pair(depth, pair):
        columns = pl.ds(pl.multiple_of(pair * 128, 128), 128)
        query = proj[0, :, columns]
        keyed = proj[1, :, columns]
        valued = proj[2, :, columns]
        grad_mixed = grad_rows[4, :, columns]
        outs = []
        for side in range(2):
            mine = lanes if side == 0 else jnp.logical_not(lanes)
            scores = dot_nt(jnp.where(mine, query, jnp.zeros_like(query)), keyed) * 0.125
            scores = jnp.where(visible, scores, masked_score)
            expo = jnp.exp(scores - jnp.max(scores, axis=-1, keepdims=True))
            probs = expo / jnp.sum(expo, axis=-1, keepdims=True)
            grad_probs = dot_nt(jnp.where(mine, grad_mixed, jnp.zeros_like(query)), valued)
            inner = jnp.sum(grad_probs * probs, axis=-1, keepdims=True)
            grad_scores = (probs * (grad_probs - inner)).astype(jnp.bfloat16)
            outs.append(
                (
                    dot_nn(grad_scores, keyed) * 0.125,
                    dot_tn(grad_scores, query) * 0.125,
                    dot_tn(probs.astype(jnp.bfloat16), grad_mixed),
                )
            )
        for which in range(3):
            grad_rows[which, :, columns] = jnp.where(
                lanes, outs[0][which], outs[1][which]
            ).astype(jnp.bfloat16)

    def layer(depth, hooks):
        base = (LAYERS - 1 - depth) * n
        piece_a, piece_f = 2 * depth, 2 * depth + 1
        load_pre(depth).wait()
        grad_two, small[0, 4 + 4 * depth : 5 + 4 * depth, :], small[0, 5 + 4 * depth : 6 + 4 * depth, :] = norm_back(
            state[...], pre[1], gains_ref[2 + 2 * depth, 0:1, :]
        )
        state[...] = grad_two
        right_f[0] = mid_ref[depth]
        right_f[1] = grad_two.astype(jnp.bfloat16)
        for step in range(n):
            ffn_turn(base + step)
            if step >= 1:
                fold(base + step - 1)
            if step == 1:
                launch(piece_f, True)
            if step == 3:
                launch(piece_f, False)
            hooks.get(("ffn", step), lambda: None)()
        fold(base + n - 1)
        hooks.get("middle", lambda: None)()
        grad_one, small[0, 2 + 4 * depth : 3 + 4 * depth, :], small[0, 3 + 4 * depth : 4 + 4 * depth, :] = norm_back(
            state[...], pre[0], gains_ref[1 + 2 * depth, 0:1, :]
        )
        if depth > 0:
            load_pre(depth - 1).start()
        state[...] = grad_one
        grad_rows[3] = grad_one.astype(jnp.bfloat16)
        load_attn(depth).wait()
        load_proj(depth).wait()
        grad_rows[4] = dot_nt(grad_rows[3], wa[3]).astype(jnp.bfloat16)

        @pl.loop(0, HEADS // 2)
        def _(pair):
            head_pair(depth, pair)

        if depth > 0:
            load_proj(depth - 1).start()
        hooks.get("heads", lambda: None)()
        for which in range(3):
            state[...] += dot_nt(grad_rows[which], wa[which])
        left_a[0] = inputs_ref[depth]
        left_a[1] = mixed_ref[depth]
        for part in range(2):
            left = 0 if part == 0 else other
            wa[part] = dot_tn(left_a[left], grad_rows[2 * other + part]).astype(jnp.bfloat16)
            if depth < LAYERS - 1:
                pl.semaphore_wait(swap_free.at[part], 1)
            swap_copy(depth, part).start()
        for part in range(2):
            left = 0 if part == 0 else core
            sum_a[depth, part] = dot_tn(left_a[left], grad_rows[2 * core + part]).astype(
                jnp.bfloat16
            )
        hooks.get("mats", lambda: None)()
        for part in range(2):
            swap_copy(depth, part).wait_recv()

            @pl.loop(0, n)
            def _(block):
                rows = rows_at(block, rows_a)
                sum_a[depth, part, rows, :] = (
                    sum_a[depth, part, rows, :].astype(jnp.float32)
                    + land_a[part, rows, :].astype(jnp.float32)
                ).astype(jnp.bfloat16)

            if depth > 0:
                pl.semaphore_signal(
                    swap_free.at[part], inc=1, device_id=spot.partner, device_id_type=MESH
                )
        launch(piece_a, True)
        launch(piece_a, False)

    def reload_attn():
        for part in range(2):
            swap_copy(1, part).wait_send()
        load_attn(0).start()

    def half_copy(which, stage):
        buffer = out_half if which == 0 else table_half
        return remote(
            buffer.at[2 * stage],
            buffer.at[2 * stage + 1],
            half_send.at[which, stage],
            half_recv.at[which, stage],
            spot.partner if stage == 0 else spot.across,
        )

    def half_rows(rows, side):
        return pl.ds(pl.multiple_of(side * (rows // 2), 16), rows // 2)

    def half_start(which, source):
        buffer = out_half if which == 0 else table_half
        buffer[0] = source[half_rows(source.shape[0], other), :].astype(jnp.bfloat16)
        half_copy(which, 0).start()

    def half_fold(which, source):
        buffer = out_half if which == 0 else table_half
        half_copy(which, 0).wait_recv()
        own = source[half_rows(source.shape[0], core), :]
        buffer[2] = (own + buffer[1].astype(jnp.float32)).astype(jnp.bfloat16)
        half_copy(which, 1).start()

    def half_out(which):
        if which == 0:
            source, target = out_done, out_sum.at[half_rows(out_sum.shape[0], core), :]
        else:
            source = table_grad.at[half_rows(table_sum.shape[0], core), :]
            target = table_sum.at[half_rows(table_sum.shape[0], core), :]
        return (
            pltpu.make_async_copy(source, target, half_sem.at[which]),
            remote(source, target, half_send.at[which, 2], half_recv.at[which, 2], spot.partner),
        )

    def add_squares(value):
        squares[...] += jnp.sum(value * value, axis=0, keepdims=True)

    def half_end(which):
        buffer = out_half if which == 0 else table_half
        half_copy(which, 1).wait_recv()
        value = buffer[2].astype(jnp.float32) + buffer[3].astype(jnp.float32)
        if which == 0:
            out_done[...] = value
        else:
            table_grad[half_rows(table_sum.shape[0], core), :] = value
        width = squares.shape[1]
        for start in range(0, value.shape[1], width):
            add_squares(value[:, start : start + width])
        for copy in half_out(which):
            copy.start()

    def small_copy(stage):
        bit = 1 << max(0, stage - 2)
        pair = spot.mp + bit - 2 * bit * ((spot.mp // bit) % 2)
        device = (spot.partner, spot.across)[stage] if stage < 2 else (spot.dp, pair)
        return remote(
            small.at[stage],
            small_in.at[stage],
            small_send.at[stage],
            small_recv.at[stage],
            device,
        )

    def small_next(stage):
        small_copy(stage).wait_recv()
        small[stage + 1] = small[stage] + small_in[stage]
        if stage < 4:
            small_copy(stage + 1).start()

    def deal_copy(offset, arriving):
        source = columns_out.at[peer(offset)]
        target = columns_in.at[peer(-offset) if arriving else spot.mp]
        return remote(
            source,
            target,
            deal_send.at[offset - 1],
            deal_recv.at[offset - 1],
            (spot.dp, peer(offset)),
        )

    def table_blocks(first, last):
        @pl.loop(first, last)
        def _(block):
            row = lax.broadcasted_iota(jnp.int32, (256, 1), 0) + block * 256
            value = jnp.zeros((columns_in.shape[1], 256), jnp.float32)
            for whose in range(n):
                chosen = (row == ids_ref[whose : whose + 1, :]).astype(jnp.bfloat16)
                value = value + dot_nt(columns_in[whose], chosen)
            table_grad[:, pl.ds(pl.multiple_of(block * 256, 256), 256)] = value

    squares[...] = jnp.zeros_like(squares)
    half_start(0, out_grad_ref)
    layer(
        1,
        {
            "middle": lambda: (relay(3, 1), half_fold(0, out_grad_ref)),
            "heads": lambda: relay(3, 2),
        },
    )
    relay(3, 3)
    finish(3)
    layer(
        0,
        {
            ("ffn", 0): reload_attn,
            ("ffn", 3): lambda: relay(2, 1),
            ("ffn", 5): lambda: conclude(3),
            "middle": lambda: (relay(2, 2), half_end(0)),
            "heads": lambda: relay(1, 1),
            "mats": lambda: (relay(2, 3), finish(2)),
        },
    )
    grad_sum, small[0, 0:1, :], small[0, 1:2, :] = norm_back(
        state[...], first_ref[...], gains_ref[0, 0:1, :]
    )
    width = squares.shape[1]
    lane = lax.broadcasted_iota(jnp.int32, (1, width), 1)
    loss = jnp.sum(losses_ref[...], axis=1, keepdims=True) * (1.0 / n)
    slots = counted_ref[0:1, 0:1] * (1.0 / n)
    small[0, 10:11, :] = jnp.where(lane == 0, loss, jnp.where(lane == 1, slots, 0.0))
    small[0, 11:16, :] = jnp.zeros((5, width), jnp.float32)
    small_copy(0).start()
    turned = grad_sum.T.astype(jnp.bfloat16)
    share = columns_in.shape[1]
    for whose in range(n):
        columns_out[whose] = turned[whose * share : (whose + 1) * share, :]
    for offset in range(1, n):
        deal_copy(offset, False).start()
    columns_in[spot.mp] = columns_out[spot.mp]
    relay(1, 2)
    small_next(0)
    conclude(2)
    for offset in range(1, n):
        deal_copy(offset, True).wait_recv()
    blocks = table_sum.shape[1] // 256
    table_blocks(0, blocks // 2)
    relay(0, 1)
    small_next(1)
    table_blocks(blocks // 2, blocks)
    half_start(1, table_grad)
    relay(1, 3)
    small_next(2)
    half_fold(1, table_grad)
    relay(0, 2)
    finish(1)
    small_next(3)
    half_end(1)
    relay(0, 3)
    conclude(1)
    small_next(4)
    finish(0)
    small_out[...] = small[5]
    conclude(0)

    square = jnp.sum(squares[...], axis=1, keepdims=True)
    square_parts[n] = jnp.broadcast_to(square, square_parts.shape[1:])
    swap = remote(
        square_parts.at[n],
        square_parts.at[n + 1],
        norm_send.at[0],
        norm_recv.at[0],
        spot.partner,
    )
    swap.start()
    swap.wait_recv()
    square_parts[spot.mp] = square_parts[n] + square_parts[n + 1]

    def norm_copy(offset, arriving):
        source = square_parts.at[spot.mp]
        target = square_parts.at[peer(-offset) if arriving else spot.mp]
        return remote(
            source, target, norm_send.at[offset], norm_recv.at[offset], (spot.dp, peer(offset))
        )

    for offset in range(1, n):
        norm_copy(offset, False).start()
    gains_grad = small[5, 0:10, :]
    square = jnp.sum(jnp.sum(gains_grad * gains_grad, axis=0, keepdims=True), axis=1, keepdims=True)
    for offset in range(1, n):
        norm_copy(offset, True).wait_recv()
    for whose in range(n):
        square = square + square_parts[whose, 0:1, :]
    square_out[...] = square

    swap.wait_send()
    for offset in range(1, n):
        norm_copy(offset, False).wait_send()
        deal_copy(offset, False).wait_send()
    for stage in range(5):
        small_copy(stage).wait_send()
    for which in range(2):
        half_copy(which, 0).wait_send()
        half_copy(which, 1).wait_send()
        local, away = half_out(which)
        local.wait()
        away.wait()
    for turn in range(total - SLOTS, total):
        core_copy(turn).wait_send()
    for part in range(2):
        swap_copy(0, part).wait_send()
    for piece in range(2 * LAYERS):
        for way, part in WAYS:
            for step in range(1, last_step(n, way, part) + 1):
                ring_copy(piece, way, part, step).wait_send()
        across_copy(piece).wait_send()
        local, away = out_copies(piece)
        if piece < 2:
            local.wait()
            away.wait_send()
        away.wait_recv()


def backward_call(
    n, ids, counted, losses, visible, grad, first, gains, out_grad, kept, attn_full, ffn_full, slope, act, table
):
    inputs, proj, mixed, pre, mid = kept
    count, width = grad.shape
    rows_f = ffn_full.shape[2] // n
    rows_a = attn_full.shape[2] // n
    rows_v = out_grad.shape[0]
    words, share = table.shape
    f32, bf16 = jnp.float32, jnp.bfloat16
    vmem = pl.BlockSpec(memory_space=pltpu.VMEM)
    anywhere = pl.BlockSpec(memory_space=pl.ANY)
    shape = jax.ShapeDtypeStruct
    dma = pltpu.SemaphoreType.DMA
    regular = pltpu.SemaphoreType.REGULAR
    ring_sems = dma((2 * LAYERS, 2, 2, n // 2))
    return pl.pallas_call(
        functools.partial(backward_kernel, n),
        out_shape=(
            shape((LAYERS, 4, rows_a, width), f32),
            shape((LAYERS, 2, rows_f, width), f32),
            shape((share, words), f32),
            shape((rows_v, width), f32),
            shape((16, width), f32),
            shape((1, 128), f32),
        ),
        in_specs=[vmem] * 11 + [anywhere] * 6,
        out_specs=(anywhere,) * 4 + (vmem,) * 2,
        scratch_shapes=[
            pltpu.VMEM((3, count, width), bf16),
            pltpu.VMEM((2, count, width), f32),
            pltpu.VMEM((4, width, width), bf16),
            pltpu.VMEM((SLOTS, 2, rows_f, width), bf16),
            pltpu.VMEM((SLOTS, count, rows_f), f32),
            pltpu.VMEM((SLOTS, count, rows_f), bf16),
            pltpu.VMEM((LAYERS, 2, width, width), bf16),
            pltpu.VMEM((LAYERS, n, rows_f, width), bf16),
            pltpu.VMEM((SLOTS, rows_f, width), bf16),
            pltpu.VMEM((SLOTS, rows_f, width), bf16),
            pltpu.VMEM((2, width, width), bf16),
            pltpu.VMEM((2, 2, n // 2, rows_a, width), bf16),
            pltpu.VMEM((2, 2, n // 2, rows_f // 2, width), bf16),
            pltpu.VMEM((count, width), f32),
            pltpu.VMEM((5, count, width), bf16),
            pltpu.VMEM((2, count, width), bf16),
            pltpu.VMEM((2, count, rows_f), bf16),
            pltpu.VMEM((2, count, width), bf16),
            pltpu.VMEM((LAYERS, 2, 2, rows_a, width), bf16),
            pltpu.VMEM((LAYERS, 2, rows_f, width), bf16),
            pltpu.VMEM((2, rows_a, width), f32),
            pltpu.VMEM((rows_f, width), f32),
            dma((1,)),
            dma((3, SLOTS)),
            dma((LAYERS * n,)),
            dma((LAYERS * n,)),
            regular((1,)),
            dma((LAYERS, 2)),
            dma((LAYERS, 2)),
            regular((2,)),
            ring_sems,
            ring_sems,
            regular((2, 2, 2)),
            dma((2 * LAYERS,)),
            dma((2 * LAYERS,)),
            dma((2 * LAYERS,)),
            dma((2 * LAYERS,)),
            dma((2 * LAYERS,)),
            pltpu.VMEM((6, 16, width), f32),
            pltpu.VMEM((5, 16, width), f32),
            pltpu.VMEM((n, share, count), bf16),
            pltpu.VMEM((n, share, count), bf16),
            pltpu.VMEM((share, words), f32),
            pltpu.VMEM((4, share // 2, words), bf16),
            pltpu.VMEM((4, rows_v // 2, width), bf16),
            pltpu.VMEM((rows_v // 2, width), f32),
            pltpu.VMEM((1, width), f32),
            pltpu.VMEM((n + 2, 8, 128), f32),
            dma((2,)),
            dma((5,)),
            dma((5,)),
            dma((n - 1,)),
            dma((n - 1,)),
            dma((2, 3)),
            dma((2, 3)),
            dma((2,)),
            dma((n,)),
            dma((n,)),
        ],
        compiler_params=pltpu.CompilerParams(
            collective_id=2, has_side_effects=True, vmem_limit_bytes=VMEM_LIMIT
        ),
        name="backward_layers",
    )(
        ids, counted, losses, visible, grad, first, gains, out_grad, inputs, mixed, mid,
        proj, pre, attn_full, ffn_full, slope, act,
    )


def merged(value, axis, join):
    pieces = jax.tree.map(lambda part: lax.all_gather(part, axis), value)
    head = jax.tree.map(lambda part: part[0], pieces)
    tail = jax.tree.map(lambda part: part[1:], pieces)
    total, _ = lax.scan(lambda total, section: (join(total, section), None), head, tail)
    return total


def sinusoid(count, width):
    places = jnp.arange(count, dtype=jnp.float32)[:, None]
    freqs = jnp.exp(jnp.arange(width // 2, dtype=jnp.float32) * (-2.0 * math.log(10000.0) / width))
    angles = places * freqs[None, :]
    return jnp.concatenate([jnp.sin(angles), jnp.cos(angles)], axis=1)


def layer_norm(values, gain, shift):
    centre = jnp.mean(values, axis=-1, keepdims=True)
    offset = values - centre
    spread = jnp.mean(offset * offset, axis=-1, keepdims=True)
    inverse = lax.rsqrt(spread + norm_eps)
    normed = offset * inverse
    return (normed * gain + shift, (normed, inverse))


def norm_backward(grad, saved, gain):
    normed, inverse = saved
    scaled = grad * gain
    centred = scaled - jnp.mean(scaled, axis=-1, keepdims=True)
    result = inverse * (centred - normed * jnp.mean(scaled * normed, axis=-1, keepdims=True))
    return (result, jnp.stack([jnp.sum(grad * normed, axis=0), jnp.sum(grad, axis=0)]))


def gelu_exact(values):
    return jax.nn.gelu(values, approximate=False)


def gelu_back(hidden, grad):
    unused, pullback = jax.vjp(gelu_exact, hidden)
    return pullback(grad)[0]


def masked_scores(query, keyed, length):
    scale = query.shape[-1] ** (-0.5)
    scores = jnp.einsum("hqe,hke->hqk", query, keyed, preferred_element_type=jnp.float32) * scale
    visible = jnp.arange(keyed.shape[1]) < length
    return jnp.where(visible[None, None, :], scores, masked_score)


def fetch_forward(attn_part, ffn_part):
    return (
        lax.all_gather(attn_part, "mp", axis=1, tiled=True),
        lax.all_gather(ffn_part, "mp", axis=1, tiled=True),
    )


def fetch_backward(attn_part, ffn_part):
    return (
        lax.all_gather(attn_part, "mp", axis=1, tiled=True),
        lax.all_gather(ffn_part, "mp", axis=1, tiled=True),
    )


def reduce_layer(attn_grad, ffn_grad):
    return (
        lax.psum_scatter(attn_grad, "mp", scatter_dimension=1, tiled=True),
        lax.psum_scatter(ffn_grad, "mp", scatter_dimension=1, tiled=True),
    )


def ffn_forward(middle_b, ffn_w, unit_mask):
    hidden = jnp.einsum("td,fd->tf", middle_b, ffn_w[0], preferred_element_type=jnp.float32)
    active = (gelu_exact(hidden) * unit_mask[None, :]).astype(jnp.bfloat16)
    output = jnp.einsum("tf,fd->td", active, ffn_w[1], preferred_element_type=jnp.float32)
    return (hidden, active, output)


def ffn_backward(grad_out, middle_b, hidden, active, ffn_w, unit_mask):
    grad_active = jnp.einsum("td,fd->tf", grad_out, ffn_w[1], preferred_element_type=jnp.float32)
    grad_hidden = gelu_back(hidden, grad_active * unit_mask[None, :]).astype(jnp.bfloat16)
    up_grad = jnp.einsum("tf,td->fd", grad_hidden, middle_b, preferred_element_type=jnp.float32)
    down_grad = jnp.einsum("tf,td->fd", active, grad_out, preferred_element_type=jnp.float32)
    from_ffn = jnp.einsum("tf,fd->td", grad_hidden, ffn_w[0], preferred_element_type=jnp.float32)
    return (jnp.stack([up_grad, down_grad]), from_ffn)


def layer_forward(states, attn_w, ffn_w, pair, length, unit_mask):
    count = states.shape[0]
    inputs = states.astype(jnp.bfloat16)
    projected = jnp.einsum(
        "td,kde->kte", inputs, attn_w[:3], preferred_element_type=jnp.float32
    ).astype(jnp.bfloat16)
    heads = projected.reshape(3, count, HEADS, -1).transpose(0, 2, 1, 3)
    scores = masked_scores(heads[0], heads[1], length)
    peak = jnp.max(scores, axis=-1, keepdims=True)
    expo = jnp.exp(scores - peak)
    total = jnp.sum(expo, axis=-1, keepdims=True)
    log_total = peak + jnp.log(total)
    probs = (expo / total).astype(jnp.bfloat16)
    mixed = jnp.einsum("hqk,hke->hqe", probs, heads[2], preferred_element_type=jnp.float32)
    mixed = mixed.transpose(1, 0, 2).reshape(count, -1).astype(jnp.bfloat16)
    branch = jnp.dot(mixed, attn_w[3], preferred_element_type=jnp.float32)
    middle, norm_one = layer_norm(states + branch, pair[0, 0], pair[0, 1])
    middle_b = middle.astype(jnp.bfloat16)
    hidden, active, output = ffn_forward(middle_b, ffn_w, unit_mask)
    result, norm_two = layer_norm(middle + output, pair[1, 0], pair[1, 1])
    return (result, (inputs, heads, log_total, mixed, norm_one, middle_b, hidden, active, norm_two))


def layer_backward(grad, attn_w, ffn_w, pair, length, unit_mask, kept):
    inputs, heads, log_total, mixed, norm_one, middle_b, hidden, active, norm_two = kept
    count = inputs.shape[0]
    grad_two, pair_two = norm_backward(grad, norm_two, pair[1, 0])
    ffn_grad, from_ffn = ffn_backward(
        grad_two.astype(jnp.bfloat16), middle_b, hidden, active, ffn_w, unit_mask
    )
    grad_one, pair_one = norm_backward(grad_two + from_ffn, norm_one, pair[0, 0])
    grad_branch = grad_one.astype(jnp.bfloat16)
    output_grad = jnp.einsum("td,te->de", mixed, grad_branch, preferred_element_type=jnp.float32)
    grad_mixed = jnp.einsum("te,de->td", grad_branch, attn_w[3], preferred_element_type=jnp.float32)
    grad_mixed = grad_mixed.astype(jnp.bfloat16).reshape(count, HEADS, -1).transpose(1, 0, 2)
    scale = heads.shape[-1] ** (-0.5)
    probs = jnp.exp(masked_scores(heads[0], heads[1], length) - log_total)
    grad_values = jnp.einsum(
        "hqk,hqe->hke", probs.astype(jnp.bfloat16), grad_mixed, preferred_element_type=jnp.float32
    )
    grad_probs = jnp.einsum(
        "hqe,hke->hqk", grad_mixed, heads[2], preferred_element_type=jnp.float32
    )
    grad_scores = probs * (grad_probs - jnp.sum(grad_probs * probs, axis=-1, keepdims=True))
    grad_scores = grad_scores.astype(jnp.bfloat16)
    grad_query = (
        jnp.einsum("hqk,hke->hqe", grad_scores, heads[1], preferred_element_type=jnp.float32)
        * scale
    )
    grad_key = (
        jnp.einsum("hqk,hqe->hke", grad_scores, heads[0], preferred_element_type=jnp.float32)
        * scale
    )
    stacked = (
        jnp.stack([grad_query, grad_key, grad_values]).transpose(0, 2, 1, 3).reshape(3, count, -1)
    )
    stacked = stacked.astype(jnp.bfloat16)
    input_grad = jnp.einsum("td,kte->kde", inputs, stacked, preferred_element_type=jnp.float32)
    from_attn = jnp.einsum("kte,kde->td", stacked, attn_w[:3], preferred_element_type=jnp.float32)
    attn_grad = jnp.concatenate([input_grad, output_grad[None]], axis=0)
    return (grad_one + from_attn, attn_grad, ffn_grad, jnp.stack([pair_one, pair_two]))


def adamw(weight, moment_one, moment_two, grad, decay, rate):
    moment_one = beta_one * moment_one + (1.0 - beta_one) * grad
    moment_two = beta_two * moment_two + (1.0 - beta_two) * grad * grad
    fixed_one = moment_one / (1.0 - beta_one**STEP)
    fixed_two = moment_two / (1.0 - beta_two**STEP)
    weight = weight - rate * (fixed_one / (jnp.sqrt(fixed_two) + adam_eps) + decay * weight)
    return (moment_one, moment_two, weight)


def combine_vocab(first, second):
    peak = jnp.maximum(first[0], second[0])
    total = first[1] * jnp.exp(first[0] - peak) + second[1] * jnp.exp(second[0] - peak)
    return (peak, total, first[2] + second[2])


def local_general(
    tokens,
    lengths,
    places,
    targets,
    ramp,
    attn,
    attn_m,
    attn_v,
    ffn,
    ffn_m,
    ffn_v,
    table,
    table_m,
    table_v,
    out_table,
    out_m,
    out_v,
    gains,
    gains_m,
    gains_v,
):
    rank = lax.axis_index("mp")
    count = tokens.shape[2]
    flat_ids = tokens.reshape(-1)
    all_lengths = lengths.reshape(-1)
    length = lax.dynamic_index_in_dim(all_lengths, rank, keepdims=False)
    masks = jnp.minimum(ramp, RAMP).astype(jnp.float32) / RAMP
    unit_masks = [masks[depth] for depth in range(LAYERS)]
    looked = jnp.take(table, flat_ids, axis=0)
    embedded = lax.all_to_all(looked, "mp", split_axis=0, concat_axis=1, tiled=True)
    states, norm_zero = layer_norm(
        embedded + sinusoid(count, embedded.shape[1]), gains[0, 0], gains[0, 1]
    )
    kept_all = []
    weights_all = []
    for depth in range(LAYERS):
        attn_w, ffn_w = fetch_forward(
            attn[depth].astype(jnp.bfloat16), ffn[depth].astype(jnp.bfloat16)
        )
        states, kept = layer_forward(
            states, attn_w, ffn_w, gains[1 + 2 * depth : 3 + 2 * depth], length, unit_masks[depth]
        )
        kept_all.append(kept)
        weights_all.append(None)
    spots = places.reshape(-1)
    picked = jnp.take(states, spots, axis=0).astype(jnp.bfloat16)
    picked_all = lax.all_gather(picked, "mp", axis=0, tiled=True)
    out_b = out_table.astype(jnp.bfloat16)
    logits = jnp.einsum("rd,vd->rv", picked_all, out_b, preferred_element_type=jnp.float32)
    labels = targets.reshape(-1)
    columns = rank * out_table.shape[0] + jnp.arange(out_table.shape[0])
    hits = (labels[:, None] == columns[None, :]).astype(jnp.float32)
    peak = jnp.max(logits, axis=1)
    expsum = jnp.sum(jnp.exp(logits - peak[:, None]), axis=1)
    target_part = jnp.sum(hits * logits, axis=1)
    peak_all, expsum_all, target_all = merged((peak, expsum, target_part), "mp", combine_vocab)
    log_total = peak_all + jnp.log(expsum_all)
    slot_count = targets.shape[2]
    counted = jnp.maximum(1, all_lengths * slot_count // count)
    valid = (jnp.arange(slot_count)[None, :] < counted[:, None]).reshape(-1)
    loss_pair = jnp.stack(
        [
            jnp.sum(jnp.where(valid, log_total - target_all, 0.0)),
            jnp.sum(counted).astype(jnp.float32),
        ]
    )
    grad_logits = jnp.where(
        valid[:, None], jnp.exp(logits - log_total[:, None]) - hits, 0.0
    ).astype(jnp.bfloat16)
    out_grad = jnp.einsum("rv,rd->vd", grad_logits, picked_all, preferred_element_type=jnp.float32)
    picked_grad = lax.psum_scatter(
        jnp.dot(grad_logits, out_b, preferred_element_type=jnp.float32),
        "mp",
        scatter_dimension=0,
        tiled=True,
    )
    grad = jnp.zeros_like(states).at[spots].add(picked_grad)
    attn_parts = [None] * LAYERS
    ffn_parts = [None] * LAYERS
    pair_grads = [None] * LAYERS
    for depth in reversed(range(LAYERS)):
        attn_w, ffn_w = fetch_backward(
            attn[depth].astype(jnp.bfloat16), ffn[depth].astype(jnp.bfloat16)
        )
        grad, attn_grad, ffn_grad, pair_grad = layer_backward(
            grad,
            attn_w,
            ffn_w,
            gains[1 + 2 * depth : 3 + 2 * depth],
            length,
            unit_masks[depth],
            kept_all[depth],
        )
        attn_parts[depth], ffn_parts[depth] = reduce_layer(attn_grad, ffn_grad)
        pair_grads[depth] = pair_grad
    grad_sum, zero_grad = norm_backward(grad, norm_zero, gains[0, 0])
    returned = lax.all_to_all(grad_sum, "mp", split_axis=1, concat_axis=0, tiled=True)
    table_grad = jnp.zeros_like(table).at[flat_ids].add(returned)
    gains_grad = jnp.concatenate([zero_grad[None]] + pair_grads, axis=0)
    attn_sum, ffn_sum, table_sum, out_sum, gains_part, loss = lax.psum(
        (jnp.stack(attn_parts), jnp.stack(ffn_parts), table_grad, out_grad, gains_grad, loss_pair),
        "dp",
    )
    shard_squares = (
        jnp.sum(attn_sum * attn_sum)
        + jnp.sum(ffn_sum * ffn_sum)
        + jnp.sum(table_sum * table_sum)
        + jnp.sum(out_sum * out_sum)
    )
    square_total, gains_sum = lax.psum((shard_squares, gains_part), "mp")
    grad_norm = jnp.sqrt(square_total + jnp.sum(gains_sum * gains_sum))
    factor = clip_limit / jnp.maximum(grad_norm, clip_limit)
    attn_m_new, attn_v_new, attn_new = adamw(
        attn, attn_m, attn_v, attn_sum * factor, weight_decay, learn_rate
    )
    ffn_m_new, ffn_v_new, ffn_new = adamw(
        ffn, ffn_m, ffn_v, ffn_sum * factor, weight_decay, learn_rate
    )
    table_m_new, table_v_new, table_new = adamw(
        table, table_m, table_v, table_sum * factor, weight_decay, learn_rate
    )
    out_m_new, out_v_new, out_new = adamw(
        out_table, out_m, out_v, out_sum * factor, weight_decay, learn_rate
    )
    gains_m_new, gains_v_new, gains_new = adamw(
        gains, gains_m, gains_v, gains_sum * factor, 0.0, gain_rate
    )
    return (
        loss,
        grad_norm.reshape(1),
        attn_m_new,
        attn_v_new,
        attn_new,
        ffn_m_new,
        ffn_v_new,
        ffn_new,
        table_m_new,
        table_v_new,
        table_new,
        out_m_new,
        out_v_new,
        out_new,
        gains_m_new,
        gains_v_new,
        gains_new,
    )


def local(
    tokens,
    lengths,
    places,
    targets,
    ramp,
    attn,
    attn_m,
    attn_v,
    ffn,
    ffn_m,
    ffn_v,
    table,
    table_m,
    table_v,
    out_table,
    out_m,
    out_v,
    gains,
    gains_m,
    gains_v,
):
    rank = lax.axis_index("mp")
    n = tokens.shape[1]
    count, width = tokens.shape[2], gains.shape[2]
    flat_ids = tokens.reshape(-1)
    all_lengths = lengths.reshape(-1)
    length = lax.dynamic_index_in_dim(all_lengths, rank, keepdims=False)
    masks = jnp.minimum(ramp, RAMP).astype(jnp.float32) / RAMP
    visible = (jnp.arange(count) < length).astype(jnp.float32)[None, :]
    slot_count = targets.shape[2]
    slots = 32 * -(-slot_count // 32)
    counted = jnp.maximum(1, all_lengths * slot_count // count)
    valid = (jnp.arange(slots)[None, :] < counted[:, None]).astype(jnp.float32).reshape(1, -1)
    extra = slots - slot_count
    spots = jnp.pad(places.reshape(-1), (0, extra), constant_values=-1)[:, None]
    labels = jnp.pad(targets[0], ((0, 0), (0, extra)), constant_values=-1).reshape(1, -1)
    where = sinusoid(count, width)
    attn_full, ffn_full, first, *kept, slope, act, grad, out_grad, losses = forward_call(
        n, tokens[0], table, where, visible, gains, masks, spots, labels, valid, out_table, attn, ffn
    )
    tally = jnp.broadcast_to(jnp.sum(counted).astype(jnp.float32), (1, 128))
    attn_sum, ffn_sum, table_turned, out_sum, small, square = backward_call(
        n, tokens[0], tally, losses, visible, grad, first, gains, out_grad, kept, attn_full, ffn_full, slope, act, table
    )
    table_sum = table_turned.T
    gains_sum = small[:10].reshape(gains.shape)
    grad_norm = jnp.sqrt(square[0, 0])
    factor = clip_limit / jnp.maximum(grad_norm, clip_limit)
    attn_m_new, attn_v_new, attn_new = adamw(
        attn, attn_m, attn_v, attn_sum * factor, weight_decay, learn_rate
    )
    ffn_m_new, ffn_v_new, ffn_new = adamw(
        ffn, ffn_m, ffn_v, ffn_sum * factor, weight_decay, learn_rate
    )
    table_m_new, table_v_new, table_new = adamw(
        table, table_m, table_v, table_sum * factor, weight_decay, learn_rate
    )
    out_m_new, out_v_new, out_new = adamw(
        out_table, out_m, out_v, out_sum * factor, weight_decay, learn_rate
    )
    gains_m_new, gains_v_new, gains_new = adamw(
        gains, gains_m, gains_v, gains_sum * factor, 0.0, gain_rate
    )
    return (
        small[10, :2],
        grad_norm.reshape(1),
        attn_m_new,
        attn_v_new,
        attn_new,
        ffn_m_new,
        ffn_v_new,
        ffn_new,
        table_m_new,
        table_v_new,
        table_new,
        out_m_new,
        out_v_new,
        out_new,
        gains_m_new,
        gains_v_new,
        gains_new,
    )


def solution(mesh):
    in_specs = (
        P("dp", None, None),
        P("dp", None),
        P("dp", "mp", None),
        P("dp", None, None),
        P(),
        P(None, None, "mp", None),
        P(None, None, "mp", None),
        P(None, None, "mp", None),
        P(None, None, "mp", None),
        P(None, None, "mp", None),
        P(None, None, "mp", None),
        P(None, "mp"),
        P(None, "mp"),
        P(None, "mp"),
        P("mp", None),
        P("mp", None),
        P("mp", None),
        P(),
        P(),
        P(),
    )
    out_specs = (
        P(),
        P(),
        P(None, None, "mp", None),
        P(None, None, "mp", None),
        P(None, None, "mp", None),
        P(None, None, "mp", None),
        P(None, None, "mp", None),
        P(None, None, "mp", None),
        P(None, "mp"),
        P(None, "mp"),
        P(None, "mp"),
        P("mp", None),
        P("mp", None),
        P("mp", None),
        P(),
        P(),
        P(),
    )
    fits = mesh.shape['mp'] == 8 and mesh.shape['dp'] == 4
    chosen = local if fits else local_general
    return jax.shard_map(chosen, mesh=mesh, in_specs=in_specs, out_specs=out_specs, check_vma=False)
```

```python
import functools
import math

import jax
import jax.numpy as jnp
from jax import lax
from jax.experimental import pallas as pl
from jax.experimental.pallas import tpu as pltpu
from jax.sharding import PartitionSpec as P

HEADS = 12
LAYERS = 2
STEP = 10
RAMP = 4


norm_eps = 1e-05
beta_one = 0.9
beta_two = 0.999
learn_rate = 0.02
gain_rate = 0.3
weight_decay = 0.01
adam_eps = 1e-08
clip_limit = 1.0
masked_score = -1000000000.0


MESH = pl.DeviceIdType.MESH
VMEM_LIMIT = 62 * 1024 * 1024
SLOTS = 3


def dot_nn(left, right):
    return lax.dot_general(
        left, right, (((1,), (0,)), ((), ())), preferred_element_type=jnp.float32
    )


def dot_nt(left, right):
    return lax.dot_general(
        left, right, (((1,), (1,)), ((), ())), preferred_element_type=jnp.float32
    )


def dot_tn(left, right):
    return lax.dot_general(
        left, right, (((0,), (0,)), ((), ())), preferred_element_type=jnp.float32
    )


def ring_index(place, n):
    late = place // (n // 2)
    return (1 - late) * 2 * place + late * (2 * (n - 1 - place) + 1)


def ring_place(index, n):
    odd = index % 2
    return (1 - odd) * (index // 2) + odd * (n - 1 - index // 2)


class Spot:
    def __init__(self, n):
        self.n = n
        self.dp = lax.axis_index("dp")
        self.mp = lax.axis_index("mp")
        self.core = self.dp % 2
        self.row = self.dp // 2
        self.place = ring_place(self.mp, n)
        self.partner = (self.dp + 1 - 2 * self.core, self.mp)
        self.across = ((self.dp + 2) % 4, self.mp)
        self.ring = (
            (self.dp, ring_index((self.place + 1) % n, n)),
            (self.dp, ring_index((self.place + n - 1) % n, n)),
        )

    def shard(self, offset):
        return ring_index((self.place + offset + self.n) % self.n, self.n)


def greet(devices):
    barrier = pltpu.get_barrier_semaphore()
    for device in devices:
        pl.semaphore_signal(barrier, inc=1, device_id=device, device_id_type=MESH)
    pl.semaphore_wait(barrier, len(devices))


def last_step(n, way, part):
    return n // 2 if way == part else n // 2 - 1


WAYS = ((0, 0), (1, 1), (0, 1), (1, 0))


def ring_columns(row, width, cut):
    return pl.ds(pl.multiple_of(row * cut, 128), width - cut)


def edge_columns(row, width, cut):
    return pl.ds(pl.multiple_of(row * (width - cut), 128), cut)


def cut_of(width, share):
    return 128 * (width // 128 // share)


def normed_of(values):
    centre = jnp.mean(values, axis=-1, keepdims=True)
    offset = values - centre
    spread = jnp.mean(offset * offset, axis=-1, keepdims=True)
    inverse = lax.rsqrt(spread + norm_eps)
    return offset * inverse, inverse


def forward_kernel(
    n,
    ids_ref,
    table_ref,
    where_ref,
    visible_ref,
    gains_ref,
    mask_ref,
    places_ref,
    labels_ref,
    valid_ref,
    out_ref,
    attn_sh,
    ffn_sh,
    attn_full,
    ffn_full,
    first_ref,
    inputs_ref,
    proj_ref,
    mixed_ref,
    pre_ref,
    mid_ref,
    slope_ref,
    act_ref,
    grad_ref,
    out_grad_ref,
    loss_ref,
    wa,
    wf,
    raw_a,
    raw_f,
    slope,
    act,
    state,
    row_out,
    row_in,
    picked,
    stats,
    back_out,
    back_in,
    raw_sem,
    out_sem,
    kept_sem,
    ring_send,
    ring_recv,
    core_send,
    core_recv,
    across_send,
    across_recv,
    fan_send,
    fan_recv,
):
    spot = Spot(n)
    core = spot.core
    rows_a = attn_sh.shape[2]
    rows_f = ffn_sh.shape[2]
    part_f = rows_f // 2
    steps = n // 2
    count, width = first_ref.shape
    share_e = table_ref.shape[0]
    words = table_ref.shape[1]
    slots = places_ref.shape[0]

    def rows_at(shard, rows):
        return pl.ds(pl.multiple_of(shard * rows, 16), rows)

    def remote(source, target, send, recv, device):
        return pltpu.make_async_remote_copy(
            src_ref=source,
            dst_ref=target,
            send_sem=send,
            recv_sem=recv,
            device_id=device,
            device_id_type=MESH,
        )

    def chunk(piece, shard, part, side, edge):
        kind, depth = piece % 2, piece // 2
        cut = cut_of(width, 6 if kind == 0 else 3)
        if edge is None:
            columns = ring_columns(spot.row, width, cut)
        else:
            columns = edge_columns(edge, width, cut)
        if kind == 0:
            return wa.at[depth, 2 * side + part, rows_at(shard, rows_a), columns]
        start = pl.multiple_of(shard * rows_f + part * part_f, 16)
        return wf.at[depth, side, pl.ds(start, part_f), columns]

    def sign(way):
        return -1 if way == 0 else 1

    def ring_copy(piece, way, part, step, arriving):
        target = chunk(piece, spot.shard(sign(way) * (step - 1 + arriving)), part, core, None)
        return remote(
            target,
            target,
            ring_send.at[piece, way, part, step - 1],
            ring_recv.at[piece, way, part, step - 1],
            spot.ring[way],
        )

    def core_copy(piece, way, part, step, side, edge):
        target = chunk(piece, spot.shard(sign(way) * step), part, side, edge)
        lane = 0 if edge is None else 1
        return remote(
            target,
            target,
            core_send.at[lane, piece, way, part, step - 1],
            core_recv.at[lane, piece, way, part, step - 1],
            spot.partner,
        )

    def across_copy(piece, way, part, step, row):
        target = chunk(piece, spot.shard(sign(way) * step), part, core, row)
        return remote(
            target,
            target,
            across_send.at[piece, way, part, step - 1],
            across_recv.at[piece, way, part, step - 1],
            spot.across,
        )

    def peer(offset):
        return (spot.mp + offset + n) % n

    def fan_copy(which, offset, source, target):
        return remote(
            source,
            target,
            fan_send.at[which, offset - 1],
            fan_recv.at[which, offset - 1],
            (spot.dp, peer(offset)),
        )

    def share(which, buffer, offset):
        return fan_copy(which, offset, buffer.at[spot.mp], buffer.at[spot.mp])

    def arrived(which, buffer, offset):
        return fan_copy(which, offset, buffer.at[peer(-offset)], buffer.at[peer(-offset)])

    def deal(which, source, target, offset):
        return fan_copy(which, offset, source.at[peer(offset)], target.at[spot.mp])

    def raw_copy(piece):
        kind, depth = piece % 2, piece // 2
        if kind == 0:
            return pltpu.make_async_copy(attn_sh.at[depth], raw_a.at[depth], raw_sem.at[piece])
        return pltpu.make_async_copy(ffn_sh.at[depth], raw_f.at[depth], raw_sem.at[piece])

    def take_own(piece):
        kind, depth = piece % 2, piece // 2
        raw_copy(piece).wait()
        if kind == 0:
            for which in range(4):
                wa[depth, which, rows_at(spot.mp, rows_a), :] = raw_a[depth, which].astype(
                    jnp.bfloat16
                )
        else:
            for which in range(2):
                wf[depth, which, rows_at(spot.mp, rows_f), :] = raw_f[depth, which].astype(
                    jnp.bfloat16
                )

    def launch(piece):
        for way, part in WAYS:
            ring_copy(piece, way, part, 1, 0).start()

    def chains(step):
        return [(way, part) for way, part in WAYS if step <= last_step(n, way, part)]

    def pass_on(piece, step):
        for way, part in chains(step):
            ring_copy(piece, way, part, step, 1).wait_recv()
            if step < last_step(n, way, part):
                ring_copy(piece, way, part, step + 1, 0).start()
            across_copy(piece, way, part, step, spot.row).start()
            core_copy(piece, way, part, step, core, None).start()

    def pass_edge(piece, step):
        for way, part in chains(step):
            across_copy(piece, way, part, step, 1 - spot.row).wait_recv()
            core_copy(piece, way, part, step, core, 1 - spot.row).start()

    def settle(piece, step):
        for way, part in chains(step):
            core_copy(piece, way, part, step, 1 - core, None).wait_recv()
            core_copy(piece, way, part, step, 1 - core, 1 - spot.row).wait_recv()

    def look_up(offset):
        whose = peer(offset)
        tokens = ids_ref[pl.ds(whose, 1), :]

        def block(index, total):
            start = pl.multiple_of(index * 256, 256)
            word = lax.broadcasted_iota(jnp.int32, (256, 1), 0) + start
            chosen = (word == tokens).astype(jnp.bfloat16)
            return total + dot_nn(table_ref[:, pl.ds(start, 256)], chosen)

        found = lax.fori_loop(
            0, words // 256, block, jnp.zeros((share_e, count), jnp.float32)
        )
        row_out[whose] = found.astype(jnp.bfloat16)
        if offset > 0:
            deal(0, row_out, row_in, offset).start()

    for piece in range(2 * LAYERS):
        raw_copy(piece).start()
    greet([spot.partner, spot.across] + [(spot.dp, peer(offset)) for offset in range(1, n)])
    take_own(0)
    launch(0)
    for offset in range(1, 4):
        look_up(offset)
    pass_on(0, 1)
    for offset in range(4, 7):
        look_up(offset)
    pass_on(0, 2)
    pass_edge(0, 1)
    take_own(1)
    launch(1)
    look_up(7)
    look_up(0)
    row_in[spot.mp] = row_out[spot.mp]
    pass_on(0, 3)
    pass_edge(0, 2)
    for offset in range(1, n):
        arrived(0, row_in, offset).wait_recv()
    first_ref[...] = where_ref[...] + row_in[...].reshape(width, count).astype(jnp.float32).T
    normed, _ = normed_of(first_ref[...])
    state[...] = normed * gains_ref[0, 0:1, :] + gains_ref[0, 1:2, :]
    take_own(2)
    take_own(3)
    pass_on(0, 4)
    pass_edge(0, 3)

    lanes = lax.broadcasted_iota(jnp.int32, (1, 128), 1) < 64
    visible = visible_ref[...] > 0.0

    def head_pair(depth, pair):
        columns = pl.ds(pl.multiple_of(pair * 128, 128), 128)
        query = proj_ref[depth, 0, :, columns]
        keyed = proj_ref[depth, 1, :, columns]
        valued = proj_ref[depth, 2, :, columns]
        outs = []
        for side in range(2):
            mine = lanes if side == 0 else jnp.logical_not(lanes)
            scores = dot_nt(jnp.where(mine, query, jnp.zeros_like(query)), keyed) * 0.125
            scores = jnp.where(visible, scores, masked_score)
            expo = jnp.exp(scores - jnp.max(scores, axis=-1, keepdims=True))
            total = jnp.sum(expo, axis=-1, keepdims=True)
            outs.append(dot_nn((expo / total).astype(jnp.bfloat16), valued))
        mixed_ref[depth, :, columns] = jnp.where(lanes, outs[0], outs[1]).astype(jnp.bfloat16)

    def kept_copies(turn, depth, shard):
        slot = turn % SLOTS
        return (
            pltpu.make_async_copy(slope.at[slot], slope_ref.at[depth, shard], kept_sem.at[0, slot]),
            pltpu.make_async_copy(act.at[slot], act_ref.at[depth, shard], kept_sem.at[1, slot]),
        )

    turns = []

    def ffn_shard(depth, offset):
        shard = spot.shard(offset)
        turn = len(turns)
        turns.append((depth, shard))
        if turn >= SLOTS:
            for copy in kept_copies(turn, *turns[turn - SLOTS]):
                copy.wait()
        rows = rows_at(shard, rows_f)
        hidden = dot_nt(mid_ref[depth], wf[depth, 0, rows, :])
        spread = 0.5 * (1.0 + lax.erf(hidden * (0.5**0.5)))
        mask = mask_ref[depth : depth + 1, pl.ds(pl.multiple_of(shard * rows_f, 128), rows_f)]
        bell = jnp.exp(hidden * hidden * -0.5) * (1.0 / math.sqrt(2.0 * math.pi))
        slope[turn % SLOTS] = (spread + hidden * bell) * mask
        active = (hidden * spread * mask).astype(jnp.bfloat16)
        act[turn % SLOTS] = active
        for copy in kept_copies(turn, depth, shard):
            copy.start()
        pre_ref[depth, 1] += dot_nn(active, wf[depth, 1, rows, :])

    out_copies = []
    for depth in range(LAYERS):
        piece_a, piece_f = 2 * depth, 2 * depth + 1
        if depth > 0:
            pass_on(piece_a, 1)
            pass_on(piece_a, 2)
            pass_edge(piece_a, 1)
            pass_on(piece_a, 3)
            pass_edge(piece_a, 2)
            launch(piece_f)
            pass_on(piece_a, 4)
            pass_edge(piece_a, 3)
        pass_edge(piece_a, 4)
        for step in range(1, steps + 1):
            settle(piece_a, step)
        copy = pltpu.make_async_copy(wa.at[depth], attn_full.at[depth], out_sem.at[piece_a])
        copy.start()
        out_copies.append(copy)
        inputs = state[...].astype(jnp.bfloat16)
        inputs_ref[depth] = inputs
        for which in range(3):
            proj_ref[depth, which] = dot_nn(inputs, wa[depth, which]).astype(jnp.bfloat16)
        pass_on(piece_f, 1)

        @pl.loop(0, HEADS // 2)
        def _(pair):
            head_pair(depth, pair)

        pre_ref[depth, 0] = state[...] + dot_nn(mixed_ref[depth], wa[depth, 3])
        normed, _ = normed_of(pre_ref[depth, 0])
        middle = (
            normed * gains_ref[1 + 2 * depth, 0:1, :] + gains_ref[1 + 2 * depth, 1:2, :]
        )
        mid_ref[depth] = middle.astype(jnp.bfloat16)
        pre_ref[depth, 1] = middle
        pass_on(piece_f, 2)
        pass_edge(piece_f, 1)
        ffn_shard(depth, 0)
        settle(piece_f, 1)
        ffn_shard(depth, -1)
        ffn_shard(depth, 1)
        pass_on(piece_f, 3)
        pass_edge(piece_f, 2)
        if depth + 1 < LAYERS:
            launch(piece_a + 2)
        settle(piece_f, 2)
        ffn_shard(depth, -2)
        ffn_shard(depth, 2)
        pass_edge(piece_f, 3)
        pass_on(piece_f, 4)
        settle(piece_f, 3)
        ffn_shard(depth, -3)
        ffn_shard(depth, 3)
        pass_edge(piece_f, 4)
        settle(piece_f, 4)
        ffn_shard(depth, 4)
        copy = pltpu.make_async_copy(wf.at[depth], ffn_full.at[depth], out_sem.at[piece_f])
        copy.start()
        out_copies.append(copy)
        normed, _ = normed_of(pre_ref[depth, 1])
        state[...] = normed * gains_ref[2 + 2 * depth, 0:1, :] + gains_ref[2 + 2 * depth, 1:2, :]

    spots = (
        lax.broadcasted_iota(jnp.int32, (slots, count), 1) == places_ref[...]
    ).astype(jnp.bfloat16)
    picked[spot.mp] = dot_nn(spots, state[...].astype(jnp.bfloat16)).astype(jnp.bfloat16)
    for offset in range(1, n):
        share(1, picked, offset).start()
    out_b = out_ref[...].astype(jnp.bfloat16)
    rows_v = out_ref.shape[0]
    hits = (
        labels_ref[...] == spot.mp * rows_v + lax.broadcasted_iota(jnp.int32, (rows_v, 1), 0)
    ).astype(jnp.float32)
    for offset in range(1, n):
        arrived(1, picked, offset).wait_recv()
    picked_all = picked[...].reshape(n * slots, -1)
    logits = dot_nt(out_b, picked_all)
    peak = jnp.max(logits, axis=0, keepdims=True)
    expsum = jnp.sum(jnp.exp(logits - peak), axis=0, keepdims=True)
    stats[spot.mp, 0:1, :] = peak
    stats[spot.mp, 1:2, :] = expsum
    stats[spot.mp, 2:3, :] = jnp.sum(hits * logits, axis=0, keepdims=True)
    for offset in range(1, n):
        share(2, stats, offset).start()
    for offset in range(1, n):
        arrived(2, stats, offset).wait_recv()
    peak = stats[0, 0:1, :]
    for whose in range(1, n):
        peak = jnp.maximum(peak, stats[whose, 0:1, :])
    expsum = stats[0, 1:2, :] * jnp.exp(stats[0, 0:1, :] - peak)
    target = stats[0, 2:3, :]
    for whose in range(1, n):
        expsum = expsum + stats[whose, 1:2, :] * jnp.exp(stats[whose, 0:1, :] - peak)
        target = target + stats[whose, 2:3, :]
    log_total = peak + jnp.log(expsum)
    valid = valid_ref[...] > 0.0
    loss_ref[...] = jnp.where(valid, log_total - target, 0.0)
    grad_logits = jnp.where(valid, jnp.exp(logits - log_total) - hits, 0.0).astype(jnp.bfloat16)
    picked_grad = dot_tn(grad_logits, out_b).astype(jnp.bfloat16)
    for whose in range(n):
        back_out[whose] = picked_grad[whose * slots : (whose + 1) * slots, :]
    for offset in range(1, n):
        deal(3, back_out, back_in, offset).start()
    back_in[spot.mp] = back_out[spot.mp]
    out_grad_ref[...] = dot_nn(grad_logits, picked_all)
    for offset in range(1, n):
        arrived(3, back_in, offset).wait_recv()
    summed = back_in[0].astype(jnp.float32)
    for whose in range(1, n):
        summed = summed + back_in[whose].astype(jnp.float32)
    high = summed.astype(jnp.bfloat16)
    low = (summed - high.astype(jnp.float32)).astype(jnp.bfloat16)
    grad_ref[...] = dot_tn(spots, high) + dot_tn(spots, low)

    for piece in range(2 * LAYERS):
        for way, part in WAYS:
            for step in range(1, last_step(n, way, part) + 1):
                ring_copy(piece, way, part, step, 0).wait_send()
                across_copy(piece, way, part, step, spot.row).wait_send()
                core_copy(piece, way, part, step, core, None).wait_send()
                core_copy(piece, way, part, step, core, 1 - spot.row).wait_send()
    for offset in range(1, n):
        deal(0, row_out, row_in, offset).wait_send()
        share(1, picked, offset).wait_send()
        share(2, stats, offset).wait_send()
        deal(3, back_out, back_in, offset).wait_send()
    for turn in range(len(turns) - SLOTS, len(turns)):
        for copy in kept_copies(turn, *turns[turn]):
            copy.wait()
    for copy in out_copies:
        copy.wait()


def forward_call(
    n, ids, table, where, visible, gains, masks, places, labels, valid, out_table, attn, ffn
):
    count, width = where.shape
    rows_f = ffn.shape[2]
    slots = places.shape[0]
    f32, bf16 = jnp.float32, jnp.bfloat16
    vmem = pl.BlockSpec(memory_space=pltpu.VMEM)
    anywhere = pl.BlockSpec(memory_space=pl.ANY)
    shape = jax.ShapeDtypeStruct
    dma = pltpu.SemaphoreType.DMA
    sems = dma((2 * LAYERS, 2, 2, n // 2))
    core_sems = dma((2, 2 * LAYERS, 2, 2, n // 2))
    return pl.pallas_call(
        functools.partial(forward_kernel, n),
        out_shape=(
            shape((LAYERS, 4, width, width), bf16),
            shape((LAYERS, 2, rows_f * n, width), bf16),
            shape((count, width), f32),
            shape((LAYERS, count, width), bf16),
            shape((LAYERS, 3, count, width), bf16),
            shape((LAYERS, count, width), bf16),
            shape((LAYERS, 2, count, width), f32),
            shape((LAYERS, count, width), bf16),
            shape((LAYERS, n, count, rows_f), f32),
            shape((LAYERS, n, count, rows_f), bf16),
            shape((count, width), f32),
            shape(out_table.shape, f32),
            shape((1, n * slots), f32),
        ),
        in_specs=[vmem] * 10 + [anywhere] * 2,
        out_specs=(anywhere,) * 2 + (vmem,) * 6 + (anywhere,) * 2 + (vmem,) * 3,
        scratch_shapes=[
            pltpu.VMEM((LAYERS, 4, width, width), bf16),
            pltpu.VMEM((LAYERS, 2, rows_f * n, width), bf16),
            pltpu.VMEM(attn.shape, f32),
            pltpu.VMEM(ffn.shape, f32),
            pltpu.VMEM((SLOTS, count, rows_f), f32),
            pltpu.VMEM((SLOTS, count, rows_f), bf16),
            pltpu.VMEM((count, width), f32),
            pltpu.VMEM((n, table.shape[0], count), bf16),
            pltpu.VMEM((n, table.shape[0], count), bf16),
            pltpu.VMEM((n, slots, width), bf16),
            pltpu.VMEM((n, 8, n * slots), f32),
            pltpu.VMEM((n, slots, width), bf16),
            pltpu.VMEM((n, slots, width), bf16),
            dma((2 * LAYERS,)),
            dma((2 * LAYERS,)),
            dma((2, SLOTS)),
            sems,
            sems,
            core_sems,
            core_sems,
            sems,
            sems,
            dma((4, n - 1)),
            dma((4, n - 1)),
        ],
        compiler_params=pltpu.CompilerParams(
            collective_id=1, has_side_effects=True, vmem_limit_bytes=VMEM_LIMIT
        ),
        name="forward_layers",
    )(ids, table, where, visible, gains, masks, places, labels, valid, out_table, attn, ffn)


def norm_back(grad, values, gain):
    normed, inverse = normed_of(values)
    scaled = grad * gain
    centred = scaled - jnp.mean(scaled, axis=-1, keepdims=True)
    result = inverse * (centred - normed * jnp.mean(scaled * normed, axis=-1, keepdims=True))
    return (
        result,
        jnp.sum(grad * normed, axis=0, keepdims=True),
        jnp.sum(grad, axis=0, keepdims=True),
    )


def backward_kernel(
    n,
    ids_ref,
    counted_ref,
    losses_ref,
    visible_ref,
    gains_ref,
    out_grad_ref,
    inputs_ref,
    mixed_ref,
    mid_ref,
    grad_ref,
    first_ref,
    proj_all,
    pre_all,
    attn_full,
    ffn_full,
    slope_all,
    act_all,
    attn_sum,
    ffn_sum,
    table_sum,
    out_sum,
    small_out,
    square_out,
    proj,
    pre,
    wa,
    wf,
    slope,
    act,
    sum_a,
    sum_f,
    theirs_f,
    land_f,
    land_a,
    ring_a,
    ring_f,
    edge_a,
    edge_f,
    state,
    grad_rows,
    left_a,
    left_f,
    right_f,
    spread_a,
    spread_f,
    done_a,
    done_f,
    wa_sem,
    load_sem,
    core_send,
    core_recv,
    core_free,
    swap_send,
    swap_recv,
    swap_free,
    ring_send,
    ring_recv,
    ring_free,
    give_send,
    give_recv,
    across_send,
    across_recv,
    out_sem,
    last_send,
    last_recv,
    small,
    small_in,
    columns_out,
    columns_in,
    table_grad,
    table_half,
    out_half,
    out_done,
    squares,
    square_parts,
    proj_sem,
    small_send,
    small_recv,
    deal_send,
    deal_recv,
    half_send,
    half_recv,
    half_sem,
    norm_send,
    norm_recv,
):
    spot = Spot(n)
    core = spot.core
    other = 1 - core
    rows_a = attn_sum.shape[2]
    rows_f = ffn_sum.shape[2]
    part_f = rows_f // 2
    width = attn_sum.shape[3]
    order = (4, 3, -3, 2, -2, 1, -1, 0)
    total = LAYERS * n

    def rows_at(shard, rows):
        return pl.ds(pl.multiple_of(shard * rows, 16), rows)

    def peer(offset):
        return (spot.mp + offset + n) % n

    def remote(source, target, send, recv, device):
        return pltpu.make_async_remote_copy(
            src_ref=source,
            dst_ref=target,
            send_sem=send,
            recv_sem=recv,
            device_id=device,
            device_id_type=MESH,
        )

    def turn_of(turn):
        return LAYERS - 1 - turn // n, spot.shard(order[turn % n])

    def loads(turn):
        depth, shard = turn_of(turn)
        slot = turn % SLOTS
        return (
            pltpu.make_async_copy(
                ffn_full.at[depth, :, rows_at(shard, rows_f), :], wf.at[slot], load_sem.at[0, slot]
            ),
            pltpu.make_async_copy(slope_all.at[depth, shard], slope.at[slot], load_sem.at[1, slot]),
            pltpu.make_async_copy(act_all.at[depth, shard], act.at[slot], load_sem.at[2, slot]),
        )

    def load_pre(depth):
        return pltpu.make_async_copy(pre_all.at[depth], pre, proj_sem.at[0])

    def load_proj(depth):
        return pltpu.make_async_copy(proj_all.at[depth], proj, proj_sem.at[1])

    def load_attn(depth):
        return pltpu.make_async_copy(attn_full.at[depth], wa, wa_sem.at[0])

    def core_copy(turn):
        slot = turn % SLOTS
        return remote(
            theirs_f.at[slot],
            land_f.at[slot],
            core_send.at[turn],
            core_recv.at[turn],
            spot.partner,
        )

    def fold(turn):
        depth, shard = turn_of(turn)
        core_copy(turn).wait_recv()
        sum_f[depth, shard] = (
            sum_f[depth, shard].astype(jnp.float32)
            + land_f[turn % SLOTS].astype(jnp.float32)
        ).astype(jnp.bfloat16)
        if turn + SLOTS < total:
            pl.semaphore_signal(
                core_free.at[0], inc=1, device_id=spot.partner, device_id_type=MESH
            )

    def swap_copy(depth, part):
        return remote(
            wa.at[part],
            land_a.at[part],
            swap_send.at[depth, part],
            swap_recv.at[depth, part],
            spot.partner,
        )

    def cut_at(piece):
        return cut_of(width, 6)

    def summed(piece, shard, part):
        kind, depth = piece % 2, piece // 2
        columns = ring_columns(spot.row, width, cut_at(piece))
        if kind == 0:
            return sum_a.at[depth, part, rows_at(shard, rows_a), columns]
        return sum_f.at[depth, shard, pl.ds(part * part_f, part_f), columns]

    def landed(piece, way, part, step):
        columns = pl.ds(0, width - cut_at(piece))
        return (ring_a if piece % 2 == 0 else ring_f).at[way, part, step - 1, :, columns]

    def give_copy(piece, index):
        kind, depth = piece % 2, piece // 2
        cut = cut_at(piece)
        give = edge_columns(1 - spot.row, width, cut)
        if kind == 0:
            source, target = sum_a.at[depth, index, :, give], edge_a.at[depth, index]
        else:
            shard = spot.shard(order[index])
            source = sum_f.at[depth, shard, :, give]
            target = edge_f.at[depth, index]
        return remote(
            source,
            target,
            give_send.at[piece, index],
            give_recv.at[piece, index],
            spot.across,
        )

    def absorb_rows(into, source):
        into[...] = (into[...].astype(jnp.float32) + source[...].astype(jnp.float32)).astype(
            jnp.bfloat16
        )

    def absorb(piece, index):
        kind, depth = piece % 2, piece // 2
        take = edge_columns(spot.row, width, cut_at(piece))
        give_copy(piece, index).wait_recv()
        if kind == 0:
            @pl.loop(0, n)
            def _(block):
                rows = rows_at(block, rows_a)
                absorb_rows(
                    sum_a.at[depth, index, rows, take], edge_a.at[depth, index, rows, :]
                )
        else:
            shard = spot.shard(order[index])
            absorb_rows(
                sum_f.at[depth, shard, :, take],
                edge_f.at[depth, index],
            )

    def ring_copy(piece, way, part, step):
        offset = last_step(n, way, part) - step + 1
        shard = spot.shard(offset if way == 0 else -offset)
        return remote(
            summed(piece, shard, part),
            landed(piece, way, part, step),
            ring_send.at[piece, way, part, step - 1],
            ring_recv.at[piece, way, part, step - 1],
            spot.ring[way],
        )

    def ring_start(piece, way, part, step):
        if piece // 2 < LAYERS - 1:
            pl.semaphore_wait(ring_free.at[piece % 2, way, part, step - 1], 1)
        ring_copy(piece, way, part, step).start()

    def release(piece, way, part, step):
        if piece // 2 > 0:
            pl.semaphore_signal(
                ring_free.at[piece % 2, way, part, step - 1],
                inc=1,
                device_id=spot.ring[1 - way],
                device_id_type=MESH,
            )

    def launch(piece, long):
        for way, part in WAYS:
            if (way == part) == long:
                ring_start(piece, way, part, 1)

    def relay(piece, step):
        if piece % 2 == 1 and step < 3:
            absorb(piece, 2 * step + 1)
            absorb(piece, 2 * step + 2)
        for way, part in WAYS:
            last = last_step(n, way, part)
            if step < last:
                ring_copy(piece, way, part, step).wait_recv()
                shard = spot.shard(last - step if way == 0 else step - last)
                absorb_rows(summed(piece, shard, part), landed(piece, way, part, step))
                ring_start(piece, way, part, step + 1)
                release(piece, way, part, step)

    def spread_of(piece, side):
        kind, depth = piece % 2, piece // 2
        columns = pl.ds(0, width - cut_at(piece))
        if kind == 0:
            return spread_a.at[depth, side, :, :, columns]
        return spread_f.at[depth, side, :, columns]

    def across_copy(piece):
        return remote(
            spread_of(piece, 0),
            spread_of(piece, 1),
            across_send.at[piece],
            across_recv.at[piece],
            spot.across,
        )

    def finish(piece):
        if piece % 2 == 1:
            absorb(piece, n - 1)
        for part in range(2):
            value = summed(piece, spot.mp, part)[...].astype(jnp.float32)
            for way in range(2):
                step = last_step(n, way, part)
                ring_copy(piece, way, part, step).wait_recv()
                value = value + landed(piece, way, part, step)[...].astype(jnp.float32)
                release(piece, way, part, step)
            value = value.astype(jnp.bfloat16)
            if piece % 2 == 0:
                spread_of(piece, 0)[part] = value
            else:
                spread_of(piece, 0)[pl.ds(part * part_f, part_f), :] = value
        across_copy(piece).start()

    def out_copies(piece):
        kind, depth = piece % 2, piece // 2
        if kind == 0:
            source, target = done_a, attn_sum.at[depth, pl.ds(2 * core, 2)]
        else:
            source, target = done_f, ffn_sum.at[depth, core]
        return (
            pltpu.make_async_copy(source, target, out_sem.at[piece]),
            remote(source, target, last_send.at[piece], last_recv.at[piece], spot.partner),
        )

    def conclude(piece):
        kind, depth = piece % 2, piece // 2
        across_copy(piece).wait_recv()
        if depth < LAYERS - 1:
            local, away = out_copies(piece + 2)
            local.wait()
            away.wait_send()
        cut = cut_at(piece)
        row = spot.row
        for part in range(2):
            if kind == 0:
                own, far, done = (
                    spread_a.at[depth, 0, part],
                    spread_a.at[depth, 1, part],
                    done_a.at[part],
                )
            else:
                rows = pl.ds(part * part_f, part_f)
                own, far, done = (
                    spread_f.at[depth, 0, rows, :],
                    spread_f.at[depth, 1, rows, :],
                    done_f.at[rows, :],
                )

            def lanes_at(start, size):
                return pl.ds(pl.multiple_of(start, 128), size)

            single = width - 2 * cut
            value = own[:, lanes_at(row * single, cut)].astype(jnp.float32)
            done[:, lanes_at(row * (width - cut), cut)] = value
            value = far[:, lanes_at((1 - row) * single, cut)].astype(jnp.float32)
            done[:, lanes_at((1 - row) * (width - cut), cut)] = value
            value = own[:, lanes_at((1 - row) * cut, single)].astype(jnp.float32) + far[
                :, lanes_at(row * cut, single)
            ].astype(jnp.float32)
            done[:, cut : width - cut] = value
            add_squares(done[...])
        for copy in out_copies(piece):
            copy.start()

    load_grad = pltpu.make_async_copy(grad_ref, state, proj_sem.at[2])
    load_grad.start()
    load_first = pltpu.make_async_copy(first_ref, pre.at[0], proj_sem.at[3])
    load_pre(LAYERS - 1).start()
    for turn in range(SLOTS):
        for copy in loads(turn):
            copy.start()
    load_attn(LAYERS - 1).start()
    load_proj(LAYERS - 1).start()
    greet([spot.partner, spot.across] + [(spot.dp, peer(offset)) for offset in range(1, n)])
    load_grad.wait()
    lanes = lax.broadcasted_iota(jnp.int32, (1, 128), 1) < 64
    visible = visible_ref[...] > 0.0

    def ffn_turn(turn):
        depth, shard = turn_of(turn)
        slot = turn % SLOTS
        for copy in loads(turn):
            copy.wait()
        grad_active = dot_nt(right_f[1], wf[slot, 1])
        left_f[0] = (grad_active * slope[slot]).astype(jnp.bfloat16)
        left_f[1] = act[slot]
        sum_f[depth, shard] = dot_tn(left_f[core], right_f[core]).astype(jnp.bfloat16)
        if turn >= SLOTS:
            core_copy(turn - SLOTS).wait_send()
        theirs_f[slot] = dot_tn(left_f[other], right_f[other]).astype(jnp.bfloat16)
        if turn >= SLOTS:
            pl.semaphore_wait(core_free.at[0], 1)
        core_copy(turn).start()
        state[...] += dot_nn(left_f[0], wf[slot, 0])
        if turn + SLOTS < total:
            for copy in loads(turn + SLOTS):
                copy.start()

    def head_pair(depth, pair):
        columns = pl.ds(pl.multiple_of(pair * 128, 128), 128)
        query = proj[0, :, columns]
        keyed = proj[1, :, columns]
        valued = proj[2, :, columns]
        grad_mixed = grad_rows[4, :, columns]
        outs = []
        for side in range(2):
            mine = lanes if side == 0 else jnp.logical_not(lanes)
            scores = dot_nt(jnp.where(mine, query, jnp.zeros_like(query)), keyed) * 0.125
            scores = jnp.where(visible, scores, masked_score)
            expo = jnp.exp(scores - jnp.max(scores, axis=-1, keepdims=True))
            probs = expo / jnp.sum(expo, axis=-1, keepdims=True)
            grad_probs = dot_nt(jnp.where(mine, grad_mixed, jnp.zeros_like(query)), valued)
            inner = jnp.sum(grad_probs * probs, axis=-1, keepdims=True)
            grad_scores = (probs * (grad_probs - inner)).astype(jnp.bfloat16)
            outs.append(
                (
                    dot_nn(grad_scores, keyed) * 0.125,
                    dot_tn(grad_scores, query) * 0.125,
                    dot_tn(probs.astype(jnp.bfloat16), grad_mixed),
                )
            )
        for which in range(3):
            grad_rows[which, :, columns] = jnp.where(
                lanes, outs[0][which], outs[1][which]
            ).astype(jnp.bfloat16)

    def layer(depth, hooks):
        base = (LAYERS - 1 - depth) * n
        piece_a, piece_f = 2 * depth, 2 * depth + 1
        load_pre(depth).wait()
        grad_two, small[0, 4 + 4 * depth : 5 + 4 * depth, :], small[0, 5 + 4 * depth : 6 + 4 * depth, :] = norm_back(
            state[...], pre[1], gains_ref[2 + 2 * depth, 0:1, :]
        )
        state[...] = grad_two
        right_f[0] = mid_ref[depth]
        right_f[1] = grad_two.astype(jnp.bfloat16)
        for step in range(n):
            ffn_turn(base + step)
            if step >= 1:
                fold(base + step - 1)
                give_copy(piece_f, step - 1).start()
            if step == 3:
                absorb(piece_f, 0)
                launch(piece_f, True)
            if step == 5:
                absorb(piece_f, 1)
                absorb(piece_f, 2)
                launch(piece_f, False)
            hooks.get(("ffn", step), lambda: None)()
        fold(base + n - 1)
        give_copy(piece_f, n - 1).start()
        hooks.get("middle", lambda: None)()
        grad_one, small[0, 2 + 4 * depth : 3 + 4 * depth, :], small[0, 3 + 4 * depth : 4 + 4 * depth, :] = norm_back(
            state[...], pre[0], gains_ref[1 + 2 * depth, 0:1, :]
        )
        if depth > 0:
            load_pre(depth - 1).start()
        else:
            load_first.start()
        state[...] = grad_one
        grad_rows[3] = grad_one.astype(jnp.bfloat16)
        load_attn(depth).wait()
        load_proj(depth).wait()
        grad_rows[4] = dot_nt(grad_rows[3], wa[3]).astype(jnp.bfloat16)

        @pl.loop(0, HEADS // 2)
        def _(pair):
            head_pair(depth, pair)

        if depth > 0:
            load_proj(depth - 1).start()
        hooks.get("heads", lambda: None)()
        for which in range(3):
            state[...] += dot_nt(grad_rows[which], wa[which])
        left_a[0] = inputs_ref[depth]
        left_a[1] = mixed_ref[depth]
        for part in range(2):
            left = 0 if part == 0 else other
            wa[part] = dot_tn(left_a[left], grad_rows[2 * other + part]).astype(jnp.bfloat16)
            if depth < LAYERS - 1:
                pl.semaphore_wait(swap_free.at[part], 1)
            swap_copy(depth, part).start()
        for part in range(2):
            left = 0 if part == 0 else core
            sum_a[depth, part] = dot_tn(left_a[left], grad_rows[2 * core + part]).astype(
                jnp.bfloat16
            )
        hooks.get("mats", lambda: None)()
        for part in range(2):
            swap_copy(depth, part).wait_recv()

            @pl.loop(0, n)
            def _(block):
                rows = rows_at(block, rows_a)
                absorb_rows(sum_a.at[depth, part, rows, :], land_a.at[part, rows, :])

            give_copy(piece_a, part).start()
            if depth > 0:
                pl.semaphore_signal(
                    swap_free.at[part], inc=1, device_id=spot.partner, device_id_type=MESH
                )
    def launch_attn(piece):
        for part in range(2):
            absorb(piece, part)
        launch(piece, True)
        launch(piece, False)

    def reload_attn():
        for part in range(2):
            swap_copy(1, part).wait_send()
        load_attn(0).start()

    def half_copy(which, stage):
        buffer = out_half if which == 0 else table_half
        return remote(
            buffer.at[2 * stage],
            buffer.at[2 * stage + 1],
            half_send.at[which, stage],
            half_recv.at[which, stage],
            spot.partner if stage == 0 else spot.across,
        )

    def half_rows(rows, side):
        return pl.ds(pl.multiple_of(side * (rows // 2), 16), rows // 2)

    def half_start(which, source):
        buffer = out_half if which == 0 else table_half
        buffer[0] = source[half_rows(source.shape[0], other), :].astype(jnp.bfloat16)
        half_copy(which, 0).start()

    def half_fold(which, source):
        buffer = out_half if which == 0 else table_half
        half_copy(which, 0).wait_recv()
        own = source[half_rows(source.shape[0], core), :]
        buffer[2] = (own + buffer[1].astype(jnp.float32)).astype(jnp.bfloat16)
        half_copy(which, 1).start()

    def half_out(which):
        if which == 0:
            source, target = out_done, out_sum.at[half_rows(out_sum.shape[0], core), :]
        else:
            source = table_grad.at[half_rows(table_sum.shape[0], core), :]
            target = table_sum.at[half_rows(table_sum.shape[0], core), :]
        return (
            pltpu.make_async_copy(source, target, half_sem.at[which]),
            remote(source, target, half_send.at[which, 2], half_recv.at[which, 2], spot.partner),
        )

    def add_squares(value):
        squares[...] += jnp.sum(value * value, axis=0, keepdims=True)

    def half_end(which):
        buffer = out_half if which == 0 else table_half
        half_copy(which, 1).wait_recv()
        value = buffer[2].astype(jnp.float32) + buffer[3].astype(jnp.float32)
        if which == 0:
            out_done[...] = value
        else:
            table_grad[half_rows(table_sum.shape[0], core), :] = value
        width = squares.shape[1]
        for start in range(0, value.shape[1], width):
            add_squares(value[:, start : start + width])
        for copy in half_out(which):
            copy.start()

    def small_copy(stage):
        bit = 1 << max(0, stage - 2)
        pair = spot.mp + bit - 2 * bit * ((spot.mp // bit) % 2)
        device = (spot.partner, spot.across)[stage] if stage < 2 else (spot.dp, pair)
        return remote(
            small.at[stage],
            small_in.at[stage],
            small_send.at[stage],
            small_recv.at[stage],
            device,
        )

    def small_next(stage):
        small_copy(stage).wait_recv()
        small[stage + 1] = small[stage] + small_in[stage]
        if stage < 4:
            small_copy(stage + 1).start()

    def deal_copy(offset, arriving):
        source = columns_out.at[peer(offset)]
        target = columns_in.at[peer(-offset) if arriving else spot.mp]
        return remote(
            source,
            target,
            deal_send.at[offset - 1],
            deal_recv.at[offset - 1],
            (spot.dp, peer(offset)),
        )

    def table_blocks(first, last):
        @pl.loop(first, last)
        def _(block):
            row = lax.broadcasted_iota(jnp.int32, (256, 1), 0) + block * 256
            value = jnp.zeros((columns_in.shape[1], 256), jnp.float32)
            for whose in range(n):
                chosen = (row == ids_ref[whose : whose + 1, :]).astype(jnp.bfloat16)
                value = value + dot_nt(columns_in[whose], chosen)
            table_grad[:, pl.ds(pl.multiple_of(block * 256, 256), 256)] = value

    squares[...] = jnp.zeros_like(squares)
    half_start(0, out_grad_ref)
    layer(
        1,
        {
            "middle": lambda: (relay(3, 1), half_fold(0, out_grad_ref)),
            "mats": lambda: relay(3, 2),
        },
    )
    layer(
        0,
        {
            ("ffn", 0): reload_attn,
            ("ffn", 1): lambda: launch_attn(2),
            ("ffn", 2): lambda: relay(3, 3),
            ("ffn", 5): lambda: relay(2, 1),
            ("ffn", 6): lambda: finish(3),
            "middle": lambda: (relay(2, 2), half_end(0)),
            "heads": lambda: (relay(1, 1), relay(2, 3), conclude(3)),
            "mats": lambda: finish(2),
        },
    )
    load_first.wait()
    grad_sum, small[0, 0:1, :], small[0, 1:2, :] = norm_back(
        state[...], pre[0], gains_ref[0, 0:1, :]
    )
    width = squares.shape[1]
    lane = lax.broadcasted_iota(jnp.int32, (1, width), 1)
    loss = jnp.sum(losses_ref[...], axis=1, keepdims=True) * (1.0 / n)
    slots = counted_ref[0:1, 0:1] * (1.0 / n)
    small[0, 10:11, :] = jnp.where(lane == 0, loss, jnp.where(lane == 1, slots, 0.0))
    small[0, 11:16, :] = jnp.zeros((5, width), jnp.float32)
    small_copy(0).start()
    turned = grad_sum.T.astype(jnp.bfloat16)
    share = columns_in.shape[1]
    for whose in range(n):
        columns_out[whose] = turned[whose * share : (whose + 1) * share, :]
    for offset in range(1, n):
        deal_copy(offset, False).start()
    columns_in[spot.mp] = columns_out[spot.mp]
    relay(1, 2)
    launch_attn(0)
    small_next(0)
    conclude(2)
    for offset in range(1, n):
        deal_copy(offset, True).wait_recv()
    blocks = table_sum.shape[1] // 256
    table_blocks(0, blocks // 2)
    relay(0, 1)
    small_next(1)
    table_blocks(blocks // 2, blocks)
    half_start(1, table_grad)
    relay(1, 3)
    small_next(2)
    half_fold(1, table_grad)
    relay(0, 2)
    finish(1)
    small_next(3)
    half_end(1)
    relay(0, 3)
    conclude(1)
    small_next(4)
    finish(0)
    small_out[...] = small[5]
    conclude(0)

    square = jnp.sum(squares[...], axis=1, keepdims=True)
    square_parts[n] = jnp.broadcast_to(square, square_parts.shape[1:])
    swap = remote(
        square_parts.at[n],
        square_parts.at[n + 1],
        norm_send.at[0],
        norm_recv.at[0],
        spot.partner,
    )
    swap.start()
    swap.wait_recv()
    square_parts[spot.mp] = square_parts[n] + square_parts[n + 1]

    def norm_copy(offset, arriving):
        source = square_parts.at[spot.mp]
        target = square_parts.at[peer(-offset) if arriving else spot.mp]
        return remote(
            source, target, norm_send.at[offset], norm_recv.at[offset], (spot.dp, peer(offset))
        )

    for offset in range(1, n):
        norm_copy(offset, False).start()
    gains_grad = small[5, 0:10, :]
    square = jnp.sum(jnp.sum(gains_grad * gains_grad, axis=0, keepdims=True), axis=1, keepdims=True)
    for offset in range(1, n):
        norm_copy(offset, True).wait_recv()
    for whose in range(n):
        square = square + square_parts[whose, 0:1, :]
    square_out[...] = square

    swap.wait_send()
    for offset in range(1, n):
        norm_copy(offset, False).wait_send()
        deal_copy(offset, False).wait_send()
    for stage in range(5):
        small_copy(stage).wait_send()
    for which in range(2):
        half_copy(which, 0).wait_send()
        half_copy(which, 1).wait_send()
        local, away = half_out(which)
        local.wait()
        away.wait()
    for turn in range(total - SLOTS, total):
        core_copy(turn).wait_send()
    for part in range(2):
        swap_copy(0, part).wait_send()
    for piece in range(2 * LAYERS):
        for way, part in WAYS:
            for step in range(1, last_step(n, way, part) + 1):
                ring_copy(piece, way, part, step).wait_send()
        across_copy(piece).wait_send()
        for index in range(2 if piece % 2 == 0 else n):
            give_copy(piece, index).wait_send()
        local, away = out_copies(piece)
        if piece < 2:
            local.wait()
            away.wait_send()
        away.wait_recv()


def backward_call(
    n, ids, counted, losses, visible, grad, first, gains, out_grad, kept, attn_full, ffn_full, slope, act, table
):
    inputs, proj, mixed, pre, mid = kept
    count, width = grad.shape
    rows_f = ffn_full.shape[2] // n
    rows_a = attn_full.shape[2] // n
    rows_v = out_grad.shape[0]
    words, share = table.shape
    f32, bf16 = jnp.float32, jnp.bfloat16
    vmem = pl.BlockSpec(memory_space=pltpu.VMEM)
    anywhere = pl.BlockSpec(memory_space=pl.ANY)
    shape = jax.ShapeDtypeStruct
    dma = pltpu.SemaphoreType.DMA
    regular = pltpu.SemaphoreType.REGULAR
    ring_sems = dma((2 * LAYERS, 2, 2, n // 2))
    return pl.pallas_call(
        functools.partial(backward_kernel, n),
        out_shape=(
            shape((LAYERS, 4, rows_a, width), f32),
            shape((LAYERS, 2, rows_f, width), f32),
            shape((share, words), f32),
            shape((rows_v, width), f32),
            shape((16, width), f32),
            shape((1, 128), f32),
        ),
        in_specs=[vmem] * 9 + [anywhere] * 8,
        out_specs=(anywhere,) * 4 + (vmem,) * 2,
        scratch_shapes=[
            pltpu.VMEM((3, count, width), bf16),
            pltpu.VMEM((2, count, width), f32),
            pltpu.VMEM((4, width, width), bf16),
            pltpu.VMEM((SLOTS, 2, rows_f, width), bf16),
            pltpu.VMEM((SLOTS, count, rows_f), f32),
            pltpu.VMEM((SLOTS, count, rows_f), bf16),
            pltpu.VMEM((LAYERS, 2, width, width), bf16),
            pltpu.VMEM((LAYERS, n, rows_f, width), bf16),
            pltpu.VMEM((SLOTS, rows_f, width), bf16),
            pltpu.VMEM((SLOTS, rows_f, width), bf16),
            pltpu.VMEM((2, width, width), bf16),
            pltpu.VMEM((2, 2, n // 2, rows_a, width - cut_of(width, 6)), bf16),
            pltpu.VMEM((2, 2, n // 2, rows_f // 2, width - cut_of(width, 6)), bf16),
            pltpu.VMEM((LAYERS, 2, width, cut_of(width, 6)), bf16),
            pltpu.VMEM((LAYERS, n, rows_f, cut_of(width, 6)), bf16),
            pltpu.VMEM((count, width), f32),
            pltpu.VMEM((5, count, width), bf16),
            pltpu.VMEM((2, count, width), bf16),
            pltpu.VMEM((2, count, rows_f), bf16),
            pltpu.VMEM((2, count, width), bf16),
            pltpu.VMEM((LAYERS, 2, 2, rows_a, width - cut_of(width, 6)), bf16),
            pltpu.VMEM((LAYERS, 2, rows_f, width - cut_of(width, 6)), bf16),
            pltpu.VMEM((2, rows_a, width), f32),
            pltpu.VMEM((rows_f, width), f32),
            dma((1,)),
            dma((3, SLOTS)),
            dma((LAYERS * n,)),
            dma((LAYERS * n,)),
            regular((1,)),
            dma((LAYERS, 2)),
            dma((LAYERS, 2)),
            regular((2,)),
            ring_sems,
            ring_sems,
            regular((2, 2, 2, n // 2)),
            dma((2 * LAYERS, n)),
            dma((2 * LAYERS, n)),
            dma((2 * LAYERS,)),
            dma((2 * LAYERS,)),
            dma((2 * LAYERS,)),
            dma((2 * LAYERS,)),
            dma((2 * LAYERS,)),
            pltpu.VMEM((6, 16, width), f32),
            pltpu.VMEM((5, 16, width), f32),
            pltpu.VMEM((n, share, count), bf16),
            pltpu.VMEM((n, share, count), bf16),
            pltpu.VMEM((share, words), f32),
            pltpu.VMEM((4, share // 2, words), bf16),
            pltpu.VMEM((4, rows_v // 2, width), bf16),
            pltpu.VMEM((rows_v // 2, width), f32),
            pltpu.VMEM((1, width), f32),
            pltpu.VMEM((n + 2, 8, 128), f32),
            dma((4,)),
            dma((5,)),
            dma((5,)),
            dma((n - 1,)),
            dma((n - 1,)),
            dma((2, 3)),
            dma((2, 3)),
            dma((2,)),
            dma((n,)),
            dma((n,)),
        ],
        compiler_params=pltpu.CompilerParams(
            collective_id=2, has_side_effects=True, vmem_limit_bytes=VMEM_LIMIT
        ),
        name="backward_layers",
    )(
        ids, counted, losses, visible, gains, out_grad, inputs, mixed, mid, grad, first,
        proj, pre, attn_full, ffn_full, slope, act,
    )


def merged(value, axis, join):
    pieces = jax.tree.map(lambda part: lax.all_gather(part, axis), value)
    head = jax.tree.map(lambda part: part[0], pieces)
    tail = jax.tree.map(lambda part: part[1:], pieces)
    total, _ = lax.scan(lambda total, section: (join(total, section), None), head, tail)
    return total


def sinusoid(count, width):
    places = jnp.arange(count, dtype=jnp.float32)[:, None]
    freqs = jnp.exp(jnp.arange(width // 2, dtype=jnp.float32) * (-2.0 * math.log(10000.0) / width))
    angles = places * freqs[None, :]
    return jnp.concatenate([jnp.sin(angles), jnp.cos(angles)], axis=1)


def layer_norm(values, gain, shift):
    centre = jnp.mean(values, axis=-1, keepdims=True)
    offset = values - centre
    spread = jnp.mean(offset * offset, axis=-1, keepdims=True)
    inverse = lax.rsqrt(spread + norm_eps)
    normed = offset * inverse
    return (normed * gain + shift, (normed, inverse))


def norm_backward(grad, saved, gain):
    normed, inverse = saved
    scaled = grad * gain
    centred = scaled - jnp.mean(scaled, axis=-1, keepdims=True)
    result = inverse * (centred - normed * jnp.mean(scaled * normed, axis=-1, keepdims=True))
    return (result, jnp.stack([jnp.sum(grad * normed, axis=0), jnp.sum(grad, axis=0)]))


def gelu_exact(values):
    return jax.nn.gelu(values, approximate=False)


def gelu_back(hidden, grad):
    unused, pullback = jax.vjp(gelu_exact, hidden)
    return pullback(grad)[0]


def masked_scores(query, keyed, length):
    scale = query.shape[-1] ** (-0.5)
    scores = jnp.einsum("hqe,hke->hqk", query, keyed, preferred_element_type=jnp.float32) * scale
    visible = jnp.arange(keyed.shape[1]) < length
    return jnp.where(visible[None, None, :], scores, masked_score)


def fetch_forward(attn_part, ffn_part):
    return (
        lax.all_gather(attn_part, "mp", axis=1, tiled=True),
        lax.all_gather(ffn_part, "mp", axis=1, tiled=True),
    )


def fetch_backward(attn_part, ffn_part):
    return (
        lax.all_gather(attn_part, "mp", axis=1, tiled=True),
        lax.all_gather(ffn_part, "mp", axis=1, tiled=True),
    )


def reduce_layer(attn_grad, ffn_grad):
    return (
        lax.psum_scatter(attn_grad, "mp", scatter_dimension=1, tiled=True),
        lax.psum_scatter(ffn_grad, "mp", scatter_dimension=1, tiled=True),
    )


def ffn_forward(middle_b, ffn_w, unit_mask):
    hidden = jnp.einsum("td,fd->tf", middle_b, ffn_w[0], preferred_element_type=jnp.float32)
    active = (gelu_exact(hidden) * unit_mask[None, :]).astype(jnp.bfloat16)
    output = jnp.einsum("tf,fd->td", active, ffn_w[1], preferred_element_type=jnp.float32)
    return (hidden, active, output)


def ffn_backward(grad_out, middle_b, hidden, active, ffn_w, unit_mask):
    grad_active = jnp.einsum("td,fd->tf", grad_out, ffn_w[1], preferred_element_type=jnp.float32)
    grad_hidden = gelu_back(hidden, grad_active * unit_mask[None, :]).astype(jnp.bfloat16)
    up_grad = jnp.einsum("tf,td->fd", grad_hidden, middle_b, preferred_element_type=jnp.float32)
    down_grad = jnp.einsum("tf,td->fd", active, grad_out, preferred_element_type=jnp.float32)
    from_ffn = jnp.einsum("tf,fd->td", grad_hidden, ffn_w[0], preferred_element_type=jnp.float32)
    return (jnp.stack([up_grad, down_grad]), from_ffn)


def layer_forward(states, attn_w, ffn_w, pair, length, unit_mask):
    count = states.shape[0]
    inputs = states.astype(jnp.bfloat16)
    projected = jnp.einsum(
        "td,kde->kte", inputs, attn_w[:3], preferred_element_type=jnp.float32
    ).astype(jnp.bfloat16)
    heads = projected.reshape(3, count, HEADS, -1).transpose(0, 2, 1, 3)
    scores = masked_scores(heads[0], heads[1], length)
    peak = jnp.max(scores, axis=-1, keepdims=True)
    expo = jnp.exp(scores - peak)
    total = jnp.sum(expo, axis=-1, keepdims=True)
    log_total = peak + jnp.log(total)
    probs = (expo / total).astype(jnp.bfloat16)
    mixed = jnp.einsum("hqk,hke->hqe", probs, heads[2], preferred_element_type=jnp.float32)
    mixed = mixed.transpose(1, 0, 2).reshape(count, -1).astype(jnp.bfloat16)
    branch = jnp.dot(mixed, attn_w[3], preferred_element_type=jnp.float32)
    middle, norm_one = layer_norm(states + branch, pair[0, 0], pair[0, 1])
    middle_b = middle.astype(jnp.bfloat16)
    hidden, active, output = ffn_forward(middle_b, ffn_w, unit_mask)
    result, norm_two = layer_norm(middle + output, pair[1, 0], pair[1, 1])
    return (result, (inputs, heads, log_total, mixed, norm_one, middle_b, hidden, active, norm_two))


def layer_backward(grad, attn_w, ffn_w, pair, length, unit_mask, kept):
    inputs, heads, log_total, mixed, norm_one, middle_b, hidden, active, norm_two = kept
    count = inputs.shape[0]
    grad_two, pair_two = norm_backward(grad, norm_two, pair[1, 0])
    ffn_grad, from_ffn = ffn_backward(
        grad_two.astype(jnp.bfloat16), middle_b, hidden, active, ffn_w, unit_mask
    )
    grad_one, pair_one = norm_backward(grad_two + from_ffn, norm_one, pair[0, 0])
    grad_branch = grad_one.astype(jnp.bfloat16)
    output_grad = jnp.einsum("td,te->de", mixed, grad_branch, preferred_element_type=jnp.float32)
    grad_mixed = jnp.einsum("te,de->td", grad_branch, attn_w[3], preferred_element_type=jnp.float32)
    grad_mixed = grad_mixed.astype(jnp.bfloat16).reshape(count, HEADS, -1).transpose(1, 0, 2)
    scale = heads.shape[-1] ** (-0.5)
    probs = jnp.exp(masked_scores(heads[0], heads[1], length) - log_total)
    grad_values = jnp.einsum(
        "hqk,hqe->hke", probs.astype(jnp.bfloat16), grad_mixed, preferred_element_type=jnp.float32
    )
    grad_probs = jnp.einsum(
        "hqe,hke->hqk", grad_mixed, heads[2], preferred_element_type=jnp.float32
    )
    grad_scores = probs * (grad_probs - jnp.sum(grad_probs * probs, axis=-1, keepdims=True))
    grad_scores = grad_scores.astype(jnp.bfloat16)
    grad_query = (
        jnp.einsum("hqk,hke->hqe", grad_scores, heads[1], preferred_element_type=jnp.float32)
        * scale
    )
    grad_key = (
        jnp.einsum("hqk,hqe->hke", grad_scores, heads[0], preferred_element_type=jnp.float32)
        * scale
    )
    stacked = (
        jnp.stack([grad_query, grad_key, grad_values]).transpose(0, 2, 1, 3).reshape(3, count, -1)
    )
    stacked = stacked.astype(jnp.bfloat16)
    input_grad = jnp.einsum("td,kte->kde", inputs, stacked, preferred_element_type=jnp.float32)
    from_attn = jnp.einsum("kte,kde->td", stacked, attn_w[:3], preferred_element_type=jnp.float32)
    attn_grad = jnp.concatenate([input_grad, output_grad[None]], axis=0)
    return (grad_one + from_attn, attn_grad, ffn_grad, jnp.stack([pair_one, pair_two]))


def adamw(weight, moment_one, moment_two, grad, decay, rate):
    moment_one = beta_one * moment_one + (1.0 - beta_one) * grad
    moment_two = beta_two * moment_two + (1.0 - beta_two) * grad * grad
    fixed_one = moment_one / (1.0 - beta_one**STEP)
    fixed_two = moment_two / (1.0 - beta_two**STEP)
    weight = weight - rate * (fixed_one / (jnp.sqrt(fixed_two) + adam_eps) + decay * weight)
    return (moment_one, moment_two, weight)


def combine_vocab(first, second):
    peak = jnp.maximum(first[0], second[0])
    total = first[1] * jnp.exp(first[0] - peak) + second[1] * jnp.exp(second[0] - peak)
    return (peak, total, first[2] + second[2])


def local_general(
    tokens,
    lengths,
    places,
    targets,
    ramp,
    attn,
    attn_m,
    attn_v,
    ffn,
    ffn_m,
    ffn_v,
    table,
    table_m,
    table_v,
    out_table,
    out_m,
    out_v,
    gains,
    gains_m,
    gains_v,
):
    rank = lax.axis_index("mp")
    count = tokens.shape[2]
    flat_ids = tokens.reshape(-1)
    all_lengths = lengths.reshape(-1)
    length = lax.dynamic_index_in_dim(all_lengths, rank, keepdims=False)
    masks = jnp.minimum(ramp, RAMP).astype(jnp.float32) / RAMP
    unit_masks = [masks[depth] for depth in range(LAYERS)]
    looked = jnp.take(table, flat_ids, axis=0)
    embedded = lax.all_to_all(looked, "mp", split_axis=0, concat_axis=1, tiled=True)
    states, norm_zero = layer_norm(
        embedded + sinusoid(count, embedded.shape[1]), gains[0, 0], gains[0, 1]
    )
    kept_all = []
    weights_all = []
    for depth in range(LAYERS):
        attn_w, ffn_w = fetch_forward(
            attn[depth].astype(jnp.bfloat16), ffn[depth].astype(jnp.bfloat16)
        )
        states, kept = layer_forward(
            states, attn_w, ffn_w, gains[1 + 2 * depth : 3 + 2 * depth], length, unit_masks[depth]
        )
        kept_all.append(kept)
        weights_all.append(None)
    spots = places.reshape(-1)
    picked = jnp.take(states, spots, axis=0).astype(jnp.bfloat16)
    picked_all = lax.all_gather(picked, "mp", axis=0, tiled=True)
    out_b = out_table.astype(jnp.bfloat16)
    logits = jnp.einsum("rd,vd->rv", picked_all, out_b, preferred_element_type=jnp.float32)
    labels = targets.reshape(-1)
    columns = rank * out_table.shape[0] + jnp.arange(out_table.shape[0])
    hits = (labels[:, None] == columns[None, :]).astype(jnp.float32)
    peak = jnp.max(logits, axis=1)
    expsum = jnp.sum(jnp.exp(logits - peak[:, None]), axis=1)
    target_part = jnp.sum(hits * logits, axis=1)
    peak_all, expsum_all, target_all = merged((peak, expsum, target_part), "mp", combine_vocab)
    log_total = peak_all + jnp.log(expsum_all)
    slot_count = targets.shape[2]
    counted = jnp.maximum(1, all_lengths * slot_count // count)
    valid = (jnp.arange(slot_count)[None, :] < counted[:, None]).reshape(-1)
    loss_pair = jnp.stack(
        [
            jnp.sum(jnp.where(valid, log_total - target_all, 0.0)),
            jnp.sum(counted).astype(jnp.float32),
        ]
    )
    grad_logits = jnp.where(
        valid[:, None], jnp.exp(logits - log_total[:, None]) - hits, 0.0
    ).astype(jnp.bfloat16)
    out_grad = jnp.einsum("rv,rd->vd", grad_logits, picked_all, preferred_element_type=jnp.float32)
    picked_grad = lax.psum_scatter(
        jnp.dot(grad_logits, out_b, preferred_element_type=jnp.float32),
        "mp",
        scatter_dimension=0,
        tiled=True,
    )
    grad = jnp.zeros_like(states).at[spots].add(picked_grad)
    attn_parts = [None] * LAYERS
    ffn_parts = [None] * LAYERS
    pair_grads = [None] * LAYERS
    for depth in reversed(range(LAYERS)):
        attn_w, ffn_w = fetch_backward(
            attn[depth].astype(jnp.bfloat16), ffn[depth].astype(jnp.bfloat16)
        )
        grad, attn_grad, ffn_grad, pair_grad = layer_backward(
            grad,
            attn_w,
            ffn_w,
            gains[1 + 2 * depth : 3 + 2 * depth],
            length,
            unit_masks[depth],
            kept_all[depth],
        )
        attn_parts[depth], ffn_parts[depth] = reduce_layer(attn_grad, ffn_grad)
        pair_grads[depth] = pair_grad
    grad_sum, zero_grad = norm_backward(grad, norm_zero, gains[0, 0])
    returned = lax.all_to_all(grad_sum, "mp", split_axis=1, concat_axis=0, tiled=True)
    table_grad = jnp.zeros_like(table).at[flat_ids].add(returned)
    gains_grad = jnp.concatenate([zero_grad[None]] + pair_grads, axis=0)
    attn_sum, ffn_sum, table_sum, out_sum, gains_part, loss = lax.psum(
        (jnp.stack(attn_parts), jnp.stack(ffn_parts), table_grad, out_grad, gains_grad, loss_pair),
        "dp",
    )
    shard_squares = (
        jnp.sum(attn_sum * attn_sum)
        + jnp.sum(ffn_sum * ffn_sum)
        + jnp.sum(table_sum * table_sum)
        + jnp.sum(out_sum * out_sum)
    )
    square_total, gains_sum = lax.psum((shard_squares, gains_part), "mp")
    grad_norm = jnp.sqrt(square_total + jnp.sum(gains_sum * gains_sum))
    factor = clip_limit / jnp.maximum(grad_norm, clip_limit)
    attn_m_new, attn_v_new, attn_new = adamw(
        attn, attn_m, attn_v, attn_sum * factor, weight_decay, learn_rate
    )
    ffn_m_new, ffn_v_new, ffn_new = adamw(
        ffn, ffn_m, ffn_v, ffn_sum * factor, weight_decay, learn_rate
    )
    table_m_new, table_v_new, table_new = adamw(
        table, table_m, table_v, table_sum * factor, weight_decay, learn_rate
    )
    out_m_new, out_v_new, out_new = adamw(
        out_table, out_m, out_v, out_sum * factor, weight_decay, learn_rate
    )
    gains_m_new, gains_v_new, gains_new = adamw(
        gains, gains_m, gains_v, gains_sum * factor, 0.0, gain_rate
    )
    return (
        loss,
        grad_norm.reshape(1),
        attn_m_new,
        attn_v_new,
        attn_new,
        ffn_m_new,
        ffn_v_new,
        ffn_new,
        table_m_new,
        table_v_new,
        table_new,
        out_m_new,
        out_v_new,
        out_new,
        gains_m_new,
        gains_v_new,
        gains_new,
    )


def local(
    tokens,
    lengths,
    places,
    targets,
    ramp,
    attn,
    attn_m,
    attn_v,
    ffn,
    ffn_m,
    ffn_v,
    table,
    table_m,
    table_v,
    out_table,
    out_m,
    out_v,
    gains,
    gains_m,
    gains_v,
):
    rank = lax.axis_index("mp")
    n = tokens.shape[1]
    count, width = tokens.shape[2], gains.shape[2]
    flat_ids = tokens.reshape(-1)
    all_lengths = lengths.reshape(-1)
    length = lax.dynamic_index_in_dim(all_lengths, rank, keepdims=False)
    masks = jnp.minimum(ramp, RAMP).astype(jnp.float32) / RAMP
    visible = (jnp.arange(count) < length).astype(jnp.float32)[None, :]
    slot_count = targets.shape[2]
    slots = 32 * -(-slot_count // 32)
    counted = jnp.maximum(1, all_lengths * slot_count // count)
    valid = (jnp.arange(slots)[None, :] < counted[:, None]).astype(jnp.float32).reshape(1, -1)
    extra = slots - slot_count
    spots = jnp.pad(places.reshape(-1), (0, extra), constant_values=-1)[:, None]
    labels = jnp.pad(targets[0], ((0, 0), (0, extra)), constant_values=-1).reshape(1, -1)
    where = sinusoid(count, width)
    attn_full, ffn_full, first, *kept, slope, act, grad, out_grad, losses = forward_call(
        n, tokens[0], table.T.astype(jnp.bfloat16), where, visible, gains, masks, spots, labels, valid, out_table, attn, ffn
    )
    tally = jnp.broadcast_to(jnp.sum(counted).astype(jnp.float32), (1, 128))
    attn_sum, ffn_sum, table_turned, out_sum, small, square = backward_call(
        n, tokens[0], tally, losses, visible, grad, first, gains, out_grad, kept, attn_full, ffn_full, slope, act, table
    )
    table_sum = table_turned.T
    gains_sum = small[:10].reshape(gains.shape)
    grad_norm = jnp.sqrt(square[0, 0])
    factor = clip_limit / jnp.maximum(grad_norm, clip_limit)
    attn_m_new, attn_v_new, attn_new = adamw(
        attn, attn_m, attn_v, attn_sum * factor, weight_decay, learn_rate
    )
    ffn_m_new, ffn_v_new, ffn_new = adamw(
        ffn, ffn_m, ffn_v, ffn_sum * factor, weight_decay, learn_rate
    )
    table_m_new, table_v_new, table_new = adamw(
        table, table_m, table_v, table_sum * factor, weight_decay, learn_rate
    )
    out_m_new, out_v_new, out_new = adamw(
        out_table, out_m, out_v, out_sum * factor, weight_decay, learn_rate
    )
    gains_m_new, gains_v_new, gains_new = adamw(
        gains, gains_m, gains_v, gains_sum * factor, 0.0, gain_rate
    )
    return (
        small[10, :2],
        grad_norm.reshape(1),
        attn_m_new,
        attn_v_new,
        attn_new,
        ffn_m_new,
        ffn_v_new,
        ffn_new,
        table_m_new,
        table_v_new,
        table_new,
        out_m_new,
        out_v_new,
        out_new,
        gains_m_new,
        gains_v_new,
        gains_new,
    )


def solution(mesh):
    in_specs = (
        P("dp", None, None),
        P("dp", None),
        P("dp", "mp", None),
        P("dp", None, None),
        P(),
        P(None, None, "mp", None),
        P(None, None, "mp", None),
        P(None, None, "mp", None),
        P(None, None, "mp", None),
        P(None, None, "mp", None),
        P(None, None, "mp", None),
        P(None, "mp"),
        P(None, "mp"),
        P(None, "mp"),
        P("mp", None),
        P("mp", None),
        P("mp", None),
        P(),
        P(),
        P(),
    )
    out_specs = (
        P(),
        P(),
        P(None, None, "mp", None),
        P(None, None, "mp", None),
        P(None, None, "mp", None),
        P(None, None, "mp", None),
        P(None, None, "mp", None),
        P(None, None, "mp", None),
        P(None, "mp"),
        P(None, "mp"),
        P(None, "mp"),
        P("mp", None),
        P("mp", None),
        P("mp", None),
        P(),
        P(),
        P(),
    )
    fits = mesh.shape['mp'] == 8 and mesh.shape['dp'] == 4
    chosen = local if fits else local_general
    return jax.shard_map(chosen, mesh=mesh, in_specs=in_specs, out_specs=out_specs, check_vma=False)
```

```python
import functools
import math

import jax
import jax.numpy as jnp
from jax import lax
from jax.experimental import pallas as pl
from jax.experimental.pallas import tpu as pltpu
from jax.sharding import PartitionSpec as P

HEADS = 12
LAYERS = 2
STEP = 10
RAMP = 4


norm_eps = 1e-05
beta_one = 0.9
beta_two = 0.999
learn_rate = 0.02
gain_rate = 0.3
weight_decay = 0.01
adam_eps = 1e-08
clip_limit = 1.0
masked_score = -1000000000.0


MESH = pl.DeviceIdType.MESH
VMEM_LIMIT = 62 * 1024 * 1024
SLOTS = 3


def dot_nn(left, right):
    return lax.dot_general(
        left, right, (((1,), (0,)), ((), ())), preferred_element_type=jnp.float32
    )


def dot_nt(left, right):
    return lax.dot_general(
        left, right, (((1,), (1,)), ((), ())), preferred_element_type=jnp.float32
    )


def dot_tn(left, right):
    return lax.dot_general(
        left, right, (((0,), (0,)), ((), ())), preferred_element_type=jnp.float32
    )


def ring_index(place, n):
    late = place // (n // 2)
    return (1 - late) * 2 * place + late * (2 * (n - 1 - place) + 1)


def ring_place(index, n):
    odd = index % 2
    return (1 - odd) * (index // 2) + odd * (n - 1 - index // 2)


class Spot:
    def __init__(self, n):
        self.n = n
        self.dp = lax.axis_index("dp")
        self.mp = lax.axis_index("mp")
        self.core = self.dp % 2
        self.row = self.dp // 2
        self.place = ring_place(self.mp, n)
        self.partner = (self.dp + 1 - 2 * self.core, self.mp)
        self.across = ((self.dp + 2) % 4, self.mp)
        self.ring = (
            (self.dp, ring_index((self.place + 1) % n, n)),
            (self.dp, ring_index((self.place + n - 1) % n, n)),
        )

    def shard(self, offset):
        return ring_index((self.place + offset + self.n) % self.n, self.n)


def greet(devices):
    barrier = pltpu.get_barrier_semaphore()
    for device in devices:
        pl.semaphore_signal(barrier, inc=1, device_id=device, device_id_type=MESH)
    pl.semaphore_wait(barrier, len(devices))


def last_step(n, way, part):
    return n // 2 if way == part else n // 2 - 1


WAYS = ((0, 0), (1, 1), (0, 1), (1, 0))


def ring_columns(row, width, cut):
    return pl.ds(pl.multiple_of(row * cut, 128), width - cut)


def edge_columns(row, width, cut):
    return pl.ds(pl.multiple_of(row * (width - cut), 128), cut)


def cut_of(width, share):
    return 128 * (width // 128 // share)


def normed_of(values):
    centre = jnp.mean(values, axis=-1, keepdims=True)
    offset = values - centre
    spread = jnp.mean(offset * offset, axis=-1, keepdims=True)
    inverse = lax.rsqrt(spread + norm_eps)
    return offset * inverse, inverse


def forward_kernel(
    n,
    ids_ref,
    table_ref,
    where_ref,
    visible_ref,
    gains_ref,
    mask_ref,
    places_ref,
    labels_ref,
    valid_ref,
    out_ref,
    attn_sh,
    ffn_sh,
    attn_full,
    ffn_full,
    first_ref,
    inputs_ref,
    proj_ref,
    mixed_ref,
    pre_ref,
    mid_ref,
    slope_ref,
    act_ref,
    grad_ref,
    out_grad_ref,
    loss_ref,
    wa,
    wf,
    raw_a,
    raw_f,
    slope,
    act,
    far_sum,
    far_out,
    far_in,
    state,
    row_out,
    row_in,
    picked,
    stats,
    back_out,
    back_in,
    raw_sem,
    out_sem,
    kept_sem,
    ring_send,
    ring_recv,
    core_send,
    core_recv,
    across_send,
    across_recv,
    pair_send,
    pair_recv,
    fan_send,
    fan_recv,
):
    spot = Spot(n)
    core = spot.core
    rows_a = attn_sh.shape[2]
    rows_f = ffn_sh.shape[2]
    half_f = rows_f // 2
    part_f = half_f // 2
    steps = n // 2
    count, width = first_ref.shape
    share_e = table_ref.shape[0]
    words = table_ref.shape[1]
    slots = places_ref.shape[0]

    def rows_at(shard, rows):
        return pl.ds(pl.multiple_of(shard * rows, 16), rows)

    def remote(source, target, send, recv, device):
        return pltpu.make_async_remote_copy(
            src_ref=source,
            dst_ref=target,
            send_sem=send,
            recv_sem=recv,
            device_id=device,
            device_id_type=MESH,
        )

    def slot_f(way, step):
        if step == 0:
            return 0, 0
        return (0, 1) if step == steps else (step, way)

    def chunk_f(piece, way, part, step, side):
        group, half = slot_f(way, step)
        return wf.at[piece // 2, group, side, pl.ds(half * half_f + part * part_f, part_f), :]

    def chunk_a(piece, shard, part, side, edge):
        cut = cut_of(width, 3)
        if edge is None:
            columns = ring_columns(spot.row, width, cut)
        else:
            columns = edge_columns(edge, width, cut)
        return wa.at[piece // 2, 2 * side + part, rows_at(shard, rows_a), columns]

    def sign(way):
        return -1 if way == 0 else 1

    def ring_copy(piece, way, part, step, arriving):
        if piece % 2 == 0:
            target = chunk_a(piece, spot.shard(sign(way) * (step - 1 + arriving)), part, core, None)
            source = target
        else:
            target = chunk_f(piece, way, part, step, core)
            source = target if arriving else chunk_f(piece, way, part, step - 1, core)
        return remote(
            source,
            target,
            ring_send.at[piece, way, part, step - 1],
            ring_recv.at[piece, way, part, step - 1],
            spot.ring[way],
        )

    def core_copy(piece, way, part, step, side, edge):
        if piece % 2 == 0:
            target = chunk_a(piece, spot.shard(sign(way) * step), part, side, edge)
        else:
            target = chunk_f(piece, way, part, step, side)
        lane = 0 if edge is None else 1
        return remote(
            target,
            target,
            core_send.at[lane, piece, way, part, step - 1],
            core_recv.at[lane, piece, way, part, step - 1],
            spot.partner,
        )

    def across_copy(piece, way, part, step, row):
        target = chunk_a(piece, spot.shard(sign(way) * step), part, core, row)
        return remote(
            target,
            target,
            across_send.at[piece, way, part, step - 1],
            across_recv.at[piece, way, part, step - 1],
            spot.across,
        )

    def pair_copy(which, depth):
        if which == 0:
            source, target = mid_ref.at[depth, 0], mid_ref.at[depth, 1]
        else:
            source, target = far_out.at[depth], far_in.at[depth]
        return remote(
            source, target, pair_send.at[which, depth], pair_recv.at[which, depth], spot.across
        )

    def peer(offset):
        return (spot.mp + offset + n) % n

    def fan_copy(which, offset, source, target):
        return remote(
            source,
            target,
            fan_send.at[which, offset - 1],
            fan_recv.at[which, offset - 1],
            (spot.dp, peer(offset)),
        )

    def share(which, buffer, offset):
        return fan_copy(which, offset, buffer.at[spot.mp], buffer.at[spot.mp])

    def arrived(which, buffer, offset):
        return fan_copy(which, offset, buffer.at[peer(-offset)], buffer.at[peer(-offset)])

    def deal(which, source, target, offset):
        return fan_copy(which, offset, source.at[peer(offset)], target.at[spot.mp])

    def raw_copy(piece):
        kind, depth = piece % 2, piece // 2
        if kind == 0:
            return pltpu.make_async_copy(attn_sh.at[depth], raw_a.at[depth], raw_sem.at[piece])
        rows = pl.ds(pl.multiple_of(spot.row * half_f, 16), half_f)
        return pltpu.make_async_copy(ffn_sh.at[depth, :, rows, :], raw_f.at[depth], raw_sem.at[piece])

    def take_own(piece):
        kind, depth = piece % 2, piece // 2
        raw_copy(piece).wait()
        if kind == 0:
            for which in range(4):
                wa[depth, which, rows_at(spot.mp, rows_a), :] = raw_a[depth, which].astype(
                    jnp.bfloat16
                )
        else:
            for which in range(2):
                wf[depth, 0, which, 0:half_f, :] = raw_f[depth, which].astype(jnp.bfloat16)

    def launch(piece):
        for way, part in WAYS:
            ring_copy(piece, way, part, 1, 0).start()

    def chains(step):
        return [(way, part) for way, part in WAYS if step <= last_step(n, way, part)]

    def pass_on(piece, step):
        for way, part in chains(step):
            ring_copy(piece, way, part, step, 1).wait_recv()
            if step < last_step(n, way, part):
                ring_copy(piece, way, part, step + 1, 0).start()
            if piece % 2 == 0:
                across_copy(piece, way, part, step, spot.row).start()
            core_copy(piece, way, part, step, core, None).start()

    def pass_edge(piece, step):
        for way, part in chains(step):
            across_copy(piece, way, part, step, 1 - spot.row).wait_recv()
            core_copy(piece, way, part, step, core, 1 - spot.row).start()

    def settle(piece, step):
        for way, part in chains(step):
            core_copy(piece, way, part, step, 1 - core, None).wait_recv()
            if piece % 2 == 0:
                core_copy(piece, way, part, step, 1 - core, 1 - spot.row).wait_recv()

    def look_up(offset):
        whose = peer(offset)
        tokens = ids_ref[pl.ds(whose, 1), :]

        def block(index, total):
            start = pl.multiple_of(index * 256, 256)
            word = lax.broadcasted_iota(jnp.int32, (256, 1), 0) + start
            chosen = (word == tokens).astype(jnp.bfloat16)
            return total + dot_nn(table_ref[:, pl.ds(start, 256)], chosen)

        found = lax.fori_loop(
            0, words // 256, block, jnp.zeros((share_e, count), jnp.float32)
        )
        row_out[whose] = found.astype(jnp.bfloat16)
        if offset > 0:
            deal(0, row_out, row_in, offset).start()

    for piece in range(2 * LAYERS):
        raw_copy(piece).start()
    greet([spot.partner, spot.across] + [(spot.dp, peer(offset)) for offset in range(1, n)])
    take_own(0)
    launch(0)
    for offset in range(1, 4):
        look_up(offset)
    pass_on(0, 1)
    for offset in range(4, 7):
        look_up(offset)
    pass_on(0, 2)
    pass_edge(0, 1)
    take_own(1)
    launch(1)
    look_up(7)
    look_up(0)
    row_in[spot.mp] = row_out[spot.mp]
    pass_on(0, 3)
    pass_edge(0, 2)
    for offset in range(1, n):
        arrived(0, row_in, offset).wait_recv()
    first_ref[...] = where_ref[...] + row_in[...].reshape(width, count).astype(jnp.float32).T
    normed, _ = normed_of(first_ref[...])
    state[...] = normed * gains_ref[0, 0:1, :] + gains_ref[0, 1:2, :]
    take_own(2)
    take_own(3)
    pass_on(0, 4)
    pass_edge(0, 3)

    lanes = lax.broadcasted_iota(jnp.int32, (1, 128), 1) < 64
    visible = visible_ref[...] > 0.0

    def head_pair(depth, pair):
        columns = pl.ds(pl.multiple_of(pair * 128, 128), 128)
        query = proj_ref[depth, 0, :, columns]
        keyed = proj_ref[depth, 1, :, columns]
        valued = proj_ref[depth, 2, :, columns]
        outs = []
        for side in range(2):
            mine = lanes if side == 0 else jnp.logical_not(lanes)
            scores = dot_nt(jnp.where(mine, query, jnp.zeros_like(query)), keyed) * 0.125
            scores = jnp.where(visible, scores, masked_score)
            expo = jnp.exp(scores - jnp.max(scores, axis=-1, keepdims=True))
            total = jnp.sum(expo, axis=-1, keepdims=True)
            outs.append(dot_nn((expo / total).astype(jnp.bfloat16), valued))
        mixed_ref[depth, :, columns] = jnp.where(lanes, outs[0], outs[1]).astype(jnp.bfloat16)

    def kept_copies(turn, depth, group, far):
        slot = turn % SLOTS
        return (
            pltpu.make_async_copy(
                slope.at[slot], slope_ref.at[depth, group, far], kept_sem.at[0, slot]
            ),
            pltpu.make_async_copy(
                act.at[slot], act_ref.at[depth, group, far], kept_sem.at[1, slot]
            ),
        )

    turns = []

    def ffn_block(depth, group, far):
        turn = len(turns)
        turns.append((depth, group, far))
        if turn >= SLOTS:
            for copy in kept_copies(turn, *turns[turn - SLOTS]):
                copy.wait()
        hidden = dot_nt(mid_ref[depth, far], wf[depth, group, 0])
        spread = 0.5 * (1.0 + lax.erf(hidden * (0.5**0.5)))
        mask = mask_ref[depth, group : group + 1, :]
        bell = jnp.exp(hidden * hidden * -0.5) * (1.0 / math.sqrt(2.0 * math.pi))
        slope[turn % SLOTS] = (spread + hidden * bell) * mask
        active = (hidden * spread * mask).astype(jnp.bfloat16)
        act[turn % SLOTS] = active
        for copy in kept_copies(turn, depth, group, far):
            copy.start()
        if far:
            far_sum[...] += dot_nn(active, wf[depth, group, 1])
        else:
            pre_ref[depth, 1] += dot_nn(active, wf[depth, group, 1])

    out_copies = []
    for depth in range(LAYERS):
        piece_a, piece_f = 2 * depth, 2 * depth + 1
        more = depth + 1 < LAYERS
        if depth > 0:
            pass_on(piece_a, 3)
            pass_edge(piece_a, 2)
            launch(piece_f)
            pass_on(piece_a, 4)
            pass_edge(piece_a, 3)
        pass_edge(piece_a, 4)
        for step in range(1, steps + 1):
            settle(piece_a, step)
        copy = pltpu.make_async_copy(wa.at[depth], attn_full.at[depth], out_sem.at[piece_a])
        copy.start()
        out_copies.append(copy)
        inputs = state[...].astype(jnp.bfloat16)
        inputs_ref[depth] = inputs
        for which in range(3):
            proj_ref[depth, which] = dot_nn(inputs, wa[depth, which]).astype(jnp.bfloat16)
        pass_on(piece_f, 1)

        @pl.loop(0, HEADS // 2)
        def _(pair):
            head_pair(depth, pair)

        pre_ref[depth, 0] = state[...] + dot_nn(mixed_ref[depth], wa[depth, 3])
        normed, _ = normed_of(pre_ref[depth, 0])
        middle = (
            normed * gains_ref[1 + 2 * depth, 0:1, :] + gains_ref[1 + 2 * depth, 1:2, :]
        )
        mid_ref[depth, 0] = middle.astype(jnp.bfloat16)
        pair_copy(0, depth).start()
        pre_ref[depth, 1] = middle
        far_sum[...] = jnp.zeros_like(far_sum)
        pass_on(piece_f, 2)
        settle(piece_f, 1)
        ffn_block(depth, 1, 0)
        pass_on(piece_f, 3)
        if more:
            launch(piece_a + 2)
        settle(piece_f, 2)
        ffn_block(depth, 2, 0)
        pair_copy(0, depth).wait_recv()
        ffn_block(depth, 1, 1)
        ffn_block(depth, 2, 1)
        pass_on(piece_f, 4)
        settle(piece_f, 3)
        ffn_block(depth, 3, 1)
        settle(piece_f, 4)
        ffn_block(depth, 0, 1)
        far_out[depth] = far_sum[...].astype(jnp.bfloat16)
        pair_copy(1, depth).start()
        if more:
            pass_on(piece_a + 2, 1)
        ffn_block(depth, 3, 0)
        ffn_block(depth, 0, 0)
        copy = pltpu.make_async_copy(wf.at[depth], ffn_full.at[depth], out_sem.at[piece_f])
        copy.start()
        out_copies.append(copy)
        if more:
            pass_on(piece_a + 2, 2)
            pass_edge(piece_a + 2, 1)
        pair_copy(1, depth).wait_recv()
        pre_ref[depth, 1] += far_in[depth].astype(jnp.float32)
        normed, _ = normed_of(pre_ref[depth, 1])
        state[...] = normed * gains_ref[2 + 2 * depth, 0:1, :] + gains_ref[2 + 2 * depth, 1:2, :]

    spots = (
        lax.broadcasted_iota(jnp.int32, (slots, count), 1) == places_ref[...]
    ).astype(jnp.bfloat16)
    picked[spot.mp] = dot_nn(spots, state[...].astype(jnp.bfloat16)).astype(jnp.bfloat16)
    for offset in range(1, n):
        share(1, picked, offset).start()
    out_b = out_ref[...].astype(jnp.bfloat16)
    rows_v = out_ref.shape[0]
    hits = (
        labels_ref[...] == spot.mp * rows_v + lax.broadcasted_iota(jnp.int32, (rows_v, 1), 0)
    ).astype(jnp.float32)
    for offset in range(1, n):
        arrived(1, picked, offset).wait_recv()
    picked_all = picked[...].reshape(n * slots, -1)
    logits = dot_nt(out_b, picked_all)
    peak = jnp.max(logits, axis=0, keepdims=True)
    expsum = jnp.sum(jnp.exp(logits - peak), axis=0, keepdims=True)
    stats[spot.mp, 0:1, :] = peak
    stats[spot.mp, 1:2, :] = expsum
    stats[spot.mp, 2:3, :] = jnp.sum(hits * logits, axis=0, keepdims=True)
    for offset in range(1, n):
        share(2, stats, offset).start()
    for offset in range(1, n):
        arrived(2, stats, offset).wait_recv()
    peak = stats[0, 0:1, :]
    for whose in range(1, n):
        peak = jnp.maximum(peak, stats[whose, 0:1, :])
    expsum = stats[0, 1:2, :] * jnp.exp(stats[0, 0:1, :] - peak)
    target = stats[0, 2:3, :]
    for whose in range(1, n):
        expsum = expsum + stats[whose, 1:2, :] * jnp.exp(stats[whose, 0:1, :] - peak)
        target = target + stats[whose, 2:3, :]
    log_total = peak + jnp.log(expsum)
    valid = valid_ref[...] > 0.0
    loss_ref[...] = jnp.where(valid, log_total - target, 0.0)
    grad_logits = jnp.where(valid, jnp.exp(logits - log_total) - hits, 0.0).astype(jnp.bfloat16)
    picked_grad = dot_tn(grad_logits, out_b).astype(jnp.bfloat16)
    for whose in range(n):
        back_out[whose] = picked_grad[whose * slots : (whose + 1) * slots, :]
    for offset in range(1, n):
        deal(3, back_out, back_in, offset).start()
    back_in[spot.mp] = back_out[spot.mp]
    out_grad_ref[...] = dot_nn(grad_logits, picked_all)
    for offset in range(1, n):
        arrived(3, back_in, offset).wait_recv()
    summed = back_in[0].astype(jnp.float32)
    for whose in range(1, n):
        summed = summed + back_in[whose].astype(jnp.float32)
    high = summed.astype(jnp.bfloat16)
    low = (summed - high.astype(jnp.float32)).astype(jnp.bfloat16)
    grad_ref[...] = dot_tn(spots, high) + dot_tn(spots, low)

    for piece in range(2 * LAYERS):
        for way, part in WAYS:
            for step in range(1, last_step(n, way, part) + 1):
                ring_copy(piece, way, part, step, 0).wait_send()
                core_copy(piece, way, part, step, core, None).wait_send()
                if piece % 2 == 0:
                    across_copy(piece, way, part, step, spot.row).wait_send()
                    core_copy(piece, way, part, step, core, 1 - spot.row).wait_send()
    for offset in range(1, n):
        deal(0, row_out, row_in, offset).wait_send()
        share(1, picked, offset).wait_send()
        share(2, stats, offset).wait_send()
        deal(3, back_out, back_in, offset).wait_send()
    for depth in range(LAYERS):
        pair_copy(0, depth).wait_send()
        pair_copy(1, depth).wait_send()
    for turn in range(len(turns) - SLOTS, len(turns)):
        for copy in kept_copies(turn, *turns[turn]):
            copy.wait()
    for copy in out_copies:
        copy.wait()


def forward_call(
    n, ids, table, where, visible, gains, masks, places, labels, valid, out_table, attn, ffn
):
    count, width = where.shape
    rows_f = ffn.shape[2]
    slots = places.shape[0]
    f32, bf16 = jnp.float32, jnp.bfloat16
    vmem = pl.BlockSpec(memory_space=pltpu.VMEM)
    anywhere = pl.BlockSpec(memory_space=pl.ANY)
    shape = jax.ShapeDtypeStruct
    dma = pltpu.SemaphoreType.DMA
    sems = dma((2 * LAYERS, 2, 2, n // 2))
    core_sems = dma((2, 2 * LAYERS, 2, 2, n // 2))
    return pl.pallas_call(
        functools.partial(forward_kernel, n),
        out_shape=(
            shape((LAYERS, 4, width, width), bf16),
            shape((LAYERS, n // 2, 2, rows_f, width), bf16),
            shape((count, width), f32),
            shape((LAYERS, count, width), bf16),
            shape((LAYERS, 3, count, width), bf16),
            shape((LAYERS, count, width), bf16),
            shape((LAYERS, 2, count, width), f32),
            shape((LAYERS, 2, count, width), bf16),
            shape((LAYERS, n // 2, 2, count, rows_f), f32),
            shape((LAYERS, n // 2, 2, count, rows_f), bf16),
            shape((count, width), f32),
            shape(out_table.shape, f32),
            shape((1, n * slots), f32),
        ),
        in_specs=[vmem] * 10 + [anywhere] * 2,
        out_specs=(anywhere,) * 2 + (vmem,) * 6 + (anywhere,) * 2 + (vmem,) * 3,
        scratch_shapes=[
            pltpu.VMEM((LAYERS, 4, width, width), bf16),
            pltpu.VMEM((LAYERS, n // 2, 2, rows_f, width), bf16),
            pltpu.VMEM(attn.shape, f32),
            pltpu.VMEM((LAYERS, 2, rows_f // 2, width), f32),
            pltpu.VMEM((SLOTS, count, rows_f), f32),
            pltpu.VMEM((SLOTS, count, rows_f), bf16),
            pltpu.VMEM((count, width), f32),
            pltpu.VMEM((LAYERS, count, width), bf16),
            pltpu.VMEM((LAYERS, count, width), bf16),
            pltpu.VMEM((count, width), f32),
            pltpu.VMEM((n, table.shape[0], count), bf16),
            pltpu.VMEM((n, table.shape[0], count), bf16),
            pltpu.VMEM((n, slots, width), bf16),
            pltpu.VMEM((n, 8, n * slots), f32),
            pltpu.VMEM((n, slots, width), bf16),
            pltpu.VMEM((n, slots, width), bf16),
            dma((2 * LAYERS,)),
            dma((2 * LAYERS,)),
            dma((2, SLOTS)),
            sems,
            sems,
            core_sems,
            core_sems,
            sems,
            sems,
            dma((2, LAYERS)),
            dma((2, LAYERS)),
            dma((4, n - 1)),
            dma((4, n - 1)),
        ],
        compiler_params=pltpu.CompilerParams(
            collective_id=1, has_side_effects=True, vmem_limit_bytes=VMEM_LIMIT
        ),
        name="forward_layers",
    )(ids, table, where, visible, gains, masks, places, labels, valid, out_table, attn, ffn)


def norm_back(grad, values, gain):
    normed, inverse = normed_of(values)
    scaled = grad * gain
    centred = scaled - jnp.mean(scaled, axis=-1, keepdims=True)
    result = inverse * (centred - normed * jnp.mean(scaled * normed, axis=-1, keepdims=True))
    return (
        result,
        jnp.sum(grad * normed, axis=0, keepdims=True),
        jnp.sum(grad, axis=0, keepdims=True),
    )


def backward_kernel(
    n,
    ids_ref,
    counted_ref,
    losses_ref,
    visible_ref,
    gains_ref,
    out_grad_ref,
    inputs_ref,
    mixed_ref,
    mid_ref,
    grad_ref,
    first_ref,
    proj_all,
    pre_all,
    attn_full,
    ffn_full,
    slope_all,
    act_all,
    attn_sum,
    ffn_sum,
    table_sum,
    out_sum,
    small_out,
    square_out,
    proj,
    pre,
    wa,
    wf,
    slope,
    sum_a,
    sum_f,
    theirs_f,
    land_f,
    land_a,
    ring_a,
    ring_f,
    edge_a,
    go_far,
    far_sum,
    far_out,
    far_in,
    state,
    grad_rows,
    left_a,
    left_f,
    right_f,
    spread_a,
    spread_f,
    done_a,
    done_f,
    wa_sem,
    load_sem,
    slope_sem,
    core_send,
    core_recv,
    core_free,
    swap_send,
    swap_recv,
    swap_free,
    ring_send,
    ring_recv,
    ring_free,
    give_send,
    give_recv,
    pair_send,
    pair_recv,
    across_send,
    across_recv,
    out_sem,
    last_send,
    last_recv,
    small,
    small_in,
    columns_out,
    columns_in,
    table_grad,
    table_half,
    out_half,
    out_done,
    squares,
    square_parts,
    proj_sem,
    small_send,
    small_recv,
    deal_send,
    deal_recv,
    half_send,
    half_recv,
    half_sem,
    norm_send,
    norm_recv,
):
    spot = Spot(n)
    core = spot.core
    other = 1 - core
    rows_a = attn_sum.shape[2]
    rows_f = ffn_sum.shape[2]
    half_f = rows_f // 2
    part_f = half_f // 2
    count = state.shape[0]
    width = attn_sum.shape[3]
    groups = n // 2
    order = (0,) + tuple(range(groups - 1, 0, -1))
    total = LAYERS * groups

    def rows_at(shard, rows):
        return pl.ds(pl.multiple_of(shard * rows, 16), rows)

    def peer(offset):
        return (spot.mp + offset + n) % n

    def remote(source, target, send, recv, device):
        return pltpu.make_async_remote_copy(
            src_ref=source,
            dst_ref=target,
            send_sem=send,
            recv_sem=recv,
            device_id=device,
            device_id_type=MESH,
        )

    def turn_of(turn):
        return LAYERS - 1 - turn // groups, order[turn % groups]

    def load_weights(depth, group):
        return pltpu.make_async_copy(
            ffn_full.at[depth, group], wf.at[group], load_sem.at[0, group]
        )

    def load_act(depth):
        return [
            pltpu.make_async_copy(
                act_all.at[depth, group, far],
                left_f.at[group, 1, pl.ds(far * count, count), :],
                load_sem.at[1 + far, group],
            )
            for group in range(groups)
            for far in range(2)
        ]

    def load_slope(index):
        depth = LAYERS - 1 - index // (2 * groups)
        far = (index // groups) % 2
        return pltpu.make_async_copy(
            slope_all.at[depth, order[index % groups], far],
            slope.at[index % SLOTS],
            slope_sem.at[index % SLOTS],
        )

    def load_pre(depth):
        return pltpu.make_async_copy(pre_all.at[depth], pre, proj_sem.at[0])

    def load_proj(depth):
        return pltpu.make_async_copy(proj_all.at[depth], proj, proj_sem.at[1])

    def load_attn(depth):
        return pltpu.make_async_copy(attn_full.at[depth], wa, wa_sem.at[0])

    def core_copy(turn):
        slot = turn % SLOTS
        return remote(
            theirs_f.at[slot],
            land_f.at[slot],
            core_send.at[turn],
            core_recv.at[turn],
            spot.partner,
        )

    def fold(turn):
        depth, group = turn_of(turn)
        core_copy(turn).wait_recv()
        sum_f[depth, group] = (
            sum_f[depth, group].astype(jnp.float32)
            + land_f[turn % SLOTS].astype(jnp.float32)
        ).astype(jnp.bfloat16)
        if turn + SLOTS < total:
            pl.semaphore_signal(
                core_free.at[0], inc=1, device_id=spot.partner, device_id_type=MESH
            )

    def swap_copy(depth, part):
        return remote(
            wa.at[part],
            land_a.at[part],
            swap_send.at[depth, part],
            swap_recv.at[depth, part],
            spot.partner,
        )

    def cut_at(piece):
        return cut_of(width, 6)

    def summed(piece, offset, part):
        kind, depth = piece % 2, piece // 2
        if kind == 0:
            columns = ring_columns(spot.row, width, cut_at(piece))
            return sum_a.at[depth, part, rows_at(spot.shard(offset), rows_a), columns]
        far = abs(offset)
        group, half = (far, int(offset > 0)) if 0 < far < groups else (0, int(far > 0))
        return sum_f.at[depth, group, pl.ds(half * half_f + part * part_f, part_f), :]

    def landed(piece, way, part, step):
        if piece % 2 == 0:
            return ring_a.at[way, part, step - 1]
        return ring_f.at[way, part, step - 1]

    def give_copy(piece, index):
        depth = piece // 2
        give = edge_columns(1 - spot.row, width, cut_at(piece))
        return remote(
            sum_a.at[depth, index, :, give],
            edge_a.at[depth, index],
            give_send.at[depth, index],
            give_recv.at[depth, index],
            spot.across,
        )

    def absorb_rows(into, source):
        into[...] = (into[...].astype(jnp.float32) + source[...].astype(jnp.float32)).astype(
            jnp.bfloat16
        )

    def absorb(piece, index):
        depth = piece // 2
        take = edge_columns(spot.row, width, cut_at(piece))
        give_copy(piece, index).wait_recv()

        @pl.loop(0, n)
        def _(block):
            rows = rows_at(block, rows_a)
            absorb_rows(sum_a.at[depth, index, rows, take], edge_a.at[depth, index, rows, :])

    def pair_copy(which, depth):
        if which == 0:
            source, target = right_f.at[1, pl.ds(0, count), :], go_far.at[depth]
        else:
            source, target = far_out.at[depth], far_in.at[depth]
        return remote(
            source, target, pair_send.at[which, depth], pair_recv.at[which, depth], spot.across
        )

    def ring_copy(piece, way, part, step):
        offset = last_step(n, way, part) - step + 1
        return remote(
            summed(piece, offset if way == 0 else -offset, part),
            landed(piece, way, part, step),
            ring_send.at[piece, way, part, step - 1],
            ring_recv.at[piece, way, part, step - 1],
            spot.ring[way],
        )

    def ring_start(piece, way, part, step):
        if piece // 2 < LAYERS - 1:
            pl.semaphore_wait(ring_free.at[piece % 2, way, part, step - 1], 1)
        ring_copy(piece, way, part, step).start()

    def release(piece, way, part, step):
        if piece // 2 > 0:
            pl.semaphore_signal(
                ring_free.at[piece % 2, way, part, step - 1],
                inc=1,
                device_id=spot.ring[1 - way],
                device_id_type=MESH,
            )

    def launch(piece, long):
        for way, part in WAYS:
            if (way == part) == long:
                ring_start(piece, way, part, 1)

    def relay(piece, step):
        for way, part in WAYS:
            last = last_step(n, way, part)
            if step < last:
                ring_copy(piece, way, part, step).wait_recv()
                offset = last - step if way == 0 else step - last
                absorb_rows(summed(piece, offset, part), landed(piece, way, part, step))
                ring_start(piece, way, part, step + 1)
                release(piece, way, part, step)

    def across_copy(piece):
        depth = piece // 2
        buffer = spread_a if piece % 2 == 0 else spread_f
        return remote(
            buffer.at[depth, 0],
            buffer.at[depth, 1],
            across_send.at[piece],
            across_recv.at[piece],
            spot.across,
        )

    def finish(piece):
        kind, depth = piece % 2, piece // 2
        for part in range(2):
            value = summed(piece, 0, part)[...].astype(jnp.float32)
            for way in range(2):
                step = last_step(n, way, part)
                ring_copy(piece, way, part, step).wait_recv()
                value = value + landed(piece, way, part, step)[...].astype(jnp.float32)
                release(piece, way, part, step)
            value = value.astype(jnp.bfloat16)
            if kind == 0:
                spread_a[depth, 0, part] = value
            else:
                spread_f[depth, 0, pl.ds(part * part_f, part_f), :] = value
        across_copy(piece).start()

    def out_copies(piece):
        kind, depth = piece % 2, piece // 2
        if kind == 0:
            source, target = done_a, attn_sum.at[depth, pl.ds(2 * core, 2)]
        else:
            source, target = done_f, ffn_sum.at[depth, core]
        return (
            pltpu.make_async_copy(source, target, out_sem.at[piece]),
            remote(source, target, last_send.at[piece], last_recv.at[piece], spot.partner),
        )

    def conclude(piece):
        kind, depth = piece % 2, piece // 2
        across_copy(piece).wait_recv()
        if depth < LAYERS - 1:
            local, away = out_copies(piece + 2)
            local.wait()
            away.wait_send()
        row = spot.row
        if kind == 1:
            for side in range(2):
                whose = row + side - 2 * row * side
                rows = pl.ds(pl.multiple_of(whose * half_f, 16), half_f)
                done_f[rows, :] = spread_f[depth, side].astype(jnp.float32)
            add_squares(done_f[...])
        else:
            cut = cut_at(piece)
            single = width - 2 * cut

            def lanes_at(start, size):
                return pl.ds(pl.multiple_of(start, 128), size)

            for part in range(2):
                own, far = spread_a.at[depth, 0, part], spread_a.at[depth, 1, part]
                done = done_a.at[part]
                done[:, lanes_at(row * (width - cut), cut)] = own[
                    :, lanes_at(row * single, cut)
                ].astype(jnp.float32)
                done[:, lanes_at((1 - row) * (width - cut), cut)] = far[
                    :, lanes_at((1 - row) * single, cut)
                ].astype(jnp.float32)
                done[:, cut : width - cut] = own[:, lanes_at((1 - row) * cut, single)].astype(
                    jnp.float32
                ) + far[:, lanes_at(row * cut, single)].astype(jnp.float32)
                add_squares(done[...])
        for copy in out_copies(piece):
            copy.start()

    load_grad = pltpu.make_async_copy(grad_ref, state, proj_sem.at[2])
    load_grad.start()
    load_first = pltpu.make_async_copy(first_ref, pre.at[0], proj_sem.at[3])
    load_pre(LAYERS - 1).start()
    for group in order:
        load_weights(LAYERS - 1, group).start()
    for index in range(SLOTS):
        load_slope(index).start()
    for copy in load_act(LAYERS - 1):
        copy.start()
    load_attn(LAYERS - 1).start()
    load_proj(LAYERS - 1).start()
    greet([spot.partner, spot.across] + [(spot.dp, peer(offset)) for offset in range(1, n)])
    load_grad.wait()
    lanes = lax.broadcasted_iota(jnp.int32, (1, 128), 1) < 64
    visible = visible_ref[...] > 0.0

    def hidden_turn(index):
        depth = LAYERS - 1 - index // (2 * groups)
        far = (index // groups) % 2
        group = order[index % groups]
        load_slope(index).wait()
        if not far:
            load_weights(depth, group).wait()
        rows = pl.ds(far * count, count)
        grad_active = dot_nt(right_f[1, rows, :], wf[group, 1])
        grad_hidden = (grad_active * slope[index % SLOTS]).astype(jnp.bfloat16)
        left_f[group, 0, rows, :] = grad_hidden
        into = far_sum if far else state
        into[...] += dot_nn(grad_hidden, wf[group, 0])
        if far and depth > 0:
            load_weights(depth - 1, group).start()
        if index + SLOTS < 2 * total:
            load_slope(index + SLOTS).start()

    def ffn_turn(turn):
        depth, group = turn_of(turn)
        slot = turn % SLOTS
        sum_f[depth, group] = dot_tn(left_f[group, core], right_f[core]).astype(jnp.bfloat16)
        if turn >= SLOTS:
            core_copy(turn - SLOTS).wait_send()
        theirs_f[slot] = dot_tn(left_f[group, other], right_f[other]).astype(jnp.bfloat16)
        if turn >= SLOTS:
            pl.semaphore_wait(core_free.at[0], 1)
        core_copy(turn).start()

    def head_pair(depth, pair):
        columns = pl.ds(pl.multiple_of(pair * 128, 128), 128)
        query = proj[0, :, columns]
        keyed = proj[1, :, columns]
        valued = proj[2, :, columns]
        grad_mixed = grad_rows[4, :, columns]
        outs = []
        for side in range(2):
            mine = lanes if side == 0 else jnp.logical_not(lanes)
            scores = dot_nt(jnp.where(mine, query, jnp.zeros_like(query)), keyed) * 0.125
            scores = jnp.where(visible, scores, masked_score)
            expo = jnp.exp(scores - jnp.max(scores, axis=-1, keepdims=True))
            probs = expo / jnp.sum(expo, axis=-1, keepdims=True)
            grad_probs = dot_nt(jnp.where(mine, grad_mixed, jnp.zeros_like(query)), valued)
            inner = jnp.sum(grad_probs * probs, axis=-1, keepdims=True)
            grad_scores = (probs * (grad_probs - inner)).astype(jnp.bfloat16)
            outs.append(
                (
                    dot_nn(grad_scores, keyed) * 0.125,
                    dot_tn(grad_scores, query) * 0.125,
                    dot_tn(probs.astype(jnp.bfloat16), grad_mixed),
                )
            )
        for which in range(3):
            grad_rows[which, :, columns] = jnp.where(
                lanes, outs[0][which], outs[1][which]
            ).astype(jnp.bfloat16)

    def layer(depth, hooks):
        base = (LAYERS - 1 - depth) * groups
        piece_a, piece_f = 2 * depth, 2 * depth + 1
        load_pre(depth).wait()
        grad_two, small[0, 4 + 4 * depth : 5 + 4 * depth, :], small[0, 5 + 4 * depth : 6 + 4 * depth, :] = norm_back(
            state[...], pre[1], gains_ref[2 + 2 * depth, 0:1, :]
        )
        state[...] = grad_two
        if depth < LAYERS - 1:
            pair_copy(0, depth + 1).wait_send()
        right_f[1, 0:count, :] = grad_two.astype(jnp.bfloat16)
        pair_copy(0, depth).start()
        right_f[0, 0:count, :] = mid_ref[depth, 0]
        right_f[0, count : 2 * count, :] = mid_ref[depth, 1]
        far_sum[...] = jnp.zeros_like(far_sum)
        for step in range(groups):
            hidden_turn(2 * base + step)
        hooks.get("own", lambda: None)()
        pair_copy(0, depth).wait_recv()
        right_f[1, count : 2 * count, :] = go_far[depth]
        for step in range(groups):
            hidden_turn(2 * base + groups + step)
        far_out[depth] = far_sum[...].astype(jnp.bfloat16)
        pair_copy(1, depth).start()
        hooks.get("far", lambda: None)()
        for copy in load_act(depth):
            copy.wait()
        for step in range(groups):
            ffn_turn(base + step)
            if step >= 1:
                fold(base + step - 1)
            if step == 1:
                launch(piece_f, True)
            if step == 2:
                launch(piece_f, False)
            hooks.get(("ffn", step), lambda: None)()
        fold(base + groups - 1)
        if depth > 0:
            for copy in load_act(depth - 1):
                copy.start()
        pair_copy(1, depth).wait_recv()
        state[...] += far_in[depth].astype(jnp.float32)
        hooks.get("middle", lambda: None)()
        grad_one, small[0, 2 + 4 * depth : 3 + 4 * depth, :], small[0, 3 + 4 * depth : 4 + 4 * depth, :] = norm_back(
            state[...], pre[0], gains_ref[1 + 2 * depth, 0:1, :]
        )
        if depth > 0:
            load_pre(depth - 1).start()
        else:
            load_first.start()
        state[...] = grad_one
        grad_rows[3] = grad_one.astype(jnp.bfloat16)
        load_attn(depth).wait()
        load_proj(depth).wait()
        grad_rows[4] = dot_nt(grad_rows[3], wa[3]).astype(jnp.bfloat16)

        @pl.loop(0, HEADS // 2)
        def _(pair):
            head_pair(depth, pair)

        if depth > 0:
            load_proj(depth - 1).start()
        hooks.get("heads", lambda: None)()
        for which in range(3):
            state[...] += dot_nt(grad_rows[which], wa[which])
        left_a[0] = inputs_ref[depth]
        left_a[1] = mixed_ref[depth]
        for part in range(2):
            left = 0 if part == 0 else other
            wa[part] = dot_tn(left_a[left], grad_rows[2 * other + part]).astype(jnp.bfloat16)
            if depth < LAYERS - 1:
                pl.semaphore_wait(swap_free.at[part], 1)
            swap_copy(depth, part).start()
        for part in range(2):
            left = 0 if part == 0 else core
            sum_a[depth, part] = dot_tn(left_a[left], grad_rows[2 * core + part]).astype(
                jnp.bfloat16
            )
        hooks.get("mats", lambda: None)()
        for part in range(2):
            swap_copy(depth, part).wait_recv()

            @pl.loop(0, n)
            def _(block):
                rows = rows_at(block, rows_a)
                absorb_rows(sum_a.at[depth, part, rows, :], land_a.at[part, rows, :])

            give_copy(piece_a, part).start()
            if depth > 0:
                pl.semaphore_signal(
                    swap_free.at[part], inc=1, device_id=spot.partner, device_id_type=MESH
                )
    def launch_attn(piece):
        for part in range(2):
            absorb(piece, part)
        launch(piece, True)
        launch(piece, False)

    def reload_attn():
        for part in range(2):
            swap_copy(1, part).wait_send()
        load_attn(0).start()

    def half_copy(which, stage):
        buffer = out_half if which == 0 else table_half
        return remote(
            buffer.at[2 * stage],
            buffer.at[2 * stage + 1],
            half_send.at[which, stage],
            half_recv.at[which, stage],
            spot.partner if stage == 0 else spot.across,
        )

    def half_rows(rows, side):
        return pl.ds(pl.multiple_of(side * (rows // 2), 16), rows // 2)

    def half_start(which, source):
        buffer = out_half if which == 0 else table_half
        buffer[0] = source[half_rows(source.shape[0], other), :].astype(jnp.bfloat16)
        half_copy(which, 0).start()

    def half_fold(which, source):
        buffer = out_half if which == 0 else table_half
        half_copy(which, 0).wait_recv()
        own = source[half_rows(source.shape[0], core), :]
        buffer[2] = (own + buffer[1].astype(jnp.float32)).astype(jnp.bfloat16)
        half_copy(which, 1).start()

    def half_out(which):
        if which == 0:
            source, target = out_done, out_sum.at[half_rows(out_sum.shape[0], core), :]
        else:
            source = table_grad.at[half_rows(table_sum.shape[0], core), :]
            target = table_sum.at[half_rows(table_sum.shape[0], core), :]
        return (
            pltpu.make_async_copy(source, target, half_sem.at[which]),
            remote(source, target, half_send.at[which, 2], half_recv.at[which, 2], spot.partner),
        )

    def add_squares(value):
        squares[...] += jnp.sum(value * value, axis=0, keepdims=True)

    def half_end(which):
        buffer = out_half if which == 0 else table_half
        half_copy(which, 1).wait_recv()
        value = buffer[2].astype(jnp.float32) + buffer[3].astype(jnp.float32)
        if which == 0:
            out_done[...] = value
        else:
            table_grad[half_rows(table_sum.shape[0], core), :] = value
        width = squares.shape[1]
        for start in range(0, value.shape[1], width):
            add_squares(value[:, start : start + width])
        for copy in half_out(which):
            copy.start()

    def small_copy(stage):
        bit = 1 << max(0, stage - 2)
        pair = spot.mp + bit - 2 * bit * ((spot.mp // bit) % 2)
        device = (spot.partner, spot.across)[stage] if stage < 2 else (spot.dp, pair)
        return remote(
            small.at[stage],
            small_in.at[stage],
            small_send.at[stage],
            small_recv.at[stage],
            device,
        )

    def small_next(stage):
        small_copy(stage).wait_recv()
        small[stage + 1] = small[stage] + small_in[stage]
        if stage < 4:
            small_copy(stage + 1).start()

    def deal_copy(offset, arriving):
        source = columns_out.at[peer(offset)]
        target = columns_in.at[peer(-offset) if arriving else spot.mp]
        return remote(
            source,
            target,
            deal_send.at[offset - 1],
            deal_recv.at[offset - 1],
            (spot.dp, peer(offset)),
        )

    def table_blocks(first, last):
        @pl.loop(first, last)
        def _(block):
            row = lax.broadcasted_iota(jnp.int32, (256, 1), 0) + block * 256
            value = jnp.zeros((columns_in.shape[1], 256), jnp.float32)
            for whose in range(n):
                chosen = (row == ids_ref[whose : whose + 1, :]).astype(jnp.bfloat16)
                value = value + dot_nt(columns_in[whose], chosen)
            table_grad[:, pl.ds(pl.multiple_of(block * 256, 256), 256)] = value

    squares[...] = jnp.zeros_like(squares)
    half_start(0, out_grad_ref)
    layer(
        1,
        {
            "far": lambda: half_fold(0, out_grad_ref),
            "heads": lambda: relay(3, 1),
            "mats": lambda: relay(3, 2),
        },
    )
    layer(
        0,
        {
            "own": lambda: (reload_attn(), launch_attn(2), relay(3, 3)),
            "far": lambda: (relay(2, 1), finish(3)),
            ("ffn", 1): lambda: relay(2, 2),
            ("ffn", 3): lambda: (conclude(3), half_end(0)),
            "middle": lambda: (relay(2, 3), relay(1, 1)),
            "heads": lambda: (finish(2), relay(1, 2)),
        },
    )
    load_first.wait()
    grad_sum, small[0, 0:1, :], small[0, 1:2, :] = norm_back(
        state[...], pre[0], gains_ref[0, 0:1, :]
    )
    width = squares.shape[1]
    lane = lax.broadcasted_iota(jnp.int32, (1, width), 1)
    loss = jnp.sum(losses_ref[...], axis=1, keepdims=True) * (1.0 / n)
    slots = counted_ref[0:1, 0:1] * (1.0 / n)
    small[0, 10:11, :] = jnp.where(lane == 0, loss, jnp.where(lane == 1, slots, 0.0))
    small[0, 11:16, :] = jnp.zeros((5, width), jnp.float32)
    small_copy(0).start()
    turned = grad_sum.T.astype(jnp.bfloat16)
    share = columns_in.shape[1]
    for whose in range(n):
        columns_out[whose] = turned[whose * share : (whose + 1) * share, :]
    for offset in range(1, n):
        deal_copy(offset, False).start()
    columns_in[spot.mp] = columns_out[spot.mp]
    relay(1, 3)
    launch_attn(0)
    small_next(0)
    conclude(2)
    for offset in range(1, n):
        deal_copy(offset, True).wait_recv()
    blocks = table_sum.shape[1] // 256
    table_blocks(0, blocks // 2)
    relay(0, 1)
    small_next(1)
    table_blocks(blocks // 2, blocks)
    half_start(1, table_grad)
    small_next(2)
    half_fold(1, table_grad)
    relay(0, 2)
    finish(1)
    small_next(3)
    half_end(1)
    relay(0, 3)
    conclude(1)
    small_next(4)
    finish(0)
    small_out[...] = small[5]
    conclude(0)

    square = jnp.sum(squares[...], axis=1, keepdims=True)
    square_parts[n] = jnp.broadcast_to(square, square_parts.shape[1:])
    swap = remote(
        square_parts.at[n],
        square_parts.at[n + 1],
        norm_send.at[0],
        norm_recv.at[0],
        spot.partner,
    )
    swap.start()
    swap.wait_recv()
    square_parts[spot.mp] = square_parts[n] + square_parts[n + 1]

    def norm_copy(offset, arriving):
        source = square_parts.at[spot.mp]
        target = square_parts.at[peer(-offset) if arriving else spot.mp]
        return remote(
            source, target, norm_send.at[offset], norm_recv.at[offset], (spot.dp, peer(offset))
        )

    for offset in range(1, n):
        norm_copy(offset, False).start()
    gains_grad = small[5, 0:10, :]
    square = jnp.sum(jnp.sum(gains_grad * gains_grad, axis=0, keepdims=True), axis=1, keepdims=True)
    for offset in range(1, n):
        norm_copy(offset, True).wait_recv()
    for whose in range(n):
        square = square + square_parts[whose, 0:1, :]
    square_out[...] = square

    pair_copy(0, 0).wait_send()
    for depth in range(LAYERS):
        pair_copy(1, depth).wait_send()
    swap.wait_send()
    for offset in range(1, n):
        norm_copy(offset, False).wait_send()
        deal_copy(offset, False).wait_send()
    for stage in range(5):
        small_copy(stage).wait_send()
    for which in range(2):
        half_copy(which, 0).wait_send()
        half_copy(which, 1).wait_send()
        local, away = half_out(which)
        local.wait()
        away.wait()
    for turn in range(total - SLOTS, total):
        core_copy(turn).wait_send()
    for part in range(2):
        swap_copy(0, part).wait_send()
    for piece in range(2 * LAYERS):
        for way, part in WAYS:
            for step in range(1, last_step(n, way, part) + 1):
                ring_copy(piece, way, part, step).wait_send()
        across_copy(piece).wait_send()
        if piece % 2 == 0:
            for index in range(2):
                give_copy(piece, index).wait_send()
        local, away = out_copies(piece)
        if piece < 2:
            local.wait()
            away.wait_send()
        away.wait_recv()


def backward_call(
    n, ids, counted, losses, visible, grad, first, gains, out_grad, kept, attn_full, ffn_full, slope, act, table
):
    inputs, proj, mixed, pre, mid = kept
    count, width = grad.shape
    rows_f = ffn_full.shape[3]
    groups = n // 2
    rows_a = attn_full.shape[2] // n
    rows_v = out_grad.shape[0]
    words, share = table.shape
    f32, bf16 = jnp.float32, jnp.bfloat16
    vmem = pl.BlockSpec(memory_space=pltpu.VMEM)
    anywhere = pl.BlockSpec(memory_space=pl.ANY)
    shape = jax.ShapeDtypeStruct
    dma = pltpu.SemaphoreType.DMA
    regular = pltpu.SemaphoreType.REGULAR
    ring_sems = dma((2 * LAYERS, 2, 2, n // 2))
    return pl.pallas_call(
        functools.partial(backward_kernel, n),
        out_shape=(
            shape((LAYERS, 4, rows_a, width), f32),
            shape((LAYERS, 2, rows_f, width), f32),
            shape((share, words), f32),
            shape((rows_v, width), f32),
            shape((16, width), f32),
            shape((1, 128), f32),
        ),
        in_specs=[vmem] * 9 + [anywhere] * 8,
        out_specs=(anywhere,) * 4 + (vmem,) * 2,
        scratch_shapes=[
            pltpu.VMEM((3, count, width), bf16),
            pltpu.VMEM((2, count, width), f32),
            pltpu.VMEM((4, width, width), bf16),
            pltpu.VMEM((groups, 2, rows_f, width), bf16),
            pltpu.VMEM((SLOTS, count, rows_f), f32),
            pltpu.VMEM((LAYERS, 2, width, width), bf16),
            pltpu.VMEM((LAYERS, groups, rows_f, width), bf16),
            pltpu.VMEM((SLOTS, rows_f, width), bf16),
            pltpu.VMEM((SLOTS, rows_f, width), bf16),
            pltpu.VMEM((2, width, width), bf16),
            pltpu.VMEM((2, 2, n // 2, rows_a, width - cut_of(width, 6)), bf16),
            pltpu.VMEM((2, 2, n // 2, rows_f // 4, width), bf16),
            pltpu.VMEM((LAYERS, 2, width, cut_of(width, 6)), bf16),
            pltpu.VMEM((LAYERS, count, width), bf16),
            pltpu.VMEM((count, width), f32),
            pltpu.VMEM((LAYERS, count, width), bf16),
            pltpu.VMEM((LAYERS, count, width), bf16),
            pltpu.VMEM((count, width), f32),
            pltpu.VMEM((5, count, width), bf16),
            pltpu.VMEM((2, count, width), bf16),
            pltpu.VMEM((groups, 2, 2 * count, rows_f), bf16),
            pltpu.VMEM((2, 2 * count, width), bf16),
            pltpu.VMEM((LAYERS, 2, 2, rows_a, width - cut_of(width, 6)), bf16),
            pltpu.VMEM((LAYERS, 2, rows_f // 2, width), bf16),
            pltpu.VMEM((2, rows_a, width), f32),
            pltpu.VMEM((rows_f, width), f32),
            dma((1,)),
            dma((3, groups)),
            dma((SLOTS,)),
            dma((LAYERS * groups,)),
            dma((LAYERS * groups,)),
            regular((1,)),
            dma((LAYERS, 2)),
            dma((LAYERS, 2)),
            regular((2,)),
            ring_sems,
            ring_sems,
            regular((2, 2, 2, n // 2)),
            dma((LAYERS, 2)),
            dma((LAYERS, 2)),
            dma((2, LAYERS)),
            dma((2, LAYERS)),
            dma((2 * LAYERS,)),
            dma((2 * LAYERS,)),
            dma((2 * LAYERS,)),
            dma((2 * LAYERS,)),
            dma((2 * LAYERS,)),
            pltpu.VMEM((6, 16, width), f32),
            pltpu.VMEM((5, 16, width), f32),
            pltpu.VMEM((n, share, count), bf16),
            pltpu.VMEM((n, share, count), bf16),
            pltpu.VMEM((share, words), f32),
            pltpu.VMEM((4, share // 2, words), bf16),
            pltpu.VMEM((4, rows_v // 2, width), bf16),
            pltpu.VMEM((rows_v // 2, width), f32),
            pltpu.VMEM((1, width), f32),
            pltpu.VMEM((n + 2, 8, 128), f32),
            dma((4,)),
            dma((5,)),
            dma((5,)),
            dma((n - 1,)),
            dma((n - 1,)),
            dma((2, 3)),
            dma((2, 3)),
            dma((2,)),
            dma((n,)),
            dma((n,)),
        ],
        compiler_params=pltpu.CompilerParams(
            collective_id=2, has_side_effects=True, vmem_limit_bytes=VMEM_LIMIT
        ),
        name="backward_layers",
    )(
        ids, counted, losses, visible, gains, out_grad, inputs, mixed, mid, grad, first,
        proj, pre, attn_full, ffn_full, slope, act,
    )


def merged(value, axis, join):
    pieces = jax.tree.map(lambda part: lax.all_gather(part, axis), value)
    head = jax.tree.map(lambda part: part[0], pieces)
    tail = jax.tree.map(lambda part: part[1:], pieces)
    total, _ = lax.scan(lambda total, section: (join(total, section), None), head, tail)
    return total


def sinusoid(count, width):
    places = jnp.arange(count, dtype=jnp.float32)[:, None]
    freqs = jnp.exp(jnp.arange(width // 2, dtype=jnp.float32) * (-2.0 * math.log(10000.0) / width))
    angles = places * freqs[None, :]
    return jnp.concatenate([jnp.sin(angles), jnp.cos(angles)], axis=1)


def layer_norm(values, gain, shift):
    centre = jnp.mean(values, axis=-1, keepdims=True)
    offset = values - centre
    spread = jnp.mean(offset * offset, axis=-1, keepdims=True)
    inverse = lax.rsqrt(spread + norm_eps)
    normed = offset * inverse
    return (normed * gain + shift, (normed, inverse))


def norm_backward(grad, saved, gain):
    normed, inverse = saved
    scaled = grad * gain
    centred = scaled - jnp.mean(scaled, axis=-1, keepdims=True)
    result = inverse * (centred - normed * jnp.mean(scaled * normed, axis=-1, keepdims=True))
    return (result, jnp.stack([jnp.sum(grad * normed, axis=0), jnp.sum(grad, axis=0)]))


def gelu_exact(values):
    return jax.nn.gelu(values, approximate=False)


def gelu_back(hidden, grad):
    unused, pullback = jax.vjp(gelu_exact, hidden)
    return pullback(grad)[0]


def masked_scores(query, keyed, length):
    scale = query.shape[-1] ** (-0.5)
    scores = jnp.einsum("hqe,hke->hqk", query, keyed, preferred_element_type=jnp.float32) * scale
    visible = jnp.arange(keyed.shape[1]) < length
    return jnp.where(visible[None, None, :], scores, masked_score)


def fetch_forward(attn_part, ffn_part):
    return (
        lax.all_gather(attn_part, "mp", axis=1, tiled=True),
        lax.all_gather(ffn_part, "mp", axis=1, tiled=True),
    )


def fetch_backward(attn_part, ffn_part):
    return (
        lax.all_gather(attn_part, "mp", axis=1, tiled=True),
        lax.all_gather(ffn_part, "mp", axis=1, tiled=True),
    )


def reduce_layer(attn_grad, ffn_grad):
    return (
        lax.psum_scatter(attn_grad, "mp", scatter_dimension=1, tiled=True),
        lax.psum_scatter(ffn_grad, "mp", scatter_dimension=1, tiled=True),
    )


def ffn_forward(middle_b, ffn_w, unit_mask):
    hidden = jnp.einsum("td,fd->tf", middle_b, ffn_w[0], preferred_element_type=jnp.float32)
    active = (gelu_exact(hidden) * unit_mask[None, :]).astype(jnp.bfloat16)
    output = jnp.einsum("tf,fd->td", active, ffn_w[1], preferred_element_type=jnp.float32)
    return (hidden, active, output)


def ffn_backward(grad_out, middle_b, hidden, active, ffn_w, unit_mask):
    grad_active = jnp.einsum("td,fd->tf", grad_out, ffn_w[1], preferred_element_type=jnp.float32)
    grad_hidden = gelu_back(hidden, grad_active * unit_mask[None, :]).astype(jnp.bfloat16)
    up_grad = jnp.einsum("tf,td->fd", grad_hidden, middle_b, preferred_element_type=jnp.float32)
    down_grad = jnp.einsum("tf,td->fd", active, grad_out, preferred_element_type=jnp.float32)
    from_ffn = jnp.einsum("tf,fd->td", grad_hidden, ffn_w[0], preferred_element_type=jnp.float32)
    return (jnp.stack([up_grad, down_grad]), from_ffn)


def layer_forward(states, attn_w, ffn_w, pair, length, unit_mask):
    count = states.shape[0]
    inputs = states.astype(jnp.bfloat16)
    projected = jnp.einsum(
        "td,kde->kte", inputs, attn_w[:3], preferred_element_type=jnp.float32
    ).astype(jnp.bfloat16)
    heads = projected.reshape(3, count, HEADS, -1).transpose(0, 2, 1, 3)
    scores = masked_scores(heads[0], heads[1], length)
    peak = jnp.max(scores, axis=-1, keepdims=True)
    expo = jnp.exp(scores - peak)
    total = jnp.sum(expo, axis=-1, keepdims=True)
    log_total = peak + jnp.log(total)
    probs = (expo / total).astype(jnp.bfloat16)
    mixed = jnp.einsum("hqk,hke->hqe", probs, heads[2], preferred_element_type=jnp.float32)
    mixed = mixed.transpose(1, 0, 2).reshape(count, -1).astype(jnp.bfloat16)
    branch = jnp.dot(mixed, attn_w[3], preferred_element_type=jnp.float32)
    middle, norm_one = layer_norm(states + branch, pair[0, 0], pair[0, 1])
    middle_b = middle.astype(jnp.bfloat16)
    hidden, active, output = ffn_forward(middle_b, ffn_w, unit_mask)
    result, norm_two = layer_norm(middle + output, pair[1, 0], pair[1, 1])
    return (result, (inputs, heads, log_total, mixed, norm_one, middle_b, hidden, active, norm_two))


def layer_backward(grad, attn_w, ffn_w, pair, length, unit_mask, kept):
    inputs, heads, log_total, mixed, norm_one, middle_b, hidden, active, norm_two = kept
    count = inputs.shape[0]
    grad_two, pair_two = norm_backward(grad, norm_two, pair[1, 0])
    ffn_grad, from_ffn = ffn_backward(
        grad_two.astype(jnp.bfloat16), middle_b, hidden, active, ffn_w, unit_mask
    )
    grad_one, pair_one = norm_backward(grad_two + from_ffn, norm_one, pair[0, 0])
    grad_branch = grad_one.astype(jnp.bfloat16)
    output_grad = jnp.einsum("td,te->de", mixed, grad_branch, preferred_element_type=jnp.float32)
    grad_mixed = jnp.einsum("te,de->td", grad_branch, attn_w[3], preferred_element_type=jnp.float32)
    grad_mixed = grad_mixed.astype(jnp.bfloat16).reshape(count, HEADS, -1).transpose(1, 0, 2)
    scale = heads.shape[-1] ** (-0.5)
    probs = jnp.exp(masked_scores(heads[0], heads[1], length) - log_total)
    grad_values = jnp.einsum(
        "hqk,hqe->hke", probs.astype(jnp.bfloat16), grad_mixed, preferred_element_type=jnp.float32
    )
    grad_probs = jnp.einsum(
        "hqe,hke->hqk", grad_mixed, heads[2], preferred_element_type=jnp.float32
    )
    grad_scores = probs * (grad_probs - jnp.sum(grad_probs * probs, axis=-1, keepdims=True))
    grad_scores = grad_scores.astype(jnp.bfloat16)
    grad_query = (
        jnp.einsum("hqk,hke->hqe", grad_scores, heads[1], preferred_element_type=jnp.float32)
        * scale
    )
    grad_key = (
        jnp.einsum("hqk,hqe->hke", grad_scores, heads[0], preferred_element_type=jnp.float32)
        * scale
    )
    stacked = (
        jnp.stack([grad_query, grad_key, grad_values]).transpose(0, 2, 1, 3).reshape(3, count, -1)
    )
    stacked = stacked.astype(jnp.bfloat16)
    input_grad = jnp.einsum("td,kte->kde", inputs, stacked, preferred_element_type=jnp.float32)
    from_attn = jnp.einsum("kte,kde->td", stacked, attn_w[:3], preferred_element_type=jnp.float32)
    attn_grad = jnp.concatenate([input_grad, output_grad[None]], axis=0)
    return (grad_one + from_attn, attn_grad, ffn_grad, jnp.stack([pair_one, pair_two]))


def adamw(weight, moment_one, moment_two, grad, decay, rate):
    moment_one = beta_one * moment_one + (1.0 - beta_one) * grad
    moment_two = beta_two * moment_two + (1.0 - beta_two) * grad * grad
    fixed_one = moment_one / (1.0 - beta_one**STEP)
    fixed_two = moment_two / (1.0 - beta_two**STEP)
    weight = weight - rate * (fixed_one / (jnp.sqrt(fixed_two) + adam_eps) + decay * weight)
    return (moment_one, moment_two, weight)


def combine_vocab(first, second):
    peak = jnp.maximum(first[0], second[0])
    total = first[1] * jnp.exp(first[0] - peak) + second[1] * jnp.exp(second[0] - peak)
    return (peak, total, first[2] + second[2])


def local_general(
    tokens,
    lengths,
    places,
    targets,
    ramp,
    attn,
    attn_m,
    attn_v,
    ffn,
    ffn_m,
    ffn_v,
    table,
    table_m,
    table_v,
    out_table,
    out_m,
    out_v,
    gains,
    gains_m,
    gains_v,
):
    rank = lax.axis_index("mp")
    count = tokens.shape[2]
    flat_ids = tokens.reshape(-1)
    all_lengths = lengths.reshape(-1)
    length = lax.dynamic_index_in_dim(all_lengths, rank, keepdims=False)
    masks = jnp.minimum(ramp, RAMP).astype(jnp.float32) / RAMP
    unit_masks = [masks[depth] for depth in range(LAYERS)]
    looked = jnp.take(table, flat_ids, axis=0)
    embedded = lax.all_to_all(looked, "mp", split_axis=0, concat_axis=1, tiled=True)
    states, norm_zero = layer_norm(
        embedded + sinusoid(count, embedded.shape[1]), gains[0, 0], gains[0, 1]
    )
    kept_all = []
    weights_all = []
    for depth in range(LAYERS):
        attn_w, ffn_w = fetch_forward(
            attn[depth].astype(jnp.bfloat16), ffn[depth].astype(jnp.bfloat16)
        )
        states, kept = layer_forward(
            states, attn_w, ffn_w, gains[1 + 2 * depth : 3 + 2 * depth], length, unit_masks[depth]
        )
        kept_all.append(kept)
        weights_all.append(None)
    spots = places.reshape(-1)
    picked = jnp.take(states, spots, axis=0).astype(jnp.bfloat16)
    picked_all = lax.all_gather(picked, "mp", axis=0, tiled=True)
    out_b = out_table.astype(jnp.bfloat16)
    logits = jnp.einsum("rd,vd->rv", picked_all, out_b, preferred_element_type=jnp.float32)
    labels = targets.reshape(-1)
    columns = rank * out_table.shape[0] + jnp.arange(out_table.shape[0])
    hits = (labels[:, None] == columns[None, :]).astype(jnp.float32)
    peak = jnp.max(logits, axis=1)
    expsum = jnp.sum(jnp.exp(logits - peak[:, None]), axis=1)
    target_part = jnp.sum(hits * logits, axis=1)
    peak_all, expsum_all, target_all = merged((peak, expsum, target_part), "mp", combine_vocab)
    log_total = peak_all + jnp.log(expsum_all)
    slot_count = targets.shape[2]
    counted = jnp.maximum(1, all_lengths * slot_count // count)
    valid = (jnp.arange(slot_count)[None, :] < counted[:, None]).reshape(-1)
    loss_pair = jnp.stack(
        [
            jnp.sum(jnp.where(valid, log_total - target_all, 0.0)),
            jnp.sum(counted).astype(jnp.float32),
        ]
    )
    grad_logits = jnp.where(
        valid[:, None], jnp.exp(logits - log_total[:, None]) - hits, 0.0
    ).astype(jnp.bfloat16)
    out_grad = jnp.einsum("rv,rd->vd", grad_logits, picked_all, preferred_element_type=jnp.float32)
    picked_grad = lax.psum_scatter(
        jnp.dot(grad_logits, out_b, preferred_element_type=jnp.float32),
        "mp",
        scatter_dimension=0,
        tiled=True,
    )
    grad = jnp.zeros_like(states).at[spots].add(picked_grad)
    attn_parts = [None] * LAYERS
    ffn_parts = [None] * LAYERS
    pair_grads = [None] * LAYERS
    for depth in reversed(range(LAYERS)):
        attn_w, ffn_w = fetch_backward(
            attn[depth].astype(jnp.bfloat16), ffn[depth].astype(jnp.bfloat16)
        )
        grad, attn_grad, ffn_grad, pair_grad = layer_backward(
            grad,
            attn_w,
            ffn_w,
            gains[1 + 2 * depth : 3 + 2 * depth],
            length,
            unit_masks[depth],
            kept_all[depth],
        )
        attn_parts[depth], ffn_parts[depth] = reduce_layer(attn_grad, ffn_grad)
        pair_grads[depth] = pair_grad
    grad_sum, zero_grad = norm_backward(grad, norm_zero, gains[0, 0])
    returned = lax.all_to_all(grad_sum, "mp", split_axis=1, concat_axis=0, tiled=True)
    table_grad = jnp.zeros_like(table).at[flat_ids].add(returned)
    gains_grad = jnp.concatenate([zero_grad[None]] + pair_grads, axis=0)
    attn_sum, ffn_sum, table_sum, out_sum, gains_part, loss = lax.psum(
        (jnp.stack(attn_parts), jnp.stack(ffn_parts), table_grad, out_grad, gains_grad, loss_pair),
        "dp",
    )
    shard_squares = (
        jnp.sum(attn_sum * attn_sum)
        + jnp.sum(ffn_sum * ffn_sum)
        + jnp.sum(table_sum * table_sum)
        + jnp.sum(out_sum * out_sum)
    )
    square_total, gains_sum = lax.psum((shard_squares, gains_part), "mp")
    grad_norm = jnp.sqrt(square_total + jnp.sum(gains_sum * gains_sum))
    factor = clip_limit / jnp.maximum(grad_norm, clip_limit)
    attn_m_new, attn_v_new, attn_new = adamw(
        attn, attn_m, attn_v, attn_sum * factor, weight_decay, learn_rate
    )
    ffn_m_new, ffn_v_new, ffn_new = adamw(
        ffn, ffn_m, ffn_v, ffn_sum * factor, weight_decay, learn_rate
    )
    table_m_new, table_v_new, table_new = adamw(
        table, table_m, table_v, table_sum * factor, weight_decay, learn_rate
    )
    out_m_new, out_v_new, out_new = adamw(
        out_table, out_m, out_v, out_sum * factor, weight_decay, learn_rate
    )
    gains_m_new, gains_v_new, gains_new = adamw(
        gains, gains_m, gains_v, gains_sum * factor, 0.0, gain_rate
    )
    return (
        loss,
        grad_norm.reshape(1),
        attn_m_new,
        attn_v_new,
        attn_new,
        ffn_m_new,
        ffn_v_new,
        ffn_new,
        table_m_new,
        table_v_new,
        table_new,
        out_m_new,
        out_v_new,
        out_new,
        gains_m_new,
        gains_v_new,
        gains_new,
    )


def local(
    tokens,
    lengths,
    places,
    targets,
    ramp,
    attn,
    attn_m,
    attn_v,
    ffn,
    ffn_m,
    ffn_v,
    table,
    table_m,
    table_v,
    out_table,
    out_m,
    out_v,
    gains,
    gains_m,
    gains_v,
):
    rank = lax.axis_index("mp")
    n = tokens.shape[1]
    count, width = tokens.shape[2], gains.shape[2]
    flat_ids = tokens.reshape(-1)
    all_lengths = lengths.reshape(-1)
    length = lax.dynamic_index_in_dim(all_lengths, rank, keepdims=False)
    masks = jnp.minimum(ramp, RAMP).astype(jnp.float32) / RAMP
    place = ring_place(rank, n)
    reach = [0, n // 2] + [side * step for step in range(1, n // 2) for side in (-1, 1)]
    near = jnp.stack([ring_index((place + offset + n) % n, n) for offset in reach])
    masks = masks.reshape(LAYERS, n, 2, -1)[:, :, lax.axis_index("dp") // 2]
    masks = jnp.take(masks, near, axis=1).reshape(LAYERS, n // 2, -1)
    visible = (jnp.arange(count) < length).astype(jnp.float32)[None, :]
    slot_count = targets.shape[2]
    slots = 32 * -(-slot_count // 32)
    counted = jnp.maximum(1, all_lengths * slot_count // count)
    valid = (jnp.arange(slots)[None, :] < counted[:, None]).astype(jnp.float32).reshape(1, -1)
    extra = slots - slot_count
    spots = jnp.pad(places.reshape(-1), (0, extra), constant_values=-1)[:, None]
    labels = jnp.pad(targets[0], ((0, 0), (0, extra)), constant_values=-1).reshape(1, -1)
    where = sinusoid(count, width)
    attn_full, ffn_full, first, *kept, slope, act, grad, out_grad, losses = forward_call(
        n, tokens[0], table.T.astype(jnp.bfloat16), where, visible, gains, masks, spots, labels, valid, out_table, attn, ffn
    )
    tally = jnp.broadcast_to(jnp.sum(counted).astype(jnp.float32), (1, 128))
    attn_sum, ffn_sum, table_turned, out_sum, small, square = backward_call(
        n, tokens[0], tally, losses, visible, grad, first, gains, out_grad, kept, attn_full, ffn_full, slope, act, table
    )
    table_sum = table_turned.T
    gains_sum = small[:10].reshape(gains.shape)
    grad_norm = jnp.sqrt(square[0, 0])
    factor = clip_limit / jnp.maximum(grad_norm, clip_limit)
    attn_m_new, attn_v_new, attn_new = adamw(
        attn, attn_m, attn_v, attn_sum * factor, weight_decay, learn_rate
    )
    ffn_m_new, ffn_v_new, ffn_new = adamw(
        ffn, ffn_m, ffn_v, ffn_sum * factor, weight_decay, learn_rate
    )
    table_m_new, table_v_new, table_new = adamw(
        table, table_m, table_v, table_sum * factor, weight_decay, learn_rate
    )
    out_m_new, out_v_new, out_new = adamw(
        out_table, out_m, out_v, out_sum * factor, weight_decay, learn_rate
    )
    gains_m_new, gains_v_new, gains_new = adamw(
        gains, gains_m, gains_v, gains_sum * factor, 0.0, gain_rate
    )
    return (
        small[10, :2],
        grad_norm.reshape(1),
        attn_m_new,
        attn_v_new,
        attn_new,
        ffn_m_new,
        ffn_v_new,
        ffn_new,
        table_m_new,
        table_v_new,
        table_new,
        out_m_new,
        out_v_new,
        out_new,
        gains_m_new,
        gains_v_new,
        gains_new,
    )


def solution(mesh):
    in_specs = (
        P("dp", None, None),
        P("dp", None),
        P("dp", "mp", None),
        P("dp", None, None),
        P(),
        P(None, None, "mp", None),
        P(None, None, "mp", None),
        P(None, None, "mp", None),
        P(None, None, "mp", None),
        P(None, None, "mp", None),
        P(None, None, "mp", None),
        P(None, "mp"),
        P(None, "mp"),
        P(None, "mp"),
        P("mp", None),
        P("mp", None),
        P("mp", None),
        P(),
        P(),
        P(),
    )
    out_specs = (
        P(),
        P(),
        P(None, None, "mp", None),
        P(None, None, "mp", None),
        P(None, None, "mp", None),
        P(None, None, "mp", None),
        P(None, None, "mp", None),
        P(None, None, "mp", None),
        P(None, "mp"),
        P(None, "mp"),
        P(None, "mp"),
        P("mp", None),
        P("mp", None),
        P("mp", None),
        P(),
        P(),
        P(),
    )
    fits = mesh.shape['mp'] == 8 and mesh.shape['dp'] == 4
    chosen = local if fits else local_general
    return jax.shard_map(chosen, mesh=mesh, in_specs=in_specs, out_specs=out_specs, check_vma=False)
```

```python
import functools
import math

import jax
import jax.numpy as jnp
import numpy as np
from jax import lax
from jax.experimental import pallas as pl
from jax.experimental.pallas import tpu as pltpu
from jax.sharding import PartitionSpec as P

HEADS = 12
LAYERS = 2
STEP = 10
RAMP = 4


norm_eps = 1e-05
beta_one = 0.9
beta_two = 0.999
learn_rate = 0.02
gain_rate = 0.3
weight_decay = 0.01
adam_eps = 1e-08
clip_limit = 1.0
masked_score = -1000000000.0


MESH = pl.DeviceIdType.MESH
VMEM_LIMIT = 62 * 1024 * 1024
SLOTS = 3


def dot_nn(left, right):
    return lax.dot_general(
        left, right, (((1,), (0,)), ((), ())), preferred_element_type=jnp.float32
    )


def dot_nt(left, right):
    return lax.dot_general(
        left, right, (((1,), (1,)), ((), ())), preferred_element_type=jnp.float32
    )


def dot_tn(left, right):
    return lax.dot_general(
        left, right, (((0,), (0,)), ((), ())), preferred_element_type=jnp.float32
    )


def positions(count, width):
    angles = np.arange(count)[:, None] * np.exp(
        np.arange(width // 2) * (-2.0 * math.log(10000.0) / width)
    )
    return np.concatenate([np.sin(angles), np.cos(angles)], axis=1).astype(np.float32)


def ring_index(place, n):
    late = place // (n // 2)
    return (1 - late) * 2 * place + late * (2 * (n - 1 - place) + 1)


def ring_place(index, n):
    odd = index % 2
    return (1 - odd) * (index // 2) + odd * (n - 1 - index // 2)


class Spot:
    def __init__(self, n):
        self.n = n
        self.dp = lax.axis_index("dp")
        self.mp = lax.axis_index("mp")
        self.core = self.dp % 2
        self.row = self.dp // 2
        self.place = ring_place(self.mp, n)
        self.partner = (self.dp + 1 - 2 * self.core, self.mp)
        self.across = ((self.dp + 2) % 4, self.mp)
        self.ring = (
            (self.dp, ring_index((self.place + 1) % n, n)),
            (self.dp, ring_index((self.place + n - 1) % n, n)),
        )

    def shard(self, offset):
        return ring_index((self.place + offset + self.n) % self.n, self.n)


def greet(devices):
    barrier = pltpu.get_barrier_semaphore()
    for device in devices:
        pl.semaphore_signal(barrier, inc=1, device_id=device, device_id_type=MESH)
    pl.semaphore_wait(barrier, len(devices))


def last_step(n, way, part):
    return n // 2 if way == part else n // 2 - 1


WAYS = ((0, 0), (1, 1), (0, 1), (1, 0))


def ring_columns(row, width, cut):
    return pl.ds(pl.multiple_of(row * cut, 128), width - cut)


def edge_columns(row, width, cut):
    return pl.ds(pl.multiple_of(row * (width - cut), 128), cut)


def cut_of(width, share):
    return 128 * (width // 128 // share)


def normed_of(values):
    centre = jnp.mean(values, axis=-1, keepdims=True)
    offset = values - centre
    spread = jnp.mean(offset * offset, axis=-1, keepdims=True)
    inverse = lax.rsqrt(spread + norm_eps)
    return offset * inverse, inverse


def forward_kernel(
    n,
    ids_ref,
    lengths_ref,
    places_ref,
    targets_ref,
    ramp_ref,
    gains_ref,
    table_ref,
    where_ref,
    out_ref,
    attn_sh,
    ffn_sh,
    attn_full,
    ffn_full,
    first_out,
    inputs_out,
    proj_out,
    mixed_out,
    pre_out,
    mid_out,
    slope_ref,
    act_ref,
    grad_ref,
    out_grad_ref,
    loss_ref,
    first_ref,
    inputs_ref,
    proj_ref,
    mixed_ref,
    pre_ref,
    mid_ref,
    mask_ref,
    places_row,
    labels_row,
    wa,
    wf,
    raw_a,
    raw_f,
    slope,
    act,
    far_sum,
    far_out,
    far_in,
    state,
    row_out,
    row_in,
    picked,
    stats,
    back_out,
    back_in,
    raw_sem,
    early_sem,
    kept_sem,
    ring_send,
    ring_recv,
    core_send,
    core_recv,
    across_send,
    across_recv,
    pair_send,
    pair_recv,
    fan_send,
    fan_recv,
):
    spot = Spot(n)
    core = spot.core
    rows_a = attn_sh.shape[2]
    rows_f = ffn_sh.shape[2]
    half_f = rows_f // 2
    part_f = half_f // 2
    steps = n // 2
    count, width = first_ref.shape
    share_e = table_ref.shape[0]
    words = table_ref.shape[1]
    slots = places_row.shape[1]
    slot_count = places_ref.shape[1]

    def rows_at(shard, rows):
        return pl.ds(pl.multiple_of(shard * rows, 16), rows)

    def remote(source, target, send, recv, device):
        return pltpu.make_async_remote_copy(
            src_ref=source,
            dst_ref=target,
            send_sem=send,
            recv_sem=recv,
            device_id=device,
            device_id_type=MESH,
        )

    def slot_f(way, step):
        if step == 0:
            return 0, 0
        return (0, 1) if step == steps else (step, way)

    def chunk_f(piece, way, part, step, side):
        group, half = slot_f(way, step)
        return wf.at[piece // 2, group, side, pl.ds(half * half_f + part * part_f, part_f), :]

    def chunk_a(piece, shard, part, side, edge):
        cut = cut_of(width, 3)
        if edge is None:
            columns = ring_columns(spot.row, width, cut)
        else:
            columns = edge_columns(edge, width, cut)
        return wa.at[piece // 2, 2 * side + part, rows_at(shard, rows_a), columns]

    def sign(way):
        return -1 if way == 0 else 1

    def ring_copy(piece, way, part, step, arriving):
        if piece % 2 == 0:
            target = chunk_a(piece, spot.shard(sign(way) * (step - 1 + arriving)), part, core, None)
            source = target
        else:
            target = chunk_f(piece, way, part, step, core)
            source = target if arriving else chunk_f(piece, way, part, step - 1, core)
        return remote(
            source,
            target,
            ring_send.at[piece, way, part, step - 1],
            ring_recv.at[piece, way, part, step - 1],
            spot.ring[way],
        )

    def core_copy(piece, way, part, step, side, edge):
        if piece % 2 == 0:
            target = chunk_a(piece, spot.shard(sign(way) * step), part, side, edge)
        else:
            target = chunk_f(piece, way, part, step, side)
        lane = 0 if edge is None else 1
        return remote(
            target,
            target,
            core_send.at[lane, piece, way, part, step - 1],
            core_recv.at[lane, piece, way, part, step - 1],
            spot.partner,
        )

    def across_copy(piece, way, part, step, row):
        target = chunk_a(piece, spot.shard(sign(way) * step), part, core, row)
        return remote(
            target,
            target,
            across_send.at[piece, way, part, step - 1],
            across_recv.at[piece, way, part, step - 1],
            spot.across,
        )

    def half_at(half):
        return pl.ds(half * (count // 2), count // 2)

    def pair_copy(which, depth, half):
        rows = half_at(half)
        if which == 0:
            source, target = mid_ref.at[depth, 0, rows, :], mid_ref.at[depth, 1, rows, :]
        else:
            source, target = far_out.at[depth, rows, :], far_in.at[depth, rows, :]
        return remote(
            source,
            target,
            pair_send.at[which, depth, half],
            pair_recv.at[which, depth, half],
            spot.across,
        )

    def peer(offset):
        return (spot.mp + offset + n) % n

    def fan_copy(which, offset, source, target):
        return remote(
            source,
            target,
            fan_send.at[which, offset - 1],
            fan_recv.at[which, offset - 1],
            (spot.dp, peer(offset)),
        )

    def share(which, buffer, offset):
        return fan_copy(which, offset, buffer.at[spot.mp], buffer.at[spot.mp])

    def arrived(which, buffer, offset):
        return fan_copy(which, offset, buffer.at[peer(-offset)], buffer.at[peer(-offset)])

    def deal(which, source, target, offset):
        return fan_copy(which, offset, source.at[peer(offset)], target.at[spot.mp])

    def raw_copy(piece):
        kind, depth = piece % 2, piece // 2
        if kind == 0:
            return pltpu.make_async_copy(attn_sh.at[depth], raw_a.at[depth], raw_sem.at[piece])
        rows = pl.ds(pl.multiple_of(spot.row * half_f, 16), half_f)
        return pltpu.make_async_copy(ffn_sh.at[depth, :, rows, :], raw_f.at[depth], raw_sem.at[piece])

    def take_own(piece):
        kind, depth = piece % 2, piece // 2
        raw_copy(piece).wait()
        if kind == 0:
            for which in range(4):
                wa[depth, which, rows_at(spot.mp, rows_a), :] = raw_a[depth, which].astype(
                    jnp.bfloat16
                )
        else:
            for which in range(2):
                wf[depth, 0, which, 0:half_f, :] = raw_f[depth, which].astype(jnp.bfloat16)

    def launch(piece):
        for way, part in WAYS:
            ring_copy(piece, way, part, 1, 0).start()

    def chains(step):
        return [(way, part) for way, part in WAYS if step <= last_step(n, way, part)]

    def pass_on(piece, step):
        for way, part in chains(step):
            ring_copy(piece, way, part, step, 1).wait_recv()
            if step < last_step(n, way, part):
                ring_copy(piece, way, part, step + 1, 0).start()
            if piece % 2 == 0:
                across_copy(piece, way, part, step, spot.row).start()
            core_copy(piece, way, part, step, core, None).start()

    def pass_edge(piece, step):
        for way, part in chains(step):
            across_copy(piece, way, part, step, 1 - spot.row).wait_recv()
            core_copy(piece, way, part, step, core, 1 - spot.row).start()

    def settle(piece, step):
        for way, part in chains(step):
            core_copy(piece, way, part, step, 1 - core, None).wait_recv()
            if piece % 2 == 0:
                core_copy(piece, way, part, step, 1 - core, 1 - spot.row).wait_recv()

    out_copies = []

    def write_out(source, target):
        copy = pltpu.make_async_copy(source, target, early_sem.at[len(out_copies)])
        copy.start()
        out_copies.append(copy)

    def look_up(offset):
        whose = peer(offset)
        tokens = ids_ref[pl.ds(whose, 1), :]

        def block(index, total):
            start = pl.multiple_of(index * 256, 256)
            word = lax.broadcasted_iota(jnp.int32, (256, 1), 0) + start
            chosen = (word == tokens).astype(jnp.bfloat16)
            return total + dot_nn(
                table_ref[:, pl.ds(start, 256)].astype(jnp.bfloat16), chosen
            )

        found = lax.fori_loop(
            0, words // 256, block, jnp.zeros((share_e, count), jnp.float32)
        )
        row_out[whose] = found.astype(jnp.bfloat16)
        if offset > 0:
            deal(0, row_out, row_in, offset).start()

    for piece in range(2 * LAYERS):
        raw_copy(piece).start()
    greet([spot.partner, spot.across] + [(spot.dp, peer(offset)) for offset in range(1, n)])
    take_own(0)
    launch(0)
    for depth in range(LAYERS):
        for index in range(n):
            offset = (0, steps)[index] if index < 2 else (index // 2) * (2 * (index % 2) - 1)
            start = pl.multiple_of(spot.shard(offset) * rows_f, 128)
            grown = jnp.minimum(ramp_ref[depth : depth + 1, pl.ds(start, rows_f)], RAMP)
            grown = grown.astype(jnp.float32) / RAMP
            lanes_to = pl.ds((index % 2) * half_f, half_f)
            mask_ref[depth, index // 2 : index // 2 + 1, lanes_to] = jnp.where(
                spot.row == 0, grown[:, 0:half_f], grown[:, half_f:rows_f]
            )
    places_row[...] = jnp.full_like(places_row, -1)
    places_row[0:1, 0:slot_count] = places_ref[...]
    labels_row[...] = jnp.full_like(labels_row, -1)
    for whose in range(n):
        labels_row[0:1, whose * slots : whose * slots + slot_count] = targets_ref[
            whose : whose + 1, :
        ]
    spans = lengths_ref[...].astype(jnp.float32)
    lane = lax.broadcasted_iota(jnp.int32, (1, n), 1)
    length = jnp.sum(jnp.where(lane == spot.mp, spans, 0.0), axis=1, keepdims=True)
    visible = lax.broadcasted_iota(jnp.int32, (1, count), 1).astype(jnp.float32) < length
    counted = jnp.maximum(jnp.floor(spans * (slot_count / count)), 1.0)
    lane = lax.broadcasted_iota(jnp.int32, (1, n * slots), 1)
    limit = jnp.zeros((1, n * slots), jnp.float32)
    for whose in range(n):
        limit = jnp.where(
            lane >= whose * slots, counted[:, whose : whose + 1] + whose * slots, limit
        )
    valid = lane.astype(jnp.float32) < limit
    loss_ref[1:2, :] = valid.astype(jnp.float32)
    for offset in range(1, 4):
        look_up(offset)
    pass_on(0, 1)
    for offset in range(4, 7):
        look_up(offset)
    pass_on(0, 2)
    pass_edge(0, 1)
    take_own(1)
    launch(1)
    look_up(7)
    look_up(0)
    row_in[spot.mp] = row_out[spot.mp]
    pass_on(0, 3)
    pass_edge(0, 2)
    for offset in range(1, n):
        arrived(0, row_in, offset).wait_recv()
    first_ref[...] = where_ref[...] + row_in[...].reshape(width, count).astype(jnp.float32).T
    write_out(first_ref, first_out)
    normed, _ = normed_of(first_ref[...])
    state[...] = normed * gains_ref[0, 0:1, :] + gains_ref[0, 1:2, :]
    take_own(2)
    take_own(3)
    pass_on(0, 4)
    pass_edge(0, 3)

    lanes = lax.broadcasted_iota(jnp.int32, (1, 128), 1) < 64

    def head_pair(depth, pair):
        columns = pl.ds(pl.multiple_of(pair * 128, 128), 128)
        query = proj_ref[depth, 0, :, columns]
        keyed = proj_ref[depth, 1, :, columns]
        valued = proj_ref[depth, 2, :, columns]
        outs = []
        for side in range(2):
            mine = lanes if side == 0 else jnp.logical_not(lanes)
            scores = dot_nt(jnp.where(mine, query, jnp.zeros_like(query)), keyed) * 0.125
            scores = jnp.where(visible, scores, masked_score)
            expo = jnp.exp(scores - jnp.max(scores, axis=-1, keepdims=True))
            total = jnp.sum(expo, axis=-1, keepdims=True)
            outs.append(dot_nn((expo / total).astype(jnp.bfloat16), valued))
        mixed_ref[depth, :, columns] = jnp.where(lanes, outs[0], outs[1]).astype(jnp.bfloat16)

    def kept_copies(turn, depth, group, far, start, size):
        slot = turn % SLOTS
        here, there = pl.ds(0, size), pl.ds(start, size)
        return (
            pltpu.make_async_copy(
                slope.at[slot, here, :],
                slope_ref.at[depth, group, far, there, :],
                kept_sem.at[0, slot],
            ),
            pltpu.make_async_copy(
                act.at[slot, here, :],
                act_ref.at[depth, group, far, there, :],
                kept_sem.at[1, slot],
            ),
        )

    turns = []

    def ffn_block(depth, group, far, start, size):
        turn = len(turns)
        turns.append((depth, group, far, start, size))
        if turn >= SLOTS:
            for copy in kept_copies(turn, *turns[turn - SLOTS]):
                copy.wait()
        slot, rows, here = turn % SLOTS, pl.ds(start, size), pl.ds(0, size)
        hidden = dot_nt(mid_ref[depth, far, rows, :], wf[depth, group, 0])
        spread = 0.5 * (1.0 + lax.erf(hidden * (0.5**0.5)))
        mask = mask_ref[depth, group : group + 1, :]
        bell = jnp.exp(hidden * hidden * -0.5) * (1.0 / math.sqrt(2.0 * math.pi))
        slope[slot, here, :] = (spread + hidden * bell) * mask
        active = (hidden * spread * mask).astype(jnp.bfloat16)
        act[slot, here, :] = active
        for copy in kept_copies(*((turn,) + turns[turn])):
            copy.start()
        if far:
            far_sum[rows, :] += dot_nn(active, wf[depth, group, 1])
        else:
            pre_ref[depth, 1, rows, :] += dot_nn(active, wf[depth, group, 1])

    def ffn_own(depth, group):
        ffn_block(depth, group, 0, 0, count)

    def ffn_far(depth, group, half):
        ffn_block(depth, group, 1, half * (count // 2), count // 2)

    for depth in range(LAYERS):
        piece_a, piece_f = 2 * depth, 2 * depth + 1
        more = depth + 1 < LAYERS
        if depth > 0:
            pass_on(piece_a, 3)
            pass_edge(piece_a, 2)
            launch(piece_f)
            pass_on(piece_a, 4)
            pass_edge(piece_a, 3)
        pass_edge(piece_a, 4)
        for step in range(1, steps + 1):
            settle(piece_a, step)
        write_out(wa.at[depth], attn_full.at[depth])
        inputs = state[...].astype(jnp.bfloat16)
        inputs_ref[depth] = inputs
        for which in range(3):
            proj_ref[depth, which] = dot_nn(inputs, wa[depth, which]).astype(jnp.bfloat16)
        pass_on(piece_f, 1)

        @pl.loop(0, HEADS // 2)
        def _(pair):
            head_pair(depth, pair)

        pre_ref[depth, 0] = state[...] + dot_nn(mixed_ref[depth], wa[depth, 3])
        normed, _ = normed_of(pre_ref[depth, 0])
        middle = (
            normed * gains_ref[1 + 2 * depth, 0:1, :] + gains_ref[1 + 2 * depth, 1:2, :]
        )
        for half in range(2):
            mid_ref[depth, 0, half_at(half), :] = middle[
                half * (count // 2) : (half + 1) * (count // 2), :
            ].astype(jnp.bfloat16)
            pair_copy(0, depth, half).start()
        pre_ref[depth, 1] = middle
        far_sum[...] = jnp.zeros_like(far_sum)
        write_out(inputs_ref.at[depth], inputs_out.at[depth])
        write_out(proj_ref.at[depth], proj_out.at[depth])
        write_out(mixed_ref.at[depth], mixed_out.at[depth])
        pass_on(piece_f, 2)
        settle(piece_f, 1)
        ffn_own(depth, 1)
        pass_on(piece_f, 3)
        if more:
            launch(piece_a + 2)
        settle(piece_f, 2)
        ffn_own(depth, 2)
        for half in range(2):
            pair_copy(0, depth, half).wait_recv()
            ffn_far(depth, 1, half)
            ffn_far(depth, 2, half)
        write_out(mid_ref.at[depth], mid_out.at[depth])
        pass_on(piece_f, 4)
        settle(piece_f, 3)
        settle(piece_f, 4)
        for half in range(2):
            ffn_far(depth, 3, half)
            ffn_far(depth, 0, half)
            far_out[depth, half_at(half), :] = far_sum[half_at(half), :].astype(jnp.bfloat16)
            pair_copy(1, depth, half).start()
        if more:
            pass_on(piece_a + 2, 1)
        ffn_own(depth, 3)
        ffn_own(depth, 0)
        write_out(wf.at[depth], ffn_full.at[depth])
        if more:
            pass_on(piece_a + 2, 2)
            pass_edge(piece_a + 2, 1)
        for half in range(2):
            pair_copy(1, depth, half).wait_recv()
        pre_ref[depth, 1] += far_in[depth].astype(jnp.float32)
        write_out(pre_ref.at[depth], pre_out.at[depth])
        normed, _ = normed_of(pre_ref[depth, 1])
        state[...] = normed * gains_ref[2 + 2 * depth, 0:1, :] + gains_ref[2 + 2 * depth, 1:2, :]

    spots = (
        lax.broadcasted_iota(jnp.int32, (count, 1), 0) == places_row[...]
    ).astype(jnp.bfloat16)
    picked[spot.mp] = dot_tn(spots, state[...].astype(jnp.bfloat16)).astype(jnp.bfloat16)
    for offset in range(1, n):
        share(1, picked, offset).start()
    out_b = out_ref[...].astype(jnp.bfloat16)
    rows_v = out_ref.shape[0]
    hits = (
        labels_row[...] == spot.mp * rows_v + lax.broadcasted_iota(jnp.int32, (rows_v, 1), 0)
    ).astype(jnp.float32)
    for offset in range(1, n):
        arrived(1, picked, offset).wait_recv()
    picked_all = picked[...].reshape(n * slots, -1)
    logits = dot_nt(out_b, picked_all)
    peak = jnp.max(logits, axis=0, keepdims=True)
    expsum = jnp.sum(jnp.exp(logits - peak), axis=0, keepdims=True)
    stats[spot.mp, 0:1, :] = peak
    stats[spot.mp, 1:2, :] = expsum
    stats[spot.mp, 2:3, :] = jnp.sum(hits * logits, axis=0, keepdims=True)
    for offset in range(1, n):
        share(2, stats, offset).start()
    for offset in range(1, n):
        arrived(2, stats, offset).wait_recv()
    peak = stats[0, 0:1, :]
    for whose in range(1, n):
        peak = jnp.maximum(peak, stats[whose, 0:1, :])
    expsum = stats[0, 1:2, :] * jnp.exp(stats[0, 0:1, :] - peak)
    target = stats[0, 2:3, :]
    for whose in range(1, n):
        expsum = expsum + stats[whose, 1:2, :] * jnp.exp(stats[whose, 0:1, :] - peak)
        target = target + stats[whose, 2:3, :]
    log_total = peak + jnp.log(expsum)
    loss_ref[0:1, :] = jnp.where(valid, log_total - target, 0.0)
    grad_logits = jnp.where(valid, jnp.exp(logits - log_total) - hits, 0.0).astype(jnp.bfloat16)
    picked_grad = dot_tn(grad_logits, out_b).astype(jnp.bfloat16)
    for whose in range(n):
        back_out[whose] = picked_grad[whose * slots : (whose + 1) * slots, :]
    for offset in range(1, n):
        deal(3, back_out, back_in, offset).start()
    back_in[spot.mp] = back_out[spot.mp]
    out_grad_ref[...] = dot_nn(grad_logits, picked_all)
    for offset in range(1, n):
        arrived(3, back_in, offset).wait_recv()
    summed = back_in[0].astype(jnp.float32)
    for whose in range(1, n):
        summed = summed + back_in[whose].astype(jnp.float32)
    high = summed.astype(jnp.bfloat16)
    low = (summed - high.astype(jnp.float32)).astype(jnp.bfloat16)
    grad_ref[...] = dot_nn(spots, high) + dot_nn(spots, low)

    for piece in range(2 * LAYERS):
        for way, part in WAYS:
            for step in range(1, last_step(n, way, part) + 1):
                ring_copy(piece, way, part, step, 0).wait_send()
                core_copy(piece, way, part, step, core, None).wait_send()
                if piece % 2 == 0:
                    across_copy(piece, way, part, step, spot.row).wait_send()
                    core_copy(piece, way, part, step, core, 1 - spot.row).wait_send()
    for offset in range(1, n):
        deal(0, row_out, row_in, offset).wait_send()
        share(1, picked, offset).wait_send()
        share(2, stats, offset).wait_send()
        deal(3, back_out, back_in, offset).wait_send()
    for depth in range(LAYERS):
        for half in range(2):
            pair_copy(0, depth, half).wait_send()
            pair_copy(1, depth, half).wait_send()
    for turn in range(len(turns) - SLOTS, len(turns)):
        for copy in kept_copies(turn, *turns[turn]):
            copy.wait()
    for copy in out_copies:
        copy.wait()


def forward_call(
    n, ids, lengths, places, targets, ramp, gains, table, where, out_table, attn, ffn
):
    count, width = where.shape
    rows_f = ffn.shape[2]
    slots = 32 * -(-places.shape[1] // 32)
    groups = n // 2
    f32, bf16 = jnp.float32, jnp.bfloat16
    vmem = pl.BlockSpec(memory_space=pltpu.VMEM)
    anywhere = pl.BlockSpec(memory_space=pl.ANY)
    shape = jax.ShapeDtypeStruct
    dma = pltpu.SemaphoreType.DMA
    sems = dma((2 * LAYERS, 2, 2, n // 2))
    core_sems = dma((2, 2 * LAYERS, 2, 2, n // 2))
    return pl.pallas_call(
        functools.partial(forward_kernel, n),
        out_shape=(
            shape((LAYERS, 4, width, width), bf16),
            shape((LAYERS, groups, 2, rows_f, width), bf16),
            shape((count, width), f32),
            shape((LAYERS, count, width), bf16),
            shape((LAYERS, 3, count, width), bf16),
            shape((LAYERS, count, width), bf16),
            shape((LAYERS, 2, count, width), f32),
            shape((LAYERS, 2, count, width), bf16),
            shape((LAYERS, groups, 2, count, rows_f), f32),
            shape((LAYERS, groups, 2, count, rows_f), bf16),
            shape((count, width), f32),
            shape(out_table.shape, f32),
            shape((2, n * slots), f32),
        ),
        in_specs=[vmem] * 9 + [anywhere] * 2,
        out_specs=(anywhere,) * 10 + (vmem,) * 3,
        scratch_shapes=[
            pltpu.VMEM((count, width), f32),
            pltpu.VMEM((LAYERS, count, width), bf16),
            pltpu.VMEM((LAYERS, 3, count, width), bf16),
            pltpu.VMEM((LAYERS, count, width), bf16),
            pltpu.VMEM((LAYERS, 2, count, width), f32),
            pltpu.VMEM((LAYERS, 2, count, width), bf16),
            pltpu.VMEM((LAYERS, groups, rows_f), f32),
            pltpu.VMEM((1, slots), jnp.int32),
            pltpu.VMEM((1, n * slots), jnp.int32),
            pltpu.VMEM((LAYERS, 4, width, width), bf16),
            pltpu.VMEM((LAYERS, groups, 2, rows_f, width), bf16),
            pltpu.VMEM(attn.shape, f32),
            pltpu.VMEM((LAYERS, 2, rows_f // 2, width), f32),
            pltpu.VMEM((SLOTS, count, rows_f), f32),
            pltpu.VMEM((SLOTS, count, rows_f), bf16),
            pltpu.VMEM((count, width), f32),
            pltpu.VMEM((LAYERS, count, width), bf16),
            pltpu.VMEM((LAYERS, count, width), bf16),
            pltpu.VMEM((count, width), f32),
            pltpu.VMEM((n, table.shape[0], count), bf16),
            pltpu.VMEM((n, table.shape[0], count), bf16),
            pltpu.VMEM((n, slots, width), bf16),
            pltpu.VMEM((n, 8, n * slots), f32),
            pltpu.VMEM((n, slots, width), bf16),
            pltpu.VMEM((n, slots, width), bf16),
            dma((2 * LAYERS,)),
            dma((1 + 7 * LAYERS,)),
            dma((2, SLOTS)),
            sems,
            sems,
            core_sems,
            core_sems,
            sems,
            sems,
            dma((2, LAYERS, 2)),
            dma((2, LAYERS, 2)),
            dma((4, n - 1)),
            dma((4, n - 1)),
        ],
        compiler_params=pltpu.CompilerParams(
            collective_id=1, has_side_effects=True, vmem_limit_bytes=VMEM_LIMIT
        ),
        name="forward_layers",
    )(ids, lengths, places, targets, ramp, gains, table, where, out_table, attn, ffn)


def norm_back(grad, values, gain):
    normed, inverse = normed_of(values)
    scaled = grad * gain
    centred = scaled - jnp.mean(scaled, axis=-1, keepdims=True)
    result = inverse * (centred - normed * jnp.mean(scaled * normed, axis=-1, keepdims=True))
    return (
        result,
        jnp.sum(grad * normed, axis=0, keepdims=True),
        jnp.sum(grad, axis=0, keepdims=True),
    )


def backward_kernel(
    n,
    ids_ref,
    lengths_ref,
    losses_ref,
    gains_ref,
    out_grad_ref,
    inputs_ref,
    mixed_ref,
    mid_all,
    grad_ref,
    first_ref,
    proj_all,
    pre_all,
    attn_full,
    ffn_full,
    slope_all,
    act_all,
    attn_sum,
    ffn_sum,
    table_sum,
    out_sum,
    small_out,
    square_out,
    proj,
    pre,
    wa,
    wf,
    slope,
    sum_a,
    sum_f,
    theirs_f,
    land_f,
    land_a,
    ring_a,
    ring_f,
    edge_a,
    go_far,
    far_sum,
    far_out,
    far_in,
    state,
    grad_rows,
    left_a,
    left_f,
    right_f,
    spread_a,
    spread_f,
    done_a,
    done_f,
    wa_sem,
    load_sem,
    slope_sem,
    mid_sem,
    core_send,
    core_recv,
    core_free,
    swap_send,
    swap_recv,
    swap_free,
    ring_send,
    ring_recv,
    ring_free,
    give_send,
    give_recv,
    pair_send,
    pair_recv,
    across_send,
    across_recv,
    out_sem,
    last_send,
    last_recv,
    small,
    small_in,
    columns_out,
    columns_in,
    table_grad,
    table_half,
    out_half,
    out_done,
    squares,
    square_parts,
    proj_sem,
    small_send,
    small_recv,
    deal_send,
    deal_recv,
    half_send,
    half_recv,
    half_sem,
    norm_send,
    norm_recv,
):
    spot = Spot(n)
    core = spot.core
    other = 1 - core
    rows_a = attn_sum.shape[2]
    rows_f = ffn_sum.shape[2]
    half_f = rows_f // 2
    part_f = half_f // 2
    count = state.shape[0]
    width = attn_sum.shape[3]
    groups = n // 2
    order = (0,) + tuple(range(groups - 1, 0, -1))
    total = LAYERS * groups

    def rows_at(shard, rows):
        return pl.ds(pl.multiple_of(shard * rows, 16), rows)

    def peer(offset):
        return (spot.mp + offset + n) % n

    def remote(source, target, send, recv, device):
        return pltpu.make_async_remote_copy(
            src_ref=source,
            dst_ref=target,
            send_sem=send,
            recv_sem=recv,
            device_id=device,
            device_id_type=MESH,
        )

    def turn_of(turn):
        return LAYERS - 1 - turn // groups, order[turn % groups]

    def load_weights(depth, group):
        return pltpu.make_async_copy(
            ffn_full.at[depth, group], wf.at[group], load_sem.at[0, group]
        )

    def load_act(depth):
        return [
            pltpu.make_async_copy(
                act_all.at[depth, group, far],
                left_f.at[group, 1, pl.ds(far * count, count), :],
                load_sem.at[1 + far, group],
            )
            for group in range(groups)
            for far in range(2)
        ] + [
            pltpu.make_async_copy(
                mid_all.at[depth, far],
                right_f.at[0, pl.ds(far * count, count), :],
                mid_sem.at[far],
            )
            for far in range(2)
        ]

    def load_slope(index):
        depth = LAYERS - 1 - index // (2 * groups)
        far = (index // groups) % 2
        return pltpu.make_async_copy(
            slope_all.at[depth, order[index % groups], far],
            slope.at[index % (groups + 1)],
            slope_sem.at[index % (groups + 1)],
        )

    def load_pre(depth):
        return pltpu.make_async_copy(pre_all.at[depth], pre, proj_sem.at[0])

    def load_proj(depth):
        return pltpu.make_async_copy(proj_all.at[depth], proj, proj_sem.at[1])

    def load_attn(depth):
        return pltpu.make_async_copy(attn_full.at[depth], wa, wa_sem.at[0])

    def core_copy(turn):
        slot = turn % SLOTS
        return remote(
            theirs_f.at[slot],
            land_f.at[slot],
            core_send.at[turn],
            core_recv.at[turn],
            spot.partner,
        )

    def fold(turn):
        depth, group = turn_of(turn)
        core_copy(turn).wait_recv()
        sum_f[depth, group] = (
            sum_f[depth, group].astype(jnp.float32)
            + land_f[turn % SLOTS].astype(jnp.float32)
        ).astype(jnp.bfloat16)
        if turn + SLOTS < total:
            pl.semaphore_signal(
                core_free.at[0], inc=1, device_id=spot.partner, device_id_type=MESH
            )

    def swap_copy(depth, part):
        return remote(
            wa.at[part],
            land_a.at[part],
            swap_send.at[depth, part],
            swap_recv.at[depth, part],
            spot.partner,
        )

    def cut_at(piece):
        return cut_of(width, 6) if piece > 0 else 0

    def summed(piece, offset, part):
        kind, depth = piece % 2, piece // 2
        if kind == 0:
            columns = ring_columns(spot.row, width, cut_at(piece))
            return sum_a.at[depth, part, rows_at(spot.shard(offset), rows_a), columns]
        far = abs(offset)
        group, half = (far, int(offset > 0)) if 0 < far < groups else (0, int(far > 0))
        return sum_f.at[depth, group, pl.ds(half * half_f + part * part_f, part_f), :]

    def landed(piece, way, part, step):
        if piece % 2 == 0:
            return ring_a.at[way, part, step - 1, :, pl.ds(0, width - cut_at(piece))]
        return ring_f.at[way, part, step - 1]

    def give_copy(piece, index):
        depth = piece // 2
        give = edge_columns(1 - spot.row, width, cut_at(piece))
        return remote(
            sum_a.at[depth, index, :, give],
            edge_a.at[depth, index],
            give_send.at[depth, index],
            give_recv.at[depth, index],
            spot.across,
        )

    def absorb_rows(into, source):
        into[...] = (into[...].astype(jnp.float32) + source[...].astype(jnp.float32)).astype(
            jnp.bfloat16
        )

    def absorb(piece, index):
        depth = piece // 2
        take = edge_columns(spot.row, width, cut_at(piece))
        give_copy(piece, index).wait_recv()

        @pl.loop(0, n)
        def _(block):
            rows = rows_at(block, rows_a)
            absorb_rows(sum_a.at[depth, index, rows, take], edge_a.at[depth, index, rows, :])

    def pair_copy(which, depth, half):
        rows = pl.ds(half * (count // 2), count // 2)
        if which == 0:
            source, target = right_f.at[1, rows, :], go_far.at[depth, rows, :]
        else:
            source, target = far_out.at[depth, rows, :], far_in.at[depth, rows, :]
        return remote(
            source,
            target,
            pair_send.at[which, depth, half],
            pair_recv.at[which, depth, half],
            spot.across,
        )

    def ring_copy(piece, way, part, step):
        offset = last_step(n, way, part) - step + 1
        return remote(
            summed(piece, offset if way == 0 else -offset, part),
            landed(piece, way, part, step),
            ring_send.at[piece, way, part, step - 1],
            ring_recv.at[piece, way, part, step - 1],
            spot.ring[way],
        )

    def ring_start(piece, way, part, step):
        if piece // 2 < LAYERS - 1:
            pl.semaphore_wait(ring_free.at[piece % 2, way, part, step - 1], 1)
        ring_copy(piece, way, part, step).start()

    def release(piece, way, part, step):
        if piece // 2 > 0:
            pl.semaphore_signal(
                ring_free.at[piece % 2, way, part, step - 1],
                inc=1,
                device_id=spot.ring[1 - way],
                device_id_type=MESH,
            )

    def launch(piece, long):
        for way, part in WAYS:
            if (way == part) == long:
                ring_start(piece, way, part, 1)

    def launch_part(piece, part):
        for way in (part, 1 - part):
            ring_start(piece, way, part, 1)

    def relay(piece, step):
        for way, part in WAYS:
            last = last_step(n, way, part)
            if step < last:
                ring_copy(piece, way, part, step).wait_recv()
                offset = last - step if way == 0 else step - last
                absorb_rows(summed(piece, offset, part), landed(piece, way, part, step))
                ring_start(piece, way, part, step + 1)
                release(piece, way, part, step)

    def across_copy(piece):
        depth = piece // 2
        if piece % 2 == 0:
            columns = pl.ds(0, width - cut_at(piece))
            source, target = [spread_a.at[depth, side, :, :, columns] for side in range(2)]
        else:
            source, target = spread_f.at[depth, 0], spread_f.at[depth, 1]
        return remote(
            source,
            target,
            across_send.at[piece],
            across_recv.at[piece],
            spot.across,
        )

    def finish(piece):
        kind, depth = piece % 2, piece // 2
        for part in range(2):
            value = summed(piece, 0, part)[...].astype(jnp.float32)
            for way in range(2):
                step = last_step(n, way, part)
                ring_copy(piece, way, part, step).wait_recv()
                value = value + landed(piece, way, part, step)[...].astype(jnp.float32)
                release(piece, way, part, step)
            value = value.astype(jnp.bfloat16)
            if kind == 0:
                spread_a[depth, 0, part, :, 0 : width - cut_at(piece)] = value
            else:
                spread_f[depth, 0, pl.ds(part * part_f, part_f), :] = value
        across_copy(piece).start()

    def out_copies(piece):
        kind, depth = piece % 2, piece // 2
        if kind == 0:
            source, target = done_a, attn_sum.at[depth, pl.ds(2 * core, 2)]
        else:
            source, target = done_f, ffn_sum.at[depth, core]
        return (
            pltpu.make_async_copy(source, target, out_sem.at[piece]),
            remote(source, target, last_send.at[piece], last_recv.at[piece], spot.partner),
        )

    def conclude(piece):
        kind, depth = piece % 2, piece // 2
        across_copy(piece).wait_recv()
        if depth < LAYERS - 1:
            local, away = out_copies(piece + 2)
            local.wait()
            away.wait_send()
        row = spot.row
        if kind == 1:
            for side in range(2):
                whose = row + side - 2 * row * side
                rows = pl.ds(pl.multiple_of(whose * half_f, 16), half_f)
                done_f[rows, :] = spread_f[depth, side].astype(jnp.float32)
            add_squares(done_f[...])
        else:
            cut = cut_at(piece)
            single = width - 2 * cut

            def lanes_at(start, size):
                return pl.ds(pl.multiple_of(start, 128), size)

            for part in range(2):
                own, far = spread_a.at[depth, 0, part], spread_a.at[depth, 1, part]
                done = done_a.at[part]
                if cut == 0:
                    done[...] = own[...].astype(jnp.float32) + far[...].astype(jnp.float32)
                    add_squares(done[...])
                    continue
                done[:, lanes_at(row * (width - cut), cut)] = own[
                    :, lanes_at(row * single, cut)
                ].astype(jnp.float32)
                done[:, lanes_at((1 - row) * (width - cut), cut)] = far[
                    :, lanes_at((1 - row) * single, cut)
                ].astype(jnp.float32)
                done[:, cut : width - cut] = own[:, lanes_at((1 - row) * cut, single)].astype(
                    jnp.float32
                ) + far[:, lanes_at(row * cut, single)].astype(jnp.float32)
                add_squares(done[...])
        for copy in out_copies(piece):
            copy.start()

    load_grad = pltpu.make_async_copy(grad_ref, state, proj_sem.at[2])
    load_grad.start()
    load_first = pltpu.make_async_copy(first_ref, pre.at[0], proj_sem.at[3])
    load_pre(LAYERS - 1).start()
    for group in order:
        load_weights(LAYERS - 1, group).start()
    for index in range(groups + 1):
        load_slope(index).start()
    for copy in load_act(LAYERS - 1):
        copy.start()
    load_attn(LAYERS - 1).start()
    load_proj(LAYERS - 1).start()
    greet([spot.partner, spot.across] + [(spot.dp, peer(offset)) for offset in range(1, n)])
    load_grad.wait()
    lanes = lax.broadcasted_iota(jnp.int32, (1, 128), 1) < 64
    spans = lengths_ref[...].astype(jnp.float32)
    lane = lax.broadcasted_iota(jnp.int32, (1, n), 1)
    length = jnp.sum(jnp.where(lane == spot.mp, spans, 0.0), axis=1, keepdims=True)
    visible = lax.broadcasted_iota(jnp.int32, (1, count), 1).astype(jnp.float32) < length

    def hidden_own(index):
        depth = LAYERS - 1 - index // (2 * groups)
        group = order[index % groups]
        load_slope(index).wait()
        load_weights(depth, group).wait()
        rows = pl.ds(0, count)
        grad_active = dot_nt(right_f[1, rows, :], wf[group, 1])
        grad_hidden = (grad_active * slope[index % (groups + 1)]).astype(jnp.bfloat16)
        left_f[group, 0, rows, :] = grad_hidden
        state[...] += dot_nn(grad_hidden, wf[group, 0])
        if index + groups + 1 < 2 * total:
            load_slope(index + groups + 1).start()

    def hidden_far(index, half):
        depth = LAYERS - 1 - index // (2 * groups)
        group = order[index % groups]
        if half == 0:
            load_slope(index).wait()
        rows = pl.ds(half * (count // 2), count // 2)
        here = pl.ds(count + half * (count // 2), count // 2)
        grad_active = dot_nt(right_f[1, here, :], wf[group, 1])
        grad_hidden = (grad_active * slope[index % (groups + 1), rows, :]).astype(jnp.bfloat16)
        left_f[group, 0, here, :] = grad_hidden
        far_sum[rows, :] += dot_nn(grad_hidden, wf[group, 0])
        if half == 1:
            if depth > 0:
                load_weights(depth - 1, group).start()
            if index + groups + 1 < 2 * total:
                load_slope(index + groups + 1).start()

    def ffn_turn(turn):
        depth, group = turn_of(turn)
        slot = turn % SLOTS
        sum_f[depth, group] = dot_tn(left_f[group, core], right_f[core]).astype(jnp.bfloat16)
        if turn >= SLOTS:
            core_copy(turn - SLOTS).wait_send()
        theirs_f[slot] = dot_tn(left_f[group, other], right_f[other]).astype(jnp.bfloat16)
        if turn >= SLOTS:
            pl.semaphore_wait(core_free.at[0], 1)
        core_copy(turn).start()

    def head_pair(depth, pair):
        columns = pl.ds(pl.multiple_of(pair * 128, 128), 128)
        query = proj[0, :, columns]
        keyed = proj[1, :, columns]
        valued = proj[2, :, columns]
        grad_mixed = grad_rows[4, :, columns]
        outs = []
        for side in range(2):
            mine = lanes if side == 0 else jnp.logical_not(lanes)
            scores = dot_nt(jnp.where(mine, query, jnp.zeros_like(query)), keyed) * 0.125
            scores = jnp.where(visible, scores, masked_score)
            expo = jnp.exp(scores - jnp.max(scores, axis=-1, keepdims=True))
            probs = expo / jnp.sum(expo, axis=-1, keepdims=True)
            grad_probs = dot_nt(jnp.where(mine, grad_mixed, jnp.zeros_like(query)), valued)
            inner = jnp.sum(grad_probs * probs, axis=-1, keepdims=True)
            grad_scores = (probs * (grad_probs - inner)).astype(jnp.bfloat16)
            outs.append(
                (
                    dot_nn(grad_scores, keyed) * 0.125,
                    dot_tn(grad_scores, query) * 0.125,
                    dot_tn(probs.astype(jnp.bfloat16), grad_mixed),
                )
            )
        for which in range(3):
            grad_rows[which, :, columns] = jnp.where(
                lanes, outs[0][which], outs[1][which]
            ).astype(jnp.bfloat16)

    def layer(depth, hooks):
        base = (LAYERS - 1 - depth) * groups
        piece_a, piece_f = 2 * depth, 2 * depth + 1
        load_pre(depth).wait()
        grad_two, small[0, 4 + 4 * depth : 5 + 4 * depth, :], small[0, 5 + 4 * depth : 6 + 4 * depth, :] = norm_back(
            state[...], pre[1], gains_ref[2 + 2 * depth, 0:1, :]
        )
        state[...] = grad_two
        for half in range(2):
            if depth < LAYERS - 1:
                pair_copy(0, depth + 1, half).wait_send()
            rows = pl.ds(half * (count // 2), count // 2)
            right_f[1, rows, :] = state[rows, :].astype(jnp.bfloat16)
            pair_copy(0, depth, half).start()
        far_sum[...] = jnp.zeros_like(far_sum)
        for step in range(groups):
            hidden_own(2 * base + step)
        hooks.get("own", lambda: None)()
        for half in range(2):
            rows = pl.ds(half * (count // 2), count // 2)
            here = pl.ds(count + half * (count // 2), count // 2)
            pair_copy(0, depth, half).wait_recv()
            right_f[1, here, :] = go_far[depth, rows, :]
            for step in range(groups):
                hidden_far(2 * base + groups + step, half)
            far_out[depth, rows, :] = far_sum[rows, :].astype(jnp.bfloat16)
            pair_copy(1, depth, half).start()
        hooks.get("far", lambda: None)()
        for copy in load_act(depth):
            copy.wait()
        for step in range(groups):
            ffn_turn(base + step)
            if step >= 1:
                fold(base + step - 1)
            if step == 1:
                launch(piece_f, True)
            if step == 2:
                launch(piece_f, False)
            hooks.get(("ffn", step), lambda: None)()
        fold(base + groups - 1)
        if depth > 0:
            for copy in load_act(depth - 1):
                copy.start()
        for half in range(2):
            pair_copy(1, depth, half).wait_recv()
        state[...] += far_in[depth].astype(jnp.float32)
        hooks.get("middle", lambda: None)()
        grad_one, small[0, 2 + 4 * depth : 3 + 4 * depth, :], small[0, 3 + 4 * depth : 4 + 4 * depth, :] = norm_back(
            state[...], pre[0], gains_ref[1 + 2 * depth, 0:1, :]
        )
        if depth > 0:
            load_pre(depth - 1).start()
        else:
            load_first.start()
        state[...] = grad_one
        grad_rows[3] = grad_one.astype(jnp.bfloat16)
        load_attn(depth).wait()
        load_proj(depth).wait()
        grad_rows[4] = dot_nt(grad_rows[3], wa[3]).astype(jnp.bfloat16)

        @pl.loop(0, HEADS // 2)
        def _(pair):
            head_pair(depth, pair)

        if depth > 0:
            load_proj(depth - 1).start()
        hooks.get("heads", lambda: None)()
        for which in range(3):
            state[...] += dot_nt(grad_rows[which], wa[which])
        left_a[0] = inputs_ref[depth]
        left_a[1] = mixed_ref[depth]
        for part in range(2):
            left = 0 if part == 0 else other
            wa[part] = dot_tn(left_a[left], grad_rows[2 * other + part]).astype(jnp.bfloat16)
            if depth < LAYERS - 1:
                pl.semaphore_wait(swap_free.at[part], 1)
            swap_copy(depth, part).start()
        for part in range(2):
            left = 0 if part == 0 else core
            sum_a[depth, part] = dot_tn(left_a[left], grad_rows[2 * core + part]).astype(
                jnp.bfloat16
            )
            swap_copy(depth, part).wait_recv()

            @pl.loop(0, n)
            def _(block):
                rows = rows_at(block, rows_a)
                absorb_rows(sum_a.at[depth, part, rows, :], land_a.at[part, rows, :])

            if depth > 0:
                give_copy(piece_a, part).start()
                pl.semaphore_signal(
                    swap_free.at[part], inc=1, device_id=spot.partner, device_id_type=MESH
                )
            else:
                launch_part(piece_a, part)
            hooks.get(("mats", part), lambda: None)()

    def launch_attn(piece):
        for part in range(2):
            absorb(piece, part)
            launch_part(piece, part)

    def reload_attn():
        for part in range(2):
            swap_copy(1, part).wait_send()
        load_attn(0).start()

    def half_copy(which, stage):
        buffer = out_half if which == 0 else table_half
        return remote(
            buffer.at[2 * stage],
            buffer.at[2 * stage + 1],
            half_send.at[which, stage],
            half_recv.at[which, stage],
            spot.partner if stage == 0 else spot.across,
        )

    def half_rows(rows, side):
        return pl.ds(pl.multiple_of(side * (rows // 2), 16), rows // 2)

    def half_start(which, source):
        buffer = out_half if which == 0 else table_half
        buffer[0] = source[half_rows(source.shape[0], other), :].astype(jnp.bfloat16)
        half_copy(which, 0).start()

    def half_fold(which, source):
        buffer = out_half if which == 0 else table_half
        half_copy(which, 0).wait_recv()
        own = source[half_rows(source.shape[0], core), :]
        buffer[2] = (own + buffer[1].astype(jnp.float32)).astype(jnp.bfloat16)
        half_copy(which, 1).start()

    def half_out(which):
        if which == 0:
            source, target = out_done, out_sum.at[half_rows(out_sum.shape[0], core), :]
        else:
            source = table_grad.at[half_rows(table_sum.shape[0], core), :]
            target = table_sum.at[half_rows(table_sum.shape[0], core), :]
        return (
            pltpu.make_async_copy(source, target, half_sem.at[which]),
            remote(source, target, half_send.at[which, 2], half_recv.at[which, 2], spot.partner),
        )

    def add_squares(value):
        squares[...] += jnp.sum(value * value, axis=0, keepdims=True)

    def half_end(which):
        buffer = out_half if which == 0 else table_half
        half_copy(which, 1).wait_recv()
        value = buffer[2].astype(jnp.float32) + buffer[3].astype(jnp.float32)
        if which == 0:
            out_done[...] = value
        else:
            table_grad[half_rows(table_sum.shape[0], core), :] = value
        width = squares.shape[1]
        for start in range(0, value.shape[1], width):
            add_squares(value[:, start : start + width])
        for copy in half_out(which):
            copy.start()

    def small_copy(stage):
        bit = 1 << max(0, stage - 2)
        pair = spot.mp + bit - 2 * bit * ((spot.mp // bit) % 2)
        device = (spot.partner, spot.across)[stage] if stage < 2 else (spot.dp, pair)
        return remote(
            small.at[stage],
            small_in.at[stage],
            small_send.at[stage],
            small_recv.at[stage],
            device,
        )

    def small_next(stage):
        small_copy(stage).wait_recv()
        small[stage + 1] = small[stage] + small_in[stage]
        if stage < 4:
            small_copy(stage + 1).start()

    def deal_copy(offset, arriving):
        source = columns_out.at[peer(offset)]
        target = columns_in.at[peer(-offset) if arriving else spot.mp]
        return remote(
            source,
            target,
            deal_send.at[offset - 1],
            deal_recv.at[offset - 1],
            (spot.dp, peer(offset)),
        )

    def table_blocks(first, last):
        @pl.loop(first, last)
        def _(block):
            row = lax.broadcasted_iota(jnp.int32, (256, 1), 0) + block * 256
            value = jnp.zeros((columns_in.shape[1], 256), jnp.float32)
            for whose in range(n):
                chosen = (row == ids_ref[whose : whose + 1, :]).astype(jnp.bfloat16)
                value = value + dot_nt(columns_in[whose], chosen)
            table_grad[:, pl.ds(pl.multiple_of(block * 256, 256), 256)] = value

    squares[...] = jnp.zeros_like(squares)
    half_start(0, out_grad_ref)
    layer(
        1,
        {
            "far": lambda: half_fold(0, out_grad_ref),
            "heads": lambda: relay(3, 1),
            ("mats", 1): lambda: relay(3, 2),
        },
    )
    layer(
        0,
        {
            "own": lambda: (reload_attn(), launch_attn(2), relay(3, 3)),
            "far": lambda: (relay(2, 1), finish(3)),
            ("ffn", 1): lambda: relay(2, 2),
            ("ffn", 3): lambda: (conclude(3), half_end(0)),
            "middle": lambda: (relay(2, 3), relay(1, 1)),
            "heads": lambda: (finish(2), relay(1, 2)),
        },
    )
    load_first.wait()
    grad_sum, small[0, 0:1, :], small[0, 1:2, :] = norm_back(
        state[...], pre[0], gains_ref[0, 0:1, :]
    )
    width = squares.shape[1]
    lane = lax.broadcasted_iota(jnp.int32, (1, width), 1)
    tally = jnp.sum(losses_ref[...], axis=1, keepdims=True) * (1.0 / n)
    loss, slots = tally[0:1, :], tally[1:2, :]
    small[0, 10:11, :] = jnp.where(lane == 0, loss, jnp.where(lane == 1, slots, 0.0))
    small[0, 11:16, :] = jnp.zeros((5, width), jnp.float32)
    small_copy(0).start()
    turned = grad_sum.T.astype(jnp.bfloat16)
    share = columns_in.shape[1]
    for whose in range(n):
        columns_out[whose] = turned[whose * share : (whose + 1) * share, :]
    for offset in range(1, n):
        deal_copy(offset, False).start()
    columns_in[spot.mp] = columns_out[spot.mp]
    relay(1, 3)
    small_next(0)
    conclude(2)
    for offset in range(1, n):
        deal_copy(offset, True).wait_recv()
    blocks = table_sum.shape[1] // 256
    table_blocks(0, blocks // 2)
    relay(0, 1)
    small_next(1)
    table_blocks(blocks // 2, blocks)
    half_start(1, table_grad)
    small_next(2)
    half_fold(1, table_grad)
    relay(0, 2)
    finish(1)
    small_next(3)
    half_end(1)
    relay(0, 3)
    conclude(1)
    small_next(4)
    finish(0)
    small_out[...] = small[5]
    conclude(0)

    square = jnp.sum(squares[...], axis=1, keepdims=True)
    square_parts[n] = jnp.broadcast_to(square, square_parts.shape[1:])
    swap = remote(
        square_parts.at[n],
        square_parts.at[n + 1],
        norm_send.at[0],
        norm_recv.at[0],
        spot.partner,
    )
    swap.start()
    swap.wait_recv()
    square_parts[spot.mp] = square_parts[n] + square_parts[n + 1]

    def norm_copy(offset, arriving):
        source = square_parts.at[spot.mp]
        target = square_parts.at[peer(-offset) if arriving else spot.mp]
        return remote(
            source, target, norm_send.at[offset], norm_recv.at[offset], (spot.dp, peer(offset))
        )

    for offset in range(1, n):
        norm_copy(offset, False).start()
    gains_grad = small[5, 0:10, :]
    square = jnp.sum(jnp.sum(gains_grad * gains_grad, axis=0, keepdims=True), axis=1, keepdims=True)
    for offset in range(1, n):
        norm_copy(offset, True).wait_recv()
    for whose in range(n):
        square = square + square_parts[whose, 0:1, :]
    square_out[...] = square

    for half in range(2):
        pair_copy(0, 0, half).wait_send()
        for depth in range(LAYERS):
            pair_copy(1, depth, half).wait_send()
    swap.wait_send()
    for offset in range(1, n):
        norm_copy(offset, False).wait_send()
        deal_copy(offset, False).wait_send()
    for stage in range(5):
        small_copy(stage).wait_send()
    for which in range(2):
        half_copy(which, 0).wait_send()
        half_copy(which, 1).wait_send()
        local, away = half_out(which)
        local.wait()
        away.wait()
    for turn in range(total - SLOTS, total):
        core_copy(turn).wait_send()
    for part in range(2):
        swap_copy(0, part).wait_send()
    for piece in range(2 * LAYERS):
        for way, part in WAYS:
            for step in range(1, last_step(n, way, part) + 1):
                ring_copy(piece, way, part, step).wait_send()
        across_copy(piece).wait_send()
        if piece % 2 == 0 and piece > 0:
            for index in range(2):
                give_copy(piece, index).wait_send()
        local, away = out_copies(piece)
        if piece < 2:
            local.wait()
            away.wait_send()
        away.wait_recv()


def backward_call(
    n, ids, lengths, losses, grad, first, gains, out_grad, kept, attn_full, ffn_full, slope, act, table
):
    inputs, proj, mixed, pre, mid = kept
    count, width = grad.shape
    rows_f = ffn_full.shape[3]
    groups = n // 2
    rows_a = attn_full.shape[2] // n
    rows_v = out_grad.shape[0]
    words, share = table.shape
    f32, bf16 = jnp.float32, jnp.bfloat16
    vmem = pl.BlockSpec(memory_space=pltpu.VMEM)
    anywhere = pl.BlockSpec(memory_space=pl.ANY)
    shape = jax.ShapeDtypeStruct
    dma = pltpu.SemaphoreType.DMA
    regular = pltpu.SemaphoreType.REGULAR
    ring_sems = dma((2 * LAYERS, 2, 2, n // 2))
    return pl.pallas_call(
        functools.partial(backward_kernel, n),
        out_shape=(
            shape((LAYERS, 4, rows_a, width), f32),
            shape((LAYERS, 2, rows_f, width), f32),
            shape((share, words), f32),
            shape((rows_v, width), f32),
            shape((16, width), f32),
            shape((1, 128), f32),
        ),
        in_specs=[vmem] * 7 + [anywhere] * 9,
        out_specs=(anywhere,) * 4 + (vmem,) * 2,
        scratch_shapes=[
            pltpu.VMEM((3, count, width), bf16),
            pltpu.VMEM((2, count, width), f32),
            pltpu.VMEM((4, width, width), bf16),
            pltpu.VMEM((groups, 2, rows_f, width), bf16),
            pltpu.VMEM((groups + 1, count, rows_f), f32),
            pltpu.VMEM((LAYERS, 2, width, width), bf16),
            pltpu.VMEM((LAYERS, groups, rows_f, width), bf16),
            pltpu.VMEM((SLOTS, rows_f, width), bf16),
            pltpu.VMEM((SLOTS, rows_f, width), bf16),
            pltpu.VMEM((2, width, width), bf16),
            pltpu.VMEM((2, 2, n // 2, rows_a, width), bf16),
            pltpu.VMEM((2, 2, n // 2, rows_f // 4, width), bf16),
            pltpu.VMEM((LAYERS, 2, width, cut_of(width, 6)), bf16),
            pltpu.VMEM((LAYERS, count, width), bf16),
            pltpu.VMEM((count, width), f32),
            pltpu.VMEM((LAYERS, count, width), bf16),
            pltpu.VMEM((LAYERS, count, width), bf16),
            pltpu.VMEM((count, width), f32),
            pltpu.VMEM((5, count, width), bf16),
            pltpu.VMEM((2, count, width), bf16),
            pltpu.VMEM((groups, 2, 2 * count, rows_f), bf16),
            pltpu.VMEM((2, 2 * count, width), bf16),
            pltpu.VMEM((LAYERS, 2, 2, rows_a, width), bf16),
            pltpu.VMEM((LAYERS, 2, rows_f // 2, width), bf16),
            pltpu.VMEM((2, rows_a, width), f32),
            pltpu.VMEM((rows_f, width), f32),
            dma((1,)),
            dma((3, groups)),
            dma((groups + 1,)),
            dma((2,)),
            dma((LAYERS * groups,)),
            dma((LAYERS * groups,)),
            regular((1,)),
            dma((LAYERS, 2)),
            dma((LAYERS, 2)),
            regular((2,)),
            ring_sems,
            ring_sems,
            regular((2, 2, 2, n // 2)),
            dma((LAYERS, 2)),
            dma((LAYERS, 2)),
            dma((2, LAYERS, 2)),
            dma((2, LAYERS, 2)),
            dma((2 * LAYERS,)),
            dma((2 * LAYERS,)),
            dma((2 * LAYERS,)),
            dma((2 * LAYERS,)),
            dma((2 * LAYERS,)),
            pltpu.VMEM((6, 16, width), f32),
            pltpu.VMEM((5, 16, width), f32),
            pltpu.VMEM((n, share, count), bf16),
            pltpu.VMEM((n, share, count), bf16),
            pltpu.VMEM((share, words), f32),
            pltpu.VMEM((4, share // 2, words), bf16),
            pltpu.VMEM((4, rows_v // 2, width), bf16),
            pltpu.VMEM((rows_v // 2, width), f32),
            pltpu.VMEM((1, width), f32),
            pltpu.VMEM((n + 2, 8, 128), f32),
            dma((4,)),
            dma((5,)),
            dma((5,)),
            dma((n - 1,)),
            dma((n - 1,)),
            dma((2, 3)),
            dma((2, 3)),
            dma((2,)),
            dma((n,)),
            dma((n,)),
        ],
        compiler_params=pltpu.CompilerParams(
            collective_id=2, has_side_effects=True, vmem_limit_bytes=VMEM_LIMIT
        ),
        name="backward_layers",
    )(
        ids, lengths, losses, gains, out_grad, inputs, mixed, mid, grad, first,
        proj, pre, attn_full, ffn_full, slope, act,
    )


def merged(value, axis, join):
    pieces = jax.tree.map(lambda part: lax.all_gather(part, axis), value)
    head = jax.tree.map(lambda part: part[0], pieces)
    tail = jax.tree.map(lambda part: part[1:], pieces)
    total, _ = lax.scan(lambda total, section: (join(total, section), None), head, tail)
    return total


def sinusoid(count, width):
    places = jnp.arange(count, dtype=jnp.float32)[:, None]
    freqs = jnp.exp(jnp.arange(width // 2, dtype=jnp.float32) * (-2.0 * math.log(10000.0) / width))
    angles = places * freqs[None, :]
    return jnp.concatenate([jnp.sin(angles), jnp.cos(angles)], axis=1)


def layer_norm(values, gain, shift):
    centre = jnp.mean(values, axis=-1, keepdims=True)
    offset = values - centre
    spread = jnp.mean(offset * offset, axis=-1, keepdims=True)
    inverse = lax.rsqrt(spread + norm_eps)
    normed = offset * inverse
    return (normed * gain + shift, (normed, inverse))


def norm_backward(grad, saved, gain):
    normed, inverse = saved
    scaled = grad * gain
    centred = scaled - jnp.mean(scaled, axis=-1, keepdims=True)
    result = inverse * (centred - normed * jnp.mean(scaled * normed, axis=-1, keepdims=True))
    return (result, jnp.stack([jnp.sum(grad * normed, axis=0), jnp.sum(grad, axis=0)]))


def gelu_exact(values):
    return jax.nn.gelu(values, approximate=False)


def gelu_back(hidden, grad):
    unused, pullback = jax.vjp(gelu_exact, hidden)
    return pullback(grad)[0]


def masked_scores(query, keyed, length):
    scale = query.shape[-1] ** (-0.5)
    scores = jnp.einsum("hqe,hke->hqk", query, keyed, preferred_element_type=jnp.float32) * scale
    visible = jnp.arange(keyed.shape[1]) < length
    return jnp.where(visible[None, None, :], scores, masked_score)


def fetch_forward(attn_part, ffn_part):
    return (
        lax.all_gather(attn_part, "mp", axis=1, tiled=True),
        lax.all_gather(ffn_part, "mp", axis=1, tiled=True),
    )


def fetch_backward(attn_part, ffn_part):
    return (
        lax.all_gather(attn_part, "mp", axis=1, tiled=True),
        lax.all_gather(ffn_part, "mp", axis=1, tiled=True),
    )


def reduce_layer(attn_grad, ffn_grad):
    return (
        lax.psum_scatter(attn_grad, "mp", scatter_dimension=1, tiled=True),
        lax.psum_scatter(ffn_grad, "mp", scatter_dimension=1, tiled=True),
    )


def ffn_forward(middle_b, ffn_w, unit_mask):
    hidden = jnp.einsum("td,fd->tf", middle_b, ffn_w[0], preferred_element_type=jnp.float32)
    active = (gelu_exact(hidden) * unit_mask[None, :]).astype(jnp.bfloat16)
    output = jnp.einsum("tf,fd->td", active, ffn_w[1], preferred_element_type=jnp.float32)
    return (hidden, active, output)


def ffn_backward(grad_out, middle_b, hidden, active, ffn_w, unit_mask):
    grad_active = jnp.einsum("td,fd->tf", grad_out, ffn_w[1], preferred_element_type=jnp.float32)
    grad_hidden = gelu_back(hidden, grad_active * unit_mask[None, :]).astype(jnp.bfloat16)
    up_grad = jnp.einsum("tf,td->fd", grad_hidden, middle_b, preferred_element_type=jnp.float32)
    down_grad = jnp.einsum("tf,td->fd", active, grad_out, preferred_element_type=jnp.float32)
    from_ffn = jnp.einsum("tf,fd->td", grad_hidden, ffn_w[0], preferred_element_type=jnp.float32)
    return (jnp.stack([up_grad, down_grad]), from_ffn)


def layer_forward(states, attn_w, ffn_w, pair, length, unit_mask):
    count = states.shape[0]
    inputs = states.astype(jnp.bfloat16)
    projected = jnp.einsum(
        "td,kde->kte", inputs, attn_w[:3], preferred_element_type=jnp.float32
    ).astype(jnp.bfloat16)
    heads = projected.reshape(3, count, HEADS, -1).transpose(0, 2, 1, 3)
    scores = masked_scores(heads[0], heads[1], length)
    peak = jnp.max(scores, axis=-1, keepdims=True)
    expo = jnp.exp(scores - peak)
    total = jnp.sum(expo, axis=-1, keepdims=True)
    log_total = peak + jnp.log(total)
    probs = (expo / total).astype(jnp.bfloat16)
    mixed = jnp.einsum("hqk,hke->hqe", probs, heads[2], preferred_element_type=jnp.float32)
    mixed = mixed.transpose(1, 0, 2).reshape(count, -1).astype(jnp.bfloat16)
    branch = jnp.dot(mixed, attn_w[3], preferred_element_type=jnp.float32)
    middle, norm_one = layer_norm(states + branch, pair[0, 0], pair[0, 1])
    middle_b = middle.astype(jnp.bfloat16)
    hidden, active, output = ffn_forward(middle_b, ffn_w, unit_mask)
    result, norm_two = layer_norm(middle + output, pair[1, 0], pair[1, 1])
    return (result, (inputs, heads, log_total, mixed, norm_one, middle_b, hidden, active, norm_two))


def layer_backward(grad, attn_w, ffn_w, pair, length, unit_mask, kept):
    inputs, heads, log_total, mixed, norm_one, middle_b, hidden, active, norm_two = kept
    count = inputs.shape[0]
    grad_two, pair_two = norm_backward(grad, norm_two, pair[1, 0])
    ffn_grad, from_ffn = ffn_backward(
        grad_two.astype(jnp.bfloat16), middle_b, hidden, active, ffn_w, unit_mask
    )
    grad_one, pair_one = norm_backward(grad_two + from_ffn, norm_one, pair[0, 0])
    grad_branch = grad_one.astype(jnp.bfloat16)
    output_grad = jnp.einsum("td,te->de", mixed, grad_branch, preferred_element_type=jnp.float32)
    grad_mixed = jnp.einsum("te,de->td", grad_branch, attn_w[3], preferred_element_type=jnp.float32)
    grad_mixed = grad_mixed.astype(jnp.bfloat16).reshape(count, HEADS, -1).transpose(1, 0, 2)
    scale = heads.shape[-1] ** (-0.5)
    probs = jnp.exp(masked_scores(heads[0], heads[1], length) - log_total)
    grad_values = jnp.einsum(
        "hqk,hqe->hke", probs.astype(jnp.bfloat16), grad_mixed, preferred_element_type=jnp.float32
    )
    grad_probs = jnp.einsum(
        "hqe,hke->hqk", grad_mixed, heads[2], preferred_element_type=jnp.float32
    )
    grad_scores = probs * (grad_probs - jnp.sum(grad_probs * probs, axis=-1, keepdims=True))
    grad_scores = grad_scores.astype(jnp.bfloat16)
    grad_query = (
        jnp.einsum("hqk,hke->hqe", grad_scores, heads[1], preferred_element_type=jnp.float32)
        * scale
    )
    grad_key = (
        jnp.einsum("hqk,hqe->hke", grad_scores, heads[0], preferred_element_type=jnp.float32)
        * scale
    )
    stacked = (
        jnp.stack([grad_query, grad_key, grad_values]).transpose(0, 2, 1, 3).reshape(3, count, -1)
    )
    stacked = stacked.astype(jnp.bfloat16)
    input_grad = jnp.einsum("td,kte->kde", inputs, stacked, preferred_element_type=jnp.float32)
    from_attn = jnp.einsum("kte,kde->td", stacked, attn_w[:3], preferred_element_type=jnp.float32)
    attn_grad = jnp.concatenate([input_grad, output_grad[None]], axis=0)
    return (grad_one + from_attn, attn_grad, ffn_grad, jnp.stack([pair_one, pair_two]))


def adamw(weight, moment_one, moment_two, grad, decay, rate):
    moment_one = beta_one * moment_one + (1.0 - beta_one) * grad
    moment_two = beta_two * moment_two + (1.0 - beta_two) * grad * grad
    fixed_one = moment_one / (1.0 - beta_one**STEP)
    fixed_two = moment_two / (1.0 - beta_two**STEP)
    weight = weight - rate * (fixed_one / (jnp.sqrt(fixed_two) + adam_eps) + decay * weight)
    return (moment_one, moment_two, weight)


def combine_vocab(first, second):
    peak = jnp.maximum(first[0], second[0])
    total = first[1] * jnp.exp(first[0] - peak) + second[1] * jnp.exp(second[0] - peak)
    return (peak, total, first[2] + second[2])


def local_general(
    tokens,
    lengths,
    places,
    targets,
    ramp,
    attn,
    attn_m,
    attn_v,
    ffn,
    ffn_m,
    ffn_v,
    table,
    table_m,
    table_v,
    out_table,
    out_m,
    out_v,
    gains,
    gains_m,
    gains_v,
):
    rank = lax.axis_index("mp")
    count = tokens.shape[2]
    flat_ids = tokens.reshape(-1)
    all_lengths = lengths.reshape(-1)
    length = lax.dynamic_index_in_dim(all_lengths, rank, keepdims=False)
    masks = jnp.minimum(ramp, RAMP).astype(jnp.float32) / RAMP
    unit_masks = [masks[depth] for depth in range(LAYERS)]
    looked = jnp.take(table, flat_ids, axis=0)
    embedded = lax.all_to_all(looked, "mp", split_axis=0, concat_axis=1, tiled=True)
    states, norm_zero = layer_norm(
        embedded + sinusoid(count, embedded.shape[1]), gains[0, 0], gains[0, 1]
    )
    kept_all = []
    weights_all = []
    for depth in range(LAYERS):
        attn_w, ffn_w = fetch_forward(
            attn[depth].astype(jnp.bfloat16), ffn[depth].astype(jnp.bfloat16)
        )
        states, kept = layer_forward(
            states, attn_w, ffn_w, gains[1 + 2 * depth : 3 + 2 * depth], length, unit_masks[depth]
        )
        kept_all.append(kept)
        weights_all.append(None)
    spots = places.reshape(-1)
    picked = jnp.take(states, spots, axis=0).astype(jnp.bfloat16)
    picked_all = lax.all_gather(picked, "mp", axis=0, tiled=True)
    out_b = out_table.astype(jnp.bfloat16)
    logits = jnp.einsum("rd,vd->rv", picked_all, out_b, preferred_element_type=jnp.float32)
    labels = targets.reshape(-1)
    columns = rank * out_table.shape[0] + jnp.arange(out_table.shape[0])
    hits = (labels[:, None] == columns[None, :]).astype(jnp.float32)
    peak = jnp.max(logits, axis=1)
    expsum = jnp.sum(jnp.exp(logits - peak[:, None]), axis=1)
    target_part = jnp.sum(hits * logits, axis=1)
    peak_all, expsum_all, target_all = merged((peak, expsum, target_part), "mp", combine_vocab)
    log_total = peak_all + jnp.log(expsum_all)
    slot_count = targets.shape[2]
    counted = jnp.maximum(1, all_lengths * slot_count // count)
    valid = (jnp.arange(slot_count)[None, :] < counted[:, None]).reshape(-1)
    loss_pair = jnp.stack(
        [
            jnp.sum(jnp.where(valid, log_total - target_all, 0.0)),
            jnp.sum(counted).astype(jnp.float32),
        ]
    )
    grad_logits = jnp.where(
        valid[:, None], jnp.exp(logits - log_total[:, None]) - hits, 0.0
    ).astype(jnp.bfloat16)
    out_grad = jnp.einsum("rv,rd->vd", grad_logits, picked_all, preferred_element_type=jnp.float32)
    picked_grad = lax.psum_scatter(
        jnp.dot(grad_logits, out_b, preferred_element_type=jnp.float32),
        "mp",
        scatter_dimension=0,
        tiled=True,
    )
    grad = jnp.zeros_like(states).at[spots].add(picked_grad)
    attn_parts = [None] * LAYERS
    ffn_parts = [None] * LAYERS
    pair_grads = [None] * LAYERS
    for depth in reversed(range(LAYERS)):
        attn_w, ffn_w = fetch_backward(
            attn[depth].astype(jnp.bfloat16), ffn[depth].astype(jnp.bfloat16)
        )
        grad, attn_grad, ffn_grad, pair_grad = layer_backward(
            grad,
            attn_w,
            ffn_w,
            gains[1 + 2 * depth : 3 + 2 * depth],
            length,
            unit_masks[depth],
            kept_all[depth],
        )
        attn_parts[depth], ffn_parts[depth] = reduce_layer(attn_grad, ffn_grad)
        pair_grads[depth] = pair_grad
    grad_sum, zero_grad = norm_backward(grad, norm_zero, gains[0, 0])
    returned = lax.all_to_all(grad_sum, "mp", split_axis=1, concat_axis=0, tiled=True)
    table_grad = jnp.zeros_like(table).at[flat_ids].add(returned)
    gains_grad = jnp.concatenate([zero_grad[None]] + pair_grads, axis=0)
    attn_sum, ffn_sum, table_sum, out_sum, gains_part, loss = lax.psum(
        (jnp.stack(attn_parts), jnp.stack(ffn_parts), table_grad, out_grad, gains_grad, loss_pair),
        "dp",
    )
    shard_squares = (
        jnp.sum(attn_sum * attn_sum)
        + jnp.sum(ffn_sum * ffn_sum)
        + jnp.sum(table_sum * table_sum)
        + jnp.sum(out_sum * out_sum)
    )
    square_total, gains_sum = lax.psum((shard_squares, gains_part), "mp")
    grad_norm = jnp.sqrt(square_total + jnp.sum(gains_sum * gains_sum))
    factor = clip_limit / jnp.maximum(grad_norm, clip_limit)
    attn_m_new, attn_v_new, attn_new = adamw(
        attn, attn_m, attn_v, attn_sum * factor, weight_decay, learn_rate
    )
    ffn_m_new, ffn_v_new, ffn_new = adamw(
        ffn, ffn_m, ffn_v, ffn_sum * factor, weight_decay, learn_rate
    )
    table_m_new, table_v_new, table_new = adamw(
        table, table_m, table_v, table_sum * factor, weight_decay, learn_rate
    )
    out_m_new, out_v_new, out_new = adamw(
        out_table, out_m, out_v, out_sum * factor, weight_decay, learn_rate
    )
    gains_m_new, gains_v_new, gains_new = adamw(
        gains, gains_m, gains_v, gains_sum * factor, 0.0, gain_rate
    )
    return (
        loss,
        grad_norm.reshape(1),
        attn_m_new,
        attn_v_new,
        attn_new,
        ffn_m_new,
        ffn_v_new,
        ffn_new,
        table_m_new,
        table_v_new,
        table_new,
        out_m_new,
        out_v_new,
        out_new,
        gains_m_new,
        gains_v_new,
        gains_new,
    )


def local(
    tokens,
    lengths,
    places,
    targets,
    ramp,
    attn,
    attn_m,
    attn_v,
    ffn,
    ffn_m,
    ffn_v,
    table,
    table_m,
    table_v,
    out_table,
    out_m,
    out_v,
    gains,
    gains_m,
    gains_v,
):
    n = tokens.shape[1]
    where = jnp.asarray(positions(tokens.shape[2], gains.shape[2]))
    attn_full, ffn_full, first, *kept, slope, act, grad, out_grad, losses = forward_call(
        n, tokens[0], lengths, places[0], targets[0], ramp, gains, table.T, where, out_table, attn, ffn
    )
    attn_sum, ffn_sum, table_turned, out_sum, small, square = backward_call(
        n, tokens[0], lengths, losses, grad, first, gains, out_grad, kept, attn_full, ffn_full, slope, act, table
    )
    table_sum = table_turned.T
    gains_sum = small[:10].reshape(gains.shape)
    grad_norm = jnp.sqrt(square[0, 0])
    factor = clip_limit / jnp.maximum(grad_norm, clip_limit)
    attn_m_new, attn_v_new, attn_new = adamw(
        attn, attn_m, attn_v, attn_sum * factor, weight_decay, learn_rate
    )
    ffn_m_new, ffn_v_new, ffn_new = adamw(
        ffn, ffn_m, ffn_v, ffn_sum * factor, weight_decay, learn_rate
    )
    table_m_new, table_v_new, table_new = adamw(
        table, table_m, table_v, table_sum * factor, weight_decay, learn_rate
    )
    out_m_new, out_v_new, out_new = adamw(
        out_table, out_m, out_v, out_sum * factor, weight_decay, learn_rate
    )
    gains_m_new, gains_v_new, gains_new = adamw(
        gains, gains_m, gains_v, gains_sum * factor, 0.0, gain_rate
    )
    return (
        small[10, :2],
        grad_norm.reshape(1),
        attn_m_new,
        attn_v_new,
        attn_new,
        ffn_m_new,
        ffn_v_new,
        ffn_new,
        table_m_new,
        table_v_new,
        table_new,
        out_m_new,
        out_v_new,
        out_new,
        gains_m_new,
        gains_v_new,
        gains_new,
    )


def solution(mesh):
    in_specs = (
        P("dp", None, None),
        P("dp", None),
        P("dp", "mp", None),
        P("dp", None, None),
        P(),
        P(None, None, "mp", None),
        P(None, None, "mp", None),
        P(None, None, "mp", None),
        P(None, None, "mp", None),
        P(None, None, "mp", None),
        P(None, None, "mp", None),
        P(None, "mp"),
        P(None, "mp"),
        P(None, "mp"),
        P("mp", None),
        P("mp", None),
        P("mp", None),
        P(),
        P(),
        P(),
    )
    out_specs = (
        P(),
        P(),
        P(None, None, "mp", None),
        P(None, None, "mp", None),
        P(None, None, "mp", None),
        P(None, None, "mp", None),
        P(None, None, "mp", None),
        P(None, None, "mp", None),
        P(None, "mp"),
        P(None, "mp"),
        P(None, "mp"),
        P("mp", None),
        P("mp", None),
        P("mp", None),
        P(),
        P(),
        P(),
    )
    fits = mesh.shape['mp'] == 8 and mesh.shape['dp'] == 4
    chosen = local if fits else local_general
    return jax.shard_map(chosen, mesh=mesh, in_specs=in_specs, out_specs=out_specs, check_vma=False)
```

```python
import functools
import math

import jax
import jax.numpy as jnp
import numpy as np
from jax import lax
from jax.experimental import pallas as pl
from jax.experimental.pallas import tpu as pltpu
from jax.sharding import PartitionSpec as P

HEADS = 12
LAYERS = 2
STEP = 10
RAMP = 4


norm_eps = 1e-05
beta_one = 0.9
beta_two = 0.999
learn_rate = 0.02
gain_rate = 0.3
weight_decay = 0.01
adam_eps = 1e-08
clip_limit = 1.0
masked_score = -1000000000.0


MESH = pl.DeviceIdType.MESH
VMEM_LIMIT = 62 * 1024 * 1024
SLOTS = 3
STRIPS = 2


def dot_nn(left, right):
    return lax.dot_general(
        left, right, (((1,), (0,)), ((), ())), preferred_element_type=jnp.float32
    )


def dot_nt(left, right):
    return lax.dot_general(
        left, right, (((1,), (1,)), ((), ())), preferred_element_type=jnp.float32
    )


def dot_tn(left, right):
    return lax.dot_general(
        left, right, (((0,), (0,)), ((), ())), preferred_element_type=jnp.float32
    )


def positions(count, width):
    angles = np.arange(count)[:, None] * np.exp(
        np.arange(width // 2) * (-2.0 * math.log(10000.0) / width)
    )
    return np.concatenate([np.sin(angles), np.cos(angles)], axis=1).astype(np.float32)


def ring_index(place, n):
    late = place // (n // 2)
    return (1 - late) * 2 * place + late * (2 * (n - 1 - place) + 1)


def ring_place(index, n):
    odd = index % 2
    return (1 - odd) * (index // 2) + odd * (n - 1 - index // 2)


class Spot:
    def __init__(self, n):
        self.n = n
        self.dp = lax.axis_index("dp")
        self.mp = lax.axis_index("mp")
        self.core = self.dp % 2
        self.row = self.dp // 2
        self.place = ring_place(self.mp, n)
        self.partner = (self.dp + 1 - 2 * self.core, self.mp)
        self.across = ((self.dp + 2) % 4, self.mp)
        self.ring = (
            (self.dp, ring_index((self.place + 1) % n, n)),
            (self.dp, ring_index((self.place + n - 1) % n, n)),
        )

    def shard(self, offset):
        return ring_index((self.place + offset + self.n) % self.n, self.n)


def greet(devices):
    barrier = pltpu.get_barrier_semaphore()
    for device in devices:
        pl.semaphore_signal(barrier, inc=1, device_id=device, device_id_type=MESH)
    pl.semaphore_wait(barrier, len(devices))


def last_step(n, way, part):
    return n // 2 if way == part else n // 2 - 1


WAYS = ((0, 0), (1, 1), (0, 1), (1, 0))


def ring_columns(row, width, cut):
    return pl.ds(pl.multiple_of(row * cut, 128), width - cut)


def edge_columns(row, width, cut):
    return pl.ds(pl.multiple_of(row * (width - cut), 128), cut)


def cut_of(width, share):
    return 128 * (width // 128 // share)


def normed_of(values):
    centre = jnp.mean(values, axis=-1, keepdims=True)
    offset = values - centre
    spread = jnp.mean(offset * offset, axis=-1, keepdims=True)
    inverse = lax.rsqrt(spread + norm_eps)
    return offset * inverse, inverse


def forward_kernel(
    n,
    ids_ref,
    lengths_ref,
    places_ref,
    targets_ref,
    ramp_ref,
    gains_ref,
    table_ref,
    where_ref,
    out_ref,
    attn_sh,
    ffn_sh,
    attn_full,
    ffn_full,
    first_out,
    inputs_out,
    proj_out,
    mixed_out,
    pre_out,
    mid_out,
    slope_ref,
    act_ref,
    grad_ref,
    out_grad_ref,
    loss_ref,
    first_ref,
    inputs_ref,
    proj_ref,
    mixed_ref,
    pre_ref,
    mid_ref,
    mask_ref,
    table_b,
    places_row,
    labels_row,
    wa,
    wf,
    raw_a,
    raw_f,
    slope,
    act,
    far_sum,
    far_out,
    far_in,
    state,
    row_out,
    row_in,
    picked,
    stats,
    back_out,
    back_in,
    raw_sem,
    early_sem,
    kept_sem,
    ring_send,
    ring_recv,
    core_send,
    core_recv,
    across_send,
    across_recv,
    pair_send,
    pair_recv,
    fan_send,
    fan_recv,
):
    spot = Spot(n)
    core = spot.core
    rows_a = attn_sh.shape[2]
    rows_f = ffn_sh.shape[2]
    half_f = rows_f // 2
    part_f = half_f // 2
    steps = n // 2
    count, width = first_ref.shape
    share_e = table_ref.shape[0]
    words = table_ref.shape[1]
    slots = places_row.shape[1]
    slot_count = places_ref.shape[1]

    def rows_at(shard, rows):
        return pl.ds(pl.multiple_of(shard * rows, 16), rows)

    def remote(source, target, send, recv, device):
        return pltpu.make_async_remote_copy(
            src_ref=source,
            dst_ref=target,
            send_sem=send,
            recv_sem=recv,
            device_id=device,
            device_id_type=MESH,
        )

    def slot_f(way, step):
        if step == 0:
            return 0, 0
        return (0, 1) if step == steps else (step, way)

    def chunk_f(piece, way, part, step, side):
        group, half = slot_f(way, step)
        return wf.at[piece // 2, group, side, pl.ds(half * half_f + part * part_f, part_f), :]

    def chunk_a(piece, shard, part, side, edge):
        cut = cut_of(width, 3)
        if edge is None:
            columns = ring_columns(spot.row, width, cut)
        else:
            columns = edge_columns(edge, width, cut)
        return wa.at[piece // 2, 2 * side + part, rows_at(shard, rows_a), columns]

    def sign(way):
        return -1 if way == 0 else 1

    def ring_copy(piece, way, part, step, arriving):
        if piece % 2 == 0:
            target = chunk_a(piece, spot.shard(sign(way) * (step - 1 + arriving)), part, core, None)
            source = target
        else:
            target = chunk_f(piece, way, part, step, core)
            source = target if arriving else chunk_f(piece, way, part, step - 1, core)
        return remote(
            source,
            target,
            ring_send.at[piece, way, part, step - 1],
            ring_recv.at[piece, way, part, step - 1],
            spot.ring[way],
        )

    def core_copy(piece, way, part, step, side, edge):
        if piece % 2 == 0:
            target = chunk_a(piece, spot.shard(sign(way) * step), part, side, edge)
        else:
            target = chunk_f(piece, way, part, step, side)
        lane = 0 if edge is None else 1
        return remote(
            target,
            target,
            core_send.at[lane, piece, way, part, step - 1],
            core_recv.at[lane, piece, way, part, step - 1],
            spot.partner,
        )

    def across_copy(piece, way, part, step, row):
        target = chunk_a(piece, spot.shard(sign(way) * step), part, core, row)
        return remote(
            target,
            target,
            across_send.at[piece, way, part, step - 1],
            across_recv.at[piece, way, part, step - 1],
            spot.across,
        )

    def half_at(half):
        return pl.ds(half * (count // STRIPS), count // STRIPS)

    def pair_copy(which, depth, half):
        rows = half_at(half)
        if which == 0:
            source, target = mid_ref.at[depth, 0, rows, :], mid_ref.at[depth, 1, rows, :]
        else:
            source, target = far_out.at[depth, rows, :], far_in.at[depth, rows, :]
        return remote(
            source,
            target,
            pair_send.at[which, depth, half],
            pair_recv.at[which, depth, half],
            spot.across,
        )

    def peer(offset):
        return (spot.mp + offset + n) % n

    def fan_copy(which, offset, source, target):
        return remote(
            source,
            target,
            fan_send.at[which, offset - 1],
            fan_recv.at[which, offset - 1],
            (spot.dp, peer(offset)),
        )

    def share(which, buffer, offset):
        return fan_copy(which, offset, buffer.at[spot.mp], buffer.at[spot.mp])

    def arrived(which, buffer, offset):
        return fan_copy(which, offset, buffer.at[peer(-offset)], buffer.at[peer(-offset)])

    def deal(which, source, target, offset):
        return fan_copy(which, offset, source.at[peer(offset)], target.at[spot.mp])

    def raw_copy(piece):
        kind, depth = piece % 2, piece // 2
        if kind == 0:
            return pltpu.make_async_copy(attn_sh.at[depth], raw_a.at[depth], raw_sem.at[piece])
        rows = pl.ds(pl.multiple_of(spot.row * half_f, 16), half_f)
        return pltpu.make_async_copy(ffn_sh.at[depth, :, rows, :], raw_f.at[depth], raw_sem.at[piece])

    def take_own(piece):
        kind, depth = piece % 2, piece // 2
        raw_copy(piece).wait()
        if kind == 0:
            for which in range(4):
                wa[depth, which, rows_at(spot.mp, rows_a), :] = raw_a[depth, which].astype(
                    jnp.bfloat16
                )
        else:
            for which in range(2):
                wf[depth, 0, which, 0:half_f, :] = raw_f[depth, which].astype(jnp.bfloat16)

    def launch(piece):
        for way, part in WAYS:
            ring_copy(piece, way, part, 1, 0).start()

    def chains(step):
        return [(way, part) for way, part in WAYS if step <= last_step(n, way, part)]

    def pass_on(piece, step):
        for way, part in chains(step):
            ring_copy(piece, way, part, step, 1).wait_recv()
            if step < last_step(n, way, part):
                ring_copy(piece, way, part, step + 1, 0).start()
            if piece % 2 == 0:
                across_copy(piece, way, part, step, spot.row).start()
            core_copy(piece, way, part, step, core, None).start()

    def pass_edge(piece, step):
        for way, part in chains(step):
            across_copy(piece, way, part, step, 1 - spot.row).wait_recv()
            core_copy(piece, way, part, step, core, 1 - spot.row).start()

    def settle(piece, step):
        for way, part in chains(step):
            core_copy(piece, way, part, step, 1 - core, None).wait_recv()
            if piece % 2 == 0:
                core_copy(piece, way, part, step, 1 - core, 1 - spot.row).wait_recv()

    out_copies = []

    def write_out(source, target):
        copy = pltpu.make_async_copy(source, target, early_sem.at[len(out_copies)])
        copy.start()
        out_copies.append(copy)

    def look_up(offset):
        whose = peer(offset)
        tokens = ids_ref[pl.ds(whose, 1), :]

        size = 768

        def block(index, total):
            start = pl.multiple_of(index * size, 128)
            word = lax.broadcasted_iota(jnp.int32, (size, 1), 0) + start
            chosen = (word == tokens).astype(jnp.bfloat16)
            return total + dot_nn(table_b[:, pl.ds(start, size)], chosen)

        found = lax.fori_loop(
            0, words // size, block, jnp.zeros((share_e, count), jnp.float32)
        )
        row_out[whose] = found.astype(jnp.bfloat16)
        if offset > 0:
            deal(0, row_out, row_in, offset).start()

    for piece in range(2 * LAYERS):
        raw_copy(piece).start()
    greet([spot.partner, spot.across] + [(spot.dp, peer(offset)) for offset in range(1, n)])
    take_own(0)
    launch(0)
    for depth in range(LAYERS):
        for index in range(n):
            offset = (0, steps)[index] if index < 2 else (index // 2) * (2 * (index % 2) - 1)
            start = pl.multiple_of(spot.shard(offset) * rows_f, 128)
            grown = jnp.minimum(ramp_ref[depth : depth + 1, pl.ds(start, rows_f)], RAMP)
            grown = grown.astype(jnp.float32) / RAMP
            lanes_to = pl.ds((index % 2) * half_f, half_f)
            mask_ref[depth, index // 2 : index // 2 + 1, lanes_to] = jnp.where(
                spot.row == 0, grown[:, 0:half_f], grown[:, half_f:rows_f]
            )
    table_b[...] = table_ref[...].astype(jnp.bfloat16)
    places_row[...] = jnp.full_like(places_row, -1)
    places_row[0:1, 0:slot_count] = places_ref[...]
    labels_row[...] = jnp.full_like(labels_row, -1)
    for whose in range(n):
        labels_row[0:1, whose * slots : whose * slots + slot_count] = targets_ref[
            whose : whose + 1, :
        ]
    spans = lengths_ref[...].astype(jnp.float32)
    lane = lax.broadcasted_iota(jnp.int32, (1, n), 1)
    length = jnp.sum(jnp.where(lane == spot.mp, spans, 0.0), axis=1, keepdims=True)
    visible = lax.broadcasted_iota(jnp.int32, (1, count), 1).astype(jnp.float32) < length
    counted = jnp.maximum(jnp.floor(spans * (slot_count / count)), 1.0)
    lane = lax.broadcasted_iota(jnp.int32, (1, n * slots), 1)
    limit = jnp.zeros((1, n * slots), jnp.float32)
    for whose in range(n):
        limit = jnp.where(
            lane >= whose * slots, counted[:, whose : whose + 1] + whose * slots, limit
        )
    valid = lane.astype(jnp.float32) < limit
    loss_ref[1:2, :] = valid.astype(jnp.float32)
    for offset in range(1, 4):
        look_up(offset)
    pass_on(0, 1)
    for offset in range(4, 7):
        look_up(offset)
    pass_on(0, 2)
    pass_edge(0, 1)
    take_own(1)
    launch(1)
    look_up(7)
    look_up(0)
    row_in[spot.mp] = row_out[spot.mp]
    pass_on(0, 3)
    pass_edge(0, 2)
    for offset in range(1, n):
        arrived(0, row_in, offset).wait_recv()
    first_ref[...] = where_ref[...] + row_in[...].reshape(width, count).astype(jnp.float32).T
    write_out(first_ref, first_out)
    normed, _ = normed_of(first_ref[...])
    state[...] = normed * gains_ref[0, 0:1, :] + gains_ref[0, 1:2, :]
    take_own(2)
    take_own(3)
    pass_on(0, 4)
    pass_edge(0, 3)

    lanes = lax.broadcasted_iota(jnp.int32, (1, 128), 1) < 64

    def head_pair(depth, pair):
        columns = pl.ds(pl.multiple_of(pair * 128, 128), 128)
        query = proj_ref[depth, 0, :, columns]
        keyed = proj_ref[depth, 1, :, columns]
        valued = proj_ref[depth, 2, :, columns]
        outs = []
        for side in range(2):
            mine = lanes if side == 0 else jnp.logical_not(lanes)
            scores = dot_nt(jnp.where(mine, query, jnp.zeros_like(query)), keyed) * 0.125
            scores = jnp.where(visible, scores, masked_score)
            expo = jnp.exp(scores - jnp.max(scores, axis=-1, keepdims=True))
            total = jnp.sum(expo, axis=-1, keepdims=True)
            outs.append(dot_nn((expo / total).astype(jnp.bfloat16), valued))
        mixed_ref[depth, :, columns] = jnp.where(lanes, outs[0], outs[1]).astype(jnp.bfloat16)

    def kept_copies(turn, depth, group, far, start, size):
        slot = turn % SLOTS
        here, there = pl.ds(0, size), pl.ds(start, size)
        return (
            pltpu.make_async_copy(
                slope.at[slot, here, :],
                slope_ref.at[depth, group, far, there, :],
                kept_sem.at[0, slot],
            ),
            pltpu.make_async_copy(
                act.at[slot, here, :],
                act_ref.at[depth, group, far, there, :],
                kept_sem.at[1, slot],
            ),
        )

    turns = []

    def ffn_block(depth, group, far, start, size):
        turn = len(turns)
        turns.append((depth, group, far, start, size))
        if turn >= SLOTS:
            for copy in kept_copies(turn, *turns[turn - SLOTS]):
                copy.wait()
        slot, rows, here = turn % SLOTS, pl.ds(start, size), pl.ds(0, size)
        hidden = dot_nt(mid_ref[depth, far, rows, :], wf[depth, group, 0])
        spread = 0.5 * (1.0 + lax.erf(hidden * (0.5**0.5)))
        mask = mask_ref[depth, group : group + 1, :]
        bell = jnp.exp(hidden * hidden * -0.5) * (1.0 / math.sqrt(2.0 * math.pi))
        slope[slot, here, :] = (spread + hidden * bell) * mask
        active = (hidden * spread * mask).astype(jnp.bfloat16)
        act[slot, here, :] = active
        for copy in kept_copies(*((turn,) + turns[turn])):
            copy.start()
        if far:
            far_sum[rows, :] += dot_nn(active, wf[depth, group, 1])
        else:
            pre_ref[depth, 1, rows, :] += dot_nn(active, wf[depth, group, 1])

    def ffn_own(depth, group):
        ffn_block(depth, group, 0, 0, count)

    def ffn_far(depth, group, half):
        ffn_block(depth, group, 1, half * (count // STRIPS), count // STRIPS)

    for depth in range(LAYERS):
        piece_a, piece_f = 2 * depth, 2 * depth + 1
        more = depth + 1 < LAYERS
        if depth > 0:
            pass_on(piece_a, 3)
            pass_edge(piece_a, 2)
            pass_on(piece_a, 4)
            pass_edge(piece_a, 3)
        pass_edge(piece_a, 4)
        for step in range(1, steps + 1):
            settle(piece_a, step)
        write_out(wa.at[depth], attn_full.at[depth])
        inputs = state[...].astype(jnp.bfloat16)
        inputs_ref[depth] = inputs
        for which in range(3):
            proj_ref[depth, which] = dot_nn(inputs, wa[depth, which]).astype(jnp.bfloat16)
        pass_on(piece_f, 1)

        @pl.loop(0, HEADS // 2)
        def _(pair):
            head_pair(depth, pair)

        pre_ref[depth, 0] = state[...] + dot_nn(mixed_ref[depth], wa[depth, 3])
        normed, _ = normed_of(pre_ref[depth, 0])
        middle = (
            normed * gains_ref[1 + 2 * depth, 0:1, :] + gains_ref[1 + 2 * depth, 1:2, :]
        )
        for half in range(STRIPS):
            mid_ref[depth, 0, half_at(half), :] = middle[
                half * (count // STRIPS) : (half + 1) * (count // STRIPS), :
            ].astype(jnp.bfloat16)
            pair_copy(0, depth, half).start()
        pre_ref[depth, 1] = middle
        far_sum[...] = jnp.zeros_like(far_sum)
        write_out(inputs_ref.at[depth], inputs_out.at[depth])
        write_out(proj_ref.at[depth], proj_out.at[depth])
        write_out(mixed_ref.at[depth], mixed_out.at[depth])
        pass_on(piece_f, 2)
        settle(piece_f, 1)
        ffn_own(depth, 1)
        pass_on(piece_f, 3)
        if more:
            launch(piece_a + 2)
        settle(piece_f, 2)
        ffn_own(depth, 2)
        for half in range(STRIPS):
            pair_copy(0, depth, half).wait_recv()
            ffn_far(depth, 1, half)
            ffn_far(depth, 2, half)
        write_out(mid_ref.at[depth], mid_out.at[depth])
        pass_on(piece_f, 4)
        settle(piece_f, 3)
        settle(piece_f, 4)
        for half in range(STRIPS):
            ffn_far(depth, 3, half)
            ffn_far(depth, 0, half)
            far_out[depth, half_at(half), :] = far_sum[half_at(half), :].astype(jnp.bfloat16)
            pair_copy(1, depth, half).start()
        if more:
            pass_on(piece_a + 2, 1)
        ffn_own(depth, 3)
        ffn_own(depth, 0)
        write_out(wf.at[depth], ffn_full.at[depth])
        if more:
            launch(piece_f + 2)
            pass_on(piece_a + 2, 2)
            pass_edge(piece_a + 2, 1)
        for half in range(STRIPS):
            pair_copy(1, depth, half).wait_recv()
        pre_ref[depth, 1] += far_in[depth].astype(jnp.float32)
        write_out(pre_ref.at[depth], pre_out.at[depth])
        normed, _ = normed_of(pre_ref[depth, 1])
        state[...] = normed * gains_ref[2 + 2 * depth, 0:1, :] + gains_ref[2 + 2 * depth, 1:2, :]

    spots = (
        lax.broadcasted_iota(jnp.int32, (count, 1), 0) == places_row[...]
    ).astype(jnp.bfloat16)
    picked[spot.mp] = dot_tn(spots, state[...].astype(jnp.bfloat16)).astype(jnp.bfloat16)
    for offset in range(1, n):
        share(1, picked, offset).start()
    out_b = out_ref[...].astype(jnp.bfloat16)
    rows_v = out_ref.shape[0]
    hits = (
        labels_row[...] == spot.mp * rows_v + lax.broadcasted_iota(jnp.int32, (rows_v, 1), 0)
    ).astype(jnp.float32)
    for offset in range(1, n):
        arrived(1, picked, offset).wait_recv()
    picked_all = picked[...].reshape(n * slots, -1)
    logits = dot_nt(out_b, picked_all)
    peak = jnp.max(logits, axis=0, keepdims=True)
    expsum = jnp.sum(jnp.exp(logits - peak), axis=0, keepdims=True)
    stats[spot.mp, 0:1, :] = peak
    stats[spot.mp, 1:2, :] = expsum
    stats[spot.mp, 2:3, :] = jnp.sum(hits * logits, axis=0, keepdims=True)
    for offset in range(1, n):
        share(2, stats, offset).start()
    for offset in range(1, n):
        arrived(2, stats, offset).wait_recv()
    peak = stats[0, 0:1, :]
    for whose in range(1, n):
        peak = jnp.maximum(peak, stats[whose, 0:1, :])
    expsum = stats[0, 1:2, :] * jnp.exp(stats[0, 0:1, :] - peak)
    target = stats[0, 2:3, :]
    for whose in range(1, n):
        expsum = expsum + stats[whose, 1:2, :] * jnp.exp(stats[whose, 0:1, :] - peak)
        target = target + stats[whose, 2:3, :]
    log_total = peak + jnp.log(expsum)
    loss_ref[0:1, :] = jnp.where(valid, log_total - target, 0.0)
    grad_logits = jnp.where(valid, jnp.exp(logits - log_total) - hits, 0.0).astype(jnp.bfloat16)
    picked_grad = dot_tn(grad_logits, out_b).astype(jnp.bfloat16)
    for whose in range(n):
        back_out[whose] = picked_grad[whose * slots : (whose + 1) * slots, :]
    for offset in range(1, n):
        deal(3, back_out, back_in, offset).start()
    back_in[spot.mp] = back_out[spot.mp]
    out_grad_ref[...] = dot_nn(grad_logits, picked_all)
    for offset in range(1, n):
        arrived(3, back_in, offset).wait_recv()
    summed = back_in[0].astype(jnp.float32)
    for whose in range(1, n):
        summed = summed + back_in[whose].astype(jnp.float32)
    high = summed.astype(jnp.bfloat16)
    low = (summed - high.astype(jnp.float32)).astype(jnp.bfloat16)
    grad_ref[...] = dot_nn(spots, high) + dot_nn(spots, low)

    for piece in range(2 * LAYERS):
        for way, part in WAYS:
            for step in range(1, last_step(n, way, part) + 1):
                ring_copy(piece, way, part, step, 0).wait_send()
                core_copy(piece, way, part, step, core, None).wait_send()
                if piece % 2 == 0:
                    across_copy(piece, way, part, step, spot.row).wait_send()
                    core_copy(piece, way, part, step, core, 1 - spot.row).wait_send()
    for offset in range(1, n):
        deal(0, row_out, row_in, offset).wait_send()
        share(1, picked, offset).wait_send()
        share(2, stats, offset).wait_send()
        deal(3, back_out, back_in, offset).wait_send()
    for depth in range(LAYERS):
        for half in range(STRIPS):
            pair_copy(0, depth, half).wait_send()
            pair_copy(1, depth, half).wait_send()
    for turn in range(len(turns) - SLOTS, len(turns)):
        for copy in kept_copies(turn, *turns[turn]):
            copy.wait()
    for copy in out_copies:
        copy.wait()


def forward_call(
    n, ids, lengths, places, targets, ramp, gains, table, where, out_table, attn, ffn
):
    count, width = where.shape
    rows_f = ffn.shape[2]
    slots = 32 * -(-places.shape[1] // 32)
    groups = n // 2
    f32, bf16 = jnp.float32, jnp.bfloat16
    vmem = pl.BlockSpec(memory_space=pltpu.VMEM)
    anywhere = pl.BlockSpec(memory_space=pl.ANY)
    shape = jax.ShapeDtypeStruct
    dma = pltpu.SemaphoreType.DMA
    sems = dma((2 * LAYERS, 2, 2, n // 2))
    core_sems = dma((2, 2 * LAYERS, 2, 2, n // 2))
    return pl.pallas_call(
        functools.partial(forward_kernel, n),
        out_shape=(
            shape((LAYERS, 4, width, width), bf16),
            shape((LAYERS, groups, 2, rows_f, width), bf16),
            shape((count, width), f32),
            shape((LAYERS, count, width), bf16),
            shape((LAYERS, 3, count, width), bf16),
            shape((LAYERS, count, width), bf16),
            shape((LAYERS, 2, count, width), f32),
            shape((LAYERS, 2, count, width), bf16),
            shape((LAYERS, groups, 2, count, rows_f), f32),
            shape((LAYERS, groups, 2, count, rows_f), bf16),
            shape((count, width), f32),
            shape(out_table.shape, f32),
            shape((2, n * slots), f32),
        ),
        in_specs=[vmem] * 9 + [anywhere] * 2,
        out_specs=(anywhere,) * 10 + (vmem,) * 3,
        scratch_shapes=[
            pltpu.VMEM((count, width), f32),
            pltpu.VMEM((LAYERS, count, width), bf16),
            pltpu.VMEM((LAYERS, 3, count, width), bf16),
            pltpu.VMEM((LAYERS, count, width), bf16),
            pltpu.VMEM((LAYERS, 2, count, width), f32),
            pltpu.VMEM((LAYERS, 2, count, width), bf16),
            pltpu.VMEM((LAYERS, groups, rows_f), f32),
            pltpu.VMEM(table.shape, bf16),
            pltpu.VMEM((1, slots), jnp.int32),
            pltpu.VMEM((1, n * slots), jnp.int32),
            pltpu.VMEM((LAYERS, 4, width, width), bf16),
            pltpu.VMEM((LAYERS, groups, 2, rows_f, width), bf16),
            pltpu.VMEM(attn.shape, f32),
            pltpu.VMEM((LAYERS, 2, rows_f // 2, width), f32),
            pltpu.VMEM((SLOTS, count, rows_f), f32),
            pltpu.VMEM((SLOTS, count, rows_f), bf16),
            pltpu.VMEM((count, width), f32),
            pltpu.VMEM((LAYERS, count, width), bf16),
            pltpu.VMEM((LAYERS, count, width), bf16),
            pltpu.VMEM((count, width), f32),
            pltpu.VMEM((n, table.shape[0], count), bf16),
            pltpu.VMEM((n, table.shape[0], count), bf16),
            pltpu.VMEM((n, slots, width), bf16),
            pltpu.VMEM((n, 8, n * slots), f32),
            pltpu.VMEM((n, slots, width), bf16),
            pltpu.VMEM((n, slots, width), bf16),
            dma((2 * LAYERS,)),
            dma((1 + 7 * LAYERS,)),
            dma((2, SLOTS)),
            sems,
            sems,
            core_sems,
            core_sems,
            sems,
            sems,
            dma((2, LAYERS, STRIPS)),
            dma((2, LAYERS, STRIPS)),
            dma((4, n - 1)),
            dma((4, n - 1)),
        ],
        compiler_params=pltpu.CompilerParams(
            collective_id=1, has_side_effects=True, vmem_limit_bytes=VMEM_LIMIT
        ),
        name="forward_layers",
    )(ids, lengths, places, targets, ramp, gains, table, where, out_table, attn, ffn)


def norm_back(grad, values, gain):
    normed, inverse = normed_of(values)
    scaled = grad * gain
    centred = scaled - jnp.mean(scaled, axis=-1, keepdims=True)
    result = inverse * (centred - normed * jnp.mean(scaled * normed, axis=-1, keepdims=True))
    return (
        result,
        jnp.sum(grad * normed, axis=0, keepdims=True),
        jnp.sum(grad, axis=0, keepdims=True),
    )


def backward_kernel(
    n,
    ids_ref,
    lengths_ref,
    losses_ref,
    gains_ref,
    out_grad_ref,
    inputs_ref,
    mixed_ref,
    mid_all,
    grad_ref,
    first_ref,
    proj_all,
    pre_all,
    attn_full,
    ffn_full,
    slope_all,
    act_all,
    attn_sum,
    ffn_sum,
    table_sum,
    out_sum,
    small_out,
    square_out,
    proj,
    pre,
    wa,
    wf,
    slope,
    sum_a,
    sum_f,
    theirs_f,
    land_f,
    land_a,
    ring_a,
    ring_f,
    go_far,
    far_sum,
    far_out,
    far_in,
    state,
    grad_rows,
    left_a,
    left_f,
    right_f,
    spread_a,
    spread_f,
    done_a,
    done_f,
    wa_sem,
    load_sem,
    slope_sem,
    mid_sem,
    core_send,
    core_recv,
    core_free,
    swap_send,
    swap_recv,
    swap_free,
    ring_send,
    ring_recv,
    ring_free,
    pair_send,
    pair_recv,
    across_send,
    across_recv,
    out_sem,
    last_send,
    last_recv,
    small,
    small_in,
    columns_out,
    columns_in,
    table_grad,
    table_half,
    out_half,
    out_done,
    squares,
    square_parts,
    proj_sem,
    small_send,
    small_recv,
    deal_send,
    deal_recv,
    half_send,
    half_recv,
    half_sem,
    norm_send,
    norm_recv,
):
    spot = Spot(n)
    core = spot.core
    other = 1 - core
    rows_a = attn_sum.shape[2]
    rows_f = ffn_sum.shape[2]
    half_f = rows_f // 2
    part_f = half_f // 2
    count = state.shape[0]
    width = attn_sum.shape[3]
    groups = n // 2
    order = (0,) + tuple(range(groups - 1, 0, -1))
    total = LAYERS * groups

    def rows_at(shard, rows):
        return pl.ds(pl.multiple_of(shard * rows, 16), rows)

    def peer(offset):
        return (spot.mp + offset + n) % n

    def remote(source, target, send, recv, device):
        return pltpu.make_async_remote_copy(
            src_ref=source,
            dst_ref=target,
            send_sem=send,
            recv_sem=recv,
            device_id=device,
            device_id_type=MESH,
        )

    def turn_of(turn):
        return LAYERS - 1 - turn // groups, order[turn % groups]

    def load_weights(depth, group):
        return pltpu.make_async_copy(
            ffn_full.at[depth, group], wf.at[group], load_sem.at[0, group]
        )

    def load_act(depth):
        return [
            pltpu.make_async_copy(
                act_all.at[depth, group, far],
                left_f.at[group, 1, pl.ds(far * count, count), :],
                load_sem.at[1 + far, group],
            )
            for group in range(groups)
            for far in range(2)
        ] + [
            pltpu.make_async_copy(
                mid_all.at[depth, far],
                right_f.at[0, pl.ds(far * count, count), :],
                mid_sem.at[far],
            )
            for far in range(2)
        ]

    def load_slope(index):
        depth = LAYERS - 1 - index // (2 * groups)
        far = (index // groups) % 2
        return pltpu.make_async_copy(
            slope_all.at[depth, order[index % groups], far],
            slope.at[index % (groups + 1)],
            slope_sem.at[index % (groups + 1)],
        )

    def load_pre(depth):
        return pltpu.make_async_copy(pre_all.at[depth], pre, proj_sem.at[0])

    def load_proj(depth):
        return pltpu.make_async_copy(proj_all.at[depth], proj, proj_sem.at[1])

    def load_attn(depth):
        return pltpu.make_async_copy(attn_full.at[depth], wa, wa_sem.at[0])

    def core_copy(turn):
        slot = turn % SLOTS
        return remote(
            theirs_f.at[slot],
            land_f.at[slot],
            core_send.at[turn],
            core_recv.at[turn],
            spot.partner,
        )

    def fold(turn):
        depth, group = turn_of(turn)
        core_copy(turn).wait_recv()
        sum_f[depth, group] = (
            sum_f[depth, group].astype(jnp.float32)
            + land_f[turn % SLOTS].astype(jnp.float32)
        ).astype(jnp.bfloat16)
        if turn + SLOTS < total:
            pl.semaphore_signal(
                core_free.at[0], inc=1, device_id=spot.partner, device_id_type=MESH
            )

    def swap_copy(depth, part):
        return remote(
            wa.at[part],
            land_a.at[part],
            swap_send.at[depth, part],
            swap_recv.at[depth, part],
            spot.partner,
        )

    def summed(piece, offset, part):
        kind, depth = piece % 2, piece // 2
        if kind == 0:
            return sum_a.at[depth, part, rows_at(spot.shard(offset), rows_a), :]
        far = abs(offset)
        group, half = (far, int(offset > 0)) if 0 < far < groups else (0, int(far > 0))
        return sum_f.at[depth, group, pl.ds(half * half_f + part * part_f, part_f), :]

    def landed(piece, way, part, step):
        if piece % 2 == 0:
            return ring_a.at[way, part, step - 1]
        return ring_f.at[way, part, step - 1]

    def absorb_rows(into, source):
        into[...] = (into[...].astype(jnp.float32) + source[...].astype(jnp.float32)).astype(
            jnp.bfloat16
        )

    def pair_copy(which, depth, half):
        rows = pl.ds(half * (count // STRIPS), count // STRIPS)
        if which == 0:
            source, target = right_f.at[1, rows, :], go_far.at[depth, rows, :]
        else:
            source, target = far_out.at[depth, rows, :], far_in.at[depth, rows, :]
        return remote(
            source,
            target,
            pair_send.at[which, depth, half],
            pair_recv.at[which, depth, half],
            spot.across,
        )

    def ring_copy(piece, way, part, step):
        offset = last_step(n, way, part) - step + 1
        return remote(
            summed(piece, offset if way == 0 else -offset, part),
            landed(piece, way, part, step),
            ring_send.at[piece, way, part, step - 1],
            ring_recv.at[piece, way, part, step - 1],
            spot.ring[way],
        )

    def ring_start(piece, way, part, step):
        if piece // 2 < LAYERS - 1:
            pl.semaphore_wait(ring_free.at[piece % 2, way, part, step - 1], 1)
        ring_copy(piece, way, part, step).start()

    def release(piece, way, part, step):
        if piece // 2 > 0:
            pl.semaphore_signal(
                ring_free.at[piece % 2, way, part, step - 1],
                inc=1,
                device_id=spot.ring[1 - way],
                device_id_type=MESH,
            )

    def launch(piece, long):
        for way, part in WAYS:
            if (way == part) == long:
                ring_start(piece, way, part, 1)

    def launch_part(piece, part):
        for way in (part, 1 - part):
            ring_start(piece, way, part, 1)

    def relay(piece, step):
        for way, part in WAYS:
            last = last_step(n, way, part)
            if step < last:
                ring_copy(piece, way, part, step).wait_recv()
                offset = last - step if way == 0 else step - last
                absorb_rows(summed(piece, offset, part), landed(piece, way, part, step))
                ring_start(piece, way, part, step + 1)
                release(piece, way, part, step)

    def across_copy(piece):
        depth = piece // 2
        buffer = spread_a if piece % 2 == 0 else spread_f
        return remote(
            buffer.at[depth, 0],
            buffer.at[depth, 1],
            across_send.at[piece],
            across_recv.at[piece],
            spot.across,
        )

    def finish(piece):
        kind, depth = piece % 2, piece // 2
        for part in range(2):
            value = summed(piece, 0, part)[...].astype(jnp.float32)
            for way in range(2):
                step = last_step(n, way, part)
                ring_copy(piece, way, part, step).wait_recv()
                value = value + landed(piece, way, part, step)[...].astype(jnp.float32)
                release(piece, way, part, step)
            value = value.astype(jnp.bfloat16)
            if kind == 0:
                spread_a[depth, 0, part] = value
            else:
                spread_f[depth, 0, pl.ds(part * part_f, part_f), :] = value
        across_copy(piece).start()

    def out_copies(piece):
        kind, depth = piece % 2, piece // 2
        if kind == 0:
            source, target = done_a, attn_sum.at[depth, pl.ds(2 * core, 2)]
        else:
            source, target = done_f, ffn_sum.at[depth, core]
        return (
            pltpu.make_async_copy(source, target, out_sem.at[piece]),
            remote(source, target, last_send.at[piece], last_recv.at[piece], spot.partner),
        )

    def conclude(piece):
        kind, depth = piece % 2, piece // 2
        across_copy(piece).wait_recv()
        if depth < LAYERS - 1:
            local, away = out_copies(piece + 2)
            local.wait()
            away.wait_send()
        row = spot.row
        if kind == 1:
            for side in range(2):
                whose = row + side - 2 * row * side
                rows = pl.ds(pl.multiple_of(whose * half_f, 16), half_f)
                done_f[rows, :] = spread_f[depth, side]
            add_squares(done_f[...].astype(jnp.float32))
        else:
            for part in range(2):
                value = spread_a[depth, 0, part].astype(jnp.float32) + spread_a[
                    depth, 1, part
                ].astype(jnp.float32)
                done_a[part] = value
                add_squares(value)
        for copy in out_copies(piece):
            copy.start()

    load_grad = pltpu.make_async_copy(grad_ref, state, proj_sem.at[2])
    load_grad.start()
    load_first = pltpu.make_async_copy(first_ref, pre.at[0], proj_sem.at[3])
    load_pre(LAYERS - 1).start()
    for group in order:
        load_weights(LAYERS - 1, group).start()
    for index in range(groups + 1):
        load_slope(index).start()
    for copy in load_act(LAYERS - 1):
        copy.start()
    load_attn(LAYERS - 1).start()
    load_proj(LAYERS - 1).start()
    greet([spot.partner, spot.across] + [(spot.dp, peer(offset)) for offset in range(1, n)])
    load_grad.wait()
    lanes = lax.broadcasted_iota(jnp.int32, (1, 128), 1) < 64
    spans = lengths_ref[...].astype(jnp.float32)
    lane = lax.broadcasted_iota(jnp.int32, (1, n), 1)
    length = jnp.sum(jnp.where(lane == spot.mp, spans, 0.0), axis=1, keepdims=True)
    visible = lax.broadcasted_iota(jnp.int32, (1, count), 1).astype(jnp.float32) < length

    def hidden_own(index):
        depth = LAYERS - 1 - index // (2 * groups)
        group = order[index % groups]
        load_slope(index).wait()
        load_weights(depth, group).wait()
        rows = pl.ds(0, count)
        grad_active = dot_nt(right_f[1, rows, :], wf[group, 1])
        grad_hidden = (grad_active * slope[index % (groups + 1)]).astype(jnp.bfloat16)
        left_f[group, 0, rows, :] = grad_hidden
        state[...] += dot_nn(grad_hidden, wf[group, 0])
        if index + groups + 1 < 2 * total:
            load_slope(index + groups + 1).start()

    def hidden_far(index, half):
        depth = LAYERS - 1 - index // (2 * groups)
        group = order[index % groups]
        if half == 0:
            load_slope(index).wait()
        rows = pl.ds(half * (count // STRIPS), count // STRIPS)
        here = pl.ds(count + half * (count // STRIPS), count // STRIPS)
        grad_active = dot_nt(right_f[1, here, :], wf[group, 1])
        grad_hidden = (grad_active * slope[index % (groups + 1), rows, :]).astype(jnp.bfloat16)
        left_f[group, 0, here, :] = grad_hidden
        far_sum[rows, :] += dot_nn(grad_hidden, wf[group, 0])
        if half == STRIPS - 1:
            if depth > 0:
                load_weights(depth - 1, group).start()
            if index + groups + 1 < 2 * total:
                load_slope(index + groups + 1).start()

    def ffn_turn(turn):
        depth, group = turn_of(turn)
        slot = turn % SLOTS
        sum_f[depth, group] = dot_tn(left_f[group, core], right_f[core]).astype(jnp.bfloat16)
        if turn >= SLOTS:
            core_copy(turn - SLOTS).wait_send()
        theirs_f[slot] = dot_tn(left_f[group, other], right_f[other]).astype(jnp.bfloat16)
        if turn >= SLOTS:
            pl.semaphore_wait(core_free.at[0], 1)
        core_copy(turn).start()

    def head_pair(depth, pair):
        columns = pl.ds(pl.multiple_of(pair * 128, 128), 128)
        query = proj[0, :, columns]
        keyed = proj[1, :, columns]
        valued = proj[2, :, columns]
        grad_mixed = grad_rows[4, :, columns]
        outs = []
        for side in range(2):
            mine = lanes if side == 0 else jnp.logical_not(lanes)
            scores = dot_nt(jnp.where(mine, query, jnp.zeros_like(query)), keyed) * 0.125
            scores = jnp.where(visible, scores, masked_score)
            expo = jnp.exp(scores - jnp.max(scores, axis=-1, keepdims=True))
            probs = expo / jnp.sum(expo, axis=-1, keepdims=True)
            grad_probs = dot_nt(jnp.where(mine, grad_mixed, jnp.zeros_like(query)), valued)
            inner = jnp.sum(grad_probs * probs, axis=-1, keepdims=True)
            grad_scores = (probs * (grad_probs - inner)).astype(jnp.bfloat16)
            outs.append(
                (
                    dot_nn(grad_scores, keyed) * 0.125,
                    dot_tn(grad_scores, query) * 0.125,
                    dot_tn(probs.astype(jnp.bfloat16), grad_mixed),
                )
            )
        for which in range(3):
            grad_rows[which, :, columns] = jnp.where(
                lanes, outs[0][which], outs[1][which]
            ).astype(jnp.bfloat16)

    def layer(depth, hooks):
        def at(name):
            for work in hooks.get(name, ()):
                work()

        base = (LAYERS - 1 - depth) * groups
        piece_a, piece_f = 2 * depth, 2 * depth + 1
        load_pre(depth).wait()
        grad_two, small[0, 4 + 4 * depth : 5 + 4 * depth, :], small[0, 5 + 4 * depth : 6 + 4 * depth, :] = norm_back(
            state[...], pre[1], gains_ref[2 + 2 * depth, 0:1, :]
        )
        state[...] = grad_two
        for half in range(STRIPS):
            if depth < LAYERS - 1:
                pair_copy(0, depth + 1, half).wait_send()
            rows = pl.ds(half * (count // STRIPS), count // STRIPS)
            right_f[1, rows, :] = state[rows, :].astype(jnp.bfloat16)
            pair_copy(0, depth, half).start()
        far_sum[...] = jnp.zeros_like(far_sum)
        for step in range(groups):
            hidden_own(2 * base + step)
        at("own")
        for half in range(STRIPS):
            rows = pl.ds(half * (count // STRIPS), count // STRIPS)
            here = pl.ds(count + half * (count // STRIPS), count // STRIPS)
            pair_copy(0, depth, half).wait_recv()
            right_f[1, here, :] = go_far[depth, rows, :]
            for step in range(groups):
                hidden_far(2 * base + groups + step, half)
            far_out[depth, rows, :] = far_sum[rows, :].astype(jnp.bfloat16)
            pair_copy(1, depth, half).start()
            at(("far", half))
        for copy in load_act(depth):
            copy.wait()
        for step in range(groups):
            ffn_turn(base + step)
            if step >= 1:
                fold(base + step - 1)
            if step == 1:
                launch(piece_f, True)
            if step == 2:
                launch(piece_f, False)
            at(("ffn", step))
        fold(base + groups - 1)
        if depth > 0:
            for copy in load_act(depth - 1):
                copy.start()
        for half in range(STRIPS):
            pair_copy(1, depth, half).wait_recv()
        state[...] += far_in[depth].astype(jnp.float32)
        at("middle")
        grad_one, small[0, 2 + 4 * depth : 3 + 4 * depth, :], small[0, 3 + 4 * depth : 4 + 4 * depth, :] = norm_back(
            state[...], pre[0], gains_ref[1 + 2 * depth, 0:1, :]
        )
        if depth > 0:
            load_pre(depth - 1).start()
        else:
            load_first.start()
        state[...] = grad_one
        grad_rows[3] = grad_one.astype(jnp.bfloat16)
        load_attn(depth).wait()
        load_proj(depth).wait()
        grad_rows[4] = dot_nt(grad_rows[3], wa[3]).astype(jnp.bfloat16)

        @pl.loop(0, HEADS // 4)
        def _(pair):
            head_pair(depth, pair)

        at("half")

        @pl.loop(HEADS // 4, HEADS // 2)
        def _(pair):
            head_pair(depth, pair)

        if depth > 0:
            load_proj(depth - 1).start()
        at("heads")
        for which in range(3):
            state[...] += dot_nt(grad_rows[which], wa[which])
        left_a[0] = inputs_ref[depth]
        left_a[1] = mixed_ref[depth]
        for part in range(2):
            left = 0 if part == 0 else other
            wa[part] = dot_tn(left_a[left], grad_rows[2 * other + part]).astype(jnp.bfloat16)
            if depth < LAYERS - 1:
                pl.semaphore_wait(swap_free.at[part], 1)
            swap_copy(depth, part).start()
        for part in range(2):
            left = 0 if part == 0 else core
            sum_a[depth, part] = dot_tn(left_a[left], grad_rows[2 * core + part]).astype(
                jnp.bfloat16
            )
            swap_copy(depth, part).wait_recv()

            @pl.loop(0, n)
            def _(block):
                rows = rows_at(block, rows_a)
                absorb_rows(sum_a.at[depth, part, rows, :], land_a.at[part, rows, :])

            if depth > 0:
                pl.semaphore_signal(
                    swap_free.at[part], inc=1, device_id=spot.partner, device_id_type=MESH
                )
            launch_part(piece_a, part)
            at(("mats", part))

    def reload_attn():
        for part in range(2):
            swap_copy(1, part).wait_send()
        load_attn(0).start()

    def half_copy(which, stage):
        buffer = out_half if which == 0 else table_half
        return remote(
            buffer.at[2 * stage],
            buffer.at[2 * stage + 1],
            half_send.at[which, stage],
            half_recv.at[which, stage],
            spot.partner if stage == 0 else spot.across,
        )

    def half_rows(rows, side):
        return pl.ds(pl.multiple_of(side * (rows // 2), 16), rows // 2)

    def half_start(which, source):
        buffer = out_half if which == 0 else table_half
        buffer[0] = source[half_rows(source.shape[0], other), :].astype(jnp.bfloat16)
        half_copy(which, 0).start()

    def half_fold(which, source):
        buffer = out_half if which == 0 else table_half
        half_copy(which, 0).wait_recv()
        own = source[half_rows(source.shape[0], core), :]
        buffer[2] = (own + buffer[1].astype(jnp.float32)).astype(jnp.bfloat16)
        half_copy(which, 1).start()

    def half_out(which):
        if which == 0:
            source, target = out_done, out_sum.at[half_rows(out_sum.shape[0], core), :]
        else:
            source = table_grad.at[half_rows(table_sum.shape[0], core), :]
            target = table_sum.at[half_rows(table_sum.shape[0], core), :]
        return (
            pltpu.make_async_copy(source, target, half_sem.at[which]),
            remote(source, target, half_send.at[which, 2], half_recv.at[which, 2], spot.partner),
        )

    def add_squares(value):
        squares[...] += jnp.sum(value * value, axis=0, keepdims=True)

    def half_end(which):
        buffer = out_half if which == 0 else table_half
        half_copy(which, 1).wait_recv()
        value = buffer[2].astype(jnp.float32) + buffer[3].astype(jnp.float32)
        if which == 0:
            out_done[...] = value
        else:
            table_grad[half_rows(table_sum.shape[0], core), :] = value
        width = squares.shape[1]
        for start in range(0, value.shape[1], width):
            add_squares(value[:, start : start + width])
        for copy in half_out(which):
            copy.start()

    def small_copy(stage):
        bit = 1 << max(0, stage - 2)
        pair = spot.mp + bit - 2 * bit * ((spot.mp // bit) % 2)
        device = (spot.partner, spot.across)[stage] if stage < 2 else (spot.dp, pair)
        return remote(
            small.at[stage],
            small_in.at[stage],
            small_send.at[stage],
            small_recv.at[stage],
            device,
        )

    def small_next(stage):
        small_copy(stage).wait_recv()
        small[stage + 1] = small[stage] + small_in[stage]
        if stage < 4:
            small_copy(stage + 1).start()

    def deal_copy(offset, arriving):
        source = columns_out.at[peer(offset)]
        target = columns_in.at[peer(-offset) if arriving else spot.mp]
        return remote(
            source,
            target,
            deal_send.at[offset - 1],
            deal_recv.at[offset - 1],
            (spot.dp, peer(offset)),
        )

    def table_blocks(first, last):
        @pl.loop(first, last)
        def _(block):
            row = lax.broadcasted_iota(jnp.int32, (256, 1), 0) + block * 256
            value = jnp.zeros((columns_in.shape[1], 256), jnp.float32)
            for whose in range(n):
                chosen = (row == ids_ref[whose : whose + 1, :]).astype(jnp.bfloat16)
                value = value + dot_nt(columns_in[whose], chosen)
            table_grad[:, pl.ds(pl.multiple_of(block * 256, 256), 256)] = value

    squares[...] = jnp.zeros_like(squares)
    half_start(0, out_grad_ref)
    layer(
        1,
        {
            ("far", 1): [lambda: half_fold(0, out_grad_ref)],
            "half": [lambda: relay(3, 1)],
            ("mats", 1): [lambda: relay(3, 2)],
        },
    )
    layer(
        0,
        {
            "own": [reload_attn],
            ("far", 0): [lambda: relay(3, 3)],
            ("far", 1): [lambda: relay(2, 1), lambda: finish(3)],
            ("ffn", 3): [lambda: relay(2, 2), lambda: conclude(3), lambda: half_end(0)],
            "half": [lambda: relay(2, 3), lambda: relay(1, 1)],
            "heads": [lambda: finish(2), lambda: relay(1, 2)],
        },
    )
    load_first.wait()
    grad_sum, small[0, 0:1, :], small[0, 1:2, :] = norm_back(
        state[...], pre[0], gains_ref[0, 0:1, :]
    )
    width = squares.shape[1]
    lane = lax.broadcasted_iota(jnp.int32, (1, width), 1)
    tally = jnp.sum(losses_ref[...], axis=1, keepdims=True) * (1.0 / n)
    loss, slots = tally[0:1, :], tally[1:2, :]
    small[0, 10:11, :] = jnp.where(lane == 0, loss, jnp.where(lane == 1, slots, 0.0))
    small[0, 11:16, :] = jnp.zeros((5, width), jnp.float32)
    small_copy(0).start()
    turned = grad_sum.T.astype(jnp.bfloat16)
    share = columns_in.shape[1]
    for whose in range(n):
        columns_out[whose] = turned[whose * share : (whose + 1) * share, :]
    for offset in range(1, n):
        deal_copy(offset, False).start()
    columns_in[spot.mp] = columns_out[spot.mp]
    blocks = table_sum.shape[1] // 256
    small_next(0)
    relay(1, 3)
    conclude(2)
    for offset in range(1, n):
        deal_copy(offset, True).wait_recv()
    table_blocks(0, 5)
    relay(0, 1)
    small_next(1)
    table_blocks(5, 10)
    finish(1)
    table_blocks(10, blocks)
    half_start(1, table_grad)
    relay(0, 2)
    small_next(2)
    conclude(1)
    half_fold(1, table_grad)
    relay(0, 3)
    small_next(3)
    half_end(1)
    finish(0)
    small_next(4)
    small_out[...] = small[5]
    conclude(0)

    square = jnp.sum(squares[...], axis=1, keepdims=True)
    square_parts[n] = jnp.broadcast_to(square, square_parts.shape[1:])
    swap = remote(
        square_parts.at[n],
        square_parts.at[n + 1],
        norm_send.at[0],
        norm_recv.at[0],
        spot.partner,
    )
    swap.start()
    swap.wait_recv()
    square_parts[spot.mp] = square_parts[n] + square_parts[n + 1]

    def norm_copy(offset, arriving):
        source = square_parts.at[spot.mp]
        target = square_parts.at[peer(-offset) if arriving else spot.mp]
        return remote(
            source, target, norm_send.at[offset], norm_recv.at[offset], (spot.dp, peer(offset))
        )

    for offset in range(1, n):
        norm_copy(offset, False).start()
    gains_grad = small[5, 0:10, :]
    square = jnp.sum(jnp.sum(gains_grad * gains_grad, axis=0, keepdims=True), axis=1, keepdims=True)
    for offset in range(1, n):
        norm_copy(offset, True).wait_recv()
    for whose in range(n):
        square = square + square_parts[whose, 0:1, :]
    square_out[...] = square

    for half in range(STRIPS):
        pair_copy(0, 0, half).wait_send()
        for depth in range(LAYERS):
            pair_copy(1, depth, half).wait_send()
    swap.wait_send()
    for offset in range(1, n):
        norm_copy(offset, False).wait_send()
        deal_copy(offset, False).wait_send()
    for stage in range(5):
        small_copy(stage).wait_send()
    for which in range(2):
        half_copy(which, 0).wait_send()
        half_copy(which, 1).wait_send()
        local, away = half_out(which)
        local.wait()
        away.wait()
    for turn in range(total - SLOTS, total):
        core_copy(turn).wait_send()
    for part in range(2):
        swap_copy(0, part).wait_send()
    for piece in range(2 * LAYERS):
        for way, part in WAYS:
            for step in range(1, last_step(n, way, part) + 1):
                ring_copy(piece, way, part, step).wait_send()
        across_copy(piece).wait_send()
        local, away = out_copies(piece)
        if piece < 2:
            local.wait()
            away.wait_send()
        away.wait_recv()


def backward_call(
    n, ids, lengths, losses, grad, first, gains, out_grad, kept, attn_full, ffn_full, slope, act, table
):
    inputs, proj, mixed, pre, mid = kept
    count, width = grad.shape
    rows_f = ffn_full.shape[3]
    groups = n // 2
    rows_a = attn_full.shape[2] // n
    rows_v = out_grad.shape[0]
    words, share = table.shape
    f32, bf16 = jnp.float32, jnp.bfloat16
    vmem = pl.BlockSpec(memory_space=pltpu.VMEM)
    anywhere = pl.BlockSpec(memory_space=pl.ANY)
    shape = jax.ShapeDtypeStruct
    dma = pltpu.SemaphoreType.DMA
    regular = pltpu.SemaphoreType.REGULAR
    ring_sems = dma((2 * LAYERS, 2, 2, n // 2))
    return pl.pallas_call(
        functools.partial(backward_kernel, n),
        out_shape=(
            shape((LAYERS, 4, rows_a, width), f32),
            shape((LAYERS, 2, rows_f, width), bf16),
            shape((share, words), f32),
            shape((rows_v, width), f32),
            shape((16, width), f32),
            shape((1, 128), f32),
        ),
        in_specs=[vmem] * 7 + [anywhere] * 9,
        out_specs=(anywhere,) * 4 + (vmem,) * 2,
        scratch_shapes=[
            pltpu.VMEM((3, count, width), bf16),
            pltpu.VMEM((2, count, width), f32),
            pltpu.VMEM((4, width, width), bf16),
            pltpu.VMEM((groups, 2, rows_f, width), bf16),
            pltpu.VMEM((groups + 1, count, rows_f), f32),
            pltpu.VMEM((LAYERS, 2, width, width), bf16),
            pltpu.VMEM((LAYERS, groups, rows_f, width), bf16),
            pltpu.VMEM((SLOTS, rows_f, width), bf16),
            pltpu.VMEM((SLOTS, rows_f, width), bf16),
            pltpu.VMEM((2, width, width), bf16),
            pltpu.VMEM((2, 2, n // 2, rows_a, width), bf16),
            pltpu.VMEM((2, 2, n // 2, rows_f // 4, width), bf16),
            pltpu.VMEM((LAYERS, count, width), bf16),
            pltpu.VMEM((count, width), f32),
            pltpu.VMEM((LAYERS, count, width), bf16),
            pltpu.VMEM((LAYERS, count, width), bf16),
            pltpu.VMEM((count, width), f32),
            pltpu.VMEM((5, count, width), bf16),
            pltpu.VMEM((2, count, width), bf16),
            pltpu.VMEM((groups, 2, 2 * count, rows_f), bf16),
            pltpu.VMEM((2, 2 * count, width), bf16),
            pltpu.VMEM((LAYERS, 2, 2, rows_a, width), bf16),
            pltpu.VMEM((LAYERS, 2, rows_f // 2, width), bf16),
            pltpu.VMEM((2, rows_a, width), f32),
            pltpu.VMEM((rows_f, width), bf16),
            dma((1,)),
            dma((3, groups)),
            dma((groups + 1,)),
            dma((2,)),
            dma((LAYERS * groups,)),
            dma((LAYERS * groups,)),
            regular((1,)),
            dma((LAYERS, 2)),
            dma((LAYERS, 2)),
            regular((2,)),
            ring_sems,
            ring_sems,
            regular((2, 2, 2, n // 2)),
            dma((2, LAYERS, STRIPS)),
            dma((2, LAYERS, STRIPS)),
            dma((2 * LAYERS,)),
            dma((2 * LAYERS,)),
            dma((2 * LAYERS,)),
            dma((2 * LAYERS,)),
            dma((2 * LAYERS,)),
            pltpu.VMEM((6, 16, width), f32),
            pltpu.VMEM((5, 16, width), f32),
            pltpu.VMEM((n, share, count), bf16),
            pltpu.VMEM((n, share, count), bf16),
            pltpu.VMEM((share, words), f32),
            pltpu.VMEM((4, share // 2, words), bf16),
            pltpu.VMEM((4, rows_v // 2, width), bf16),
            pltpu.VMEM((rows_v // 2, width), f32),
            pltpu.VMEM((1, width), f32),
            pltpu.VMEM((n + 2, 8, 128), f32),
            dma((4,)),
            dma((5,)),
            dma((5,)),
            dma((n - 1,)),
            dma((n - 1,)),
            dma((2, 3)),
            dma((2, 3)),
            dma((2,)),
            dma((n,)),
            dma((n,)),
        ],
        compiler_params=pltpu.CompilerParams(
            collective_id=2, has_side_effects=True, vmem_limit_bytes=VMEM_LIMIT
        ),
        name="backward_layers",
    )(
        ids, lengths, losses, gains, out_grad, inputs, mixed, mid, grad, first,
        proj, pre, attn_full, ffn_full, slope, act,
    )


def merged(value, axis, join):
    pieces = jax.tree.map(lambda part: lax.all_gather(part, axis), value)
    head = jax.tree.map(lambda part: part[0], pieces)
    tail = jax.tree.map(lambda part: part[1:], pieces)
    total, _ = lax.scan(lambda total, section: (join(total, section), None), head, tail)
    return total


def sinusoid(count, width):
    places = jnp.arange(count, dtype=jnp.float32)[:, None]
    freqs = jnp.exp(jnp.arange(width // 2, dtype=jnp.float32) * (-2.0 * math.log(10000.0) / width))
    angles = places * freqs[None, :]
    return jnp.concatenate([jnp.sin(angles), jnp.cos(angles)], axis=1)


def layer_norm(values, gain, shift):
    centre = jnp.mean(values, axis=-1, keepdims=True)
    offset = values - centre
    spread = jnp.mean(offset * offset, axis=-1, keepdims=True)
    inverse = lax.rsqrt(spread + norm_eps)
    normed = offset * inverse
    return (normed * gain + shift, (normed, inverse))


def norm_backward(grad, saved, gain):
    normed, inverse = saved
    scaled = grad * gain
    centred = scaled - jnp.mean(scaled, axis=-1, keepdims=True)
    result = inverse * (centred - normed * jnp.mean(scaled * normed, axis=-1, keepdims=True))
    return (result, jnp.stack([jnp.sum(grad * normed, axis=0), jnp.sum(grad, axis=0)]))


def gelu_exact(values):
    return jax.nn.gelu(values, approximate=False)


def gelu_back(hidden, grad):
    unused, pullback = jax.vjp(gelu_exact, hidden)
    return pullback(grad)[0]


def masked_scores(query, keyed, length):
    scale = query.shape[-1] ** (-0.5)
    scores = jnp.einsum("hqe,hke->hqk", query, keyed, preferred_element_type=jnp.float32) * scale
    visible = jnp.arange(keyed.shape[1]) < length
    return jnp.where(visible[None, None, :], scores, masked_score)


def fetch_forward(attn_part, ffn_part):
    return (
        lax.all_gather(attn_part, "mp", axis=1, tiled=True),
        lax.all_gather(ffn_part, "mp", axis=1, tiled=True),
    )


def fetch_backward(attn_part, ffn_part):
    return (
        lax.all_gather(attn_part, "mp", axis=1, tiled=True),
        lax.all_gather(ffn_part, "mp", axis=1, tiled=True),
    )


def reduce_layer(attn_grad, ffn_grad):
    return (
        lax.psum_scatter(attn_grad, "mp", scatter_dimension=1, tiled=True),
        lax.psum_scatter(ffn_grad, "mp", scatter_dimension=1, tiled=True),
    )


def ffn_forward(middle_b, ffn_w, unit_mask):
    hidden = jnp.einsum("td,fd->tf", middle_b, ffn_w[0], preferred_element_type=jnp.float32)
    active = (gelu_exact(hidden) * unit_mask[None, :]).astype(jnp.bfloat16)
    output = jnp.einsum("tf,fd->td", active, ffn_w[1], preferred_element_type=jnp.float32)
    return (hidden, active, output)


def ffn_backward(grad_out, middle_b, hidden, active, ffn_w, unit_mask):
    grad_active = jnp.einsum("td,fd->tf", grad_out, ffn_w[1], preferred_element_type=jnp.float32)
    grad_hidden = gelu_back(hidden, grad_active * unit_mask[None, :]).astype(jnp.bfloat16)
    up_grad = jnp.einsum("tf,td->fd", grad_hidden, middle_b, preferred_element_type=jnp.float32)
    down_grad = jnp.einsum("tf,td->fd", active, grad_out, preferred_element_type=jnp.float32)
    from_ffn = jnp.einsum("tf,fd->td", grad_hidden, ffn_w[0], preferred_element_type=jnp.float32)
    return (jnp.stack([up_grad, down_grad]), from_ffn)


def layer_forward(states, attn_w, ffn_w, pair, length, unit_mask):
    count = states.shape[0]
    inputs = states.astype(jnp.bfloat16)
    projected = jnp.einsum(
        "td,kde->kte", inputs, attn_w[:3], preferred_element_type=jnp.float32
    ).astype(jnp.bfloat16)
    heads = projected.reshape(3, count, HEADS, -1).transpose(0, 2, 1, 3)
    scores = masked_scores(heads[0], heads[1], length)
    peak = jnp.max(scores, axis=-1, keepdims=True)
    expo = jnp.exp(scores - peak)
    total = jnp.sum(expo, axis=-1, keepdims=True)
    log_total = peak + jnp.log(total)
    probs = (expo / total).astype(jnp.bfloat16)
    mixed = jnp.einsum("hqk,hke->hqe", probs, heads[2], preferred_element_type=jnp.float32)
    mixed = mixed.transpose(1, 0, 2).reshape(count, -1).astype(jnp.bfloat16)
    branch = jnp.dot(mixed, attn_w[3], preferred_element_type=jnp.float32)
    middle, norm_one = layer_norm(states + branch, pair[0, 0], pair[0, 1])
    middle_b = middle.astype(jnp.bfloat16)
    hidden, active, output = ffn_forward(middle_b, ffn_w, unit_mask)
    result, norm_two = layer_norm(middle + output, pair[1, 0], pair[1, 1])
    return (result, (inputs, heads, log_total, mixed, norm_one, middle_b, hidden, active, norm_two))


def layer_backward(grad, attn_w, ffn_w, pair, length, unit_mask, kept):
    inputs, heads, log_total, mixed, norm_one, middle_b, hidden, active, norm_two = kept
    count = inputs.shape[0]
    grad_two, pair_two = norm_backward(grad, norm_two, pair[1, 0])
    ffn_grad, from_ffn = ffn_backward(
        grad_two.astype(jnp.bfloat16), middle_b, hidden, active, ffn_w, unit_mask
    )
    grad_one, pair_one = norm_backward(grad_two + from_ffn, norm_one, pair[0, 0])
    grad_branch = grad_one.astype(jnp.bfloat16)
    output_grad = jnp.einsum("td,te->de", mixed, grad_branch, preferred_element_type=jnp.float32)
    grad_mixed = jnp.einsum("te,de->td", grad_branch, attn_w[3], preferred_element_type=jnp.float32)
    grad_mixed = grad_mixed.astype(jnp.bfloat16).reshape(count, HEADS, -1).transpose(1, 0, 2)
    scale = heads.shape[-1] ** (-0.5)
    probs = jnp.exp(masked_scores(heads[0], heads[1], length) - log_total)
    grad_values = jnp.einsum(
        "hqk,hqe->hke", probs.astype(jnp.bfloat16), grad_mixed, preferred_element_type=jnp.float32
    )
    grad_probs = jnp.einsum(
        "hqe,hke->hqk", grad_mixed, heads[2], preferred_element_type=jnp.float32
    )
    grad_scores = probs * (grad_probs - jnp.sum(grad_probs * probs, axis=-1, keepdims=True))
    grad_scores = grad_scores.astype(jnp.bfloat16)
    grad_query = (
        jnp.einsum("hqk,hke->hqe", grad_scores, heads[1], preferred_element_type=jnp.float32)
        * scale
    )
    grad_key = (
        jnp.einsum("hqk,hqe->hke", grad_scores, heads[0], preferred_element_type=jnp.float32)
        * scale
    )
    stacked = (
        jnp.stack([grad_query, grad_key, grad_values]).transpose(0, 2, 1, 3).reshape(3, count, -1)
    )
    stacked = stacked.astype(jnp.bfloat16)
    input_grad = jnp.einsum("td,kte->kde", inputs, stacked, preferred_element_type=jnp.float32)
    from_attn = jnp.einsum("kte,kde->td", stacked, attn_w[:3], preferred_element_type=jnp.float32)
    attn_grad = jnp.concatenate([input_grad, output_grad[None]], axis=0)
    return (grad_one + from_attn, attn_grad, ffn_grad, jnp.stack([pair_one, pair_two]))


def adamw(weight, moment_one, moment_two, grad, decay, rate):
    moment_one = beta_one * moment_one + (1.0 - beta_one) * grad
    moment_two = beta_two * moment_two + (1.0 - beta_two) * grad * grad
    fixed_one = moment_one / (1.0 - beta_one**STEP)
    fixed_two = moment_two / (1.0 - beta_two**STEP)
    weight = weight - rate * (fixed_one / (jnp.sqrt(fixed_two) + adam_eps) + decay * weight)
    return (moment_one, moment_two, weight)


def combine_vocab(first, second):
    peak = jnp.maximum(first[0], second[0])
    total = first[1] * jnp.exp(first[0] - peak) + second[1] * jnp.exp(second[0] - peak)
    return (peak, total, first[2] + second[2])


def local_general(
    tokens,
    lengths,
    places,
    targets,
    ramp,
    attn,
    attn_m,
    attn_v,
    ffn,
    ffn_m,
    ffn_v,
    table,
    table_m,
    table_v,
    out_table,
    out_m,
    out_v,
    gains,
    gains_m,
    gains_v,
):
    rank = lax.axis_index("mp")
    count = tokens.shape[2]
    flat_ids = tokens.reshape(-1)
    all_lengths = lengths.reshape(-1)
    length = lax.dynamic_index_in_dim(all_lengths, rank, keepdims=False)
    masks = jnp.minimum(ramp, RAMP).astype(jnp.float32) / RAMP
    unit_masks = [masks[depth] for depth in range(LAYERS)]
    looked = jnp.take(table, flat_ids, axis=0)
    embedded = lax.all_to_all(looked, "mp", split_axis=0, concat_axis=1, tiled=True)
    states, norm_zero = layer_norm(
        embedded + sinusoid(count, embedded.shape[1]), gains[0, 0], gains[0, 1]
    )
    kept_all = []
    weights_all = []
    for depth in range(LAYERS):
        attn_w, ffn_w = fetch_forward(
            attn[depth].astype(jnp.bfloat16), ffn[depth].astype(jnp.bfloat16)
        )
        states, kept = layer_forward(
            states, attn_w, ffn_w, gains[1 + 2 * depth : 3 + 2 * depth], length, unit_masks[depth]
        )
        kept_all.append(kept)
        weights_all.append(None)
    spots = places.reshape(-1)
    picked = jnp.take(states, spots, axis=0).astype(jnp.bfloat16)
    picked_all = lax.all_gather(picked, "mp", axis=0, tiled=True)
    out_b = out_table.astype(jnp.bfloat16)
    logits = jnp.einsum("rd,vd->rv", picked_all, out_b, preferred_element_type=jnp.float32)
    labels = targets.reshape(-1)
    columns = rank * out_table.shape[0] + jnp.arange(out_table.shape[0])
    hits = (labels[:, None] == columns[None, :]).astype(jnp.float32)
    peak = jnp.max(logits, axis=1)
    expsum = jnp.sum(jnp.exp(logits - peak[:, None]), axis=1)
    target_part = jnp.sum(hits * logits, axis=1)
    peak_all, expsum_all, target_all = merged((peak, expsum, target_part), "mp", combine_vocab)
    log_total = peak_all + jnp.log(expsum_all)
    slot_count = targets.shape[2]
    counted = jnp.maximum(1, all_lengths * slot_count // count)
    valid = (jnp.arange(slot_count)[None, :] < counted[:, None]).reshape(-1)
    loss_pair = jnp.stack(
        [
            jnp.sum(jnp.where(valid, log_total - target_all, 0.0)),
            jnp.sum(counted).astype(jnp.float32),
        ]
    )
    grad_logits = jnp.where(
        valid[:, None], jnp.exp(logits - log_total[:, None]) - hits, 0.0
    ).astype(jnp.bfloat16)
    out_grad = jnp.einsum("rv,rd->vd", grad_logits, picked_all, preferred_element_type=jnp.float32)
    picked_grad = lax.psum_scatter(
        jnp.dot(grad_logits, out_b, preferred_element_type=jnp.float32),
        "mp",
        scatter_dimension=0,
        tiled=True,
    )
    grad = jnp.zeros_like(states).at[spots].add(picked_grad)
    attn_parts = [None] * LAYERS
    ffn_parts = [None] * LAYERS
    pair_grads = [None] * LAYERS
    for depth in reversed(range(LAYERS)):
        attn_w, ffn_w = fetch_backward(
            attn[depth].astype(jnp.bfloat16), ffn[depth].astype(jnp.bfloat16)
        )
        grad, attn_grad, ffn_grad, pair_grad = layer_backward(
            grad,
            attn_w,
            ffn_w,
            gains[1 + 2 * depth : 3 + 2 * depth],
            length,
            unit_masks[depth],
            kept_all[depth],
        )
        attn_parts[depth], ffn_parts[depth] = reduce_layer(attn_grad, ffn_grad)
        pair_grads[depth] = pair_grad
    grad_sum, zero_grad = norm_backward(grad, norm_zero, gains[0, 0])
    returned = lax.all_to_all(grad_sum, "mp", split_axis=1, concat_axis=0, tiled=True)
    table_grad = jnp.zeros_like(table).at[flat_ids].add(returned)
    gains_grad = jnp.concatenate([zero_grad[None]] + pair_grads, axis=0)
    attn_sum, ffn_sum, table_sum, out_sum, gains_part, loss = lax.psum(
        (jnp.stack(attn_parts), jnp.stack(ffn_parts), table_grad, out_grad, gains_grad, loss_pair),
        "dp",
    )
    shard_squares = (
        jnp.sum(attn_sum * attn_sum)
        + jnp.sum(ffn_sum * ffn_sum)
        + jnp.sum(table_sum * table_sum)
        + jnp.sum(out_sum * out_sum)
    )
    square_total, gains_sum = lax.psum((shard_squares, gains_part), "mp")
    grad_norm = jnp.sqrt(square_total + jnp.sum(gains_sum * gains_sum))
    factor = clip_limit / jnp.maximum(grad_norm, clip_limit)
    attn_m_new, attn_v_new, attn_new = adamw(
        attn, attn_m, attn_v, attn_sum * factor, weight_decay, learn_rate
    )
    ffn_m_new, ffn_v_new, ffn_new = adamw(
        ffn, ffn_m, ffn_v, ffn_sum * factor, weight_decay, learn_rate
    )
    table_m_new, table_v_new, table_new = adamw(
        table, table_m, table_v, table_sum * factor, weight_decay, learn_rate
    )
    out_m_new, out_v_new, out_new = adamw(
        out_table, out_m, out_v, out_sum * factor, weight_decay, learn_rate
    )
    gains_m_new, gains_v_new, gains_new = adamw(
        gains, gains_m, gains_v, gains_sum * factor, 0.0, gain_rate
    )
    return (
        loss,
        grad_norm.reshape(1),
        attn_m_new,
        attn_v_new,
        attn_new,
        ffn_m_new,
        ffn_v_new,
        ffn_new,
        table_m_new,
        table_v_new,
        table_new,
        out_m_new,
        out_v_new,
        out_new,
        gains_m_new,
        gains_v_new,
        gains_new,
    )


def local(
    tokens,
    lengths,
    places,
    targets,
    ramp,
    attn,
    attn_m,
    attn_v,
    ffn,
    ffn_m,
    ffn_v,
    table,
    table_m,
    table_v,
    out_table,
    out_m,
    out_v,
    gains,
    gains_m,
    gains_v,
):
    n = tokens.shape[1]
    where = jnp.asarray(positions(tokens.shape[2], gains.shape[2]))
    attn_full, ffn_full, first, *kept, slope, act, grad, out_grad, losses = forward_call(
        n, tokens[0], lengths, places[0], targets[0], ramp, gains, table.T, where, out_table, attn, ffn
    )
    attn_sum, ffn_sum, table_turned, out_sum, small, square = backward_call(
        n, tokens[0], lengths, losses, grad, first, gains, out_grad, kept, attn_full, ffn_full, slope, act, table
    )
    table_sum = table_turned.T
    ffn_sum = ffn_sum.astype(jnp.float32)
    gains_sum = small[:10].reshape(gains.shape)
    grad_norm = jnp.sqrt(square[0, 0])
    factor = clip_limit / jnp.maximum(grad_norm, clip_limit)
    attn_m_new, attn_v_new, attn_new = adamw(
        attn, attn_m, attn_v, attn_sum * factor, weight_decay, learn_rate
    )
    ffn_m_new, ffn_v_new, ffn_new = adamw(
        ffn, ffn_m, ffn_v, ffn_sum * factor, weight_decay, learn_rate
    )
    table_m_new, table_v_new, table_new = adamw(
        table, table_m, table_v, table_sum * factor, weight_decay, learn_rate
    )
    out_m_new, out_v_new, out_new = adamw(
        out_table, out_m, out_v, out_sum * factor, weight_decay, learn_rate
    )
    gains_m_new, gains_v_new, gains_new = adamw(
        gains, gains_m, gains_v, gains_sum * factor, 0.0, gain_rate
    )
    return (
        small[10, :2],
        grad_norm.reshape(1),
        attn_m_new,
        attn_v_new,
        attn_new,
        ffn_m_new,
        ffn_v_new,
        ffn_new,
        table_m_new,
        table_v_new,
        table_new,
        out_m_new,
        out_v_new,
        out_new,
        gains_m_new,
        gains_v_new,
        gains_new,
    )


def solution(mesh):
    in_specs = (
        P("dp", None, None),
        P("dp", None),
        P("dp", "mp", None),
        P("dp", None, None),
        P(),
        P(None, None, "mp", None),
        P(None, None, "mp", None),
        P(None, None, "mp", None),
        P(None, None, "mp", None),
        P(None, None, "mp", None),
        P(None, None, "mp", None),
        P(None, "mp"),
        P(None, "mp"),
        P(None, "mp"),
        P("mp", None),
        P("mp", None),
        P("mp", None),
        P(),
        P(),
        P(),
    )
    out_specs = (
        P(),
        P(),
        P(None, None, "mp", None),
        P(None, None, "mp", None),
        P(None, None, "mp", None),
        P(None, None, "mp", None),
        P(None, None, "mp", None),
        P(None, None, "mp", None),
        P(None, "mp"),
        P(None, "mp"),
        P(None, "mp"),
        P("mp", None),
        P("mp", None),
        P("mp", None),
        P(),
        P(),
        P(),
    )
    fits = mesh.shape['mp'] == 8 and mesh.shape['dp'] == 4
    chosen = local if fits else local_general
    return jax.shard_map(chosen, mesh=mesh, in_specs=in_specs, out_specs=out_specs, check_vma=False)
```

```python
import functools
import math

import jax
import jax.numpy as jnp
import numpy as np
from jax import lax
from jax.experimental import pallas as pl
from jax.experimental.pallas import tpu as pltpu
from jax.sharding import PartitionSpec as P

HEADS = 12
LAYERS = 2
STEP = 10
RAMP = 4


norm_eps = 1e-05
beta_one = 0.9
beta_two = 0.999
learn_rate = 0.02
gain_rate = 0.3
weight_decay = 0.01
adam_eps = 1e-08
clip_limit = 1.0
masked_score = -1000000000.0


MESH = pl.DeviceIdType.MESH
VMEM_LIMIT = 62 * 1024 * 1024
SLOTS = 3
STRIPS = 2


def dot_nn(left, right):
    return lax.dot_general(
        left, right, (((1,), (0,)), ((), ())), preferred_element_type=jnp.float32
    )


def dot_nt(left, right):
    return lax.dot_general(
        left, right, (((1,), (1,)), ((), ())), preferred_element_type=jnp.float32
    )


def dot_tn(left, right):
    return lax.dot_general(
        left, right, (((0,), (0,)), ((), ())), preferred_element_type=jnp.float32
    )


def positions(count, width):
    angles = np.arange(count)[:, None] * np.exp(
        np.arange(width // 2) * (-2.0 * math.log(10000.0) / width)
    )
    return np.concatenate([np.sin(angles), np.cos(angles)], axis=1).astype(np.float32)


def ring_index(place, n):
    late = place // (n // 2)
    return (1 - late) * 2 * place + late * (2 * (n - 1 - place) + 1)


def ring_place(index, n):
    odd = index % 2
    return (1 - odd) * (index // 2) + odd * (n - 1 - index // 2)


class Spot:
    def __init__(self, n):
        self.n = n
        self.dp = lax.axis_index("dp")
        self.mp = lax.axis_index("mp")
        self.core = self.dp % 2
        self.row = self.dp // 2
        self.place = ring_place(self.mp, n)
        self.partner = (self.dp + 1 - 2 * self.core, self.mp)
        self.across = ((self.dp + 2) % 4, self.mp)
        self.ring = (
            (self.dp, ring_index((self.place + 1) % n, n)),
            (self.dp, ring_index((self.place + n - 1) % n, n)),
        )

    def shard(self, offset):
        return ring_index((self.place + offset + self.n) % self.n, self.n)


def greet(devices):
    barrier = pltpu.get_barrier_semaphore()
    for device in devices:
        pl.semaphore_signal(barrier, inc=1, device_id=device, device_id_type=MESH)
    pl.semaphore_wait(barrier, len(devices))


def last_step(n, way, part):
    return n // 2 if way == part else n // 2 - 1


WAYS = ((0, 0), (1, 1), (0, 1), (1, 0))


def ring_columns(row, width, cut):
    return pl.ds(pl.multiple_of(row * cut, 128), width - cut)


def edge_columns(row, width, cut):
    return pl.ds(pl.multiple_of(row * (width - cut), 128), cut)


def cut_of(width, share):
    return 128 * (width // 128 // share)


def normed_of(values):
    centre = jnp.mean(values, axis=-1, keepdims=True)
    offset = values - centre
    spread = jnp.mean(offset * offset, axis=-1, keepdims=True)
    inverse = lax.rsqrt(spread + norm_eps)
    return offset * inverse, inverse


def forward_kernel(
    n,
    ids_ref,
    lengths_ref,
    places_ref,
    targets_ref,
    ramp_ref,
    gains_ref,
    table_ref,
    where_ref,
    out_sh,
    attn_sh,
    ffn_sh,
    attn_full,
    ffn_full,
    first_out,
    inputs_out,
    proj_out,
    mixed_out,
    pre_out,
    mid_out,
    slope_ref,
    act_ref,
    grad_ref,
    out_grad_ref,
    loss_ref,
    first_ref,
    out_ref,
    inputs_ref,
    proj_ref,
    mixed_ref,
    pre_ref,
    mid_ref,
    mask_ref,
    table_b,
    places_row,
    labels_row,
    wa,
    wf,
    raw_a,
    raw_f,
    slope,
    act,
    far_sum,
    far_out,
    far_in,
    state,
    row_out,
    row_in,
    picked,
    stats,
    back_out,
    back_in,
    raw_sem,
    late_sem,
    early_sem,
    kept_sem,
    ring_send,
    ring_recv,
    core_send,
    core_recv,
    across_send,
    across_recv,
    pair_send,
    pair_recv,
    fan_send,
    fan_recv,
    beside_send,
    beside_recv,
):
    spot = Spot(n)
    core = spot.core
    rows_a = attn_sh.shape[2]
    rows_f = ffn_sh.shape[2]
    half_f = rows_f // 2
    part_f = half_f // 2
    steps = n // 2
    count, width = first_ref.shape
    share_e = table_ref.shape[0]
    words = table_ref.shape[1]
    slots = places_row.shape[1]
    slot_count = places_ref.shape[1]

    def rows_at(shard, rows):
        return pl.ds(pl.multiple_of(shard * rows, 16), rows)

    def remote(source, target, send, recv, device):
        return pltpu.make_async_remote_copy(
            src_ref=source,
            dst_ref=target,
            send_sem=send,
            recv_sem=recv,
            device_id=device,
            device_id_type=MESH,
        )

    def slot_f(way, step):
        if step == 0:
            return 0, 0
        return (0, 1) if step == steps else (step, way)

    def chunk_f(piece, way, part, step, side):
        group, half = slot_f(way, step)
        return wf.at[piece // 2, group, side, pl.ds(half * half_f + part * part_f, part_f), :]

    def chunk_a(piece, shard, part, side, edge):
        cut = cut_of(width, 3)
        if edge is None:
            columns = ring_columns(spot.row, width, cut)
        else:
            columns = edge_columns(edge, width, cut)
        return wa.at[piece // 2, 2 * side + part, rows_at(shard, rows_a), columns]

    def sign(way):
        return -1 if way == 0 else 1

    def ring_copy(piece, way, part, step, arriving):
        if piece % 2 == 0:
            target = chunk_a(piece, spot.shard(sign(way) * (step - 1 + arriving)), part, core, None)
            source = target
        else:
            target = chunk_f(piece, way, part, step, core)
            source = target if arriving else chunk_f(piece, way, part, step - 1, core)
        return remote(
            source,
            target,
            ring_send.at[piece, way, part, step - 1],
            ring_recv.at[piece, way, part, step - 1],
            spot.ring[way],
        )

    def core_copy(piece, way, part, step, side, edge):
        if piece % 2 == 0:
            target = chunk_a(piece, spot.shard(sign(way) * step), part, side, edge)
        else:
            target = chunk_f(piece, way, part, step, side)
        lane = 0 if edge is None else 1
        return remote(
            target,
            target,
            core_send.at[lane, piece, way, part, step - 1],
            core_recv.at[lane, piece, way, part, step - 1],
            spot.partner,
        )

    def across_copy(piece, way, part, step, row):
        target = chunk_a(piece, spot.shard(sign(way) * step), part, core, row)
        return remote(
            target,
            target,
            across_send.at[piece, way, part, step - 1],
            across_recv.at[piece, way, part, step - 1],
            spot.across,
        )

    def half_at(half):
        return pl.ds(half * (count // STRIPS), count // STRIPS)

    def pair_copy(which, depth, half):
        rows = half_at(half)
        if which == 0:
            source, target = mid_ref.at[depth, 0, rows, :], mid_ref.at[depth, 1, rows, :]
        else:
            source, target = far_out.at[depth, rows, :], far_in.at[depth, rows, :]
        return remote(
            source,
            target,
            pair_send.at[which, depth, half],
            pair_recv.at[which, depth, half],
            spot.across,
        )

    def peer(offset):
        return (spot.mp + offset + n) % n

    def fan_copy(which, offset, source, target):
        return remote(
            source,
            target,
            fan_send.at[which, offset - 1],
            fan_recv.at[which, offset - 1],
            (spot.dp, peer(offset)),
        )

    def share(which, buffer, offset):
        return fan_copy(which, offset, buffer.at[spot.mp], buffer.at[spot.mp])

    def arrived(which, buffer, offset):
        return fan_copy(which, offset, buffer.at[peer(-offset)], buffer.at[peer(-offset)])

    def deal(which, source, target, offset):
        return fan_copy(which, offset, source.at[peer(offset)], target.at[spot.mp])

    def raw_copy(piece):
        kind, depth = piece % 2, piece // 2
        if kind == 0:
            return pltpu.make_async_copy(attn_sh.at[depth], raw_a.at[depth], raw_sem.at[piece])
        rows = pl.ds(pl.multiple_of(spot.row * half_f, 16), half_f)
        return pltpu.make_async_copy(ffn_sh.at[depth, :, rows, :], raw_f.at[depth], raw_sem.at[piece])

    def take_own(piece):
        kind, depth = piece % 2, piece // 2
        raw_copy(piece).wait()
        if kind == 0:
            for which in range(4):
                wa[depth, which, rows_at(spot.mp, rows_a), :] = raw_a[depth, which].astype(
                    jnp.bfloat16
                )
        else:
            for which in range(2):
                wf[depth, 0, which, 0:half_f, :] = raw_f[depth, which].astype(jnp.bfloat16)

    def launch(piece):
        for way, part in WAYS:
            ring_copy(piece, way, part, 1, 0).start()

    def chains(step):
        return [(way, part) for way, part in WAYS if step <= last_step(n, way, part)]

    def pass_on(piece, step):
        for way, part in chains(step):
            ring_copy(piece, way, part, step, 1).wait_recv()
            if step < last_step(n, way, part):
                ring_copy(piece, way, part, step + 1, 0).start()
            if piece % 2 == 0:
                across_copy(piece, way, part, step, spot.row).start()
            core_copy(piece, way, part, step, core, None).start()

    def pass_edge(piece, step):
        for way, part in chains(step):
            across_copy(piece, way, part, step, 1 - spot.row).wait_recv()
            core_copy(piece, way, part, step, core, 1 - spot.row).start()

    def settle(piece, step):
        for way, part in chains(step):
            core_copy(piece, way, part, step, 1 - core, None).wait_recv()
            if piece % 2 == 0:
                core_copy(piece, way, part, step, 1 - core, 1 - spot.row).wait_recv()

    out_copies = []

    def write_out(source, target):
        copy = pltpu.make_async_copy(source, target, early_sem.at[len(out_copies)])
        copy.start()
        out_copies.append(copy)

    def look_up(offset):
        whose = peer(offset)
        tokens = ids_ref[pl.ds(whose, 1), :]

        size = 768

        def block(index, total):
            start = pl.multiple_of(index * size, 128)
            word = lax.broadcasted_iota(jnp.int32, (size, 1), 0) + start
            chosen = (word == tokens).astype(jnp.bfloat16)
            return total + dot_nn(table_b[:, pl.ds(start, size)], chosen)

        found = lax.fori_loop(
            0, words // size, block, jnp.zeros((share_e, count), jnp.float32)
        )
        row_out[whose] = found.astype(jnp.bfloat16)
        if offset > 0:
            deal(0, row_out, row_in, offset).start()

    raw_copy(0).start()
    late = (
        pltpu.make_async_copy(where_ref, first_ref, late_sem.at[0]),
        pltpu.make_async_copy(out_sh, out_ref, late_sem.at[1]),
    )
    for copy in late:
        copy.start()
    for piece in range(1, 2 * LAYERS):
        raw_copy(piece).start()
    greet([spot.partner, spot.across] + [(spot.dp, peer(offset)) for offset in range(1, n)])
    take_own(0)
    launch(0)
    for depth in range(LAYERS):
        for index in range(n):
            offset = (0, steps)[index] if index < 2 else (index // 2) * (2 * (index % 2) - 1)
            start = pl.multiple_of(spot.shard(offset) * rows_f, 128)
            grown = jnp.minimum(ramp_ref[depth : depth + 1, pl.ds(start, rows_f)], RAMP)
            grown = grown.astype(jnp.float32) / RAMP
            lanes_to = pl.ds((index % 2) * half_f, half_f)
            mask_ref[depth, index // 2 : index // 2 + 1, lanes_to] = jnp.where(
                spot.row == 0, grown[:, 0:half_f], grown[:, half_f:rows_f]
            )
    table_b[...] = table_ref[...].astype(jnp.bfloat16)
    places_row[...] = jnp.full_like(places_row, -1)
    places_row[0:1, 0:slot_count] = places_ref[...]
    labels_row[...] = jnp.full_like(labels_row, -1)
    for whose in range(n):
        labels_row[0:1, whose * slots : whose * slots + slot_count] = targets_ref[
            whose : whose + 1, :
        ]
    spans = lengths_ref[...].astype(jnp.float32)
    lane = lax.broadcasted_iota(jnp.int32, (1, n), 1)
    length = jnp.sum(jnp.where(lane == spot.mp, spans, 0.0), axis=1, keepdims=True)
    visible = lax.broadcasted_iota(jnp.int32, (1, count), 1).astype(jnp.float32) < length
    counted = jnp.maximum(jnp.floor(spans * (slot_count / count)), 1.0)
    lane = lax.broadcasted_iota(jnp.int32, (1, n * slots), 1)
    limit = jnp.zeros((1, n * slots), jnp.float32)
    for whose in range(n):
        limit = jnp.where(
            lane >= whose * slots, counted[:, whose : whose + 1] + whose * slots, limit
        )
    valid = lane.astype(jnp.float32) < limit
    loss_ref[1:2, :] = valid.astype(jnp.float32)
    for offset in range(1, 4):
        look_up(offset)
    pass_on(0, 1)
    for offset in range(4, 7):
        look_up(offset)
    pass_on(0, 2)
    pass_edge(0, 1)
    take_own(1)
    launch(1)
    look_up(7)
    look_up(0)
    row_in[spot.mp] = row_out[spot.mp]
    pass_on(0, 3)
    pass_edge(0, 2)
    for offset in range(1, n):
        arrived(0, row_in, offset).wait_recv()
    late[0].wait()
    first_ref[...] += row_in[...].reshape(width, count).astype(jnp.float32).T
    write_out(first_ref, first_out)
    normed, _ = normed_of(first_ref[...])
    state[...] = normed * gains_ref[0, 0:1, :] + gains_ref[0, 1:2, :]
    take_own(2)
    take_own(3)
    pass_on(0, 4)
    pass_edge(0, 3)

    lanes = lax.broadcasted_iota(jnp.int32, (1, 128), 1) < 64

    def head_pair(depth, pair):
        columns = pl.ds(pl.multiple_of(pair * 128, 128), 128)
        query = proj_ref[depth, 0, :, columns]
        keyed = proj_ref[depth, 1, :, columns]
        valued = proj_ref[depth, 2, :, columns]
        outs = []
        for side in range(2):
            mine = lanes if side == 0 else jnp.logical_not(lanes)
            scores = dot_nt(jnp.where(mine, query, jnp.zeros_like(query)), keyed) * 0.125
            scores = jnp.where(visible, scores, masked_score)
            expo = jnp.exp(scores - jnp.max(scores, axis=-1, keepdims=True))
            total = jnp.sum(expo, axis=-1, keepdims=True)
            outs.append(dot_nn((expo / total).astype(jnp.bfloat16), valued))
        mixed_ref[depth, :, columns] = jnp.where(lanes, outs[0], outs[1]).astype(jnp.bfloat16)

    def kept_copies(turn, depth, group, far, start, size):
        slot = turn % SLOTS
        here, there = pl.ds(0, size), pl.ds(start, size)
        return (
            pltpu.make_async_copy(
                slope.at[slot, here, :],
                slope_ref.at[depth, group, far, there, :],
                kept_sem.at[0, slot],
            ),
            pltpu.make_async_copy(
                act.at[slot, here, :],
                act_ref.at[depth, group, far, there, :],
                kept_sem.at[1, slot],
            ),
        )

    turns = []

    def ffn_block(depth, group, far, start, size):
        turn = len(turns)
        turns.append((depth, group, far, start, size))
        if turn >= SLOTS:
            for copy in kept_copies(turn, *turns[turn - SLOTS]):
                copy.wait()
        slot, rows, here = turn % SLOTS, pl.ds(start, size), pl.ds(0, size)
        hidden = dot_nt(mid_ref[depth, far, rows, :], wf[depth, group, 0])
        spread = 0.5 * (1.0 + lax.erf(hidden * (0.5**0.5)))
        mask = mask_ref[depth, group : group + 1, :]
        bell = jnp.exp(hidden * hidden * -0.5) * (1.0 / math.sqrt(2.0 * math.pi))
        slope[slot, here, :] = (spread + hidden * bell) * mask
        active = (hidden * spread * mask).astype(jnp.bfloat16)
        act[slot, here, :] = active
        for copy in kept_copies(*((turn,) + turns[turn])):
            copy.start()
        if far:
            far_sum[rows, :] += dot_nn(active, wf[depth, group, 1])
        else:
            pre_ref[depth, 1, rows, :] += dot_nn(active, wf[depth, group, 1])

    def ffn_own(depth, group):
        ffn_block(depth, group, 0, 0, count)

    def ffn_far(depth, group, half):
        ffn_block(depth, group, 1, half * (count // STRIPS), count // STRIPS)

    for depth in range(LAYERS):
        piece_a, piece_f = 2 * depth, 2 * depth + 1
        more = depth + 1 < LAYERS
        if depth > 0:
            pass_on(piece_a, 3)
            pass_edge(piece_a, 2)
            pass_on(piece_a, 4)
            pass_edge(piece_a, 3)
        pass_edge(piece_a, 4)
        for step in range(1, steps + 1):
            settle(piece_a, step)
        write_out(wa.at[depth], attn_full.at[depth])
        inputs = state[...].astype(jnp.bfloat16)
        inputs_ref[depth] = inputs
        for which in range(3):
            proj_ref[depth, which] = dot_nn(inputs, wa[depth, which]).astype(jnp.bfloat16)
        pass_on(piece_f, 1)

        @pl.loop(0, HEADS // 2)
        def _(pair):
            head_pair(depth, pair)

        pre_ref[depth, 0] = state[...] + dot_nn(mixed_ref[depth], wa[depth, 3])
        normed, _ = normed_of(pre_ref[depth, 0])
        middle = (
            normed * gains_ref[1 + 2 * depth, 0:1, :] + gains_ref[1 + 2 * depth, 1:2, :]
        )
        for half in range(STRIPS):
            mid_ref[depth, 0, half_at(half), :] = middle[
                half * (count // STRIPS) : (half + 1) * (count // STRIPS), :
            ].astype(jnp.bfloat16)
            pair_copy(0, depth, half).start()
        pre_ref[depth, 1] = middle
        far_sum[...] = jnp.zeros_like(far_sum)
        write_out(inputs_ref.at[depth], inputs_out.at[depth])
        write_out(proj_ref.at[depth], proj_out.at[depth])
        write_out(mixed_ref.at[depth], mixed_out.at[depth])
        pass_on(piece_f, 2)
        settle(piece_f, 1)
        ffn_own(depth, 1)
        pass_on(piece_f, 3)
        if more:
            launch(piece_a + 2)
        settle(piece_f, 2)
        ffn_own(depth, 2)
        for half in range(STRIPS):
            pair_copy(0, depth, half).wait_recv()
            ffn_far(depth, 1, half)
            ffn_far(depth, 2, half)
        write_out(mid_ref.at[depth], mid_out.at[depth])
        settle(piece_f, 3)
        for half in range(STRIPS):
            ffn_far(depth, 3, half)
        pass_on(piece_f, 4)
        settle(piece_f, 4)
        for half in range(STRIPS):
            ffn_far(depth, 0, half)
            far_out[depth, half_at(half), :] = far_sum[half_at(half), :].astype(jnp.bfloat16)
            pair_copy(1, depth, half).start()
        if more:
            pass_on(piece_a + 2, 1)
        ffn_own(depth, 3)
        ffn_own(depth, 0)
        write_out(wf.at[depth], ffn_full.at[depth])
        if more:
            launch(piece_f + 2)
            pass_on(piece_a + 2, 2)
            pass_edge(piece_a + 2, 1)
        for half in range(STRIPS):
            pair_copy(1, depth, half).wait_recv()
        pre_ref[depth, 1] += far_in[depth].astype(jnp.float32)
        write_out(pre_ref.at[depth], pre_out.at[depth])
        normed, _ = normed_of(pre_ref[depth, 1])
        state[...] = normed * gains_ref[2 + 2 * depth, 0:1, :] + gains_ref[2 + 2 * depth, 1:2, :]

    spots = (
        lax.broadcasted_iota(jnp.int32, (count, 1), 0) == places_row[...]
    ).astype(jnp.bfloat16)
    picked[spot.mp] = dot_tn(spots, state[...].astype(jnp.bfloat16)).astype(jnp.bfloat16)
    beside = spot.mp + 1 - 2 * (spot.mp % 2)

    def beside_copy(step, arriving):
        whose = ((beside if arriving else spot.mp) - 2 * step + n) % n
        return remote(
            picked.at[whose],
            picked.at[whose],
            beside_send.at[step],
            beside_recv.at[step],
            (spot.dp, beside),
        )

    for step in range(1, n // 2):
        share(1, picked, 2 * step).start()
    beside_copy(0, False).start()
    late[1].wait()
    out_b = out_ref[...].astype(jnp.bfloat16)
    rows_v = out_ref.shape[0]
    hits = (
        labels_row[...] == spot.mp * rows_v + lax.broadcasted_iota(jnp.int32, (rows_v, 1), 0)
    ).astype(jnp.float32)
    for step in range(1, n // 2):
        arrived(1, picked, 2 * step).wait_recv()
        beside_copy(step, False).start()
    for step in range(n // 2):
        beside_copy(step, True).wait_recv()
    picked_all = picked[...].reshape(n * slots, -1)
    logits = dot_nt(out_b, picked_all)
    peak = jnp.max(logits, axis=0, keepdims=True)
    expsum = jnp.sum(jnp.exp(logits - peak), axis=0, keepdims=True)
    stats[spot.mp, 0:1, :] = peak
    stats[spot.mp, 1:2, :] = expsum
    stats[spot.mp, 2:3, :] = jnp.sum(hits * logits, axis=0, keepdims=True)
    for offset in range(1, n):
        share(2, stats, offset).start()
    for offset in range(1, n):
        arrived(2, stats, offset).wait_recv()
    peak = stats[0, 0:1, :]
    for whose in range(1, n):
        peak = jnp.maximum(peak, stats[whose, 0:1, :])
    expsum = stats[0, 1:2, :] * jnp.exp(stats[0, 0:1, :] - peak)
    target = stats[0, 2:3, :]
    for whose in range(1, n):
        expsum = expsum + stats[whose, 1:2, :] * jnp.exp(stats[whose, 0:1, :] - peak)
        target = target + stats[whose, 2:3, :]
    log_total = peak + jnp.log(expsum)
    loss_ref[0:1, :] = jnp.where(valid, log_total - target, 0.0)
    grad_logits = jnp.where(valid, jnp.exp(logits - log_total) - hits, 0.0).astype(jnp.bfloat16)
    picked_grad = dot_tn(grad_logits, out_b).astype(jnp.bfloat16)
    for whose in range(n):
        back_out[whose] = picked_grad[whose * slots : (whose + 1) * slots, :]
    for offset in range(1, n):
        deal(3, back_out, back_in, offset).start()
    back_in[spot.mp] = back_out[spot.mp]
    out_grad_ref[...] = dot_nn(grad_logits, picked_all)
    for offset in range(1, n):
        arrived(3, back_in, offset).wait_recv()
    summed = back_in[0].astype(jnp.float32)
    for whose in range(1, n):
        summed = summed + back_in[whose].astype(jnp.float32)
    high = summed.astype(jnp.bfloat16)
    low = (summed - high.astype(jnp.float32)).astype(jnp.bfloat16)
    grad_ref[...] = dot_nn(spots, high) + dot_nn(spots, low)

    for piece in range(2 * LAYERS):
        for way, part in WAYS:
            for step in range(1, last_step(n, way, part) + 1):
                ring_copy(piece, way, part, step, 0).wait_send()
                core_copy(piece, way, part, step, core, None).wait_send()
                if piece % 2 == 0:
                    across_copy(piece, way, part, step, spot.row).wait_send()
                    core_copy(piece, way, part, step, core, 1 - spot.row).wait_send()
    for offset in range(1, n):
        deal(0, row_out, row_in, offset).wait_send()
        share(2, stats, offset).wait_send()
        deal(3, back_out, back_in, offset).wait_send()
    for step in range(n // 2):
        beside_copy(step, False).wait_send()
        if step > 0:
            share(1, picked, 2 * step).wait_send()
    for depth in range(LAYERS):
        for half in range(STRIPS):
            pair_copy(0, depth, half).wait_send()
            pair_copy(1, depth, half).wait_send()
    for turn in range(len(turns) - SLOTS, len(turns)):
        for copy in kept_copies(turn, *turns[turn]):
            copy.wait()
    for copy in out_copies:
        copy.wait()


def forward_call(
    n, ids, lengths, places, targets, ramp, gains, table, where, out_table, attn, ffn
):
    count, width = where.shape
    rows_f = ffn.shape[2]
    slots = 32 * -(-places.shape[1] // 32)
    groups = n // 2
    f32, bf16 = jnp.float32, jnp.bfloat16
    vmem = pl.BlockSpec(memory_space=pltpu.VMEM)
    anywhere = pl.BlockSpec(memory_space=pl.ANY)
    shape = jax.ShapeDtypeStruct
    dma = pltpu.SemaphoreType.DMA
    sems = dma((2 * LAYERS, 2, 2, n // 2))
    core_sems = dma((2, 2 * LAYERS, 2, 2, n // 2))
    return pl.pallas_call(
        functools.partial(forward_kernel, n),
        out_shape=(
            shape((LAYERS, 4, width, width), bf16),
            shape((LAYERS, groups, 2, rows_f, width), bf16),
            shape((count, width), f32),
            shape((LAYERS, count, width), bf16),
            shape((LAYERS, 3, count, width), bf16),
            shape((LAYERS, count, width), bf16),
            shape((LAYERS, 2, count, width), f32),
            shape((LAYERS, 2, count, width), bf16),
            shape((LAYERS, groups, 2, count, rows_f), f32),
            shape((LAYERS, groups, 2, count, rows_f), bf16),
            shape((count, width), f32),
            shape(out_table.shape, f32),
            shape((2, n * slots), f32),
        ),
        in_specs=[vmem] * 7 + [anywhere] * 4,
        out_specs=(anywhere,) * 10 + (vmem,) * 3,
        scratch_shapes=[
            pltpu.VMEM((count, width), f32),
            pltpu.VMEM(out_table.shape, f32),
            pltpu.VMEM((LAYERS, count, width), bf16),
            pltpu.VMEM((LAYERS, 3, count, width), bf16),
            pltpu.VMEM((LAYERS, count, width), bf16),
            pltpu.VMEM((LAYERS, 2, count, width), f32),
            pltpu.VMEM((LAYERS, 2, count, width), bf16),
            pltpu.VMEM((LAYERS, groups, rows_f), f32),
            pltpu.VMEM(table.shape, bf16),
            pltpu.VMEM((1, slots), jnp.int32),
            pltpu.VMEM((1, n * slots), jnp.int32),
            pltpu.VMEM((LAYERS, 4, width, width), bf16),
            pltpu.VMEM((LAYERS, groups, 2, rows_f, width), bf16),
            pltpu.VMEM(attn.shape, f32),
            pltpu.VMEM((LAYERS, 2, rows_f // 2, width), f32),
            pltpu.VMEM((SLOTS, count, rows_f), f32),
            pltpu.VMEM((SLOTS, count, rows_f), bf16),
            pltpu.VMEM((count, width), f32),
            pltpu.VMEM((LAYERS, count, width), bf16),
            pltpu.VMEM((LAYERS, count, width), bf16),
            pltpu.VMEM((count, width), f32),
            pltpu.VMEM((n, table.shape[0], count), bf16),
            pltpu.VMEM((n, table.shape[0], count), bf16),
            pltpu.VMEM((n, slots, width), bf16),
            pltpu.VMEM((n, 8, n * slots), f32),
            pltpu.VMEM((n, slots, width), bf16),
            pltpu.VMEM((n, slots, width), bf16),
            dma((2 * LAYERS,)),
            dma((2,)),
            dma((1 + 7 * LAYERS,)),
            dma((2, SLOTS)),
            sems,
            sems,
            core_sems,
            core_sems,
            sems,
            sems,
            dma((2, LAYERS, STRIPS)),
            dma((2, LAYERS, STRIPS)),
            dma((4, n - 1)),
            dma((4, n - 1)),
            dma((n // 2,)),
            dma((n // 2,)),
        ],
        compiler_params=pltpu.CompilerParams(
            collective_id=1, has_side_effects=True, vmem_limit_bytes=VMEM_LIMIT
        ),
        name="forward_layers",
    )(ids, lengths, places, targets, ramp, gains, table, where, out_table, attn, ffn)


def norm_back(grad, values, gain):
    normed, inverse = normed_of(values)
    scaled = grad * gain
    centred = scaled - jnp.mean(scaled, axis=-1, keepdims=True)
    result = inverse * (centred - normed * jnp.mean(scaled * normed, axis=-1, keepdims=True))
    return (
        result,
        jnp.sum(grad * normed, axis=0, keepdims=True),
        jnp.sum(grad, axis=0, keepdims=True),
    )


def backward_kernel(
    n,
    ids_ref,
    lengths_ref,
    losses_ref,
    gains_ref,
    out_grad_all,
    inputs_all,
    mixed_all,
    mid_all,
    grad_ref,
    first_ref,
    proj_all,
    pre_all,
    attn_full,
    ffn_full,
    slope_all,
    act_all,
    attn_sum,
    ffn_sum,
    table_sum,
    out_sum,
    loss_out,
    gains_out,
    norm_out,
    out_grad_ref,
    proj,
    pre,
    wa,
    wf,
    slope,
    sum_a,
    sum_f,
    theirs_f,
    land_f,
    land_a,
    ring_a,
    ring_f,
    go_far,
    far_sum,
    far_out,
    far_in,
    state,
    grad_rows,
    left_a,
    left_f,
    right_f,
    spread_a,
    spread_f,
    done_a,
    done_f,
    wa_sem,
    load_sem,
    slope_sem,
    mid_sem,
    left_sem,
    core_send,
    core_recv,
    core_free,
    swap_send,
    swap_recv,
    swap_free,
    ring_send,
    ring_recv,
    ring_free,
    pair_send,
    pair_recv,
    across_send,
    across_recv,
    out_sem,
    last_send,
    last_recv,
    small,
    small_in,
    columns_out,
    columns_in,
    table_grad,
    table_half,
    out_half,
    out_done,
    squares,
    square_parts,
    proj_sem,
    small_send,
    small_recv,
    deal_send,
    deal_recv,
    half_send,
    half_recv,
    half_sem,
    norm_send,
    norm_recv,
):
    spot = Spot(n)
    core = spot.core
    other = 1 - core
    rows_a = attn_sum.shape[2]
    rows_f = ffn_sum.shape[2]
    half_f = rows_f // 2
    part_f = half_f // 2
    count = state.shape[0]
    width = attn_sum.shape[3]
    groups = n // 2
    order = (0,) + tuple(range(groups - 1, 0, -1))
    total = LAYERS * groups

    def rows_at(shard, rows):
        return pl.ds(pl.multiple_of(shard * rows, 16), rows)

    def peer(offset):
        return (spot.mp + offset + n) % n

    def remote(source, target, send, recv, device):
        return pltpu.make_async_remote_copy(
            src_ref=source,
            dst_ref=target,
            send_sem=send,
            recv_sem=recv,
            device_id=device,
            device_id_type=MESH,
        )

    def turn_of(turn):
        return LAYERS - 1 - turn // groups, order[turn % groups]

    def load_weights(depth, group):
        return pltpu.make_async_copy(
            ffn_full.at[depth, group], wf.at[group], load_sem.at[0, group]
        )

    def load_act(depth):
        return [
            pltpu.make_async_copy(
                act_all.at[depth, group, far],
                left_f.at[group, 1, pl.ds(far * count, count), :],
                load_sem.at[1 + far, group],
            )
            for group in range(groups)
            for far in range(2)
        ] + [
            pltpu.make_async_copy(
                mid_all.at[depth, far],
                right_f.at[0, pl.ds(far * count, count), :],
                mid_sem.at[far],
            )
            for far in range(2)
        ]

    def load_slope(index):
        depth = LAYERS - 1 - index // (2 * groups)
        far = (index // groups) % 2
        return pltpu.make_async_copy(
            slope_all.at[depth, order[index % groups], far],
            slope.at[index % (groups + 1)],
            slope_sem.at[index % (groups + 1)],
        )

    def load_pre(depth):
        return pltpu.make_async_copy(pre_all.at[depth], pre, proj_sem.at[0])

    def load_left(depth):
        return (
            pltpu.make_async_copy(inputs_all.at[depth], left_a.at[0], left_sem.at[0]),
            pltpu.make_async_copy(mixed_all.at[depth], left_a.at[1], left_sem.at[1]),
        )

    def load_proj(depth):
        return pltpu.make_async_copy(proj_all.at[depth], proj, proj_sem.at[1])

    def load_attn(depth):
        return pltpu.make_async_copy(attn_full.at[depth], wa, wa_sem.at[0])

    def core_copy(turn):
        slot = turn % SLOTS
        return remote(
            theirs_f.at[slot],
            land_f.at[slot],
            core_send.at[turn],
            core_recv.at[turn],
            spot.partner,
        )

    def fold(turn):
        depth, group = turn_of(turn)
        core_copy(turn).wait_recv()
        sum_f[depth, group] = (
            sum_f[depth, group].astype(jnp.float32)
            + land_f[turn % SLOTS].astype(jnp.float32)
        ).astype(jnp.bfloat16)
        if turn + SLOTS < total:
            pl.semaphore_signal(
                core_free.at[0], inc=1, device_id=spot.partner, device_id_type=MESH
            )

    def swap_copy(depth, part):
        return remote(
            wa.at[part],
            land_a.at[part],
            swap_send.at[depth, part],
            swap_recv.at[depth, part],
            spot.partner,
        )

    def summed(piece, offset, part):
        kind, depth = piece % 2, piece // 2
        if kind == 0:
            return sum_a.at[depth, part, rows_at(spot.shard(offset), rows_a), :]
        far = abs(offset)
        group, half = (far, int(offset > 0)) if 0 < far < groups else (0, int(far > 0))
        return sum_f.at[depth, group, pl.ds(half * half_f + part * part_f, part_f), :]

    def landed(piece, way, part, step):
        if piece % 2 == 0:
            return ring_a.at[way, part, step - 1]
        return ring_f.at[way, part, step - 1]

    def absorb_rows(into, source):
        into[...] = (into[...].astype(jnp.float32) + source[...].astype(jnp.float32)).astype(
            jnp.bfloat16
        )

    def pair_copy(which, depth, half):
        rows = pl.ds(half * (count // STRIPS), count // STRIPS)
        if which == 0:
            source, target = right_f.at[1, rows, :], go_far.at[depth, rows, :]
        else:
            source, target = far_out.at[depth, rows, :], far_in.at[depth, rows, :]
        return remote(
            source,
            target,
            pair_send.at[which, depth, half],
            pair_recv.at[which, depth, half],
            spot.across,
        )

    def ring_copy(piece, way, part, step):
        offset = last_step(n, way, part) - step + 1
        return remote(
            summed(piece, offset if way == 0 else -offset, part),
            landed(piece, way, part, step),
            ring_send.at[piece, way, part, step - 1],
            ring_recv.at[piece, way, part, step - 1],
            spot.ring[way],
        )

    def ring_start(piece, way, part, step):
        if piece // 2 < LAYERS - 1:
            pl.semaphore_wait(ring_free.at[piece % 2, way, part, step - 1], 1)
        ring_copy(piece, way, part, step).start()

    def release(piece, way, part, step):
        if piece // 2 > 0:
            pl.semaphore_signal(
                ring_free.at[piece % 2, way, part, step - 1],
                inc=1,
                device_id=spot.ring[1 - way],
                device_id_type=MESH,
            )

    def launch(piece, long):
        for way, part in WAYS:
            if (way == part) == long:
                ring_start(piece, way, part, 1)

    def launch_part(piece, part):
        for way in (part, 1 - part):
            ring_start(piece, way, part, 1)

    def relay(piece, step):
        for way, part in WAYS:
            last = last_step(n, way, part)
            if step < last:
                ring_copy(piece, way, part, step).wait_recv()
                offset = last - step if way == 0 else step - last
                absorb_rows(summed(piece, offset, part), landed(piece, way, part, step))
                ring_start(piece, way, part, step + 1)
                release(piece, way, part, step)

    def across_copy(piece, part):
        depth = piece // 2
        if piece % 2 == 0:
            source, target = spread_a.at[depth, 0, part], spread_a.at[depth, 1, part]
        else:
            rows = pl.ds(part * part_f, part_f)
            source, target = spread_f.at[depth, 0, rows, :], spread_f.at[depth, 1, rows, :]
        return remote(
            source,
            target,
            across_send.at[piece, part],
            across_recv.at[piece, part],
            spot.across,
        )

    def finish(piece):
        kind, depth = piece % 2, piece // 2
        for part in range(2):
            value = summed(piece, 0, part)[...].astype(jnp.float32)
            for way in range(2):
                step = last_step(n, way, part)
                ring_copy(piece, way, part, step).wait_recv()
                value = value + landed(piece, way, part, step)[...].astype(jnp.float32)
                release(piece, way, part, step)
            value = value.astype(jnp.bfloat16)
            if kind == 0:
                spread_a[depth, 0, part] = value
            else:
                spread_f[depth, 0, pl.ds(part * part_f, part_f), :] = value
            across_copy(piece, part).start()

    def out_copies(piece):
        kind, depth = piece % 2, piece // 2
        if kind == 0:
            source, target = done_a, attn_sum.at[depth, pl.ds(2 * core, 2)]
        else:
            source, target = done_f, ffn_sum.at[depth, core]
        return (
            pltpu.make_async_copy(source, target, out_sem.at[piece]),
            remote(source, target, last_send.at[piece], last_recv.at[piece], spot.partner),
        )

    def conclude(piece):
        kind, depth = piece % 2, piece // 2
        for part in range(2):
            across_copy(piece, part).wait_recv()
        if depth < LAYERS - 1:
            local, away = out_copies(piece + 2)
            local.wait()
            away.wait_send()
        row = spot.row
        if kind == 1:
            for side in range(2):
                whose = row + side - 2 * row * side
                rows = pl.ds(pl.multiple_of(whose * half_f, 16), half_f)
                done_f[rows, :] = spread_f[depth, side]
            add_squares(done_f[...].astype(jnp.float32))
        else:
            for part in range(2):
                value = spread_a[depth, 0, part].astype(jnp.float32) + spread_a[
                    depth, 1, part
                ].astype(jnp.float32)
                done_a[part] = value
                add_squares(value)
        for copy in out_copies(piece):
            copy.start()

    load_grad = pltpu.make_async_copy(grad_ref, state, proj_sem.at[2])
    load_grad.start()
    load_first = pltpu.make_async_copy(first_ref, pre.at[0], proj_sem.at[3])
    load_pre(LAYERS - 1).start()
    for group in order:
        load_weights(LAYERS - 1, group).start()
    for index in range(groups + 1):
        load_slope(index).start()
    for copy in load_act(LAYERS - 1):
        copy.start()
    load_attn(LAYERS - 1).start()
    load_proj(LAYERS - 1).start()
    load_out = pltpu.make_async_copy(out_grad_all, out_grad_ref, left_sem.at[2])
    load_out.start()
    for copy in load_left(LAYERS - 1):
        copy.start()
    greet(
        [spot.partner, spot.across]
        + [(whose, peer(offset)) for offset in range(1, n) for whose in (spot.dp, spot.partner[0])]
    )
    load_grad.wait()
    lanes = lax.broadcasted_iota(jnp.int32, (1, 128), 1) < 64
    spans = lengths_ref[...].astype(jnp.float32)
    lane = lax.broadcasted_iota(jnp.int32, (1, n), 1)
    length = jnp.sum(jnp.where(lane == spot.mp, spans, 0.0), axis=1, keepdims=True)
    visible = lax.broadcasted_iota(jnp.int32, (1, count), 1).astype(jnp.float32) < length

    def hidden_own(index):
        depth = LAYERS - 1 - index // (2 * groups)
        group = order[index % groups]
        load_slope(index).wait()
        load_weights(depth, group).wait()
        rows = pl.ds(0, count)
        grad_active = dot_nt(right_f[1, rows, :], wf[group, 1])
        grad_hidden = (grad_active * slope[index % (groups + 1)]).astype(jnp.bfloat16)
        left_f[group, 0, rows, :] = grad_hidden
        state[...] += dot_nn(grad_hidden, wf[group, 0])
        if index + groups + 1 < 2 * total:
            load_slope(index + groups + 1).start()

    def hidden_far(index, half):
        depth = LAYERS - 1 - index // (2 * groups)
        group = order[index % groups]
        if half == 0:
            load_slope(index).wait()
        rows = pl.ds(half * (count // STRIPS), count // STRIPS)
        here = pl.ds(count + half * (count // STRIPS), count // STRIPS)
        grad_active = dot_nt(right_f[1, here, :], wf[group, 1])
        grad_hidden = (grad_active * slope[index % (groups + 1), rows, :]).astype(jnp.bfloat16)
        left_f[group, 0, here, :] = grad_hidden
        far_sum[rows, :] += dot_nn(grad_hidden, wf[group, 0])
        if half == STRIPS - 1:
            if depth > 0:
                load_weights(depth - 1, group).start()
            if index + groups + 1 < 2 * total:
                load_slope(index + groups + 1).start()

    def ffn_turn(turn):
        depth, group = turn_of(turn)
        slot = turn % SLOTS
        sum_f[depth, group] = dot_tn(left_f[group, core], right_f[core]).astype(jnp.bfloat16)
        if turn >= SLOTS:
            core_copy(turn - SLOTS).wait_send()
        theirs_f[slot] = dot_tn(left_f[group, other], right_f[other]).astype(jnp.bfloat16)
        if turn >= SLOTS:
            pl.semaphore_wait(core_free.at[0], 1)
        core_copy(turn).start()

    def head_pair(depth, pair):
        columns = pl.ds(pl.multiple_of(pair * 128, 128), 128)
        query = proj[0, :, columns]
        keyed = proj[1, :, columns]
        valued = proj[2, :, columns]
        grad_mixed = grad_rows[4, :, columns]
        outs = []
        for side in range(2):
            mine = lanes if side == 0 else jnp.logical_not(lanes)
            scores = dot_nt(jnp.where(mine, query, jnp.zeros_like(query)), keyed) * 0.125
            scores = jnp.where(visible, scores, masked_score)
            expo = jnp.exp(scores - jnp.max(scores, axis=-1, keepdims=True))
            probs = expo / jnp.sum(expo, axis=-1, keepdims=True)
            grad_probs = dot_nt(jnp.where(mine, grad_mixed, jnp.zeros_like(query)), valued)
            inner = jnp.sum(grad_probs * probs, axis=-1, keepdims=True)
            grad_scores = (probs * (grad_probs - inner)).astype(jnp.bfloat16)
            outs.append(
                (
                    dot_nn(grad_scores, keyed) * 0.125,
                    dot_tn(grad_scores, query) * 0.125,
                    dot_tn(probs.astype(jnp.bfloat16), grad_mixed),
                )
            )
        for which in range(3):
            grad_rows[which, :, columns] = jnp.where(
                lanes, outs[0][which], outs[1][which]
            ).astype(jnp.bfloat16)

    def layer(depth, hooks):
        def at(name):
            for work in hooks.get(name, ()):
                work()

        base = (LAYERS - 1 - depth) * groups
        piece_a, piece_f = 2 * depth, 2 * depth + 1
        load_pre(depth).wait()
        grad_two, small[0, 4 + 4 * depth : 5 + 4 * depth, :], small[0, 5 + 4 * depth : 6 + 4 * depth, :] = norm_back(
            state[...], pre[1], gains_ref[2 + 2 * depth, 0:1, :]
        )
        state[...] = grad_two
        for half in range(STRIPS):
            if depth < LAYERS - 1:
                pair_copy(0, depth + 1, half).wait_send()
            rows = pl.ds(half * (count // STRIPS), count // STRIPS)
            right_f[1, rows, :] = state[rows, :].astype(jnp.bfloat16)
            pair_copy(0, depth, half).start()
        far_sum[...] = jnp.zeros_like(far_sum)
        for step in range(groups):
            hidden_own(2 * base + step)
        at("own")
        for half in range(STRIPS):
            rows = pl.ds(half * (count // STRIPS), count // STRIPS)
            here = pl.ds(count + half * (count // STRIPS), count // STRIPS)
            pair_copy(0, depth, half).wait_recv()
            right_f[1, here, :] = go_far[depth, rows, :]
            for step in range(groups):
                hidden_far(2 * base + groups + step, half)
            far_out[depth, rows, :] = far_sum[rows, :].astype(jnp.bfloat16)
            pair_copy(1, depth, half).start()
            at(("far", half))
        for copy in load_act(depth):
            copy.wait()
        for step in range(groups):
            ffn_turn(base + step)
            if step >= 1:
                fold(base + step - 1)
            if step == 1:
                launch(piece_f, True)
            if step == 2:
                launch(piece_f, False)
            at(("ffn", step))
        fold(base + groups - 1)
        if depth > 0:
            for copy in load_act(depth - 1):
                copy.start()
        for half in range(STRIPS):
            pair_copy(1, depth, half).wait_recv()
        state[...] += far_in[depth].astype(jnp.float32)
        at("middle")
        grad_one, small[0, 2 + 4 * depth : 3 + 4 * depth, :], small[0, 3 + 4 * depth : 4 + 4 * depth, :] = norm_back(
            state[...], pre[0], gains_ref[1 + 2 * depth, 0:1, :]
        )
        if depth > 0:
            load_pre(depth - 1).start()
        else:
            load_first.start()
        state[...] = grad_one
        grad_rows[3] = grad_one.astype(jnp.bfloat16)
        load_attn(depth).wait()
        load_proj(depth).wait()
        grad_rows[4] = dot_nt(grad_rows[3], wa[3]).astype(jnp.bfloat16)

        @pl.loop(0, HEADS // 4)
        def _(pair):
            head_pair(depth, pair)

        at("half")

        @pl.loop(HEADS // 4, HEADS // 2)
        def _(pair):
            head_pair(depth, pair)

        if depth > 0:
            load_proj(depth - 1).start()
        at("heads")
        for which in range(3):
            state[...] += dot_nt(grad_rows[which], wa[which])
        for copy in load_left(depth):
            copy.wait()
        for part in range(2):
            left = 0 if part == 0 else other
            wa[part] = dot_tn(left_a[left], grad_rows[2 * other + part]).astype(jnp.bfloat16)
            if depth < LAYERS - 1:
                pl.semaphore_wait(swap_free.at[part], 1)
            swap_copy(depth, part).start()
        for part in range(2):
            left = 0 if part == 0 else core
            sum_a[depth, part] = dot_tn(left_a[left], grad_rows[2 * core + part]).astype(
                jnp.bfloat16
            )
            swap_copy(depth, part).wait_recv()

            @pl.loop(0, n)
            def _(block):
                rows = rows_at(block, rows_a)
                absorb_rows(sum_a.at[depth, part, rows, :], land_a.at[part, rows, :])

            if depth > 0:
                pl.semaphore_signal(
                    swap_free.at[part], inc=1, device_id=spot.partner, device_id_type=MESH
                )
            launch_part(piece_a, part)
            if depth > 0 and part == 1:
                for copy in load_left(depth - 1):
                    copy.start()
            at(("mats", part))

    def reload_attn():
        for part in range(2):
            swap_copy(1, part).wait_send()
        load_attn(0).start()

    def half_copy(which, stage):
        buffer = out_half if which == 0 else table_half
        return remote(
            buffer.at[2 * stage],
            buffer.at[2 * stage + 1],
            half_send.at[which, stage],
            half_recv.at[which, stage],
            spot.partner if stage == 0 else spot.across,
        )

    def half_rows(rows, side):
        return pl.ds(pl.multiple_of(side * (rows // 2), 16), rows // 2)

    def half_start(which, source):
        buffer = out_half if which == 0 else table_half
        buffer[0] = source[half_rows(source.shape[0], other), :].astype(jnp.bfloat16)
        half_copy(which, 0).start()

    def half_fold(which, source):
        buffer = out_half if which == 0 else table_half
        half_copy(which, 0).wait_recv()
        own = source[half_rows(source.shape[0], core), :]
        buffer[2] = (own + buffer[1].astype(jnp.float32)).astype(jnp.bfloat16)
        half_copy(which, 1).start()

    def half_out(which):
        if which == 0:
            source, target = out_done, out_sum.at[half_rows(out_sum.shape[0], core), :]
        else:
            source = table_grad.at[half_rows(table_sum.shape[0], core), :]
            target = table_sum.at[half_rows(table_sum.shape[0], core), :]
        return (
            pltpu.make_async_copy(source, target, half_sem.at[which]),
            remote(source, target, half_send.at[which, 2], half_recv.at[which, 2], spot.partner),
        )

    def add_squares(value):
        squares[...] += jnp.sum(value * value, axis=0, keepdims=True)

    def half_end(which):
        buffer = out_half if which == 0 else table_half
        half_copy(which, 1).wait_recv()
        value = buffer[2].astype(jnp.float32) + buffer[3].astype(jnp.float32)
        if which == 0:
            out_done[...] = value
        else:
            table_grad[half_rows(table_sum.shape[0], core), :] = value
        width = squares.shape[1]
        for start in range(0, value.shape[1], width):
            add_squares(value[:, start : start + width])
        for copy in half_out(which):
            copy.start()

    def small_copy(stage):
        bit = 1 << max(0, stage - 2)
        pair = spot.mp + bit - 2 * bit * ((spot.mp // bit) % 2)
        device = (spot.partner, spot.across)[stage] if stage < 2 else (spot.dp, pair)
        return remote(
            small.at[stage],
            small_in.at[stage],
            small_send.at[stage],
            small_recv.at[stage],
            device,
        )

    def small_next(stage):
        small_copy(stage).wait_recv()
        small[stage + 1] = small[stage] + small_in[stage]
        if stage < 4:
            small_copy(stage + 1).start()

    def deal_copy(offset, arriving):
        source = columns_out.at[peer(offset)]
        target = columns_in.at[peer(-offset) if arriving else spot.mp]
        return remote(
            source,
            target,
            deal_send.at[offset - 1],
            deal_recv.at[offset - 1],
            (spot.dp, peer(offset)),
        )

    def table_blocks(first, last):
        @pl.loop(first, last)
        def _(block):
            row = lax.broadcasted_iota(jnp.int32, (256, 1), 0) + block * 256
            value = jnp.zeros((columns_in.shape[1], 256), jnp.float32)
            for whose in range(n):
                chosen = (row == ids_ref[whose : whose + 1, :]).astype(jnp.bfloat16)
                value = value + dot_nt(columns_in[whose], chosen)
            table_grad[:, pl.ds(pl.multiple_of(block * 256, 256), 256)] = value

    squares[...] = jnp.zeros_like(squares)
    layer(
        1,
        {
            "own": [load_out.wait, lambda: half_start(0, out_grad_ref)],
            ("far", 1): [lambda: half_fold(0, out_grad_ref)],
            "half": [lambda: relay(3, 1)],
            ("mats", 1): [lambda: relay(3, 2)],
        },
    )
    layer(
        0,
        {
            "own": [reload_attn],
            ("far", 0): [lambda: relay(3, 3)],
            ("far", 1): [lambda: relay(2, 1), lambda: finish(3)],
            ("ffn", 3): [lambda: relay(2, 2), lambda: conclude(3), lambda: half_end(0)],
            "half": [lambda: relay(2, 3), lambda: relay(1, 1)],
            "heads": [lambda: finish(2), lambda: relay(1, 2)],
        },
    )
    load_first.wait()
    grad_sum, small[0, 0:1, :], small[0, 1:2, :] = norm_back(
        state[...], pre[0], gains_ref[0, 0:1, :]
    )
    width = squares.shape[1]
    lane = lax.broadcasted_iota(jnp.int32, (1, width), 1)
    tally = jnp.sum(losses_ref[...], axis=1, keepdims=True) * (1.0 / n)
    loss, slots = tally[0:1, :], tally[1:2, :]
    small[0, 10:11, :] = jnp.where(lane == 0, loss, jnp.where(lane == 1, slots, 0.0))
    small[0, 11:16, :] = jnp.zeros((5, width), jnp.float32)
    small_copy(0).start()
    turned = grad_sum.T.astype(jnp.bfloat16)
    share = columns_in.shape[1]
    for whose in range(n):
        columns_out[whose] = turned[whose * share : (whose + 1) * share, :]
    for offset in range(1, n):
        deal_copy(offset, False).start()
    columns_in[spot.mp] = columns_out[spot.mp]
    blocks = table_sum.shape[1] // 256
    small_next(0)
    relay(1, 3)
    conclude(2)
    for offset in range(1, n):
        deal_copy(offset, True).wait_recv()
    table_blocks(0, 5)
    relay(0, 1)
    small_next(1)
    table_blocks(5, 10)
    finish(1)
    table_blocks(10, blocks)
    half_start(1, table_grad)
    relay(0, 2)
    small_next(2)
    conclude(1)
    half_fold(1, table_grad)
    relay(0, 3)
    small_next(3)
    half_end(1)
    finish(0)
    small_next(4)
    loss_out[...] = small[5, 10:11, 0:128]
    for index in range(5):
        gains_out[index] = small[5, 2 * index : 2 * index + 2, :]
    conclude(0)

    square = jnp.sum(squares[...], axis=1, keepdims=True)
    square_parts[core * n + spot.mp] = jnp.broadcast_to(square, square_parts.shape[1:])

    def norm_copy(side, offset, arriving):
        own = square_parts.at[core * n + spot.mp]
        whose = (core + side - 2 * core * side) * n + peer(-offset)
        return remote(
            own,
            square_parts.at[whose] if arriving else own,
            norm_send.at[side, offset],
            norm_recv.at[side, offset],
            ((spot.dp, spot.partner[0])[side], peer(offset)),
        )

    far_squares = [(side, offset) for offset in range(n) for side in range(2)][1:]
    for side, offset in far_squares:
        norm_copy(side, offset, False).start()
    gains_grad = small[5, 0:10, :]
    square = jnp.sum(jnp.sum(gains_grad * gains_grad, axis=0, keepdims=True), axis=1, keepdims=True)
    for side, offset in far_squares:
        norm_copy(side, offset, True).wait_recv()
    for whose in range(2 * n):
        square = square + square_parts[whose, 0:1, :]
    grad_norm = jnp.sqrt(square)
    norm_out[0:1, :] = grad_norm
    norm_out[1:2, :] = clip_limit / jnp.maximum(grad_norm, clip_limit)

    for half in range(STRIPS):
        pair_copy(0, 0, half).wait_send()
        for depth in range(LAYERS):
            pair_copy(1, depth, half).wait_send()
    for side, offset in far_squares:
        norm_copy(side, offset, False).wait_send()
    for offset in range(1, n):
        deal_copy(offset, False).wait_send()
    for stage in range(5):
        small_copy(stage).wait_send()
    for which in range(2):
        half_copy(which, 0).wait_send()
        half_copy(which, 1).wait_send()
        local, away = half_out(which)
        local.wait()
        away.wait()
    for turn in range(total - SLOTS, total):
        core_copy(turn).wait_send()
    for part in range(2):
        swap_copy(0, part).wait_send()
    for piece in range(2 * LAYERS):
        for way, part in WAYS:
            for step in range(1, last_step(n, way, part) + 1):
                ring_copy(piece, way, part, step).wait_send()
        for part in range(2):
            across_copy(piece, part).wait_send()
        local, away = out_copies(piece)
        if piece < 2:
            local.wait()
            away.wait_send()
        away.wait_recv()


def backward_call(
    n, ids, lengths, losses, grad, first, gains, out_grad, kept, attn_full, ffn_full, slope, act, table
):
    inputs, proj, mixed, pre, mid = kept
    count, width = grad.shape
    rows_f = ffn_full.shape[3]
    groups = n // 2
    rows_a = attn_full.shape[2] // n
    rows_v = out_grad.shape[0]
    words, share = table.shape
    f32, bf16 = jnp.float32, jnp.bfloat16
    vmem = pl.BlockSpec(memory_space=pltpu.VMEM)
    anywhere = pl.BlockSpec(memory_space=pl.ANY)
    shape = jax.ShapeDtypeStruct
    dma = pltpu.SemaphoreType.DMA
    regular = pltpu.SemaphoreType.REGULAR
    ring_sems = dma((2 * LAYERS, 2, 2, n // 2))
    return pl.pallas_call(
        functools.partial(backward_kernel, n),
        out_shape=(
            shape((LAYERS, 4, rows_a, width), f32),
            shape((LAYERS, 2, rows_f, width), bf16),
            shape((share, words), f32),
            shape((rows_v, width), f32),
            shape((1, 128), f32),
            shape(gains.shape, f32),
            shape((2, 128), f32),
        ),
        in_specs=[vmem] * 4 + [anywhere] * 12,
        out_specs=(anywhere,) * 4 + (vmem,) * 3,
        scratch_shapes=[
            pltpu.VMEM(out_grad.shape, f32),
            pltpu.VMEM((3, count, width), bf16),
            pltpu.VMEM((2, count, width), f32),
            pltpu.VMEM((4, width, width), bf16),
            pltpu.VMEM((groups, 2, rows_f, width), bf16),
            pltpu.VMEM((groups + 1, count, rows_f), f32),
            pltpu.VMEM((LAYERS, 2, width, width), bf16),
            pltpu.VMEM((LAYERS, groups, rows_f, width), bf16),
            pltpu.VMEM((SLOTS, rows_f, width), bf16),
            pltpu.VMEM((SLOTS, rows_f, width), bf16),
            pltpu.VMEM((2, width, width), bf16),
            pltpu.VMEM((2, 2, n // 2, rows_a, width), bf16),
            pltpu.VMEM((2, 2, n // 2, rows_f // 4, width), bf16),
            pltpu.VMEM((LAYERS, count, width), bf16),
            pltpu.VMEM((count, width), f32),
            pltpu.VMEM((LAYERS, count, width), bf16),
            pltpu.VMEM((LAYERS, count, width), bf16),
            pltpu.VMEM((count, width), f32),
            pltpu.VMEM((5, count, width), bf16),
            pltpu.VMEM((2, count, width), bf16),
            pltpu.VMEM((groups, 2, 2 * count, rows_f), bf16),
            pltpu.VMEM((2, 2 * count, width), bf16),
            pltpu.VMEM((LAYERS, 2, 2, rows_a, width), bf16),
            pltpu.VMEM((LAYERS, 2, rows_f // 2, width), bf16),
            pltpu.VMEM((2, rows_a, width), f32),
            pltpu.VMEM((rows_f, width), bf16),
            dma((1,)),
            dma((3, groups)),
            dma((groups + 1,)),
            dma((2,)),
            dma((3,)),
            dma((LAYERS * groups,)),
            dma((LAYERS * groups,)),
            regular((1,)),
            dma((LAYERS, 2)),
            dma((LAYERS, 2)),
            regular((2,)),
            ring_sems,
            ring_sems,
            regular((2, 2, 2, n // 2)),
            dma((2, LAYERS, STRIPS)),
            dma((2, LAYERS, STRIPS)),
            dma((2 * LAYERS, 2)),
            dma((2 * LAYERS, 2)),
            dma((2 * LAYERS,)),
            dma((2 * LAYERS,)),
            dma((2 * LAYERS,)),
            pltpu.VMEM((6, 16, width), f32),
            pltpu.VMEM((5, 16, width), f32),
            pltpu.VMEM((n, share, count), bf16),
            pltpu.VMEM((n, share, count), bf16),
            pltpu.VMEM((share, words), f32),
            pltpu.VMEM((4, share // 2, words), bf16),
            pltpu.VMEM((4, rows_v // 2, width), bf16),
            pltpu.VMEM((rows_v // 2, width), f32),
            pltpu.VMEM((1, width), f32),
            pltpu.VMEM((2 * n, 8, 128), f32),
            dma((4,)),
            dma((5,)),
            dma((5,)),
            dma((n - 1,)),
            dma((n - 1,)),
            dma((2, 3)),
            dma((2, 3)),
            dma((2,)),
            dma((2, n)),
            dma((2, n)),
        ],
        compiler_params=pltpu.CompilerParams(
            collective_id=2, has_side_effects=True, vmem_limit_bytes=VMEM_LIMIT
        ),
        name="backward_layers",
    )(
        ids, lengths, losses, gains, out_grad, inputs, mixed, mid, grad, first,
        proj, pre, attn_full, ffn_full, slope, act,
    )


def merged(value, axis, join):
    pieces = jax.tree.map(lambda part: lax.all_gather(part, axis), value)
    head = jax.tree.map(lambda part: part[0], pieces)
    tail = jax.tree.map(lambda part: part[1:], pieces)
    total, _ = lax.scan(lambda total, section: (join(total, section), None), head, tail)
    return total


def sinusoid(count, width):
    places = jnp.arange(count, dtype=jnp.float32)[:, None]
    freqs = jnp.exp(jnp.arange(width // 2, dtype=jnp.float32) * (-2.0 * math.log(10000.0) / width))
    angles = places * freqs[None, :]
    return jnp.concatenate([jnp.sin(angles), jnp.cos(angles)], axis=1)


def layer_norm(values, gain, shift):
    centre = jnp.mean(values, axis=-1, keepdims=True)
    offset = values - centre
    spread = jnp.mean(offset * offset, axis=-1, keepdims=True)
    inverse = lax.rsqrt(spread + norm_eps)
    normed = offset * inverse
    return (normed * gain + shift, (normed, inverse))


def norm_backward(grad, saved, gain):
    normed, inverse = saved
    scaled = grad * gain
    centred = scaled - jnp.mean(scaled, axis=-1, keepdims=True)
    result = inverse * (centred - normed * jnp.mean(scaled * normed, axis=-1, keepdims=True))
    return (result, jnp.stack([jnp.sum(grad * normed, axis=0), jnp.sum(grad, axis=0)]))


def gelu_exact(values):
    return jax.nn.gelu(values, approximate=False)


def gelu_back(hidden, grad):
    unused, pullback = jax.vjp(gelu_exact, hidden)
    return pullback(grad)[0]


def masked_scores(query, keyed, length):
    scale = query.shape[-1] ** (-0.5)
    scores = jnp.einsum("hqe,hke->hqk", query, keyed, preferred_element_type=jnp.float32) * scale
    visible = jnp.arange(keyed.shape[1]) < length
    return jnp.where(visible[None, None, :], scores, masked_score)


def fetch_forward(attn_part, ffn_part):
    return (
        lax.all_gather(attn_part, "mp", axis=1, tiled=True),
        lax.all_gather(ffn_part, "mp", axis=1, tiled=True),
    )


def fetch_backward(attn_part, ffn_part):
    return (
        lax.all_gather(attn_part, "mp", axis=1, tiled=True),
        lax.all_gather(ffn_part, "mp", axis=1, tiled=True),
    )


def reduce_layer(attn_grad, ffn_grad):
    return (
        lax.psum_scatter(attn_grad, "mp", scatter_dimension=1, tiled=True),
        lax.psum_scatter(ffn_grad, "mp", scatter_dimension=1, tiled=True),
    )


def ffn_forward(middle_b, ffn_w, unit_mask):
    hidden = jnp.einsum("td,fd->tf", middle_b, ffn_w[0], preferred_element_type=jnp.float32)
    active = (gelu_exact(hidden) * unit_mask[None, :]).astype(jnp.bfloat16)
    output = jnp.einsum("tf,fd->td", active, ffn_w[1], preferred_element_type=jnp.float32)
    return (hidden, active, output)


def ffn_backward(grad_out, middle_b, hidden, active, ffn_w, unit_mask):
    grad_active = jnp.einsum("td,fd->tf", grad_out, ffn_w[1], preferred_element_type=jnp.float32)
    grad_hidden = gelu_back(hidden, grad_active * unit_mask[None, :]).astype(jnp.bfloat16)
    up_grad = jnp.einsum("tf,td->fd", grad_hidden, middle_b, preferred_element_type=jnp.float32)
    down_grad = jnp.einsum("tf,td->fd", active, grad_out, preferred_element_type=jnp.float32)
    from_ffn = jnp.einsum("tf,fd->td", grad_hidden, ffn_w[0], preferred_element_type=jnp.float32)
    return (jnp.stack([up_grad, down_grad]), from_ffn)


def layer_forward(states, attn_w, ffn_w, pair, length, unit_mask):
    count = states.shape[0]
    inputs = states.astype(jnp.bfloat16)
    projected = jnp.einsum(
        "td,kde->kte", inputs, attn_w[:3], preferred_element_type=jnp.float32
    ).astype(jnp.bfloat16)
    heads = projected.reshape(3, count, HEADS, -1).transpose(0, 2, 1, 3)
    scores = masked_scores(heads[0], heads[1], length)
    peak = jnp.max(scores, axis=-1, keepdims=True)
    expo = jnp.exp(scores - peak)
    total = jnp.sum(expo, axis=-1, keepdims=True)
    log_total = peak + jnp.log(total)
    probs = (expo / total).astype(jnp.bfloat16)
    mixed = jnp.einsum("hqk,hke->hqe", probs, heads[2], preferred_element_type=jnp.float32)
    mixed = mixed.transpose(1, 0, 2).reshape(count, -1).astype(jnp.bfloat16)
    branch = jnp.dot(mixed, attn_w[3], preferred_element_type=jnp.float32)
    middle, norm_one = layer_norm(states + branch, pair[0, 0], pair[0, 1])
    middle_b = middle.astype(jnp.bfloat16)
    hidden, active, output = ffn_forward(middle_b, ffn_w, unit_mask)
    result, norm_two = layer_norm(middle + output, pair[1, 0], pair[1, 1])
    return (result, (inputs, heads, log_total, mixed, norm_one, middle_b, hidden, active, norm_two))


def layer_backward(grad, attn_w, ffn_w, pair, length, unit_mask, kept):
    inputs, heads, log_total, mixed, norm_one, middle_b, hidden, active, norm_two = kept
    count = inputs.shape[0]
    grad_two, pair_two = norm_backward(grad, norm_two, pair[1, 0])
    ffn_grad, from_ffn = ffn_backward(
        grad_two.astype(jnp.bfloat16), middle_b, hidden, active, ffn_w, unit_mask
    )
    grad_one, pair_one = norm_backward(grad_two + from_ffn, norm_one, pair[0, 0])
    grad_branch = grad_one.astype(jnp.bfloat16)
    output_grad = jnp.einsum("td,te->de", mixed, grad_branch, preferred_element_type=jnp.float32)
    grad_mixed = jnp.einsum("te,de->td", grad_branch, attn_w[3], preferred_element_type=jnp.float32)
    grad_mixed = grad_mixed.astype(jnp.bfloat16).reshape(count, HEADS, -1).transpose(1, 0, 2)
    scale = heads.shape[-1] ** (-0.5)
    probs = jnp.exp(masked_scores(heads[0], heads[1], length) - log_total)
    grad_values = jnp.einsum(
        "hqk,hqe->hke", probs.astype(jnp.bfloat16), grad_mixed, preferred_element_type=jnp.float32
    )
    grad_probs = jnp.einsum(
        "hqe,hke->hqk", grad_mixed, heads[2], preferred_element_type=jnp.float32
    )
    grad_scores = probs * (grad_probs - jnp.sum(grad_probs * probs, axis=-1, keepdims=True))
    grad_scores = grad_scores.astype(jnp.bfloat16)
    grad_query = (
        jnp.einsum("hqk,hke->hqe", grad_scores, heads[1], preferred_element_type=jnp.float32)
        * scale
    )
    grad_key = (
        jnp.einsum("hqk,hqe->hke", grad_scores, heads[0], preferred_element_type=jnp.float32)
        * scale
    )
    stacked = (
        jnp.stack([grad_query, grad_key, grad_values]).transpose(0, 2, 1, 3).reshape(3, count, -1)
    )
    stacked = stacked.astype(jnp.bfloat16)
    input_grad = jnp.einsum("td,kte->kde", inputs, stacked, preferred_element_type=jnp.float32)
    from_attn = jnp.einsum("kte,kde->td", stacked, attn_w[:3], preferred_element_type=jnp.float32)
    attn_grad = jnp.concatenate([input_grad, output_grad[None]], axis=0)
    return (grad_one + from_attn, attn_grad, ffn_grad, jnp.stack([pair_one, pair_two]))


def adamw(weight, moment_one, moment_two, grad, decay, rate):
    moment_one = beta_one * moment_one + (1.0 - beta_one) * grad
    moment_two = beta_two * moment_two + (1.0 - beta_two) * grad * grad
    fixed_one = moment_one / (1.0 - beta_one**STEP)
    fixed_two = moment_two / (1.0 - beta_two**STEP)
    weight = weight - rate * (fixed_one / (jnp.sqrt(fixed_two) + adam_eps) + decay * weight)
    return (moment_one, moment_two, weight)


def combine_vocab(first, second):
    peak = jnp.maximum(first[0], second[0])
    total = first[1] * jnp.exp(first[0] - peak) + second[1] * jnp.exp(second[0] - peak)
    return (peak, total, first[2] + second[2])


def local_general(
    tokens,
    lengths,
    places,
    targets,
    ramp,
    attn,
    attn_m,
    attn_v,
    ffn,
    ffn_m,
    ffn_v,
    table,
    table_m,
    table_v,
    out_table,
    out_m,
    out_v,
    gains,
    gains_m,
    gains_v,
):
    rank = lax.axis_index("mp")
    count = tokens.shape[2]
    flat_ids = tokens.reshape(-1)
    all_lengths = lengths.reshape(-1)
    length = lax.dynamic_index_in_dim(all_lengths, rank, keepdims=False)
    masks = jnp.minimum(ramp, RAMP).astype(jnp.float32) / RAMP
    unit_masks = [masks[depth] for depth in range(LAYERS)]
    looked = jnp.take(table, flat_ids, axis=0)
    embedded = lax.all_to_all(looked, "mp", split_axis=0, concat_axis=1, tiled=True)
    states, norm_zero = layer_norm(
        embedded + sinusoid(count, embedded.shape[1]), gains[0, 0], gains[0, 1]
    )
    kept_all = []
    weights_all = []
    for depth in range(LAYERS):
        attn_w, ffn_w = fetch_forward(
            attn[depth].astype(jnp.bfloat16), ffn[depth].astype(jnp.bfloat16)
        )
        states, kept = layer_forward(
            states, attn_w, ffn_w, gains[1 + 2 * depth : 3 + 2 * depth], length, unit_masks[depth]
        )
        kept_all.append(kept)
        weights_all.append(None)
    spots = places.reshape(-1)
    picked = jnp.take(states, spots, axis=0).astype(jnp.bfloat16)
    picked_all = lax.all_gather(picked, "mp", axis=0, tiled=True)
    out_b = out_table.astype(jnp.bfloat16)
    logits = jnp.einsum("rd,vd->rv", picked_all, out_b, preferred_element_type=jnp.float32)
    labels = targets.reshape(-1)
    columns = rank * out_table.shape[0] + jnp.arange(out_table.shape[0])
    hits = (labels[:, None] == columns[None, :]).astype(jnp.float32)
    peak = jnp.max(logits, axis=1)
    expsum = jnp.sum(jnp.exp(logits - peak[:, None]), axis=1)
    target_part = jnp.sum(hits * logits, axis=1)
    peak_all, expsum_all, target_all = merged((peak, expsum, target_part), "mp", combine_vocab)
    log_total = peak_all + jnp.log(expsum_all)
    slot_count = targets.shape[2]
    counted = jnp.maximum(1, all_lengths * slot_count // count)
    valid = (jnp.arange(slot_count)[None, :] < counted[:, None]).reshape(-1)
    loss_pair = jnp.stack(
        [
            jnp.sum(jnp.where(valid, log_total - target_all, 0.0)),
            jnp.sum(counted).astype(jnp.float32),
        ]
    )
    grad_logits = jnp.where(
        valid[:, None], jnp.exp(logits - log_total[:, None]) - hits, 0.0
    ).astype(jnp.bfloat16)
    out_grad = jnp.einsum("rv,rd->vd", grad_logits, picked_all, preferred_element_type=jnp.float32)
    picked_grad = lax.psum_scatter(
        jnp.dot(grad_logits, out_b, preferred_element_type=jnp.float32),
        "mp",
        scatter_dimension=0,
        tiled=True,
    )
    grad = jnp.zeros_like(states).at[spots].add(picked_grad)
    attn_parts = [None] * LAYERS
    ffn_parts = [None] * LAYERS
    pair_grads = [None] * LAYERS
    for depth in reversed(range(LAYERS)):
        attn_w, ffn_w = fetch_backward(
            attn[depth].astype(jnp.bfloat16), ffn[depth].astype(jnp.bfloat16)
        )
        grad, attn_grad, ffn_grad, pair_grad = layer_backward(
            grad,
            attn_w,
            ffn_w,
            gains[1 + 2 * depth : 3 + 2 * depth],
            length,
            unit_masks[depth],
            kept_all[depth],
        )
        attn_parts[depth], ffn_parts[depth] = reduce_layer(attn_grad, ffn_grad)
        pair_grads[depth] = pair_grad
    grad_sum, zero_grad = norm_backward(grad, norm_zero, gains[0, 0])
    returned = lax.all_to_all(grad_sum, "mp", split_axis=1, concat_axis=0, tiled=True)
    table_grad = jnp.zeros_like(table).at[flat_ids].add(returned)
    gains_grad = jnp.concatenate([zero_grad[None]] + pair_grads, axis=0)
    attn_sum, ffn_sum, table_sum, out_sum, gains_part, loss = lax.psum(
        (jnp.stack(attn_parts), jnp.stack(ffn_parts), table_grad, out_grad, gains_grad, loss_pair),
        "dp",
    )
    shard_squares = (
        jnp.sum(attn_sum * attn_sum)
        + jnp.sum(ffn_sum * ffn_sum)
        + jnp.sum(table_sum * table_sum)
        + jnp.sum(out_sum * out_sum)
    )
    square_total, gains_sum = lax.psum((shard_squares, gains_part), "mp")
    grad_norm = jnp.sqrt(square_total + jnp.sum(gains_sum * gains_sum))
    factor = clip_limit / jnp.maximum(grad_norm, clip_limit)
    attn_m_new, attn_v_new, attn_new = adamw(
        attn, attn_m, attn_v, attn_sum * factor, weight_decay, learn_rate
    )
    ffn_m_new, ffn_v_new, ffn_new = adamw(
        ffn, ffn_m, ffn_v, ffn_sum * factor, weight_decay, learn_rate
    )
    table_m_new, table_v_new, table_new = adamw(
        table, table_m, table_v, table_sum * factor, weight_decay, learn_rate
    )
    out_m_new, out_v_new, out_new = adamw(
        out_table, out_m, out_v, out_sum * factor, weight_decay, learn_rate
    )
    gains_m_new, gains_v_new, gains_new = adamw(
        gains, gains_m, gains_v, gains_sum * factor, 0.0, gain_rate
    )
    return (
        loss,
        grad_norm.reshape(1),
        attn_m_new,
        attn_v_new,
        attn_new,
        ffn_m_new,
        ffn_v_new,
        ffn_new,
        table_m_new,
        table_v_new,
        table_new,
        out_m_new,
        out_v_new,
        out_new,
        gains_m_new,
        gains_v_new,
        gains_new,
    )


def local(
    tokens,
    lengths,
    places,
    targets,
    ramp,
    attn,
    attn_m,
    attn_v,
    ffn,
    ffn_m,
    ffn_v,
    table,
    table_m,
    table_v,
    out_table,
    out_m,
    out_v,
    gains,
    gains_m,
    gains_v,
):
    n = tokens.shape[1]
    where = jnp.asarray(positions(tokens.shape[2], gains.shape[2]))
    attn_full, ffn_full, first, *kept, slope, act, grad, out_grad, losses = forward_call(
        n, tokens[0], lengths, places[0], targets[0], ramp, gains, table.T, where, out_table, attn, ffn
    )
    attn_sum, ffn_sum, table_turned, out_sum, loss, gains_sum, norm = backward_call(
        n, tokens[0], lengths, losses, grad, first, gains, out_grad, kept, attn_full, ffn_full, slope, act, table
    )
    table_sum = table_turned.T
    ffn_sum = ffn_sum.astype(jnp.float32)
    grad_norm = norm[0, 0]
    factor = norm[1, 0]
    attn_m_new, attn_v_new, attn_new = adamw(
        attn, attn_m, attn_v, attn_sum * factor, weight_decay, learn_rate
    )
    ffn_m_new, ffn_v_new, ffn_new = adamw(
        ffn, ffn_m, ffn_v, ffn_sum * factor, weight_decay, learn_rate
    )
    table_m_new, table_v_new, table_new = adamw(
        table, table_m, table_v, table_sum * factor, weight_decay, learn_rate
    )
    out_m_new, out_v_new, out_new = adamw(
        out_table, out_m, out_v, out_sum * factor, weight_decay, learn_rate
    )
    gains_m_new, gains_v_new, gains_new = adamw(
        gains, gains_m, gains_v, gains_sum * factor, 0.0, gain_rate
    )
    return (
        loss[0, :2],
        grad_norm.reshape(1),
        attn_m_new,
        attn_v_new,
        attn_new,
        ffn_m_new,
        ffn_v_new,
        ffn_new,
        table_m_new,
        table_v_new,
        table_new,
        out_m_new,
        out_v_new,
        out_new,
        gains_m_new,
        gains_v_new,
        gains_new,
    )


def solution(mesh):
    in_specs = (
        P("dp", None, None),
        P("dp", None),
        P("dp", "mp", None),
        P("dp", None, None),
        P(),
        P(None, None, "mp", None),
        P(None, None, "mp", None),
        P(None, None, "mp", None),
        P(None, None, "mp", None),
        P(None, None, "mp", None),
        P(None, None, "mp", None),
        P(None, "mp"),
        P(None, "mp"),
        P(None, "mp"),
        P("mp", None),
        P("mp", None),
        P("mp", None),
        P(),
        P(),
        P(),
    )
    out_specs = (
        P(),
        P(),
        P(None, None, "mp", None),
        P(None, None, "mp", None),
        P(None, None, "mp", None),
        P(None, None, "mp", None),
        P(None, None, "mp", None),
        P(None, None, "mp", None),
        P(None, "mp"),
        P(None, "mp"),
        P(None, "mp"),
        P("mp", None),
        P("mp", None),
        P("mp", None),
        P(),
        P(),
        P(),
    )
    fits = mesh.shape['mp'] == 8 and mesh.shape['dp'] == 4
    chosen = local if fits else local_general
    return jax.shard_map(chosen, mesh=mesh, in_specs=in_specs, out_specs=out_specs, check_vma=False)
```

```python
import functools
import math

import jax
import jax.numpy as jnp
import numpy as np
from jax import lax
from jax.experimental import pallas as pl
from jax.experimental.pallas import tpu as pltpu
from jax.sharding import PartitionSpec as P

HEADS = 12
LAYERS = 2
STEP = 10
RAMP = 4


norm_eps = 1e-05
beta_one = 0.9
beta_two = 0.999
learn_rate = 0.02
gain_rate = 0.3
weight_decay = 0.01
adam_eps = 1e-08
clip_limit = 1.0
masked_score = -1000000000.0


MESH = pl.DeviceIdType.MESH
VMEM_LIMIT = 62 * 1024 * 1024
SLOTS = 3
STRIPS = 2


def dot_nn(left, right):
    return lax.dot_general(
        left, right, (((1,), (0,)), ((), ())), preferred_element_type=jnp.float32
    )


def dot_nt(left, right):
    return lax.dot_general(
        left, right, (((1,), (1,)), ((), ())), preferred_element_type=jnp.float32
    )


def dot_tn(left, right):
    return lax.dot_general(
        left, right, (((0,), (0,)), ((), ())), preferred_element_type=jnp.float32
    )


def positions(count, width):
    angles = np.arange(count)[:, None] * np.exp(
        np.arange(width // 2) * (-2.0 * math.log(10000.0) / width)
    )
    return np.concatenate([np.sin(angles), np.cos(angles)], axis=1).astype(np.float32)


def ring_index(place, n):
    late = place // (n // 2)
    return (1 - late) * 2 * place + late * (2 * (n - 1 - place) + 1)


def ring_place(index, n):
    odd = index % 2
    return (1 - odd) * (index // 2) + odd * (n - 1 - index // 2)


class Spot:
    def __init__(self, n):
        self.n = n
        self.dp = lax.axis_index("dp")
        self.mp = lax.axis_index("mp")
        self.core = self.dp % 2
        self.row = self.dp // 2
        self.place = ring_place(self.mp, n)
        self.partner = (self.dp + 1 - 2 * self.core, self.mp)
        self.across = ((self.dp + 2) % 4, self.mp)
        self.ring = (
            (self.dp, ring_index((self.place + 1) % n, n)),
            (self.dp, ring_index((self.place + n - 1) % n, n)),
        )

    def shard(self, offset):
        return ring_index((self.place + offset + self.n) % self.n, self.n)


def greet(devices):
    barrier = pltpu.get_barrier_semaphore()
    for device in devices:
        pl.semaphore_signal(barrier, inc=1, device_id=device, device_id_type=MESH)
    pl.semaphore_wait(barrier, len(devices))


def last_step(n, way, part):
    return n // 2 if way == part else n // 2 - 1


WAYS = ((0, 0), (1, 1), (0, 1), (1, 0))


def ring_columns(row, width, cut):
    return pl.ds(pl.multiple_of(row * cut, 128), width - cut)


def edge_columns(row, width, cut):
    return pl.ds(pl.multiple_of(row * (width - cut), 128), cut)


def cut_of(width, share):
    return 128 * (width // 128 // share)


def normed_of(values):
    centre = jnp.mean(values, axis=-1, keepdims=True)
    offset = values - centre
    spread = jnp.mean(offset * offset, axis=-1, keepdims=True)
    inverse = lax.rsqrt(spread + norm_eps)
    return offset * inverse, inverse


def forward_kernel(
    n,
    ids_ref,
    lengths_ref,
    places_ref,
    targets_ref,
    ramp_ref,
    gains_ref,
    table_ref,
    where_ref,
    out_sh,
    attn_sh,
    ffn_sh,
    attn_full,
    ffn_full,
    first_out,
    inputs_out,
    proj_out,
    mixed_out,
    pre_out,
    mid_out,
    slope_ref,
    act_ref,
    grad_ref,
    out_grad_ref,
    loss_ref,
    first_ref,
    out_ref,
    inputs_ref,
    proj_ref,
    mixed_ref,
    pre_ref,
    mid_ref,
    mask_ref,
    table_b,
    places_row,
    labels_row,
    wa,
    wf,
    raw_a,
    raw_f,
    slope,
    act,
    far_sum,
    far_out,
    far_in,
    state,
    row_out,
    row_in,
    picked,
    stats,
    back_out,
    back_in,
    raw_sem,
    late_sem,
    early_sem,
    kept_sem,
    ring_send,
    ring_recv,
    core_send,
    core_recv,
    across_send,
    across_recv,
    pair_send,
    pair_recv,
    fan_send,
    fan_recv,
    beside_send,
    beside_recv,
):
    spot = Spot(n)
    core = spot.core
    rows_a = attn_sh.shape[2]
    rows_f = ffn_sh.shape[2]
    half_f = rows_f // 2
    part_f = half_f // 2
    steps = n // 2
    count, width = first_ref.shape
    share_e = table_ref.shape[0]
    words = table_ref.shape[1]
    slots = places_row.shape[1]
    slot_count = places_ref.shape[1]

    def rows_at(shard, rows):
        return pl.ds(pl.multiple_of(shard * rows, 16), rows)

    def remote(source, target, send, recv, device):
        return pltpu.make_async_remote_copy(
            src_ref=source,
            dst_ref=target,
            send_sem=send,
            recv_sem=recv,
            device_id=device,
            device_id_type=MESH,
        )

    def slot_f(way, step):
        if step == 0:
            return 0, 0
        return (0, 1) if step == steps else (step, way)

    def chunk_f(piece, way, part, step, side):
        group, half = slot_f(way, step)
        return wf.at[piece // 2, group, side, pl.ds(half * half_f + part * part_f, part_f), :]

    def chunk_a(piece, shard, part, side, edge):
        cut = cut_of(width, 3)
        if edge is None:
            columns = ring_columns(spot.row, width, cut)
        else:
            columns = edge_columns(edge, width, cut)
        return wa.at[piece // 2, 2 * side + part, rows_at(shard, rows_a), columns]

    def sign(way):
        return -1 if way == 0 else 1

    def ring_copy(piece, way, part, step, arriving):
        if piece % 2 == 0:
            target = chunk_a(piece, spot.shard(sign(way) * (step - 1 + arriving)), part, core, None)
            source = target
        else:
            target = chunk_f(piece, way, part, step, core)
            source = target if arriving else chunk_f(piece, way, part, step - 1, core)
        return remote(
            source,
            target,
            ring_send.at[piece, way, part, step - 1],
            ring_recv.at[piece, way, part, step - 1],
            spot.ring[way],
        )

    def core_copy(piece, way, part, step, side, edge):
        if piece % 2 == 0:
            target = chunk_a(piece, spot.shard(sign(way) * step), part, side, edge)
        else:
            target = chunk_f(piece, way, part, step, side)
        lane = 0 if edge is None else 1
        return remote(
            target,
            target,
            core_send.at[lane, piece, way, part, step - 1],
            core_recv.at[lane, piece, way, part, step - 1],
            spot.partner,
        )

    def across_copy(piece, way, part, step, row):
        target = chunk_a(piece, spot.shard(sign(way) * step), part, core, row)
        return remote(
            target,
            target,
            across_send.at[piece, way, part, step - 1],
            across_recv.at[piece, way, part, step - 1],
            spot.across,
        )

    def half_at(half):
        return pl.ds(half * (count // STRIPS), count // STRIPS)

    def pair_copy(which, depth, half):
        rows = half_at(half)
        if which == 0:
            source, target = mid_ref.at[depth, 0, rows, :], mid_ref.at[depth, 1, rows, :]
        else:
            source, target = far_out.at[depth, rows, :], far_in.at[depth, rows, :]
        return remote(
            source,
            target,
            pair_send.at[which, depth, half],
            pair_recv.at[which, depth, half],
            spot.across,
        )

    def peer(offset):
        return (spot.mp + offset + n) % n

    def fan_copy(which, offset, source, target):
        return remote(
            source,
            target,
            fan_send.at[which, offset - 1],
            fan_recv.at[which, offset - 1],
            (spot.dp, peer(offset)),
        )

    def share(which, buffer, offset):
        return fan_copy(which, offset, buffer.at[spot.mp], buffer.at[spot.mp])

    def arrived(which, buffer, offset):
        return fan_copy(which, offset, buffer.at[peer(-offset)], buffer.at[peer(-offset)])

    def deal(which, source, target, offset):
        return fan_copy(which, offset, source.at[peer(offset)], target.at[spot.mp])

    def raw_copy(piece):
        kind, depth = piece % 2, piece // 2
        if kind == 0:
            return pltpu.make_async_copy(attn_sh.at[depth], raw_a.at[depth], raw_sem.at[piece])
        rows = pl.ds(pl.multiple_of(spot.row * half_f, 16), half_f)
        return pltpu.make_async_copy(ffn_sh.at[depth, :, rows, :], raw_f.at[depth], raw_sem.at[piece])

    def take_own(piece):
        kind, depth = piece % 2, piece // 2
        raw_copy(piece).wait()
        if kind == 0:
            for which in range(4):
                wa[depth, which, rows_at(spot.mp, rows_a), :] = raw_a[depth, which].astype(
                    jnp.bfloat16
                )
        else:
            for which in range(2):
                wf[depth, 0, which, 0:half_f, :] = raw_f[depth, which].astype(jnp.bfloat16)

    def launch(piece):
        for way, part in WAYS:
            ring_copy(piece, way, part, 1, 0).start()

    def chains(step):
        return [(way, part) for way, part in WAYS if step <= last_step(n, way, part)]

    def pass_on(piece, step):
        for way, part in chains(step):
            ring_copy(piece, way, part, step, 1).wait_recv()
            if step < last_step(n, way, part):
                ring_copy(piece, way, part, step + 1, 0).start()
            if piece % 2 == 0:
                across_copy(piece, way, part, step, spot.row).start()
            core_copy(piece, way, part, step, core, None).start()

    def pass_edge(piece, step):
        for way, part in chains(step):
            across_copy(piece, way, part, step, 1 - spot.row).wait_recv()
            core_copy(piece, way, part, step, core, 1 - spot.row).start()

    def settle(piece, step):
        for way, part in chains(step):
            core_copy(piece, way, part, step, 1 - core, None).wait_recv()
            if piece % 2 == 0:
                core_copy(piece, way, part, step, 1 - core, 1 - spot.row).wait_recv()

    out_copies = []

    def write_out(source, target):
        copy = pltpu.make_async_copy(source, target, early_sem.at[len(out_copies)])
        copy.start()
        out_copies.append(copy)

    def look_up(offset):
        whose = peer(offset)
        tokens = ids_ref[pl.ds(whose, 1), :]

        size = 768

        def block(index, total):
            start = pl.multiple_of(index * size, 128)
            word = lax.broadcasted_iota(jnp.int32, (size, 1), 0) + start
            chosen = (word == tokens).astype(jnp.bfloat16)
            return total + dot_nn(table_b[:, pl.ds(start, size)], chosen)

        found = lax.fori_loop(
            0, words // size, block, jnp.zeros((share_e, count), jnp.float32)
        )
        row_out[whose] = found.astype(jnp.bfloat16)
        if offset > 0:
            deal(0, row_out, row_in, offset).start()

    raw_copy(0).start()
    late = (
        pltpu.make_async_copy(where_ref, first_ref, late_sem.at[0]),
        pltpu.make_async_copy(out_sh, out_ref, late_sem.at[1]),
    )
    for copy in late:
        copy.start()
    for piece in range(1, 2 * LAYERS):
        raw_copy(piece).start()
    greet([spot.partner, spot.across] + [(spot.dp, peer(offset)) for offset in range(1, n)])
    take_own(0)
    launch(0)
    for depth in range(LAYERS):
        for index in range(n):
            offset = (0, steps)[index] if index < 2 else (index // 2) * (2 * (index % 2) - 1)
            start = pl.multiple_of(spot.shard(offset) * rows_f, 128)
            grown = jnp.minimum(ramp_ref[depth : depth + 1, pl.ds(start, rows_f)], RAMP)
            grown = grown.astype(jnp.float32) / RAMP
            lanes_to = pl.ds((index % 2) * half_f, half_f)
            mask_ref[depth, index // 2 : index // 2 + 1, lanes_to] = jnp.where(
                spot.row == 0, grown[:, 0:half_f], grown[:, half_f:rows_f]
            )
    table_b[...] = table_ref[...].astype(jnp.bfloat16)
    places_row[...] = jnp.full_like(places_row, -1)
    places_row[0:1, 0:slot_count] = places_ref[...]
    labels_row[...] = jnp.full_like(labels_row, -1)
    for whose in range(n):
        labels_row[0:1, whose * slots : whose * slots + slot_count] = targets_ref[
            whose : whose + 1, :
        ]
    spans = lengths_ref[...].astype(jnp.float32)
    lane = lax.broadcasted_iota(jnp.int32, (1, n), 1)
    length = jnp.sum(jnp.where(lane == spot.mp, spans, 0.0), axis=1, keepdims=True)
    visible = lax.broadcasted_iota(jnp.int32, (1, count), 1).astype(jnp.float32) < length
    counted = jnp.maximum(jnp.floor(spans * (slot_count / count)), 1.0)
    lane = lax.broadcasted_iota(jnp.int32, (1, n * slots), 1)
    limit = jnp.zeros((1, n * slots), jnp.float32)
    for whose in range(n):
        limit = jnp.where(
            lane >= whose * slots, counted[:, whose : whose + 1] + whose * slots, limit
        )
    valid = lane.astype(jnp.float32) < limit
    loss_ref[1:2, :] = valid.astype(jnp.float32)
    for offset in range(1, 4):
        look_up(offset)
    pass_on(0, 1)
    for offset in range(4, 7):
        look_up(offset)
    pass_on(0, 2)
    pass_edge(0, 1)
    take_own(1)
    launch(1)
    look_up(7)
    look_up(0)
    row_in[spot.mp] = row_out[spot.mp]
    pass_on(0, 3)
    pass_edge(0, 2)
    for offset in range(1, n):
        arrived(0, row_in, offset).wait_recv()
    late[0].wait()
    first_ref[...] += row_in[...].reshape(width, count).astype(jnp.float32).T
    write_out(first_ref, first_out)
    normed, _ = normed_of(first_ref[...])
    state[...] = normed * gains_ref[0, 0:1, :] + gains_ref[0, 1:2, :]
    take_own(2)
    take_own(3)
    pass_on(0, 4)
    pass_edge(0, 3)

    lanes = lax.broadcasted_iota(jnp.int32, (1, 128), 1) < 64

    def head_pair(depth, pair):
        columns = pl.ds(pl.multiple_of(pair * 128, 128), 128)
        query = proj_ref[depth, 0, :, columns]
        keyed = proj_ref[depth, 1, :, columns]
        valued = proj_ref[depth, 2, :, columns]
        outs = []
        for side in range(2):
            mine = lanes if side == 0 else jnp.logical_not(lanes)
            scores = dot_nt(jnp.where(mine, query, jnp.zeros_like(query)), keyed) * 0.125
            scores = jnp.where(visible, scores, masked_score)
            expo = jnp.exp(scores - jnp.max(scores, axis=-1, keepdims=True))
            total = jnp.sum(expo, axis=-1, keepdims=True)
            outs.append(dot_nn((expo / total).astype(jnp.bfloat16), valued))
        mixed_ref[depth, :, columns] = jnp.where(lanes, outs[0], outs[1]).astype(jnp.bfloat16)

    def kept_copies(turn, depth, group, far, start, size):
        slot = turn % SLOTS
        here, there = pl.ds(0, size), pl.ds(start, size)
        return (
            pltpu.make_async_copy(
                slope.at[slot, here, :],
                slope_ref.at[depth, group, far, there, :],
                kept_sem.at[0, slot],
            ),
            pltpu.make_async_copy(
                act.at[slot, here, :],
                act_ref.at[depth, group, far, there, :],
                kept_sem.at[1, slot],
            ),
        )

    turns = []

    def ffn_block(depth, group, far, start, size):
        turn = len(turns)
        turns.append((depth, group, far, start, size))
        if turn >= SLOTS:
            for copy in kept_copies(turn, *turns[turn - SLOTS]):
                copy.wait()
        slot, rows, here = turn % SLOTS, pl.ds(start, size), pl.ds(0, size)
        hidden = dot_nt(mid_ref[depth, far, rows, :], wf[depth, group, 0])
        spread = 0.5 * (1.0 + lax.erf(hidden * (0.5**0.5)))
        mask = mask_ref[depth, group : group + 1, :]
        bell = jnp.exp(hidden * hidden * -0.5) * (1.0 / math.sqrt(2.0 * math.pi))
        slope[slot, here, :] = (spread + hidden * bell) * mask
        active = (hidden * spread * mask).astype(jnp.bfloat16)
        act[slot, here, :] = active
        for copy in kept_copies(*((turn,) + turns[turn])):
            copy.start()
        if far:
            far_sum[rows, :] += dot_nn(active, wf[depth, group, 1])
        else:
            pre_ref[depth, 1, rows, :] += dot_nn(active, wf[depth, group, 1])

    def ffn_own(depth, group):
        ffn_block(depth, group, 0, 0, count)

    def ffn_far(depth, group, half):
        ffn_block(depth, group, 1, half * (count // STRIPS), count // STRIPS)

    for depth in range(LAYERS):
        piece_a, piece_f = 2 * depth, 2 * depth + 1
        more = depth + 1 < LAYERS
        if depth > 0:
            pass_on(piece_a, 3)
            pass_edge(piece_a, 2)
            pass_on(piece_a, 4)
            pass_edge(piece_a, 3)
        pass_edge(piece_a, 4)
        for step in range(1, steps + 1):
            settle(piece_a, step)
        write_out(wa.at[depth], attn_full.at[depth])
        inputs = state[...].astype(jnp.bfloat16)
        inputs_ref[depth] = inputs
        for which in range(3):
            proj_ref[depth, which] = dot_nn(inputs, wa[depth, which]).astype(jnp.bfloat16)
        pass_on(piece_f, 1)

        @pl.loop(0, HEADS // 2)
        def _(pair):
            head_pair(depth, pair)

        pre_ref[depth, 0] = state[...] + dot_nn(mixed_ref[depth], wa[depth, 3])
        normed, _ = normed_of(pre_ref[depth, 0])
        middle = (
            normed * gains_ref[1 + 2 * depth, 0:1, :] + gains_ref[1 + 2 * depth, 1:2, :]
        )
        for half in range(STRIPS):
            mid_ref[depth, 0, half_at(half), :] = middle[
                half * (count // STRIPS) : (half + 1) * (count // STRIPS), :
            ].astype(jnp.bfloat16)
            pair_copy(0, depth, half).start()
        pre_ref[depth, 1] = middle
        far_sum[...] = jnp.zeros_like(far_sum)
        write_out(inputs_ref.at[depth], inputs_out.at[depth])
        write_out(proj_ref.at[depth], proj_out.at[depth])
        write_out(mixed_ref.at[depth], mixed_out.at[depth])
        pass_on(piece_f, 2)
        settle(piece_f, 1)
        ffn_own(depth, 1)
        pass_on(piece_f, 3)
        if more:
            launch(piece_a + 2)
        settle(piece_f, 2)
        ffn_own(depth, 2)
        for half in range(STRIPS):
            pair_copy(0, depth, half).wait_recv()
            ffn_far(depth, 1, half)
            ffn_far(depth, 2, half)
        write_out(mid_ref.at[depth], mid_out.at[depth])
        settle(piece_f, 3)
        for half in range(STRIPS):
            ffn_far(depth, 3, half)
        pass_on(piece_f, 4)
        settle(piece_f, 4)
        for half in range(STRIPS):
            ffn_far(depth, 0, half)
            far_out[depth, half_at(half), :] = far_sum[half_at(half), :].astype(jnp.bfloat16)
            pair_copy(1, depth, half).start()
        if more:
            pass_on(piece_a + 2, 1)
        ffn_own(depth, 3)
        ffn_own(depth, 0)
        write_out(wf.at[depth], ffn_full.at[depth])
        if more:
            launch(piece_f + 2)
            pass_on(piece_a + 2, 2)
            pass_edge(piece_a + 2, 1)
        for half in range(STRIPS):
            pair_copy(1, depth, half).wait_recv()
        pre_ref[depth, 1] += far_in[depth].astype(jnp.float32)
        write_out(pre_ref.at[depth], pre_out.at[depth])
        normed, _ = normed_of(pre_ref[depth, 1])
        state[...] = normed * gains_ref[2 + 2 * depth, 0:1, :] + gains_ref[2 + 2 * depth, 1:2, :]

    spots = (
        lax.broadcasted_iota(jnp.int32, (count, 1), 0) == places_row[...]
    ).astype(jnp.bfloat16)
    picked[spot.mp] = dot_tn(spots, state[...].astype(jnp.bfloat16)).astype(jnp.bfloat16)
    beside = spot.mp + 1 - 2 * (spot.mp % 2)

    def beside_copy(step, arriving):
        whose = ((beside if arriving else spot.mp) - 2 * step + n) % n
        return remote(
            picked.at[whose],
            picked.at[whose],
            beside_send.at[step],
            beside_recv.at[step],
            (spot.dp, beside),
        )

    for step in range(1, n // 2):
        share(1, picked, 2 * step).start()
    beside_copy(0, False).start()
    late[1].wait()
    out_b = out_ref[...].astype(jnp.bfloat16)
    rows_v = out_ref.shape[0]
    hits = (
        labels_row[...] == spot.mp * rows_v + lax.broadcasted_iota(jnp.int32, (rows_v, 1), 0)
    ).astype(jnp.float32)
    for step in range(1, n // 2):
        arrived(1, picked, 2 * step).wait_recv()
        beside_copy(step, False).start()
    for step in range(n // 2):
        beside_copy(step, True).wait_recv()
    picked_all = picked[...].reshape(n * slots, -1)
    logits = dot_nt(out_b, picked_all)
    peak = jnp.max(logits, axis=0, keepdims=True)
    expsum = jnp.sum(jnp.exp(logits - peak), axis=0, keepdims=True)
    stats[spot.mp, 0:1, :] = peak
    stats[spot.mp, 1:2, :] = expsum
    stats[spot.mp, 2:3, :] = jnp.sum(hits * logits, axis=0, keepdims=True)
    for offset in range(1, n):
        share(2, stats, offset).start()
    for offset in range(1, n):
        arrived(2, stats, offset).wait_recv()
    peak = stats[0, 0:1, :]
    for whose in range(1, n):
        peak = jnp.maximum(peak, stats[whose, 0:1, :])
    expsum = stats[0, 1:2, :] * jnp.exp(stats[0, 0:1, :] - peak)
    target = stats[0, 2:3, :]
    for whose in range(1, n):
        expsum = expsum + stats[whose, 1:2, :] * jnp.exp(stats[whose, 0:1, :] - peak)
        target = target + stats[whose, 2:3, :]
    log_total = peak + jnp.log(expsum)
    loss_ref[0:1, :] = jnp.where(valid, log_total - target, 0.0)
    grad_logits = jnp.where(valid, jnp.exp(logits - log_total) - hits, 0.0).astype(jnp.bfloat16)
    picked_grad = dot_tn(grad_logits, out_b).astype(jnp.bfloat16)
    for whose in range(n):
        back_out[whose] = picked_grad[whose * slots : (whose + 1) * slots, :]
    for offset in range(1, n):
        deal(3, back_out, back_in, offset).start()
    back_in[spot.mp] = back_out[spot.mp]
    out_grad_ref[...] = dot_nn(grad_logits, picked_all)
    for offset in range(1, n):
        arrived(3, back_in, offset).wait_recv()
    summed = back_in[0].astype(jnp.float32)
    for whose in range(1, n):
        summed = summed + back_in[whose].astype(jnp.float32)
    high = summed.astype(jnp.bfloat16)
    low = (summed - high.astype(jnp.float32)).astype(jnp.bfloat16)
    grad_ref[...] = dot_nn(spots, high) + dot_nn(spots, low)

    for piece in range(2 * LAYERS):
        for way, part in WAYS:
            for step in range(1, last_step(n, way, part) + 1):
                ring_copy(piece, way, part, step, 0).wait_send()
                core_copy(piece, way, part, step, core, None).wait_send()
                if piece % 2 == 0:
                    across_copy(piece, way, part, step, spot.row).wait_send()
                    core_copy(piece, way, part, step, core, 1 - spot.row).wait_send()
    for offset in range(1, n):
        deal(0, row_out, row_in, offset).wait_send()
        share(2, stats, offset).wait_send()
        deal(3, back_out, back_in, offset).wait_send()
    for step in range(n // 2):
        beside_copy(step, False).wait_send()
        if step > 0:
            share(1, picked, 2 * step).wait_send()
    for depth in range(LAYERS):
        for half in range(STRIPS):
            pair_copy(0, depth, half).wait_send()
            pair_copy(1, depth, half).wait_send()
    for turn in range(len(turns) - SLOTS, len(turns)):
        for copy in kept_copies(turn, *turns[turn]):
            copy.wait()
    for copy in out_copies:
        copy.wait()


def forward_call(
    n, ids, lengths, places, targets, ramp, gains, table, where, out_table, attn, ffn
):
    count, width = where.shape
    rows_f = ffn.shape[2]
    slots = 32 * -(-places.shape[1] // 32)
    groups = n // 2
    f32, bf16 = jnp.float32, jnp.bfloat16
    vmem = pl.BlockSpec(memory_space=pltpu.VMEM)
    anywhere = pl.BlockSpec(memory_space=pl.ANY)
    shape = jax.ShapeDtypeStruct
    dma = pltpu.SemaphoreType.DMA
    sems = dma((2 * LAYERS, 2, 2, n // 2))
    core_sems = dma((2, 2 * LAYERS, 2, 2, n // 2))
    return pl.pallas_call(
        functools.partial(forward_kernel, n),
        out_shape=(
            shape((LAYERS, 4, width, width), bf16),
            shape((LAYERS, groups, 2, rows_f, width), bf16),
            shape((count, width), f32),
            shape((LAYERS, count, width), bf16),
            shape((LAYERS, 3, count, width), bf16),
            shape((LAYERS, count, width), bf16),
            shape((LAYERS, 2, count, width), f32),
            shape((LAYERS, 2, count, width), bf16),
            shape((LAYERS, groups, 2, count, rows_f), f32),
            shape((LAYERS, groups, 2, count, rows_f), bf16),
            shape((count, width), f32),
            shape(out_table.shape, f32),
            shape((2, n * slots), f32),
        ),
        in_specs=[vmem] * 7 + [anywhere] * 4,
        out_specs=(anywhere,) * 10 + (vmem,) * 3,
        scratch_shapes=[
            pltpu.VMEM((count, width), f32),
            pltpu.VMEM(out_table.shape, f32),
            pltpu.VMEM((LAYERS, count, width), bf16),
            pltpu.VMEM((LAYERS, 3, count, width), bf16),
            pltpu.VMEM((LAYERS, count, width), bf16),
            pltpu.VMEM((LAYERS, 2, count, width), f32),
            pltpu.VMEM((LAYERS, 2, count, width), bf16),
            pltpu.VMEM((LAYERS, groups, rows_f), f32),
            pltpu.VMEM(table.shape, bf16),
            pltpu.VMEM((1, slots), jnp.int32),
            pltpu.VMEM((1, n * slots), jnp.int32),
            pltpu.VMEM((LAYERS, 4, width, width), bf16),
            pltpu.VMEM((LAYERS, groups, 2, rows_f, width), bf16),
            pltpu.VMEM(attn.shape, f32),
            pltpu.VMEM((LAYERS, 2, rows_f // 2, width), f32),
            pltpu.VMEM((SLOTS, count, rows_f), f32),
            pltpu.VMEM((SLOTS, count, rows_f), bf16),
            pltpu.VMEM((count, width), f32),
            pltpu.VMEM((LAYERS, count, width), bf16),
            pltpu.VMEM((LAYERS, count, width), bf16),
            pltpu.VMEM((count, width), f32),
            pltpu.VMEM((n, table.shape[0], count), bf16),
            pltpu.VMEM((n, table.shape[0], count), bf16),
            pltpu.VMEM((n, slots, width), bf16),
            pltpu.VMEM((n, 8, n * slots), f32),
            pltpu.VMEM((n, slots, width), bf16),
            pltpu.VMEM((n, slots, width), bf16),
            dma((2 * LAYERS,)),
            dma((2,)),
            dma((1 + 7 * LAYERS,)),
            dma((2, SLOTS)),
            sems,
            sems,
            core_sems,
            core_sems,
            sems,
            sems,
            dma((2, LAYERS, STRIPS)),
            dma((2, LAYERS, STRIPS)),
            dma((4, n - 1)),
            dma((4, n - 1)),
            dma((n // 2,)),
            dma((n // 2,)),
        ],
        compiler_params=pltpu.CompilerParams(
            collective_id=1, has_side_effects=True, vmem_limit_bytes=VMEM_LIMIT
        ),
        name="forward_layers",
    )(ids, lengths, places, targets, ramp, gains, table, where, out_table, attn, ffn)


def norm_back(grad, values, gain):
    normed, inverse = normed_of(values)
    scaled = grad * gain
    centred = scaled - jnp.mean(scaled, axis=-1, keepdims=True)
    result = inverse * (centred - normed * jnp.mean(scaled * normed, axis=-1, keepdims=True))
    return (
        result,
        jnp.sum(grad * normed, axis=0, keepdims=True),
        jnp.sum(grad, axis=0, keepdims=True),
    )


def backward_kernel(
    n,
    ids_ref,
    lengths_ref,
    losses_ref,
    gains_ref,
    out_grad_all,
    inputs_all,
    mixed_all,
    mid_all,
    grad_ref,
    first_ref,
    proj_all,
    pre_all,
    attn_full,
    ffn_full,
    slope_all,
    act_all,
    attn_sum,
    ffn_sum,
    table_sum,
    out_sum,
    loss_out,
    gains_out,
    square_out,
    out_grad_ref,
    proj,
    pre,
    wa,
    wf,
    slope,
    sum_a,
    sum_f,
    theirs_f,
    land_f,
    land_a,
    ring_a,
    ring_f,
    go_far,
    far_sum,
    far_out,
    far_in,
    state,
    grad_rows,
    left_a,
    left_f,
    right_f,
    spread_a,
    spread_f,
    done_a,
    done_f,
    wa_sem,
    load_sem,
    slope_sem,
    mid_sem,
    left_sem,
    core_send,
    core_recv,
    core_free,
    swap_send,
    swap_recv,
    swap_free,
    ring_send,
    ring_recv,
    ring_free,
    pair_send,
    pair_recv,
    across_send,
    across_recv,
    out_sem,
    last_send,
    last_recv,
    small,
    small_in,
    columns_out,
    columns_in,
    table_grad,
    table_half,
    out_half,
    out_done,
    squares,
    square_parts,
    proj_sem,
    small_send,
    small_recv,
    deal_send,
    deal_recv,
    half_send,
    half_recv,
    half_sem,
    norm_send,
    norm_recv,
):
    spot = Spot(n)
    core = spot.core
    other = 1 - core
    rows_a = attn_sum.shape[2]
    rows_f = ffn_sum.shape[2]
    half_f = rows_f // 2
    part_f = half_f // 2
    count = state.shape[0]
    width = attn_sum.shape[3]
    groups = n // 2
    order = (0,) + tuple(range(groups - 1, 0, -1))
    total = LAYERS * groups

    def rows_at(shard, rows):
        return pl.ds(pl.multiple_of(shard * rows, 16), rows)

    def peer(offset):
        return (spot.mp + offset + n) % n

    def remote(source, target, send, recv, device):
        return pltpu.make_async_remote_copy(
            src_ref=source,
            dst_ref=target,
            send_sem=send,
            recv_sem=recv,
            device_id=device,
            device_id_type=MESH,
        )

    def turn_of(turn):
        return LAYERS - 1 - turn // groups, order[turn % groups]

    def load_weights(depth, group):
        return pltpu.make_async_copy(
            ffn_full.at[depth, group], wf.at[group], load_sem.at[0, group]
        )

    def load_act(depth):
        return [
            pltpu.make_async_copy(
                act_all.at[depth, group, far],
                left_f.at[group, 1, pl.ds(far * count, count), :],
                load_sem.at[1 + far, group],
            )
            for group in range(groups)
            for far in range(2)
        ] + [
            pltpu.make_async_copy(
                mid_all.at[depth, far],
                right_f.at[0, pl.ds(far * count, count), :],
                mid_sem.at[far],
            )
            for far in range(2)
        ]

    def load_slope(index):
        depth = LAYERS - 1 - index // (2 * groups)
        far = (index // groups) % 2
        return pltpu.make_async_copy(
            slope_all.at[depth, order[index % groups], far],
            slope.at[index % (groups + 1)],
            slope_sem.at[index % (groups + 1)],
        )

    def load_pre(depth):
        return pltpu.make_async_copy(pre_all.at[depth], pre, proj_sem.at[0])

    def load_left(depth):
        return (
            pltpu.make_async_copy(inputs_all.at[depth], left_a.at[0], left_sem.at[0]),
            pltpu.make_async_copy(mixed_all.at[depth], left_a.at[1], left_sem.at[1]),
        )

    def load_proj(depth):
        return pltpu.make_async_copy(proj_all.at[depth], proj, proj_sem.at[1])

    def load_attn(depth):
        return pltpu.make_async_copy(attn_full.at[depth], wa, wa_sem.at[0])

    def core_copy(turn):
        slot = turn % SLOTS
        return remote(
            theirs_f.at[slot],
            land_f.at[slot],
            core_send.at[turn],
            core_recv.at[turn],
            spot.partner,
        )

    def fold(turn):
        depth, group = turn_of(turn)
        core_copy(turn).wait_recv()
        sum_f[depth, group] = (
            sum_f[depth, group].astype(jnp.float32)
            + land_f[turn % SLOTS].astype(jnp.float32)
        ).astype(jnp.bfloat16)
        if turn + SLOTS < total:
            pl.semaphore_signal(
                core_free.at[0], inc=1, device_id=spot.partner, device_id_type=MESH
            )

    def swap_copy(depth, part):
        return remote(
            wa.at[part],
            land_a.at[part],
            swap_send.at[depth, part],
            swap_recv.at[depth, part],
            spot.partner,
        )

    def summed(piece, offset, part):
        kind, depth = piece % 2, piece // 2
        if kind == 0:
            return sum_a.at[depth, part, rows_at(spot.shard(offset), rows_a), :]
        far = abs(offset)
        group, half = (far, int(offset > 0)) if 0 < far < groups else (0, int(far > 0))
        return sum_f.at[depth, group, pl.ds(half * half_f + part * part_f, part_f), :]

    def landed(piece, way, part, step):
        if piece % 2 == 0:
            return ring_a.at[way, part, step - 1]
        return ring_f.at[way, part, step - 1]

    def absorb_rows(into, source):
        into[...] = (into[...].astype(jnp.float32) + source[...].astype(jnp.float32)).astype(
            jnp.bfloat16
        )

    def pair_copy(which, depth, half):
        rows = pl.ds(half * (count // STRIPS), count // STRIPS)
        if which == 0:
            source, target = right_f.at[1, rows, :], go_far.at[depth, rows, :]
        else:
            source, target = far_out.at[depth, rows, :], far_in.at[depth, rows, :]
        return remote(
            source,
            target,
            pair_send.at[which, depth, half],
            pair_recv.at[which, depth, half],
            spot.across,
        )

    def ring_copy(piece, way, part, step):
        offset = last_step(n, way, part) - step + 1
        return remote(
            summed(piece, offset if way == 0 else -offset, part),
            landed(piece, way, part, step),
            ring_send.at[piece, way, part, step - 1],
            ring_recv.at[piece, way, part, step - 1],
            spot.ring[way],
        )

    def ring_start(piece, way, part, step):
        if piece // 2 < LAYERS - 1:
            pl.semaphore_wait(ring_free.at[piece % 2, way, part, step - 1], 1)
        ring_copy(piece, way, part, step).start()

    def release(piece, way, part, step):
        if piece // 2 > 0:
            pl.semaphore_signal(
                ring_free.at[piece % 2, way, part, step - 1],
                inc=1,
                device_id=spot.ring[1 - way],
                device_id_type=MESH,
            )

    def launch(piece, long):
        for way, part in WAYS:
            if (way == part) == long:
                ring_start(piece, way, part, 1)

    def launch_part(piece, part):
        for way in (part, 1 - part):
            ring_start(piece, way, part, 1)

    def relay(piece, step):
        for way, part in WAYS:
            last = last_step(n, way, part)
            if step < last:
                ring_copy(piece, way, part, step).wait_recv()
                offset = last - step if way == 0 else step - last
                absorb_rows(summed(piece, offset, part), landed(piece, way, part, step))
                ring_start(piece, way, part, step + 1)
                release(piece, way, part, step)

    def across_copy(piece, part):
        depth = piece // 2
        if piece % 2 == 0:
            source, target = spread_a.at[depth, 0, part], spread_a.at[depth, 1, part]
        else:
            rows = pl.ds(part * part_f, part_f)
            source, target = spread_f.at[depth, 0, rows, :], spread_f.at[depth, 1, rows, :]
        return remote(
            source,
            target,
            across_send.at[piece, part],
            across_recv.at[piece, part],
            spot.across,
        )

    def finish(piece):
        kind, depth = piece % 2, piece // 2
        for part in range(2):
            value = summed(piece, 0, part)[...].astype(jnp.float32)
            for way in range(2):
                step = last_step(n, way, part)
                ring_copy(piece, way, part, step).wait_recv()
                value = value + landed(piece, way, part, step)[...].astype(jnp.float32)
                release(piece, way, part, step)
            value = value.astype(jnp.bfloat16)
            if kind == 0:
                spread_a[depth, 0, part] = value
            else:
                spread_f[depth, 0, pl.ds(part * part_f, part_f), :] = value
            across_copy(piece, part).start()

    def out_copies(piece):
        kind, depth = piece % 2, piece // 2
        if kind == 0:
            source, target = done_a, attn_sum.at[depth, pl.ds(2 * core, 2)]
        else:
            source, target = done_f, ffn_sum.at[depth, core]
        return (
            pltpu.make_async_copy(source, target, out_sem.at[piece]),
            remote(source, target, last_send.at[piece], last_recv.at[piece], spot.partner),
        )

    def conclude(piece):
        kind, depth = piece % 2, piece // 2
        for part in range(2):
            across_copy(piece, part).wait_recv()
        if depth < LAYERS - 1:
            local, away = out_copies(piece + 2)
            local.wait()
            away.wait_send()
        row = spot.row
        if kind == 1:
            for side in range(2):
                whose = row + side - 2 * row * side
                rows = pl.ds(pl.multiple_of(whose * half_f, 16), half_f)
                done_f[rows, :] = spread_f[depth, side]
            add_squares(done_f[...].astype(jnp.float32))
        else:
            for part in range(2):
                value = spread_a[depth, 0, part].astype(jnp.float32) + spread_a[
                    depth, 1, part
                ].astype(jnp.float32)
                done_a[part] = value
                add_squares(value)
        for copy in out_copies(piece):
            copy.start()

    load_grad = pltpu.make_async_copy(grad_ref, state, proj_sem.at[2])
    load_grad.start()
    load_first = pltpu.make_async_copy(first_ref, pre.at[0], proj_sem.at[3])
    load_pre(LAYERS - 1).start()
    for group in order:
        load_weights(LAYERS - 1, group).start()
    for index in range(groups + 1):
        load_slope(index).start()
    for copy in load_act(LAYERS - 1):
        copy.start()
    load_attn(LAYERS - 1).start()
    load_proj(LAYERS - 1).start()
    load_out = pltpu.make_async_copy(out_grad_all, out_grad_ref, left_sem.at[2])
    load_out.start()
    for copy in load_left(LAYERS - 1):
        copy.start()
    greet(
        [spot.partner, spot.across]
        + [(whose, peer(offset)) for offset in range(1, n) for whose in (spot.dp, spot.partner[0])]
    )
    load_grad.wait()
    lanes = lax.broadcasted_iota(jnp.int32, (1, 128), 1) < 64
    spans = lengths_ref[...].astype(jnp.float32)
    lane = lax.broadcasted_iota(jnp.int32, (1, n), 1)
    length = jnp.sum(jnp.where(lane == spot.mp, spans, 0.0), axis=1, keepdims=True)
    visible = lax.broadcasted_iota(jnp.int32, (1, count), 1).astype(jnp.float32) < length

    def hidden_own(index):
        depth = LAYERS - 1 - index // (2 * groups)
        group = order[index % groups]
        load_slope(index).wait()
        load_weights(depth, group).wait()
        rows = pl.ds(0, count)
        grad_active = dot_nt(right_f[1, rows, :], wf[group, 1])
        grad_hidden = (grad_active * slope[index % (groups + 1)]).astype(jnp.bfloat16)
        left_f[group, 0, rows, :] = grad_hidden
        state[...] += dot_nn(grad_hidden, wf[group, 0])
        if index + groups + 1 < 2 * total:
            load_slope(index + groups + 1).start()

    def hidden_far(index, half):
        depth = LAYERS - 1 - index // (2 * groups)
        group = order[index % groups]
        if half == 0:
            load_slope(index).wait()
        rows = pl.ds(half * (count // STRIPS), count // STRIPS)
        here = pl.ds(count + half * (count // STRIPS), count // STRIPS)
        grad_active = dot_nt(right_f[1, here, :], wf[group, 1])
        grad_hidden = (grad_active * slope[index % (groups + 1), rows, :]).astype(jnp.bfloat16)
        left_f[group, 0, here, :] = grad_hidden
        far_sum[rows, :] += dot_nn(grad_hidden, wf[group, 0])
        if half == STRIPS - 1:
            if depth > 0:
                load_weights(depth - 1, group).start()
            if index + groups + 1 < 2 * total:
                load_slope(index + groups + 1).start()

    def ffn_turn(turn):
        depth, group = turn_of(turn)
        slot = turn % SLOTS
        sum_f[depth, group] = dot_tn(left_f[group, core], right_f[core]).astype(jnp.bfloat16)
        if turn >= SLOTS:
            core_copy(turn - SLOTS).wait_send()
        theirs_f[slot] = dot_tn(left_f[group, other], right_f[other]).astype(jnp.bfloat16)
        if turn >= SLOTS:
            pl.semaphore_wait(core_free.at[0], 1)
        core_copy(turn).start()

    def head_pair(depth, pair):
        columns = pl.ds(pl.multiple_of(pair * 128, 128), 128)
        query = proj[0, :, columns]
        keyed = proj[1, :, columns]
        valued = proj[2, :, columns]
        grad_mixed = grad_rows[4, :, columns]
        outs = []
        for side in range(2):
            mine = lanes if side == 0 else jnp.logical_not(lanes)
            scores = dot_nt(jnp.where(mine, query, jnp.zeros_like(query)), keyed) * 0.125
            scores = jnp.where(visible, scores, masked_score)
            expo = jnp.exp(scores - jnp.max(scores, axis=-1, keepdims=True))
            probs = expo / jnp.sum(expo, axis=-1, keepdims=True)
            grad_probs = dot_nt(jnp.where(mine, grad_mixed, jnp.zeros_like(query)), valued)
            inner = jnp.sum(grad_probs * probs, axis=-1, keepdims=True)
            grad_scores = (probs * (grad_probs - inner)).astype(jnp.bfloat16)
            outs.append(
                (
                    dot_nn(grad_scores, keyed) * 0.125,
                    dot_tn(grad_scores, query) * 0.125,
                    dot_tn(probs.astype(jnp.bfloat16), grad_mixed),
                )
            )
        for which in range(3):
            grad_rows[which, :, columns] = jnp.where(
                lanes, outs[0][which], outs[1][which]
            ).astype(jnp.bfloat16)

    def layer(depth, hooks):
        def at(name):
            for work in hooks.get(name, ()):
                work()

        base = (LAYERS - 1 - depth) * groups
        piece_a, piece_f = 2 * depth, 2 * depth + 1
        load_pre(depth).wait()
        grad_two, small[0, 4 + 4 * depth : 5 + 4 * depth, :], small[0, 5 + 4 * depth : 6 + 4 * depth, :] = norm_back(
            state[...], pre[1], gains_ref[2 + 2 * depth, 0:1, :]
        )
        state[...] = grad_two
        for half in range(STRIPS):
            if depth < LAYERS - 1:
                pair_copy(0, depth + 1, half).wait_send()
            rows = pl.ds(half * (count // STRIPS), count // STRIPS)
            right_f[1, rows, :] = state[rows, :].astype(jnp.bfloat16)
            pair_copy(0, depth, half).start()
        far_sum[...] = jnp.zeros_like(far_sum)
        for step in range(groups):
            hidden_own(2 * base + step)
        at("own")
        for half in range(STRIPS):
            rows = pl.ds(half * (count // STRIPS), count // STRIPS)
            here = pl.ds(count + half * (count // STRIPS), count // STRIPS)
            pair_copy(0, depth, half).wait_recv()
            right_f[1, here, :] = go_far[depth, rows, :]
            for step in range(groups):
                hidden_far(2 * base + groups + step, half)
            far_out[depth, rows, :] = far_sum[rows, :].astype(jnp.bfloat16)
            pair_copy(1, depth, half).start()
            at(("far", half))
        for copy in load_act(depth):
            copy.wait()
        for step in range(groups):
            ffn_turn(base + step)
            if step >= 1:
                fold(base + step - 1)
            if step == 1:
                launch(piece_f, True)
            if step == 2:
                launch(piece_f, False)
            at(("ffn", step))
        fold(base + groups - 1)
        if depth > 0:
            for copy in load_act(depth - 1):
                copy.start()
        for half in range(STRIPS):
            pair_copy(1, depth, half).wait_recv()
        state[...] += far_in[depth].astype(jnp.float32)
        at("middle")
        grad_one, small[0, 2 + 4 * depth : 3 + 4 * depth, :], small[0, 3 + 4 * depth : 4 + 4 * depth, :] = norm_back(
            state[...], pre[0], gains_ref[1 + 2 * depth, 0:1, :]
        )
        if depth > 0:
            load_pre(depth - 1).start()
        else:
            load_first.start()
        state[...] = grad_one
        grad_rows[3] = grad_one.astype(jnp.bfloat16)
        load_attn(depth).wait()
        load_proj(depth).wait()
        grad_rows[4] = dot_nt(grad_rows[3], wa[3]).astype(jnp.bfloat16)

        @pl.loop(0, HEADS // 4)
        def _(pair):
            head_pair(depth, pair)

        at("half")

        @pl.loop(HEADS // 4, HEADS // 2)
        def _(pair):
            head_pair(depth, pair)

        if depth > 0:
            load_proj(depth - 1).start()
        at("heads")
        for which in range(3):
            state[...] += dot_nt(grad_rows[which], wa[which])
        for copy in load_left(depth):
            copy.wait()
        for part in range(2):
            left = 0 if part == 0 else other
            wa[part] = dot_tn(left_a[left], grad_rows[2 * other + part]).astype(jnp.bfloat16)
            if depth < LAYERS - 1:
                pl.semaphore_wait(swap_free.at[part], 1)
            swap_copy(depth, part).start()
        for part in range(2):
            left = 0 if part == 0 else core
            sum_a[depth, part] = dot_tn(left_a[left], grad_rows[2 * core + part]).astype(
                jnp.bfloat16
            )
            swap_copy(depth, part).wait_recv()

            @pl.loop(0, n)
            def _(block):
                rows = rows_at(block, rows_a)
                absorb_rows(sum_a.at[depth, part, rows, :], land_a.at[part, rows, :])

            if depth > 0:
                pl.semaphore_signal(
                    swap_free.at[part], inc=1, device_id=spot.partner, device_id_type=MESH
                )
            launch_part(piece_a, part)
            if depth > 0 and part == 1:
                for copy in load_left(depth - 1):
                    copy.start()
            at(("mats", part))

    def reload_attn():
        for part in range(2):
            swap_copy(1, part).wait_send()
        load_attn(0).start()

    def half_copy(which, stage):
        buffer = out_half if which == 0 else table_half
        return remote(
            buffer.at[2 * stage],
            buffer.at[2 * stage + 1],
            half_send.at[which, stage],
            half_recv.at[which, stage],
            spot.partner if stage == 0 else spot.across,
        )

    def half_rows(rows, side):
        return pl.ds(pl.multiple_of(side * (rows // 2), 16), rows // 2)

    def half_start(which, source):
        buffer = out_half if which == 0 else table_half
        buffer[0] = source[half_rows(source.shape[0], other), :].astype(jnp.bfloat16)
        half_copy(which, 0).start()

    def half_fold(which, source):
        buffer = out_half if which == 0 else table_half
        half_copy(which, 0).wait_recv()
        own = source[half_rows(source.shape[0], core), :]
        buffer[2] = (own + buffer[1].astype(jnp.float32)).astype(jnp.bfloat16)
        half_copy(which, 1).start()

    def half_out(which):
        if which == 0:
            source, target = out_done, out_sum.at[half_rows(out_sum.shape[0], core), :]
        else:
            source = table_grad.at[half_rows(table_sum.shape[0], core), :]
            target = table_sum.at[half_rows(table_sum.shape[0], core), :]
        return (
            pltpu.make_async_copy(source, target, half_sem.at[which]),
            remote(source, target, half_send.at[which, 2], half_recv.at[which, 2], spot.partner),
        )

    def add_squares(value):
        squares[...] += jnp.sum(value * value, axis=0, keepdims=True)

    def half_end(which):
        buffer = out_half if which == 0 else table_half
        half_copy(which, 1).wait_recv()
        value = buffer[2].astype(jnp.float32) + buffer[3].astype(jnp.float32)
        if which == 0:
            out_done[...] = value
        else:
            table_grad[half_rows(table_sum.shape[0], core), :] = value
        width = squares.shape[1]
        for start in range(0, value.shape[1], width):
            add_squares(value[:, start : start + width])
        for copy in half_out(which):
            copy.start()

    def small_copy(stage):
        bit = 1 << max(0, stage - 2)
        pair = spot.mp + bit - 2 * bit * ((spot.mp // bit) % 2)
        device = (spot.partner, spot.across)[stage] if stage < 2 else (spot.dp, pair)
        return remote(
            small.at[stage],
            small_in.at[stage],
            small_send.at[stage],
            small_recv.at[stage],
            device,
        )

    def small_next(stage):
        small_copy(stage).wait_recv()
        small[stage + 1] = small[stage] + small_in[stage]
        if stage < 4:
            small_copy(stage + 1).start()

    def deal_copy(offset, arriving):
        source = columns_out.at[peer(offset)]
        target = columns_in.at[peer(-offset) if arriving else spot.mp]
        return remote(
            source,
            target,
            deal_send.at[offset - 1],
            deal_recv.at[offset - 1],
            (spot.dp, peer(offset)),
        )

    def table_blocks(first, last):
        @pl.loop(first, last)
        def _(block):
            row = lax.broadcasted_iota(jnp.int32, (256, 1), 0) + block * 256
            value = jnp.zeros((columns_in.shape[1], 256), jnp.float32)
            for whose in range(n):
                chosen = (row == ids_ref[whose : whose + 1, :]).astype(jnp.bfloat16)
                value = value + dot_nt(columns_in[whose], chosen)
            table_grad[:, pl.ds(pl.multiple_of(block * 256, 256), 256)] = value

    squares[...] = jnp.zeros_like(squares)
    layer(
        1,
        {
            "own": [load_out.wait, lambda: half_start(0, out_grad_ref)],
            ("far", 1): [lambda: half_fold(0, out_grad_ref)],
            "half": [lambda: relay(3, 1)],
            ("mats", 1): [lambda: relay(3, 2)],
        },
    )
    layer(
        0,
        {
            "own": [reload_attn],
            ("far", 0): [lambda: relay(3, 3)],
            ("far", 1): [lambda: relay(2, 1), lambda: finish(3)],
            ("ffn", 3): [lambda: relay(2, 2), lambda: conclude(3), lambda: half_end(0)],
            "half": [lambda: relay(2, 3), lambda: relay(1, 1)],
            "heads": [lambda: finish(2), lambda: relay(1, 2)],
        },
    )
    load_first.wait()
    grad_sum, small[0, 0:1, :], small[0, 1:2, :] = norm_back(
        state[...], pre[0], gains_ref[0, 0:1, :]
    )
    width = squares.shape[1]
    lane = lax.broadcasted_iota(jnp.int32, (1, width), 1)
    tally = jnp.sum(losses_ref[...], axis=1, keepdims=True) * (1.0 / n)
    loss, slots = tally[0:1, :], tally[1:2, :]
    small[0, 10:11, :] = jnp.where(lane == 0, loss, jnp.where(lane == 1, slots, 0.0))
    small[0, 11:16, :] = jnp.zeros((5, width), jnp.float32)
    small_copy(0).start()
    turned = grad_sum.T.astype(jnp.bfloat16)
    share = columns_in.shape[1]
    for whose in range(n):
        columns_out[whose] = turned[whose * share : (whose + 1) * share, :]
    for offset in range(1, n):
        deal_copy(offset, False).start()
    columns_in[spot.mp] = columns_out[spot.mp]
    blocks = table_sum.shape[1] // 256
    small_next(0)
    relay(1, 3)
    conclude(2)
    for offset in range(1, n):
        deal_copy(offset, True).wait_recv()
    table_blocks(0, 5)
    relay(0, 1)
    small_next(1)
    table_blocks(5, 10)
    finish(1)
    table_blocks(10, blocks)
    half_start(1, table_grad)
    relay(0, 2)
    small_next(2)
    conclude(1)
    half_fold(1, table_grad)
    relay(0, 3)
    small_next(3)
    half_end(1)
    finish(0)
    small_next(4)
    loss_out[...] = small[5, 10:11, 0:128]
    for index in range(5):
        gains_out[index] = small[5, 2 * index : 2 * index + 2, :]
    conclude(0)

    square = jnp.sum(squares[...], axis=1, keepdims=True)
    square_parts[core * n + spot.mp] = jnp.broadcast_to(square, square_parts.shape[1:])

    def norm_copy(side, offset, arriving):
        own = square_parts.at[core * n + spot.mp]
        whose = (core + side - 2 * core * side) * n + peer(-offset)
        return remote(
            own,
            square_parts.at[whose] if arriving else own,
            norm_send.at[side, offset],
            norm_recv.at[side, offset],
            ((spot.dp, spot.partner[0])[side], peer(offset)),
        )

    far_squares = [(side, offset) for offset in range(n) for side in range(2)][1:]
    for side, offset in far_squares:
        norm_copy(side, offset, False).start()
    gains_grad = small[5, 0:10, :]
    square = jnp.sum(jnp.sum(gains_grad * gains_grad, axis=0, keepdims=True), axis=1, keepdims=True)
    for side, offset in far_squares:
        norm_copy(side, offset, True).wait_recv()
    for whose in range(2 * n):
        square = square + square_parts[whose, 0:1, :]
    square_out[...] = square

    for half in range(STRIPS):
        pair_copy(0, 0, half).wait_send()
        for depth in range(LAYERS):
            pair_copy(1, depth, half).wait_send()
    for side, offset in far_squares:
        norm_copy(side, offset, False).wait_send()
    for offset in range(1, n):
        deal_copy(offset, False).wait_send()
    for stage in range(5):
        small_copy(stage).wait_send()
    for which in range(2):
        half_copy(which, 0).wait_send()
        half_copy(which, 1).wait_send()
        local, away = half_out(which)
        local.wait()
        away.wait()
    for turn in range(total - SLOTS, total):
        core_copy(turn).wait_send()
    for part in range(2):
        swap_copy(0, part).wait_send()
    for piece in range(2 * LAYERS):
        for way, part in WAYS:
            for step in range(1, last_step(n, way, part) + 1):
                ring_copy(piece, way, part, step).wait_send()
        for part in range(2):
            across_copy(piece, part).wait_send()
        local, away = out_copies(piece)
        if piece < 2:
            local.wait()
            away.wait_send()
        away.wait_recv()


def backward_call(
    n, ids, lengths, losses, grad, first, gains, out_grad, kept, attn_full, ffn_full, slope, act, table
):
    inputs, proj, mixed, pre, mid = kept
    count, width = grad.shape
    rows_f = ffn_full.shape[3]
    groups = n // 2
    rows_a = attn_full.shape[2] // n
    rows_v = out_grad.shape[0]
    words, share = table.shape
    f32, bf16 = jnp.float32, jnp.bfloat16
    vmem = pl.BlockSpec(memory_space=pltpu.VMEM)
    anywhere = pl.BlockSpec(memory_space=pl.ANY)
    shape = jax.ShapeDtypeStruct
    dma = pltpu.SemaphoreType.DMA
    regular = pltpu.SemaphoreType.REGULAR
    ring_sems = dma((2 * LAYERS, 2, 2, n // 2))
    return pl.pallas_call(
        functools.partial(backward_kernel, n),
        out_shape=(
            shape((LAYERS, 4, rows_a, width), f32),
            shape((LAYERS, 2, rows_f, width), bf16),
            shape((share, words), f32),
            shape((rows_v, width), f32),
            shape((1, 128), f32),
            shape(gains.shape, f32),
            shape((1, 128), f32),
        ),
        in_specs=[vmem] * 4 + [anywhere] * 12,
        out_specs=(anywhere,) * 4 + (vmem,) * 3,
        scratch_shapes=[
            pltpu.VMEM(out_grad.shape, f32),
            pltpu.VMEM((3, count, width), bf16),
            pltpu.VMEM((2, count, width), f32),
            pltpu.VMEM((4, width, width), bf16),
            pltpu.VMEM((groups, 2, rows_f, width), bf16),
            pltpu.VMEM((groups + 1, count, rows_f), f32),
            pltpu.VMEM((LAYERS, 2, width, width), bf16),
            pltpu.VMEM((LAYERS, groups, rows_f, width), bf16),
            pltpu.VMEM((SLOTS, rows_f, width), bf16),
            pltpu.VMEM((SLOTS, rows_f, width), bf16),
            pltpu.VMEM((2, width, width), bf16),
            pltpu.VMEM((2, 2, n // 2, rows_a, width), bf16),
            pltpu.VMEM((2, 2, n // 2, rows_f // 4, width), bf16),
            pltpu.VMEM((LAYERS, count, width), bf16),
            pltpu.VMEM((count, width), f32),
            pltpu.VMEM((LAYERS, count, width), bf16),
            pltpu.VMEM((LAYERS, count, width), bf16),
            pltpu.VMEM((count, width), f32),
            pltpu.VMEM((5, count, width), bf16),
            pltpu.VMEM((2, count, width), bf16),
            pltpu.VMEM((groups, 2, 2 * count, rows_f), bf16),
            pltpu.VMEM((2, 2 * count, width), bf16),
            pltpu.VMEM((LAYERS, 2, 2, rows_a, width), bf16),
            pltpu.VMEM((LAYERS, 2, rows_f // 2, width), bf16),
            pltpu.VMEM((2, rows_a, width), f32),
            pltpu.VMEM((rows_f, width), bf16),
            dma((1,)),
            dma((3, groups)),
            dma((groups + 1,)),
            dma((2,)),
            dma((3,)),
            dma((LAYERS * groups,)),
            dma((LAYERS * groups,)),
            regular((1,)),
            dma((LAYERS, 2)),
            dma((LAYERS, 2)),
            regular((2,)),
            ring_sems,
            ring_sems,
            regular((2, 2, 2, n // 2)),
            dma((2, LAYERS, STRIPS)),
            dma((2, LAYERS, STRIPS)),
            dma((2 * LAYERS, 2)),
            dma((2 * LAYERS, 2)),
            dma((2 * LAYERS,)),
            dma((2 * LAYERS,)),
            dma((2 * LAYERS,)),
            pltpu.VMEM((6, 16, width), f32),
            pltpu.VMEM((5, 16, width), f32),
            pltpu.VMEM((n, share, count), bf16),
            pltpu.VMEM((n, share, count), bf16),
            pltpu.VMEM((share, words), f32),
            pltpu.VMEM((4, share // 2, words), bf16),
            pltpu.VMEM((4, rows_v // 2, width), bf16),
            pltpu.VMEM((rows_v // 2, width), f32),
            pltpu.VMEM((1, width), f32),
            pltpu.VMEM((2 * n, 8, 128), f32),
            dma((4,)),
            dma((5,)),
            dma((5,)),
            dma((n - 1,)),
            dma((n - 1,)),
            dma((2, 3)),
            dma((2, 3)),
            dma((2,)),
            dma((2, n)),
            dma((2, n)),
        ],
        compiler_params=pltpu.CompilerParams(
            collective_id=2, has_side_effects=True, vmem_limit_bytes=VMEM_LIMIT
        ),
        name="backward_layers",
    )(
        ids, lengths, losses, gains, out_grad, inputs, mixed, mid, grad, first,
        proj, pre, attn_full, ffn_full, slope, act,
    )


def merged(value, axis, join):
    pieces = jax.tree.map(lambda part: lax.all_gather(part, axis), value)
    head = jax.tree.map(lambda part: part[0], pieces)
    tail = jax.tree.map(lambda part: part[1:], pieces)
    total, _ = lax.scan(lambda total, section: (join(total, section), None), head, tail)
    return total


def sinusoid(count, width):
    places = jnp.arange(count, dtype=jnp.float32)[:, None]
    freqs = jnp.exp(jnp.arange(width // 2, dtype=jnp.float32) * (-2.0 * math.log(10000.0) / width))
    angles = places * freqs[None, :]
    return jnp.concatenate([jnp.sin(angles), jnp.cos(angles)], axis=1)


def layer_norm(values, gain, shift):
    centre = jnp.mean(values, axis=-1, keepdims=True)
    offset = values - centre
    spread = jnp.mean(offset * offset, axis=-1, keepdims=True)
    inverse = lax.rsqrt(spread + norm_eps)
    normed = offset * inverse
    return (normed * gain + shift, (normed, inverse))


def norm_backward(grad, saved, gain):
    normed, inverse = saved
    scaled = grad * gain
    centred = scaled - jnp.mean(scaled, axis=-1, keepdims=True)
    result = inverse * (centred - normed * jnp.mean(scaled * normed, axis=-1, keepdims=True))
    return (result, jnp.stack([jnp.sum(grad * normed, axis=0), jnp.sum(grad, axis=0)]))


def gelu_exact(values):
    return jax.nn.gelu(values, approximate=False)


def gelu_back(hidden, grad):
    unused, pullback = jax.vjp(gelu_exact, hidden)
    return pullback(grad)[0]


def masked_scores(query, keyed, length):
    scale = query.shape[-1] ** (-0.5)
    scores = jnp.einsum("hqe,hke->hqk", query, keyed, preferred_element_type=jnp.float32) * scale
    visible = jnp.arange(keyed.shape[1]) < length
    return jnp.where(visible[None, None, :], scores, masked_score)


def fetch_forward(attn_part, ffn_part):
    return (
        lax.all_gather(attn_part, "mp", axis=1, tiled=True),
        lax.all_gather(ffn_part, "mp", axis=1, tiled=True),
    )


def fetch_backward(attn_part, ffn_part):
    return (
        lax.all_gather(attn_part, "mp", axis=1, tiled=True),
        lax.all_gather(ffn_part, "mp", axis=1, tiled=True),
    )


def reduce_layer(attn_grad, ffn_grad):
    return (
        lax.psum_scatter(attn_grad, "mp", scatter_dimension=1, tiled=True),
        lax.psum_scatter(ffn_grad, "mp", scatter_dimension=1, tiled=True),
    )


def ffn_forward(middle_b, ffn_w, unit_mask):
    hidden = jnp.einsum("td,fd->tf", middle_b, ffn_w[0], preferred_element_type=jnp.float32)
    active = (gelu_exact(hidden) * unit_mask[None, :]).astype(jnp.bfloat16)
    output = jnp.einsum("tf,fd->td", active, ffn_w[1], preferred_element_type=jnp.float32)
    return (hidden, active, output)


def ffn_backward(grad_out, middle_b, hidden, active, ffn_w, unit_mask):
    grad_active = jnp.einsum("td,fd->tf", grad_out, ffn_w[1], preferred_element_type=jnp.float32)
    grad_hidden = gelu_back(hidden, grad_active * unit_mask[None, :]).astype(jnp.bfloat16)
    up_grad = jnp.einsum("tf,td->fd", grad_hidden, middle_b, preferred_element_type=jnp.float32)
    down_grad = jnp.einsum("tf,td->fd", active, grad_out, preferred_element_type=jnp.float32)
    from_ffn = jnp.einsum("tf,fd->td", grad_hidden, ffn_w[0], preferred_element_type=jnp.float32)
    return (jnp.stack([up_grad, down_grad]), from_ffn)


def layer_forward(states, attn_w, ffn_w, pair, length, unit_mask):
    count = states.shape[0]
    inputs = states.astype(jnp.bfloat16)
    projected = jnp.einsum(
        "td,kde->kte", inputs, attn_w[:3], preferred_element_type=jnp.float32
    ).astype(jnp.bfloat16)
    heads = projected.reshape(3, count, HEADS, -1).transpose(0, 2, 1, 3)
    scores = masked_scores(heads[0], heads[1], length)
    peak = jnp.max(scores, axis=-1, keepdims=True)
    expo = jnp.exp(scores - peak)
    total = jnp.sum(expo, axis=-1, keepdims=True)
    log_total = peak + jnp.log(total)
    probs = (expo / total).astype(jnp.bfloat16)
    mixed = jnp.einsum("hqk,hke->hqe", probs, heads[2], preferred_element_type=jnp.float32)
    mixed = mixed.transpose(1, 0, 2).reshape(count, -1).astype(jnp.bfloat16)
    branch = jnp.dot(mixed, attn_w[3], preferred_element_type=jnp.float32)
    middle, norm_one = layer_norm(states + branch, pair[0, 0], pair[0, 1])
    middle_b = middle.astype(jnp.bfloat16)
    hidden, active, output = ffn_forward(middle_b, ffn_w, unit_mask)
    result, norm_two = layer_norm(middle + output, pair[1, 0], pair[1, 1])
    return (result, (inputs, heads, log_total, mixed, norm_one, middle_b, hidden, active, norm_two))


def layer_backward(grad, attn_w, ffn_w, pair, length, unit_mask, kept):
    inputs, heads, log_total, mixed, norm_one, middle_b, hidden, active, norm_two = kept
    count = inputs.shape[0]
    grad_two, pair_two = norm_backward(grad, norm_two, pair[1, 0])
    ffn_grad, from_ffn = ffn_backward(
        grad_two.astype(jnp.bfloat16), middle_b, hidden, active, ffn_w, unit_mask
    )
    grad_one, pair_one = norm_backward(grad_two + from_ffn, norm_one, pair[0, 0])
    grad_branch = grad_one.astype(jnp.bfloat16)
    output_grad = jnp.einsum("td,te->de", mixed, grad_branch, preferred_element_type=jnp.float32)
    grad_mixed = jnp.einsum("te,de->td", grad_branch, attn_w[3], preferred_element_type=jnp.float32)
    grad_mixed = grad_mixed.astype(jnp.bfloat16).reshape(count, HEADS, -1).transpose(1, 0, 2)
    scale = heads.shape[-1] ** (-0.5)
    probs = jnp.exp(masked_scores(heads[0], heads[1], length) - log_total)
    grad_values = jnp.einsum(
        "hqk,hqe->hke", probs.astype(jnp.bfloat16), grad_mixed, preferred_element_type=jnp.float32
    )
    grad_probs = jnp.einsum(
        "hqe,hke->hqk", grad_mixed, heads[2], preferred_element_type=jnp.float32
    )
    grad_scores = probs * (grad_probs - jnp.sum(grad_probs * probs, axis=-1, keepdims=True))
    grad_scores = grad_scores.astype(jnp.bfloat16)
    grad_query = (
        jnp.einsum("hqk,hke->hqe", grad_scores, heads[1], preferred_element_type=jnp.float32)
        * scale
    )
    grad_key = (
        jnp.einsum("hqk,hqe->hke", grad_scores, heads[0], preferred_element_type=jnp.float32)
        * scale
    )
    stacked = (
        jnp.stack([grad_query, grad_key, grad_values]).transpose(0, 2, 1, 3).reshape(3, count, -1)
    )
    stacked = stacked.astype(jnp.bfloat16)
    input_grad = jnp.einsum("td,kte->kde", inputs, stacked, preferred_element_type=jnp.float32)
    from_attn = jnp.einsum("kte,kde->td", stacked, attn_w[:3], preferred_element_type=jnp.float32)
    attn_grad = jnp.concatenate([input_grad, output_grad[None]], axis=0)
    return (grad_one + from_attn, attn_grad, ffn_grad, jnp.stack([pair_one, pair_two]))


def adamw(weight, moment_one, moment_two, grad, decay, rate):
    moment_one = beta_one * moment_one + (1.0 - beta_one) * grad
    moment_two = beta_two * moment_two + (1.0 - beta_two) * grad * grad
    fixed_one = moment_one / (1.0 - beta_one**STEP)
    fixed_two = moment_two / (1.0 - beta_two**STEP)
    weight = weight - rate * (fixed_one / (jnp.sqrt(fixed_two) + adam_eps) + decay * weight)
    return (moment_one, moment_two, weight)


def combine_vocab(first, second):
    peak = jnp.maximum(first[0], second[0])
    total = first[1] * jnp.exp(first[0] - peak) + second[1] * jnp.exp(second[0] - peak)
    return (peak, total, first[2] + second[2])


def local_general(
    tokens,
    lengths,
    places,
    targets,
    ramp,
    attn,
    attn_m,
    attn_v,
    ffn,
    ffn_m,
    ffn_v,
    table,
    table_m,
    table_v,
    out_table,
    out_m,
    out_v,
    gains,
    gains_m,
    gains_v,
):
    rank = lax.axis_index("mp")
    count = tokens.shape[2]
    flat_ids = tokens.reshape(-1)
    all_lengths = lengths.reshape(-1)
    length = lax.dynamic_index_in_dim(all_lengths, rank, keepdims=False)
    masks = jnp.minimum(ramp, RAMP).astype(jnp.float32) / RAMP
    unit_masks = [masks[depth] for depth in range(LAYERS)]
    looked = jnp.take(table, flat_ids, axis=0)
    embedded = lax.all_to_all(looked, "mp", split_axis=0, concat_axis=1, tiled=True)
    states, norm_zero = layer_norm(
        embedded + sinusoid(count, embedded.shape[1]), gains[0, 0], gains[0, 1]
    )
    kept_all = []
    weights_all = []
    for depth in range(LAYERS):
        attn_w, ffn_w = fetch_forward(
            attn[depth].astype(jnp.bfloat16), ffn[depth].astype(jnp.bfloat16)
        )
        states, kept = layer_forward(
            states, attn_w, ffn_w, gains[1 + 2 * depth : 3 + 2 * depth], length, unit_masks[depth]
        )
        kept_all.append(kept)
        weights_all.append(None)
    spots = places.reshape(-1)
    picked = jnp.take(states, spots, axis=0).astype(jnp.bfloat16)
    picked_all = lax.all_gather(picked, "mp", axis=0, tiled=True)
    out_b = out_table.astype(jnp.bfloat16)
    logits = jnp.einsum("rd,vd->rv", picked_all, out_b, preferred_element_type=jnp.float32)
    labels = targets.reshape(-1)
    columns = rank * out_table.shape[0] + jnp.arange(out_table.shape[0])
    hits = (labels[:, None] == columns[None, :]).astype(jnp.float32)
    peak = jnp.max(logits, axis=1)
    expsum = jnp.sum(jnp.exp(logits - peak[:, None]), axis=1)
    target_part = jnp.sum(hits * logits, axis=1)
    peak_all, expsum_all, target_all = merged((peak, expsum, target_part), "mp", combine_vocab)
    log_total = peak_all + jnp.log(expsum_all)
    slot_count = targets.shape[2]
    counted = jnp.maximum(1, all_lengths * slot_count // count)
    valid = (jnp.arange(slot_count)[None, :] < counted[:, None]).reshape(-1)
    loss_pair = jnp.stack(
        [
            jnp.sum(jnp.where(valid, log_total - target_all, 0.0)),
            jnp.sum(counted).astype(jnp.float32),
        ]
    )
    grad_logits = jnp.where(
        valid[:, None], jnp.exp(logits - log_total[:, None]) - hits, 0.0
    ).astype(jnp.bfloat16)
    out_grad = jnp.einsum("rv,rd->vd", grad_logits, picked_all, preferred_element_type=jnp.float32)
    picked_grad = lax.psum_scatter(
        jnp.dot(grad_logits, out_b, preferred_element_type=jnp.float32),
        "mp",
        scatter_dimension=0,
        tiled=True,
    )
    grad = jnp.zeros_like(states).at[spots].add(picked_grad)
    attn_parts = [None] * LAYERS
    ffn_parts = [None] * LAYERS
    pair_grads = [None] * LAYERS
    for depth in reversed(range(LAYERS)):
        attn_w, ffn_w = fetch_backward(
            attn[depth].astype(jnp.bfloat16), ffn[depth].astype(jnp.bfloat16)
        )
        grad, attn_grad, ffn_grad, pair_grad = layer_backward(
            grad,
            attn_w,
            ffn_w,
            gains[1 + 2 * depth : 3 + 2 * depth],
            length,
            unit_masks[depth],
            kept_all[depth],
        )
        attn_parts[depth], ffn_parts[depth] = reduce_layer(attn_grad, ffn_grad)
        pair_grads[depth] = pair_grad
    grad_sum, zero_grad = norm_backward(grad, norm_zero, gains[0, 0])
    returned = lax.all_to_all(grad_sum, "mp", split_axis=1, concat_axis=0, tiled=True)
    table_grad = jnp.zeros_like(table).at[flat_ids].add(returned)
    gains_grad = jnp.concatenate([zero_grad[None]] + pair_grads, axis=0)
    attn_sum, ffn_sum, table_sum, out_sum, gains_part, loss = lax.psum(
        (jnp.stack(attn_parts), jnp.stack(ffn_parts), table_grad, out_grad, gains_grad, loss_pair),
        "dp",
    )
    shard_squares = (
        jnp.sum(attn_sum * attn_sum)
        + jnp.sum(ffn_sum * ffn_sum)
        + jnp.sum(table_sum * table_sum)
        + jnp.sum(out_sum * out_sum)
    )
    square_total, gains_sum = lax.psum((shard_squares, gains_part), "mp")
    grad_norm = jnp.sqrt(square_total + jnp.sum(gains_sum * gains_sum))
    factor = clip_limit / jnp.maximum(grad_norm, clip_limit)
    attn_m_new, attn_v_new, attn_new = adamw(
        attn, attn_m, attn_v, attn_sum * factor, weight_decay, learn_rate
    )
    ffn_m_new, ffn_v_new, ffn_new = adamw(
        ffn, ffn_m, ffn_v, ffn_sum * factor, weight_decay, learn_rate
    )
    table_m_new, table_v_new, table_new = adamw(
        table, table_m, table_v, table_sum * factor, weight_decay, learn_rate
    )
    out_m_new, out_v_new, out_new = adamw(
        out_table, out_m, out_v, out_sum * factor, weight_decay, learn_rate
    )
    gains_m_new, gains_v_new, gains_new = adamw(
        gains, gains_m, gains_v, gains_sum * factor, 0.0, gain_rate
    )
    return (
        loss,
        grad_norm.reshape(1),
        attn_m_new,
        attn_v_new,
        attn_new,
        ffn_m_new,
        ffn_v_new,
        ffn_new,
        table_m_new,
        table_v_new,
        table_new,
        out_m_new,
        out_v_new,
        out_new,
        gains_m_new,
        gains_v_new,
        gains_new,
    )


def local(
    tokens,
    lengths,
    places,
    targets,
    ramp,
    attn,
    attn_m,
    attn_v,
    ffn,
    ffn_m,
    ffn_v,
    table,
    table_m,
    table_v,
    out_table,
    out_m,
    out_v,
    gains,
    gains_m,
    gains_v,
):
    n = tokens.shape[1]
    where = jnp.asarray(positions(tokens.shape[2], gains.shape[2]))
    attn_full, ffn_full, first, *kept, slope, act, grad, out_grad, losses = forward_call(
        n, tokens[0], lengths, places[0], targets[0], ramp, gains, table.T, where, out_table, attn, ffn
    )
    attn_sum, ffn_sum, table_turned, out_sum, loss, gains_sum, square = backward_call(
        n, tokens[0], lengths, losses, grad, first, gains, out_grad, kept, attn_full, ffn_full, slope, act, table
    )
    table_sum = table_turned.T
    ffn_sum = ffn_sum.astype(jnp.float32)
    grad_norm = jnp.sqrt(square[0, 0])
    factor = clip_limit / jnp.maximum(grad_norm, clip_limit)
    attn_m_new, attn_v_new, attn_new = adamw(
        attn, attn_m, attn_v, attn_sum * factor, weight_decay, learn_rate
    )
    ffn_m_new, ffn_v_new, ffn_new = adamw(
        ffn, ffn_m, ffn_v, ffn_sum * factor, weight_decay, learn_rate
    )
    table_m_new, table_v_new, table_new = adamw(
        table, table_m, table_v, table_sum * factor, weight_decay, learn_rate
    )
    out_m_new, out_v_new, out_new = adamw(
        out_table, out_m, out_v, out_sum * factor, weight_decay, learn_rate
    )
    gains_m_new, gains_v_new, gains_new = adamw(
        gains, gains_m, gains_v, gains_sum * factor, 0.0, gain_rate
    )
    return (
        loss[0, :2],
        grad_norm.reshape(1),
        attn_m_new,
        attn_v_new,
        attn_new,
        ffn_m_new,
        ffn_v_new,
        ffn_new,
        table_m_new,
        table_v_new,
        table_new,
        out_m_new,
        out_v_new,
        out_new,
        gains_m_new,
        gains_v_new,
        gains_new,
    )


def solution(mesh):
    in_specs = (
        P("dp", None, None),
        P("dp", None),
        P("dp", "mp", None),
        P("dp", None, None),
        P(),
        P(None, None, "mp", None),
        P(None, None, "mp", None),
        P(None, None, "mp", None),
        P(None, None, "mp", None),
        P(None, None, "mp", None),
        P(None, None, "mp", None),
        P(None, "mp"),
        P(None, "mp"),
        P(None, "mp"),
        P("mp", None),
        P("mp", None),
        P("mp", None),
        P(),
        P(),
        P(),
    )
    out_specs = (
        P(),
        P(),
        P(None, None, "mp", None),
        P(None, None, "mp", None),
        P(None, None, "mp", None),
        P(None, None, "mp", None),
        P(None, None, "mp", None),
        P(None, None, "mp", None),
        P(None, "mp"),
        P(None, "mp"),
        P(None, "mp"),
        P("mp", None),
        P("mp", None),
        P("mp", None),
        P(),
        P(),
        P(),
    )
    fits = mesh.shape['mp'] == 8 and mesh.shape['dp'] == 4
    chosen = local if fits else local_general
    return jax.shard_map(chosen, mesh=mesh, in_specs=in_specs, out_specs=out_specs, check_vma=False)
```

```python
import functools
import math

import jax
import jax.numpy as jnp
import numpy as np
from jax import lax
from jax.experimental import pallas as pl
from jax.experimental.pallas import tpu as pltpu
from jax.sharding import PartitionSpec as P

HEADS = 12
LAYERS = 2
STEP = 10
RAMP = 4


norm_eps = 1e-05
beta_one = 0.9
beta_two = 0.999
learn_rate = 0.02
gain_rate = 0.3
weight_decay = 0.01
adam_eps = 1e-08
clip_limit = 1.0
masked_score = -1000000000.0


MESH = pl.DeviceIdType.MESH
VMEM_LIMIT = 62 * 1024 * 1024
BACKWARD_LIMIT = 59 * 1024 * 1024
SLOTS = 3
STRIPS = 2


def dot_nn(left, right):
    return lax.dot_general(
        left, right, (((1,), (0,)), ((), ())), preferred_element_type=jnp.float32
    )


def dot_nt(left, right):
    return lax.dot_general(
        left, right, (((1,), (1,)), ((), ())), preferred_element_type=jnp.float32
    )


def dot_tn(left, right):
    return lax.dot_general(
        left, right, (((0,), (0,)), ((), ())), preferred_element_type=jnp.float32
    )


def positions(count, width):
    angles = np.arange(count)[:, None] * np.exp(
        np.arange(width // 2) * (-2.0 * math.log(10000.0) / width)
    )
    return np.concatenate([np.sin(angles), np.cos(angles)], axis=1).astype(np.float32)


def ring_index(place, n):
    late = place // (n // 2)
    return (1 - late) * 2 * place + late * (2 * (n - 1 - place) + 1)


def ring_place(index, n):
    odd = index % 2
    return (1 - odd) * (index // 2) + odd * (n - 1 - index // 2)


class Spot:
    def __init__(self, n):
        self.n = n
        self.dp = lax.axis_index("dp")
        self.mp = lax.axis_index("mp")
        self.core = self.dp % 2
        self.row = self.dp // 2
        self.place = ring_place(self.mp, n)
        self.partner = (self.dp + 1 - 2 * self.core, self.mp)
        self.across = ((self.dp + 2) % 4, self.mp)
        self.ring = (
            (self.dp, ring_index((self.place + 1) % n, n)),
            (self.dp, ring_index((self.place + n - 1) % n, n)),
        )

    def shard(self, offset):
        return ring_index((self.place + offset + self.n) % self.n, self.n)


def greet(devices):
    barrier = pltpu.get_barrier_semaphore()
    for device in devices:
        pl.semaphore_signal(barrier, inc=1, device_id=device, device_id_type=MESH)
    pl.semaphore_wait(barrier, len(devices))


def last_step(n, way, part):
    return n // 2 if way == part else n // 2 - 1


WAYS = ((0, 0), (1, 1), (0, 1), (1, 0))


def ring_columns(row, width, cut):
    return pl.ds(pl.multiple_of(row * cut, 128), width - cut)


def edge_columns(row, width, cut):
    return pl.ds(pl.multiple_of(row * (width - cut), 128), cut)


def cut_of(width, share):
    return 128 * (width // 128 // share)


def normed_of(values):
    centre = jnp.mean(values, axis=-1, keepdims=True)
    offset = values - centre
    spread = jnp.mean(offset * offset, axis=-1, keepdims=True)
    inverse = lax.rsqrt(spread + norm_eps)
    return offset * inverse, inverse


def forward_kernel(
    n,
    ids_ref,
    lengths_ref,
    places_ref,
    targets_ref,
    ramp_ref,
    gains_ref,
    table_ref,
    where_ref,
    out_sh,
    attn_sh,
    ffn_sh,
    attn_full,
    ffn_full,
    first_out,
    inputs_out,
    proj_out,
    mixed_out,
    pre_out,
    mid_out,
    slope_ref,
    act_ref,
    grad_ref,
    out_grad_ref,
    loss_ref,
    first_ref,
    out_ref,
    inputs_ref,
    proj_ref,
    mixed_ref,
    pre_ref,
    mid_ref,
    mask_ref,
    table_b,
    places_row,
    labels_row,
    wa,
    wf,
    raw_a,
    raw_f,
    slope,
    act,
    far_sum,
    far_out,
    far_in,
    state,
    row_out,
    row_in,
    picked,
    stats,
    back_out,
    back_in,
    raw_sem,
    late_sem,
    early_sem,
    kept_sem,
    ring_send,
    ring_recv,
    core_send,
    core_recv,
    across_send,
    across_recv,
    pair_send,
    pair_recv,
    fan_send,
    fan_recv,
    beside_send,
    beside_recv,
):
    spot = Spot(n)
    core = spot.core
    rows_a = attn_sh.shape[2]
    rows_f = ffn_sh.shape[2]
    half_f = rows_f // 2
    part_f = half_f // 2
    steps = n // 2
    count, width = first_ref.shape
    share_e = table_ref.shape[0]
    words = table_ref.shape[1]
    slots = places_row.shape[1]
    slot_count = places_ref.shape[1]

    def rows_at(shard, rows):
        return pl.ds(pl.multiple_of(shard * rows, 16), rows)

    def remote(source, target, send, recv, device):
        return pltpu.make_async_remote_copy(
            src_ref=source,
            dst_ref=target,
            send_sem=send,
            recv_sem=recv,
            device_id=device,
            device_id_type=MESH,
        )

    def slot_f(way, step):
        if step == 0:
            return 0, 0
        return (0, 1) if step == steps else (step, way)

    def chunk_f(piece, way, part, step, side):
        group, half = slot_f(way, step)
        return wf.at[piece // 2, group, side, pl.ds(half * half_f + part * part_f, part_f), :]

    def chunk_a(piece, shard, part, side, edge):
        cut = cut_of(width, 3)
        if edge is None:
            columns = ring_columns(spot.row, width, cut)
        else:
            columns = edge_columns(edge, width, cut)
        return wa.at[piece // 2, 2 * side + part, rows_at(shard, rows_a), columns]

    def sign(way):
        return -1 if way == 0 else 1

    def ring_copy(piece, way, part, step, arriving):
        if piece % 2 == 0:
            target = chunk_a(piece, spot.shard(sign(way) * (step - 1 + arriving)), part, core, None)
            source = target
        else:
            target = chunk_f(piece, way, part, step, core)
            source = target if arriving else chunk_f(piece, way, part, step - 1, core)
        return remote(
            source,
            target,
            ring_send.at[piece, way, part, step - 1],
            ring_recv.at[piece, way, part, step - 1],
            spot.ring[way],
        )

    def core_copy(piece, way, part, step, side, edge):
        if piece % 2 == 0:
            target = chunk_a(piece, spot.shard(sign(way) * step), part, side, edge)
        else:
            target = chunk_f(piece, way, part, step, side)
        lane = 0 if edge is None else 1
        return remote(
            target,
            target,
            core_send.at[lane, piece, way, part, step - 1],
            core_recv.at[lane, piece, way, part, step - 1],
            spot.partner,
        )

    def across_copy(piece, way, part, step, row):
        target = chunk_a(piece, spot.shard(sign(way) * step), part, core, row)
        return remote(
            target,
            target,
            across_send.at[piece, way, part, step - 1],
            across_recv.at[piece, way, part, step - 1],
            spot.across,
        )

    def half_at(half):
        return pl.ds(half * (count // STRIPS), count // STRIPS)

    def pair_copy(which, depth, half):
        rows = half_at(half)
        if which == 0:
            source, target = mid_ref.at[depth, 0, rows, :], mid_ref.at[depth, 1, rows, :]
        else:
            source, target = far_out.at[depth, rows, :], far_in.at[depth, rows, :]
        return remote(
            source,
            target,
            pair_send.at[which, depth, half],
            pair_recv.at[which, depth, half],
            spot.across,
        )

    def peer(offset):
        return (spot.mp + offset + n) % n

    def fan_copy(which, offset, source, target):
        return remote(
            source,
            target,
            fan_send.at[which, offset - 1],
            fan_recv.at[which, offset - 1],
            (spot.dp, peer(offset)),
        )

    def share(which, buffer, offset):
        return fan_copy(which, offset, buffer.at[spot.mp], buffer.at[spot.mp])

    def arrived(which, buffer, offset):
        return fan_copy(which, offset, buffer.at[peer(-offset)], buffer.at[peer(-offset)])

    def deal(which, source, target, offset):
        return fan_copy(which, offset, source.at[peer(offset)], target.at[spot.mp])

    def raw_copy(piece):
        kind, depth = piece % 2, piece // 2
        if kind == 0:
            return pltpu.make_async_copy(attn_sh.at[depth], raw_a.at[depth], raw_sem.at[piece])
        rows = pl.ds(pl.multiple_of(spot.row * half_f, 16), half_f)
        return pltpu.make_async_copy(ffn_sh.at[depth, :, rows, :], raw_f.at[depth], raw_sem.at[piece])

    def take_own(piece):
        kind, depth = piece % 2, piece // 2
        raw_copy(piece).wait()
        if kind == 0:
            for which in range(4):
                wa[depth, which, rows_at(spot.mp, rows_a), :] = raw_a[depth, which].astype(
                    jnp.bfloat16
                )
        else:
            for which in range(2):
                wf[depth, 0, which, 0:half_f, :] = raw_f[depth, which].astype(jnp.bfloat16)

    def launch(piece):
        for way, part in WAYS:
            ring_copy(piece, way, part, 1, 0).start()

    def chains(step):
        return [(way, part) for way, part in WAYS if step <= last_step(n, way, part)]

    def pass_on(piece, step):
        for way, part in chains(step):
            ring_copy(piece, way, part, step, 1).wait_recv()
            if step < last_step(n, way, part):
                ring_copy(piece, way, part, step + 1, 0).start()
            if piece % 2 == 0:
                across_copy(piece, way, part, step, spot.row).start()
            core_copy(piece, way, part, step, core, None).start()

    def pass_edge(piece, step):
        for way, part in chains(step):
            across_copy(piece, way, part, step, 1 - spot.row).wait_recv()
            core_copy(piece, way, part, step, core, 1 - spot.row).start()

    def settle(piece, step):
        for way, part in chains(step):
            core_copy(piece, way, part, step, 1 - core, None).wait_recv()
            if piece % 2 == 0:
                core_copy(piece, way, part, step, 1 - core, 1 - spot.row).wait_recv()

    out_copies = []

    def write_out(source, target):
        copy = pltpu.make_async_copy(source, target, early_sem.at[len(out_copies)])
        copy.start()
        out_copies.append(copy)

    def look_up(offset):
        whose = peer(offset)
        tokens = ids_ref[pl.ds(whose, 1), :]

        size = 768

        def block(index, total):
            start = pl.multiple_of(index * size, 128)
            word = lax.broadcasted_iota(jnp.int32, (size, 1), 0) + start
            chosen = (word == tokens).astype(jnp.bfloat16)
            return total + dot_nn(table_b[:, pl.ds(start, size)], chosen)

        found = lax.fori_loop(
            0, words // size, block, jnp.zeros((share_e, count), jnp.float32)
        )
        row_out[whose] = found.astype(jnp.bfloat16)
        if offset > 0:
            deal(0, row_out, row_in, offset).start()

    raw_copy(0).start()
    late = (
        pltpu.make_async_copy(where_ref, first_ref, late_sem.at[0]),
        pltpu.make_async_copy(out_sh, out_ref, late_sem.at[1]),
    )
    for copy in late:
        copy.start()
    for piece in range(1, 2 * LAYERS):
        raw_copy(piece).start()
    greet([spot.partner, spot.across] + [(spot.dp, peer(offset)) for offset in range(1, n)])
    take_own(0)
    launch(0)
    for depth in range(LAYERS):
        for index in range(n):
            offset = (0, steps)[index] if index < 2 else (index // 2) * (2 * (index % 2) - 1)
            start = pl.multiple_of(spot.shard(offset) * rows_f, 128)
            grown = jnp.minimum(ramp_ref[depth : depth + 1, pl.ds(start, rows_f)], RAMP)
            grown = grown.astype(jnp.float32) / RAMP
            lanes_to = pl.ds((index % 2) * half_f, half_f)
            mask_ref[depth, index // 2 : index // 2 + 1, lanes_to] = jnp.where(
                spot.row == 0, grown[:, 0:half_f], grown[:, half_f:rows_f]
            )
    table_b[...] = table_ref[...].astype(jnp.bfloat16)
    places_row[...] = jnp.full_like(places_row, -1)
    places_row[0:1, 0:slot_count] = places_ref[...]
    labels_row[...] = jnp.full_like(labels_row, -1)
    for whose in range(n):
        labels_row[0:1, whose * slots : whose * slots + slot_count] = targets_ref[
            whose : whose + 1, :
        ]
    spans = lengths_ref[...].astype(jnp.float32)
    lane = lax.broadcasted_iota(jnp.int32, (1, n), 1)
    length = jnp.sum(jnp.where(lane == spot.mp, spans, 0.0), axis=1, keepdims=True)
    visible = lax.broadcasted_iota(jnp.int32, (1, count), 1).astype(jnp.float32) < length
    counted = jnp.maximum(jnp.floor(spans * (slot_count / count)), 1.0)
    lane = lax.broadcasted_iota(jnp.int32, (1, n * slots), 1)
    limit = jnp.zeros((1, n * slots), jnp.float32)
    for whose in range(n):
        limit = jnp.where(
            lane >= whose * slots, counted[:, whose : whose + 1] + whose * slots, limit
        )
    valid = lane.astype(jnp.float32) < limit
    loss_ref[1:2, :] = valid.astype(jnp.float32)
    for offset in range(1, 4):
        look_up(offset)
    pass_on(0, 1)
    for offset in range(4, 7):
        look_up(offset)
    pass_on(0, 2)
    pass_edge(0, 1)
    take_own(1)
    launch(1)
    look_up(7)
    look_up(0)
    row_in[spot.mp] = row_out[spot.mp]
    pass_on(0, 3)
    pass_edge(0, 2)
    for offset in range(1, n):
        arrived(0, row_in, offset).wait_recv()
    late[0].wait()
    first_ref[...] += row_in[...].reshape(width, count).astype(jnp.float32).T
    write_out(first_ref, first_out)
    normed, _ = normed_of(first_ref[...])
    state[...] = normed * gains_ref[0, 0:1, :] + gains_ref[0, 1:2, :]
    take_own(2)
    take_own(3)
    pass_on(0, 4)
    pass_edge(0, 3)

    lanes = lax.broadcasted_iota(jnp.int32, (1, 128), 1) < 64

    def head_pair(depth, pair):
        columns = pl.ds(pl.multiple_of(pair * 128, 128), 128)
        query = proj_ref[depth, 0, :, columns]
        keyed = proj_ref[depth, 1, :, columns]
        valued = proj_ref[depth, 2, :, columns]
        outs = []
        for side in range(2):
            mine = lanes if side == 0 else jnp.logical_not(lanes)
            scores = dot_nt(jnp.where(mine, query, jnp.zeros_like(query)), keyed) * 0.125
            scores = jnp.where(visible, scores, masked_score)
            expo = jnp.exp(scores - jnp.max(scores, axis=-1, keepdims=True))
            total = jnp.sum(expo, axis=-1, keepdims=True)
            outs.append(dot_nn((expo / total).astype(jnp.bfloat16), valued))
        mixed_ref[depth, :, columns] = jnp.where(lanes, outs[0], outs[1]).astype(jnp.bfloat16)

    def kept_copies(turn, depth, group, far, start, size):
        slot = turn % SLOTS
        here, there = pl.ds(0, size), pl.ds(start, size)
        return (
            pltpu.make_async_copy(
                slope.at[slot, here, :],
                slope_ref.at[depth, group, far, there, :],
                kept_sem.at[0, slot],
            ),
            pltpu.make_async_copy(
                act.at[slot, here, :],
                act_ref.at[depth, group, far, there, :],
                kept_sem.at[1, slot],
            ),
        )

    turns = []

    def ffn_block(depth, group, far, start, size):
        turn = len(turns)
        turns.append((depth, group, far, start, size))
        if turn >= SLOTS:
            for copy in kept_copies(turn, *turns[turn - SLOTS]):
                copy.wait()
        slot, rows, here = turn % SLOTS, pl.ds(start, size), pl.ds(0, size)
        hidden = dot_nt(mid_ref[depth, far, rows, :], wf[depth, group, 0])
        spread = 0.5 * (1.0 + lax.erf(hidden * (0.5**0.5)))
        mask = mask_ref[depth, group : group + 1, :]
        bell = jnp.exp(hidden * hidden * -0.5) * (1.0 / math.sqrt(2.0 * math.pi))
        slope[slot, here, :] = (spread + hidden * bell) * mask
        active = (hidden * spread * mask).astype(jnp.bfloat16)
        act[slot, here, :] = active
        for copy in kept_copies(*((turn,) + turns[turn])):
            copy.start()
        if far:
            far_sum[rows, :] += dot_nn(active, wf[depth, group, 1])
        else:
            pre_ref[depth, 1, rows, :] += dot_nn(active, wf[depth, group, 1])

    def ffn_own(depth, group):
        ffn_block(depth, group, 0, 0, count)

    def ffn_far(depth, group, half):
        ffn_block(depth, group, 1, half * (count // STRIPS), count // STRIPS)

    for depth in range(LAYERS):
        piece_a, piece_f = 2 * depth, 2 * depth + 1
        more = depth + 1 < LAYERS
        if depth > 0:
            pass_on(piece_a, 3)
            pass_edge(piece_a, 2)
            pass_on(piece_a, 4)
            pass_edge(piece_a, 3)
        pass_edge(piece_a, 4)
        for step in range(1, steps + 1):
            settle(piece_a, step)
        write_out(wa.at[depth], attn_full.at[depth])
        inputs = state[...].astype(jnp.bfloat16)
        inputs_ref[depth] = inputs
        for which in range(3):
            proj_ref[depth, which] = dot_nn(inputs, wa[depth, which]).astype(jnp.bfloat16)
        pass_on(piece_f, 1)

        @pl.loop(0, HEADS // 2)
        def _(pair):
            head_pair(depth, pair)

        pre_ref[depth, 0] = state[...] + dot_nn(mixed_ref[depth], wa[depth, 3])
        normed, _ = normed_of(pre_ref[depth, 0])
        middle = (
            normed * gains_ref[1 + 2 * depth, 0:1, :] + gains_ref[1 + 2 * depth, 1:2, :]
        )
        for half in range(STRIPS):
            mid_ref[depth, 0, half_at(half), :] = middle[
                half * (count // STRIPS) : (half + 1) * (count // STRIPS), :
            ].astype(jnp.bfloat16)
            pair_copy(0, depth, half).start()
        pre_ref[depth, 1] = middle
        far_sum[...] = jnp.zeros_like(far_sum)
        write_out(inputs_ref.at[depth], inputs_out.at[depth])
        write_out(proj_ref.at[depth], proj_out.at[depth])
        write_out(mixed_ref.at[depth], mixed_out.at[depth])
        pass_on(piece_f, 2)
        settle(piece_f, 1)
        ffn_own(depth, 1)
        pass_on(piece_f, 3)
        if more:
            launch(piece_a + 2)
        settle(piece_f, 2)
        ffn_own(depth, 2)
        for half in range(STRIPS):
            pair_copy(0, depth, half).wait_recv()
            ffn_far(depth, 1, half)
            ffn_far(depth, 2, half)
        write_out(mid_ref.at[depth], mid_out.at[depth])
        settle(piece_f, 3)
        for half in range(STRIPS):
            ffn_far(depth, 3, half)
        pass_on(piece_f, 4)
        settle(piece_f, 4)
        for half in range(STRIPS):
            ffn_far(depth, 0, half)
            far_out[depth, half_at(half), :] = far_sum[half_at(half), :].astype(jnp.bfloat16)
            pair_copy(1, depth, half).start()
        if more:
            pass_on(piece_a + 2, 1)
        ffn_own(depth, 3)
        ffn_own(depth, 0)
        write_out(wf.at[depth], ffn_full.at[depth])
        if more:
            launch(piece_f + 2)
            pass_on(piece_a + 2, 2)
            pass_edge(piece_a + 2, 1)
        for half in range(STRIPS):
            pair_copy(1, depth, half).wait_recv()
        pre_ref[depth, 1] += far_in[depth].astype(jnp.float32)
        write_out(pre_ref.at[depth], pre_out.at[depth])
        normed, _ = normed_of(pre_ref[depth, 1])
        state[...] = normed * gains_ref[2 + 2 * depth, 0:1, :] + gains_ref[2 + 2 * depth, 1:2, :]

    spots = (
        lax.broadcasted_iota(jnp.int32, (count, 1), 0) == places_row[...]
    ).astype(jnp.bfloat16)
    picked[spot.mp] = dot_tn(spots, state[...].astype(jnp.bfloat16)).astype(jnp.bfloat16)
    beside = spot.mp + 1 - 2 * (spot.mp % 2)

    def beside_copy(step, arriving):
        whose = ((beside if arriving else spot.mp) - 2 * step + n) % n
        return remote(
            picked.at[whose],
            picked.at[whose],
            beside_send.at[step],
            beside_recv.at[step],
            (spot.dp, beside),
        )

    for step in range(1, n // 2):
        share(1, picked, 2 * step).start()
    beside_copy(0, False).start()
    late[1].wait()
    out_b = out_ref[...].astype(jnp.bfloat16)
    rows_v = out_ref.shape[0]
    hits = (
        labels_row[...] == spot.mp * rows_v + lax.broadcasted_iota(jnp.int32, (rows_v, 1), 0)
    ).astype(jnp.float32)
    for step in range(1, n // 2):
        arrived(1, picked, 2 * step).wait_recv()
        beside_copy(step, False).start()
    for step in range(n // 2):
        beside_copy(step, True).wait_recv()
    picked_all = picked[...].reshape(n * slots, -1)
    logits = dot_nt(out_b, picked_all)
    peak = jnp.max(logits, axis=0, keepdims=True)
    expsum = jnp.sum(jnp.exp(logits - peak), axis=0, keepdims=True)
    stats[spot.mp, 0:1, :] = peak
    stats[spot.mp, 1:2, :] = expsum
    stats[spot.mp, 2:3, :] = jnp.sum(hits * logits, axis=0, keepdims=True)
    for offset in range(1, n):
        share(2, stats, offset).start()
    for offset in range(1, n):
        arrived(2, stats, offset).wait_recv()
    peak = stats[0, 0:1, :]
    for whose in range(1, n):
        peak = jnp.maximum(peak, stats[whose, 0:1, :])
    expsum = stats[0, 1:2, :] * jnp.exp(stats[0, 0:1, :] - peak)
    target = stats[0, 2:3, :]
    for whose in range(1, n):
        expsum = expsum + stats[whose, 1:2, :] * jnp.exp(stats[whose, 0:1, :] - peak)
        target = target + stats[whose, 2:3, :]
    log_total = peak + jnp.log(expsum)
    loss_ref[0:1, :] = jnp.where(valid, log_total - target, 0.0)
    grad_logits = jnp.where(valid, jnp.exp(logits - log_total) - hits, 0.0).astype(jnp.bfloat16)
    picked_grad = dot_tn(grad_logits, out_b).astype(jnp.bfloat16)
    for whose in range(n):
        back_out[whose] = picked_grad[whose * slots : (whose + 1) * slots, :]
    for offset in range(1, n):
        deal(3, back_out, back_in, offset).start()
    back_in[spot.mp] = back_out[spot.mp]
    out_grad_ref[...] = dot_nn(grad_logits, picked_all)
    for offset in range(1, n):
        arrived(3, back_in, offset).wait_recv()
    summed = back_in[0].astype(jnp.float32)
    for whose in range(1, n):
        summed = summed + back_in[whose].astype(jnp.float32)
    high = summed.astype(jnp.bfloat16)
    low = (summed - high.astype(jnp.float32)).astype(jnp.bfloat16)
    grad_ref[...] = dot_nn(spots, high) + dot_nn(spots, low)

    for piece in range(2 * LAYERS):
        for way, part in WAYS:
            for step in range(1, last_step(n, way, part) + 1):
                ring_copy(piece, way, part, step, 0).wait_send()
                core_copy(piece, way, part, step, core, None).wait_send()
                if piece % 2 == 0:
                    across_copy(piece, way, part, step, spot.row).wait_send()
                    core_copy(piece, way, part, step, core, 1 - spot.row).wait_send()
    for offset in range(1, n):
        deal(0, row_out, row_in, offset).wait_send()
        share(2, stats, offset).wait_send()
        deal(3, back_out, back_in, offset).wait_send()
    for step in range(n // 2):
        beside_copy(step, False).wait_send()
        if step > 0:
            share(1, picked, 2 * step).wait_send()
    for depth in range(LAYERS):
        for half in range(STRIPS):
            pair_copy(0, depth, half).wait_send()
            pair_copy(1, depth, half).wait_send()
    for turn in range(len(turns) - SLOTS, len(turns)):
        for copy in kept_copies(turn, *turns[turn]):
            copy.wait()
    for copy in out_copies:
        copy.wait()


def forward_call(
    n, ids, lengths, places, targets, ramp, gains, table, where, out_table, attn, ffn
):
    count, width = where.shape
    rows_f = ffn.shape[2]
    slots = 32 * -(-places.shape[1] // 32)
    groups = n // 2
    f32, bf16 = jnp.float32, jnp.bfloat16
    vmem = pl.BlockSpec(memory_space=pltpu.VMEM)
    anywhere = pl.BlockSpec(memory_space=pl.ANY)
    shape = jax.ShapeDtypeStruct
    dma = pltpu.SemaphoreType.DMA
    sems = dma((2 * LAYERS, 2, 2, n // 2))
    core_sems = dma((2, 2 * LAYERS, 2, 2, n // 2))
    return pl.pallas_call(
        functools.partial(forward_kernel, n),
        out_shape=(
            shape((LAYERS, 4, width, width), bf16),
            shape((LAYERS, groups, 2, rows_f, width), bf16),
            shape((count, width), f32),
            shape((LAYERS, count, width), bf16),
            shape((LAYERS, 3, count, width), bf16),
            shape((LAYERS, count, width), bf16),
            shape((LAYERS, 2, count, width), f32),
            shape((LAYERS, 2, count, width), bf16),
            shape((LAYERS, groups, 2, count, rows_f), f32),
            shape((LAYERS, groups, 2, count, rows_f), bf16),
            shape((count, width), f32),
            shape(out_table.shape, f32),
            shape((2, n * slots), f32),
        ),
        in_specs=[vmem] * 7 + [anywhere] * 4,
        out_specs=(anywhere,) * 10 + (vmem,) * 3,
        scratch_shapes=[
            pltpu.VMEM((count, width), f32),
            pltpu.VMEM(out_table.shape, f32),
            pltpu.VMEM((LAYERS, count, width), bf16),
            pltpu.VMEM((LAYERS, 3, count, width), bf16),
            pltpu.VMEM((LAYERS, count, width), bf16),
            pltpu.VMEM((LAYERS, 2, count, width), f32),
            pltpu.VMEM((LAYERS, 2, count, width), bf16),
            pltpu.VMEM((LAYERS, groups, rows_f), f32),
            pltpu.VMEM(table.shape, bf16),
            pltpu.VMEM((1, slots), jnp.int32),
            pltpu.VMEM((1, n * slots), jnp.int32),
            pltpu.VMEM((LAYERS, 4, width, width), bf16),
            pltpu.VMEM((LAYERS, groups, 2, rows_f, width), bf16),
            pltpu.VMEM(attn.shape, f32),
            pltpu.VMEM((LAYERS, 2, rows_f // 2, width), f32),
            pltpu.VMEM((SLOTS, count, rows_f), f32),
            pltpu.VMEM((SLOTS, count, rows_f), bf16),
            pltpu.VMEM((count, width), f32),
            pltpu.VMEM((LAYERS, count, width), bf16),
            pltpu.VMEM((LAYERS, count, width), bf16),
            pltpu.VMEM((count, width), f32),
            pltpu.VMEM((n, table.shape[0], count), bf16),
            pltpu.VMEM((n, table.shape[0], count), bf16),
            pltpu.VMEM((n, slots, width), bf16),
            pltpu.VMEM((n, 8, n * slots), f32),
            pltpu.VMEM((n, slots, width), bf16),
            pltpu.VMEM((n, slots, width), bf16),
            dma((2 * LAYERS,)),
            dma((2,)),
            dma((1 + 7 * LAYERS,)),
            dma((2, SLOTS)),
            sems,
            sems,
            core_sems,
            core_sems,
            sems,
            sems,
            dma((2, LAYERS, STRIPS)),
            dma((2, LAYERS, STRIPS)),
            dma((4, n - 1)),
            dma((4, n - 1)),
            dma((n // 2,)),
            dma((n // 2,)),
        ],
        compiler_params=pltpu.CompilerParams(
            collective_id=1, has_side_effects=True, vmem_limit_bytes=VMEM_LIMIT
        ),
        name="forward_layers",
    )(ids, lengths, places, targets, ramp, gains, table, where, out_table, attn, ffn)


def norm_back(grad, values, gain):
    normed, inverse = normed_of(values)
    scaled = grad * gain
    centred = scaled - jnp.mean(scaled, axis=-1, keepdims=True)
    result = inverse * (centred - normed * jnp.mean(scaled * normed, axis=-1, keepdims=True))
    return (
        result,
        jnp.sum(grad * normed, axis=0, keepdims=True),
        jnp.sum(grad, axis=0, keepdims=True),
    )


def backward_kernel(
    n,
    ids_ref,
    lengths_ref,
    losses_ref,
    gains_ref,
    out_grad_all,
    inputs_all,
    mixed_all,
    mid_all,
    grad_ref,
    first_ref,
    proj_all,
    pre_all,
    attn_full,
    ffn_full,
    slope_all,
    act_all,
    attn_sum,
    ffn_sum,
    table_sum,
    out_sum,
    loss_out,
    gains_out,
    square_out,
    out_grad_ref,
    proj,
    pre,
    wa,
    wf,
    slope,
    sum_a,
    sum_f,
    theirs_f,
    land_f,
    land_a,
    ring_a,
    ring_f,
    go_far,
    far_sum,
    far_out,
    far_in,
    state,
    grad_rows,
    left_a,
    left_f,
    right_f,
    spread_a,
    spread_f,
    done_a,
    done_f,
    wa_sem,
    load_sem,
    slope_sem,
    mid_sem,
    left_sem,
    core_send,
    core_recv,
    core_free,
    swap_send,
    swap_recv,
    swap_free,
    ring_send,
    ring_recv,
    ring_free,
    pair_send,
    pair_recv,
    across_send,
    across_recv,
    out_sem,
    last_send,
    last_recv,
    small,
    small_in,
    columns_out,
    columns_in,
    table_grad,
    table_half,
    out_half,
    out_done,
    squares,
    square_parts,
    proj_sem,
    small_send,
    small_recv,
    deal_send,
    deal_recv,
    half_send,
    half_recv,
    half_sem,
    norm_send,
    norm_recv,
):
    spot = Spot(n)
    core = spot.core
    other = 1 - core
    rows_a = attn_sum.shape[2]
    rows_f = ffn_sum.shape[2]
    half_f = rows_f // 2
    part_f = half_f // 2
    count = state.shape[0]
    width = attn_sum.shape[3]
    groups = n // 2
    order = (0,) + tuple(range(groups - 1, 0, -1))
    total = LAYERS * groups

    def rows_at(shard, rows):
        return pl.ds(pl.multiple_of(shard * rows, 16), rows)

    def peer(offset):
        return (spot.mp + offset + n) % n

    def remote(source, target, send, recv, device):
        return pltpu.make_async_remote_copy(
            src_ref=source,
            dst_ref=target,
            send_sem=send,
            recv_sem=recv,
            device_id=device,
            device_id_type=MESH,
        )

    def turn_of(turn):
        return LAYERS - 1 - turn // groups, order[turn % groups]

    def load_weights(depth, group):
        return pltpu.make_async_copy(
            ffn_full.at[depth, group], wf.at[group], load_sem.at[0, group]
        )

    def load_act(depth):
        return [
            pltpu.make_async_copy(
                act_all.at[depth, group, far],
                left_f.at[group, 1, pl.ds(far * count, count), :],
                load_sem.at[1 + far, group],
            )
            for group in range(groups)
            for far in range(2)
        ] + [
            pltpu.make_async_copy(
                mid_all.at[depth, far],
                right_f.at[0, pl.ds(far * count, count), :],
                mid_sem.at[far],
            )
            for far in range(2)
        ]

    def load_slope(index):
        depth = LAYERS - 1 - index // (2 * groups)
        far = (index // groups) % 2
        return pltpu.make_async_copy(
            slope_all.at[depth, order[index % groups], far],
            slope.at[index % (groups + 1)],
            slope_sem.at[index % (groups + 1)],
        )

    def load_pre(depth):
        return pltpu.make_async_copy(pre_all.at[depth], pre, proj_sem.at[0])

    def load_left(depth):
        return (
            pltpu.make_async_copy(inputs_all.at[depth], left_a.at[0], left_sem.at[0]),
            pltpu.make_async_copy(mixed_all.at[depth], left_a.at[1], left_sem.at[1]),
        )

    def load_proj(depth):
        return pltpu.make_async_copy(proj_all.at[depth], proj, proj_sem.at[1])

    def load_attn(depth):
        return pltpu.make_async_copy(attn_full.at[depth], wa, wa_sem.at[0])

    def core_copy(turn):
        slot = turn % SLOTS
        return remote(
            theirs_f.at[slot],
            land_f.at[slot],
            core_send.at[turn],
            core_recv.at[turn],
            spot.partner,
        )

    def fold(turn):
        depth, group = turn_of(turn)
        core_copy(turn).wait_recv()
        sum_f[depth, group] = (
            sum_f[depth, group].astype(jnp.float32)
            + land_f[turn % SLOTS].astype(jnp.float32)
        ).astype(jnp.bfloat16)
        if turn + SLOTS < total:
            pl.semaphore_signal(
                core_free.at[0], inc=1, device_id=spot.partner, device_id_type=MESH
            )

    def swap_copy(depth, part):
        return remote(
            wa.at[part],
            land_a.at[part],
            swap_send.at[depth, part],
            swap_recv.at[depth, part],
            spot.partner,
        )

    def summed(piece, offset, part):
        kind, depth = piece % 2, piece // 2
        if kind == 0:
            return sum_a.at[depth, part, rows_at(spot.shard(offset), rows_a), :]
        far = abs(offset)
        group, half = (far, int(offset > 0)) if 0 < far < groups else (0, int(far > 0))
        return sum_f.at[depth, group, pl.ds(half * half_f + part * part_f, part_f), :]

    def landed(piece, way, part, step):
        if piece % 2 == 0:
            return ring_a.at[way, part, step - 1]
        return ring_f.at[way, part, step - 1]

    def absorb_rows(into, source):
        into[...] = (into[...].astype(jnp.float32) + source[...].astype(jnp.float32)).astype(
            jnp.bfloat16
        )

    def pair_copy(which, depth, half):
        rows = pl.ds(half * (count // STRIPS), count // STRIPS)
        if which == 0:
            source, target = right_f.at[1, rows, :], go_far.at[depth, rows, :]
        else:
            source, target = far_out.at[depth, rows, :], far_in.at[depth, rows, :]
        return remote(
            source,
            target,
            pair_send.at[which, depth, half],
            pair_recv.at[which, depth, half],
            spot.across,
        )

    def ring_copy(piece, way, part, step):
        offset = last_step(n, way, part) - step + 1
        return remote(
            summed(piece, offset if way == 0 else -offset, part),
            landed(piece, way, part, step),
            ring_send.at[piece, way, part, step - 1],
            ring_recv.at[piece, way, part, step - 1],
            spot.ring[way],
        )

    def ring_start(piece, way, part, step):
        if piece // 2 < LAYERS - 1:
            pl.semaphore_wait(ring_free.at[piece % 2, way, part, step - 1], 1)
        ring_copy(piece, way, part, step).start()

    def release(piece, way, part, step):
        if piece // 2 > 0:
            pl.semaphore_signal(
                ring_free.at[piece % 2, way, part, step - 1],
                inc=1,
                device_id=spot.ring[1 - way],
                device_id_type=MESH,
            )

    def launch(piece, long):
        for way, part in WAYS:
            if (way == part) == long:
                ring_start(piece, way, part, 1)

    def launch_part(piece, part):
        for way in (part, 1 - part):
            ring_start(piece, way, part, 1)

    def relay(piece, step):
        for way, part in WAYS:
            last = last_step(n, way, part)
            if step < last:
                ring_copy(piece, way, part, step).wait_recv()
                offset = last - step if way == 0 else step - last
                absorb_rows(summed(piece, offset, part), landed(piece, way, part, step))
                ring_start(piece, way, part, step + 1)
                release(piece, way, part, step)

    def across_copy(piece, part):
        depth = piece // 2
        if piece % 2 == 0:
            source, target = spread_a.at[depth, 0, part], spread_a.at[depth, 1, part]
        else:
            rows = pl.ds(part * part_f, part_f)
            source, target = spread_f.at[depth, 0, rows, :], spread_f.at[depth, 1, rows, :]
        return remote(
            source,
            target,
            across_send.at[piece, part],
            across_recv.at[piece, part],
            spot.across,
        )

    def finish(piece):
        kind, depth = piece % 2, piece // 2
        for part in range(2):
            value = summed(piece, 0, part)[...].astype(jnp.float32)
            for way in range(2):
                step = last_step(n, way, part)
                ring_copy(piece, way, part, step).wait_recv()
                value = value + landed(piece, way, part, step)[...].astype(jnp.float32)
                release(piece, way, part, step)
            value = value.astype(jnp.bfloat16)
            if kind == 0:
                spread_a[depth, 0, part] = value
            else:
                spread_f[depth, 0, pl.ds(part * part_f, part_f), :] = value
            across_copy(piece, part).start()

    def out_copies(piece):
        kind, depth = piece % 2, piece // 2
        if kind == 0:
            source, target = done_a, attn_sum.at[depth, pl.ds(2 * core, 2)]
        else:
            source, target = done_f, ffn_sum.at[depth, core]
        return (
            pltpu.make_async_copy(source, target, out_sem.at[piece]),
            remote(source, target, last_send.at[piece], last_recv.at[piece], spot.partner),
        )

    def conclude(piece):
        kind, depth = piece % 2, piece // 2
        for part in range(2):
            across_copy(piece, part).wait_recv()
        if depth < LAYERS - 1:
            local, away = out_copies(piece + 2)
            local.wait()
            away.wait_send()
        row = spot.row
        if kind == 1:
            for side in range(2):
                whose = row + side - 2 * row * side
                rows = pl.ds(pl.multiple_of(whose * half_f, 16), half_f)
                done_f[rows, :] = spread_f[depth, side]
            add_squares(done_f[...].astype(jnp.float32))
        else:
            for part in range(2):
                value = spread_a[depth, 0, part].astype(jnp.float32) + spread_a[
                    depth, 1, part
                ].astype(jnp.float32)
                done_a[part] = value
                add_squares(value)
        for copy in out_copies(piece):
            copy.start()

    load_grad = pltpu.make_async_copy(grad_ref, state, proj_sem.at[2])
    load_grad.start()
    load_first = pltpu.make_async_copy(first_ref, pre.at[0], proj_sem.at[3])
    load_pre(LAYERS - 1).start()
    for group in order:
        load_weights(LAYERS - 1, group).start()
    for index in range(groups + 1):
        load_slope(index).start()
    for copy in load_act(LAYERS - 1):
        copy.start()
    load_attn(LAYERS - 1).start()
    load_proj(LAYERS - 1).start()
    load_out = pltpu.make_async_copy(out_grad_all, out_grad_ref, left_sem.at[2])
    load_out.start()
    for copy in load_left(LAYERS - 1):
        copy.start()
    greet(
        [spot.partner, spot.across]
        + [(whose, peer(offset)) for offset in range(1, n) for whose in (spot.dp, spot.partner[0])]
    )
    load_grad.wait()
    lanes = lax.broadcasted_iota(jnp.int32, (1, 128), 1) < 64
    spans = lengths_ref[...].astype(jnp.float32)
    lane = lax.broadcasted_iota(jnp.int32, (1, n), 1)
    length = jnp.sum(jnp.where(lane == spot.mp, spans, 0.0), axis=1, keepdims=True)
    visible = lax.broadcasted_iota(jnp.int32, (1, count), 1).astype(jnp.float32) < length

    def hidden_own(index):
        depth = LAYERS - 1 - index // (2 * groups)
        group = order[index % groups]
        load_slope(index).wait()
        load_weights(depth, group).wait()
        rows = pl.ds(0, count)
        grad_active = dot_nt(right_f[1, rows, :], wf[group, 1])
        grad_hidden = (grad_active * slope[index % (groups + 1)]).astype(jnp.bfloat16)
        left_f[group, 0, rows, :] = grad_hidden
        state[...] += dot_nn(grad_hidden, wf[group, 0])
        if index + groups + 1 < 2 * total:
            load_slope(index + groups + 1).start()

    def hidden_far(index, half):
        depth = LAYERS - 1 - index // (2 * groups)
        group = order[index % groups]
        if half == 0:
            load_slope(index).wait()
        rows = pl.ds(half * (count // STRIPS), count // STRIPS)
        here = pl.ds(count + half * (count // STRIPS), count // STRIPS)
        grad_active = dot_nt(right_f[1, here, :], wf[group, 1])
        grad_hidden = (grad_active * slope[index % (groups + 1), rows, :]).astype(jnp.bfloat16)
        left_f[group, 0, here, :] = grad_hidden
        far_sum[rows, :] += dot_nn(grad_hidden, wf[group, 0])
        if half == STRIPS - 1:
            if depth > 0:
                load_weights(depth - 1, group).start()
            if index + groups + 1 < 2 * total:
                load_slope(index + groups + 1).start()

    def ffn_turn(turn):
        depth, group = turn_of(turn)
        slot = turn % SLOTS
        sum_f[depth, group] = dot_tn(left_f[group, core], right_f[core]).astype(jnp.bfloat16)
        if turn >= SLOTS:
            core_copy(turn - SLOTS).wait_send()
        theirs_f[slot] = dot_tn(left_f[group, other], right_f[other]).astype(jnp.bfloat16)
        if turn >= SLOTS:
            pl.semaphore_wait(core_free.at[0], 1)
        core_copy(turn).start()

    def head_pair(depth, pair):
        columns = pl.ds(pl.multiple_of(pair * 128, 128), 128)
        query = proj[0, :, columns]
        keyed = proj[1, :, columns]
        valued = proj[2, :, columns]
        grad_mixed = grad_rows[4, :, columns]
        outs = []
        for side in range(2):
            mine = lanes if side == 0 else jnp.logical_not(lanes)
            scores = dot_nt(jnp.where(mine, query, jnp.zeros_like(query)), keyed) * 0.125
            scores = jnp.where(visible, scores, masked_score)
            expo = jnp.exp(scores - jnp.max(scores, axis=-1, keepdims=True))
            probs = expo / jnp.sum(expo, axis=-1, keepdims=True)
            grad_probs = dot_nt(jnp.where(mine, grad_mixed, jnp.zeros_like(query)), valued)
            inner = jnp.sum(grad_probs * probs, axis=-1, keepdims=True)
            grad_scores = (probs * (grad_probs - inner)).astype(jnp.bfloat16)
            outs.append(
                (
                    dot_nn(grad_scores, keyed) * 0.125,
                    dot_tn(grad_scores, query) * 0.125,
                    dot_tn(probs.astype(jnp.bfloat16), grad_mixed),
                )
            )
        for which in range(3):
            grad_rows[which, :, columns] = jnp.where(
                lanes, outs[0][which], outs[1][which]
            ).astype(jnp.bfloat16)

    def layer(depth, hooks):
        def at(name):
            for work in hooks.get(name, ()):
                work()

        base = (LAYERS - 1 - depth) * groups
        piece_a, piece_f = 2 * depth, 2 * depth + 1
        load_pre(depth).wait()
        grad_two, small[0, 4 + 4 * depth : 5 + 4 * depth, :], small[0, 5 + 4 * depth : 6 + 4 * depth, :] = norm_back(
            state[...], pre[1], gains_ref[2 + 2 * depth, 0:1, :]
        )
        state[...] = grad_two
        for half in range(STRIPS):
            if depth < LAYERS - 1:
                pair_copy(0, depth + 1, half).wait_send()
            rows = pl.ds(half * (count // STRIPS), count // STRIPS)
            right_f[1, rows, :] = state[rows, :].astype(jnp.bfloat16)
            pair_copy(0, depth, half).start()
        far_sum[...] = jnp.zeros_like(far_sum)
        for step in range(groups):
            hidden_own(2 * base + step)
        at("own")
        for half in range(STRIPS):
            rows = pl.ds(half * (count // STRIPS), count // STRIPS)
            here = pl.ds(count + half * (count // STRIPS), count // STRIPS)
            pair_copy(0, depth, half).wait_recv()
            right_f[1, here, :] = go_far[depth, rows, :]
            for step in range(groups):
                hidden_far(2 * base + groups + step, half)
            far_out[depth, rows, :] = far_sum[rows, :].astype(jnp.bfloat16)
            pair_copy(1, depth, half).start()
            at(("far", half))
        for copy in load_act(depth):
            copy.wait()
        for step in range(groups):
            ffn_turn(base + step)
            if step >= 1:
                fold(base + step - 1)
            if step == 1:
                launch(piece_f, True)
            if step == 2:
                launch(piece_f, False)
            at(("ffn", step))
        fold(base + groups - 1)
        if depth > 0:
            for copy in load_act(depth - 1):
                copy.start()
        for half in range(STRIPS):
            pair_copy(1, depth, half).wait_recv()
        state[...] += far_in[depth].astype(jnp.float32)
        at("middle")
        grad_one, small[0, 2 + 4 * depth : 3 + 4 * depth, :], small[0, 3 + 4 * depth : 4 + 4 * depth, :] = norm_back(
            state[...], pre[0], gains_ref[1 + 2 * depth, 0:1, :]
        )
        if depth > 0:
            load_pre(depth - 1).start()
        else:
            load_first.start()
        state[...] = grad_one
        grad_rows[3] = grad_one.astype(jnp.bfloat16)
        load_attn(depth).wait()
        load_proj(depth).wait()
        grad_rows[4] = dot_nt(grad_rows[3], wa[3]).astype(jnp.bfloat16)

        @pl.loop(0, HEADS // 4)
        def _(pair):
            head_pair(depth, pair)

        at("half")

        @pl.loop(HEADS // 4, HEADS // 2)
        def _(pair):
            head_pair(depth, pair)

        if depth > 0:
            load_proj(depth - 1).start()
        at("heads")
        for which in range(3):
            state[...] += dot_nt(grad_rows[which], wa[which])
        for copy in load_left(depth):
            copy.wait()
        for part in range(2):
            left = 0 if part == 0 else other
            wa[part] = dot_tn(left_a[left], grad_rows[2 * other + part]).astype(jnp.bfloat16)
            if depth < LAYERS - 1:
                pl.semaphore_wait(swap_free.at[part], 1)
            swap_copy(depth, part).start()
        for part in range(2):
            left = 0 if part == 0 else core
            sum_a[depth, part] = dot_tn(left_a[left], grad_rows[2 * core + part]).astype(
                jnp.bfloat16
            )
            swap_copy(depth, part).wait_recv()

            @pl.loop(0, n)
            def _(block):
                rows = rows_at(block, rows_a)
                absorb_rows(sum_a.at[depth, part, rows, :], land_a.at[part, rows, :])

            if depth > 0:
                pl.semaphore_signal(
                    swap_free.at[part], inc=1, device_id=spot.partner, device_id_type=MESH
                )
            launch_part(piece_a, part)
            if depth > 0 and part == 1:
                for copy in load_left(depth - 1):
                    copy.start()
            at(("mats", part))

    def reload_attn():
        for part in range(2):
            swap_copy(1, part).wait_send()
        load_attn(0).start()

    def half_copy(which, stage):
        buffer = out_half if which == 0 else table_half
        return remote(
            buffer.at[2 * stage],
            buffer.at[2 * stage + 1],
            half_send.at[which, stage],
            half_recv.at[which, stage],
            spot.partner if stage == 0 else spot.across,
        )

    def half_rows(rows, side):
        return pl.ds(pl.multiple_of(side * (rows // 2), 16), rows // 2)

    def half_start(which, source):
        buffer = out_half if which == 0 else table_half
        buffer[0] = source[half_rows(source.shape[0], other), :].astype(jnp.bfloat16)
        half_copy(which, 0).start()

    def half_fold(which, source):
        buffer = out_half if which == 0 else table_half
        half_copy(which, 0).wait_recv()
        own = source[half_rows(source.shape[0], core), :]
        buffer[2] = (own + buffer[1].astype(jnp.float32)).astype(jnp.bfloat16)
        half_copy(which, 1).start()

    def half_out(which):
        if which == 0:
            source, target = out_done, out_sum.at[half_rows(out_sum.shape[0], core), :]
        else:
            source = table_grad.at[half_rows(table_sum.shape[0], core), :]
            target = table_sum.at[half_rows(table_sum.shape[0], core), :]
        return (
            pltpu.make_async_copy(source, target, half_sem.at[which]),
            remote(source, target, half_send.at[which, 2], half_recv.at[which, 2], spot.partner),
        )

    def add_squares(value):
        squares[...] += jnp.sum(value * value, axis=0, keepdims=True)

    def half_end(which):
        buffer = out_half if which == 0 else table_half
        half_copy(which, 1).wait_recv()
        value = buffer[2].astype(jnp.float32) + buffer[3].astype(jnp.float32)
        if which == 0:
            out_done[...] = value
        else:
            table_grad[half_rows(table_sum.shape[0], core), :] = value
        width = squares.shape[1]
        for start in range(0, value.shape[1], width):
            add_squares(value[:, start : start + width])
        for copy in half_out(which):
            copy.start()

    def small_copy(stage):
        bit = 1 << max(0, stage - 2)
        pair = spot.mp + bit - 2 * bit * ((spot.mp // bit) % 2)
        device = (spot.partner, spot.across)[stage] if stage < 2 else (spot.dp, pair)
        return remote(
            small.at[stage],
            small_in.at[stage],
            small_send.at[stage],
            small_recv.at[stage],
            device,
        )

    def small_next(stage):
        small_copy(stage).wait_recv()
        small[stage + 1] = small[stage] + small_in[stage]
        if stage < 4:
            small_copy(stage + 1).start()

    def deal_copy(offset, arriving):
        source = columns_out.at[peer(offset)]
        target = columns_in.at[peer(-offset) if arriving else spot.mp]
        return remote(
            source,
            target,
            deal_send.at[offset - 1],
            deal_recv.at[offset - 1],
            (spot.dp, peer(offset)),
        )

    def table_blocks(first, last):
        @pl.loop(first, last)
        def _(block):
            row = lax.broadcasted_iota(jnp.int32, (256, 1), 0) + block * 256
            value = jnp.zeros((columns_in.shape[1], 256), jnp.float32)
            for whose in range(n):
                chosen = (row == ids_ref[whose : whose + 1, :]).astype(jnp.bfloat16)
                value = value + dot_nt(columns_in[whose], chosen)
            table_grad[:, pl.ds(pl.multiple_of(block * 256, 256), 256)] = value

    squares[...] = jnp.zeros_like(squares)
    layer(
        1,
        {
            "own": [load_out.wait, lambda: half_start(0, out_grad_ref)],
            ("far", 1): [lambda: half_fold(0, out_grad_ref)],
            "half": [lambda: relay(3, 1)],
            ("mats", 1): [lambda: relay(3, 2)],
        },
    )
    layer(
        0,
        {
            "own": [reload_attn],
            ("far", 0): [lambda: relay(3, 3)],
            ("far", 1): [lambda: relay(2, 1), lambda: finish(3)],
            ("ffn", 3): [lambda: relay(2, 2), lambda: conclude(3), lambda: half_end(0)],
            "half": [lambda: relay(2, 3), lambda: relay(1, 1)],
            "heads": [lambda: finish(2), lambda: relay(1, 2)],
        },
    )
    load_first.wait()
    grad_sum, small[0, 0:1, :], small[0, 1:2, :] = norm_back(
        state[...], pre[0], gains_ref[0, 0:1, :]
    )
    width = squares.shape[1]
    lane = lax.broadcasted_iota(jnp.int32, (1, width), 1)
    tally = jnp.sum(losses_ref[...], axis=1, keepdims=True) * (1.0 / n)
    loss, slots = tally[0:1, :], tally[1:2, :]
    small[0, 10:11, :] = jnp.where(lane == 0, loss, jnp.where(lane == 1, slots, 0.0))
    small[0, 11:16, :] = jnp.zeros((5, width), jnp.float32)
    small_copy(0).start()
    turned = grad_sum.T.astype(jnp.bfloat16)
    share = columns_in.shape[1]
    for whose in range(n):
        columns_out[whose] = turned[whose * share : (whose + 1) * share, :]
    for offset in range(1, n):
        deal_copy(offset, False).start()
    columns_in[spot.mp] = columns_out[spot.mp]
    blocks = table_sum.shape[1] // 256
    small_next(0)
    relay(1, 3)
    conclude(2)
    for offset in range(1, n):
        deal_copy(offset, True).wait_recv()
    table_blocks(0, 5)
    relay(0, 1)
    small_next(1)
    table_blocks(5, 10)
    finish(1)
    table_blocks(10, blocks)
    half_start(1, table_grad)
    relay(0, 2)
    small_next(2)
    conclude(1)
    half_fold(1, table_grad)
    relay(0, 3)
    small_next(3)
    half_end(1)
    finish(0)
    small_next(4)
    loss_out[...] = small[5, 10:11, 0:128]
    for index in range(5):
        gains_out[index] = small[5, 2 * index : 2 * index + 2, :]
    conclude(0)

    square = jnp.sum(squares[...], axis=1, keepdims=True)
    square_parts[core * n + spot.mp] = jnp.broadcast_to(square, square_parts.shape[1:])

    def norm_copy(side, offset, arriving):
        own = square_parts.at[core * n + spot.mp]
        whose = (core + side - 2 * core * side) * n + peer(-offset)
        return remote(
            own,
            square_parts.at[whose] if arriving else own,
            norm_send.at[side, offset],
            norm_recv.at[side, offset],
            ((spot.dp, spot.partner[0])[side], peer(offset)),
        )

    far_squares = [(side, offset) for offset in range(n) for side in range(2)][1:]
    for side, offset in far_squares:
        norm_copy(side, offset, False).start()
    gains_grad = small[5, 0:10, :]
    square = jnp.sum(jnp.sum(gains_grad * gains_grad, axis=0, keepdims=True), axis=1, keepdims=True)
    for side, offset in far_squares:
        norm_copy(side, offset, True).wait_recv()
    for whose in range(2 * n):
        square = square + square_parts[whose, 0:1, :]
    square_out[...] = square

    for half in range(STRIPS):
        pair_copy(0, 0, half).wait_send()
        for depth in range(LAYERS):
            pair_copy(1, depth, half).wait_send()
    for side, offset in far_squares:
        norm_copy(side, offset, False).wait_send()
    for offset in range(1, n):
        deal_copy(offset, False).wait_send()
    for stage in range(5):
        small_copy(stage).wait_send()
    for which in range(2):
        half_copy(which, 0).wait_send()
        half_copy(which, 1).wait_send()
        local, away = half_out(which)
        local.wait()
        away.wait()
    for turn in range(total - SLOTS, total):
        core_copy(turn).wait_send()
    for part in range(2):
        swap_copy(0, part).wait_send()
    for piece in range(2 * LAYERS):
        for way, part in WAYS:
            for step in range(1, last_step(n, way, part) + 1):
                ring_copy(piece, way, part, step).wait_send()
        for part in range(2):
            across_copy(piece, part).wait_send()
        local, away = out_copies(piece)
        if piece < 2:
            local.wait()
            away.wait_send()
        away.wait_recv()


def backward_call(
    n, ids, lengths, losses, grad, first, gains, out_grad, kept, attn_full, ffn_full, slope, act, table
):
    inputs, proj, mixed, pre, mid = kept
    count, width = grad.shape
    rows_f = ffn_full.shape[3]
    groups = n // 2
    rows_a = attn_full.shape[2] // n
    rows_v = out_grad.shape[0]
    words, share = table.shape
    f32, bf16 = jnp.float32, jnp.bfloat16
    vmem = pl.BlockSpec(memory_space=pltpu.VMEM)
    anywhere = pl.BlockSpec(memory_space=pl.ANY)
    shape = jax.ShapeDtypeStruct
    dma = pltpu.SemaphoreType.DMA
    regular = pltpu.SemaphoreType.REGULAR
    ring_sems = dma((2 * LAYERS, 2, 2, n // 2))
    return pl.pallas_call(
        functools.partial(backward_kernel, n),
        out_shape=(
            shape((LAYERS, 4, rows_a, width), f32),
            shape((LAYERS, 2, rows_f, width), bf16),
            shape((share, words), f32),
            shape((rows_v, width), f32),
            shape((1, 128), f32),
            shape(gains.shape, f32),
            shape((1, 128), f32),
        ),
        in_specs=[vmem] * 4 + [anywhere] * 12,
        out_specs=(anywhere,) * 4 + (vmem,) * 3,
        scratch_shapes=[
            pltpu.VMEM(out_grad.shape, f32),
            pltpu.VMEM((3, count, width), bf16),
            pltpu.VMEM((2, count, width), f32),
            pltpu.VMEM((4, width, width), bf16),
            pltpu.VMEM((groups, 2, rows_f, width), bf16),
            pltpu.VMEM((groups + 1, count, rows_f), f32),
            pltpu.VMEM((LAYERS, 2, width, width), bf16),
            pltpu.VMEM((LAYERS, groups, rows_f, width), bf16),
            pltpu.VMEM((SLOTS, rows_f, width), bf16),
            pltpu.VMEM((SLOTS, rows_f, width), bf16),
            pltpu.VMEM((2, width, width), bf16),
            pltpu.VMEM((2, 2, n // 2, rows_a, width), bf16),
            pltpu.VMEM((2, 2, n // 2, rows_f // 4, width), bf16),
            pltpu.VMEM((LAYERS, count, width), bf16),
            pltpu.VMEM((count, width), f32),
            pltpu.VMEM((LAYERS, count, width), bf16),
            pltpu.VMEM((LAYERS, count, width), bf16),
            pltpu.VMEM((count, width), f32),
            pltpu.VMEM((5, count, width), bf16),
            pltpu.VMEM((2, count, width), bf16),
            pltpu.VMEM((groups, 2, 2 * count, rows_f), bf16),
            pltpu.VMEM((2, 2 * count, width), bf16),
            pltpu.VMEM((LAYERS, 2, 2, rows_a, width), bf16),
            pltpu.VMEM((LAYERS, 2, rows_f // 2, width), bf16),
            pltpu.VMEM((2, rows_a, width), f32),
            pltpu.VMEM((rows_f, width), bf16),
            dma((1,)),
            dma((3, groups)),
            dma((groups + 1,)),
            dma((2,)),
            dma((3,)),
            dma((LAYERS * groups,)),
            dma((LAYERS * groups,)),
            regular((1,)),
            dma((LAYERS, 2)),
            dma((LAYERS, 2)),
            regular((2,)),
            ring_sems,
            ring_sems,
            regular((2, 2, 2, n // 2)),
            dma((2, LAYERS, STRIPS)),
            dma((2, LAYERS, STRIPS)),
            dma((2 * LAYERS, 2)),
            dma((2 * LAYERS, 2)),
            dma((2 * LAYERS,)),
            dma((2 * LAYERS,)),
            dma((2 * LAYERS,)),
            pltpu.VMEM((6, 16, width), f32),
            pltpu.VMEM((5, 16, width), f32),
            pltpu.VMEM((n, share, count), bf16),
            pltpu.VMEM((n, share, count), bf16),
            pltpu.VMEM((share, words), f32),
            pltpu.VMEM((4, share // 2, words), bf16),
            pltpu.VMEM((4, rows_v // 2, width), bf16),
            pltpu.VMEM((rows_v // 2, width), f32),
            pltpu.VMEM((1, width), f32),
            pltpu.VMEM((2 * n, 8, 128), f32),
            dma((4,)),
            dma((5,)),
            dma((5,)),
            dma((n - 1,)),
            dma((n - 1,)),
            dma((2, 3)),
            dma((2, 3)),
            dma((2,)),
            dma((2, n)),
            dma((2, n)),
        ],
        compiler_params=pltpu.CompilerParams(
            collective_id=2, has_side_effects=True, vmem_limit_bytes=BACKWARD_LIMIT
        ),
        name="backward_layers",
    )(
        ids, lengths, losses, gains, out_grad, inputs, mixed, mid, grad, first,
        proj, pre, attn_full, ffn_full, slope, act,
    )


def merged(value, axis, join):
    pieces = jax.tree.map(lambda part: lax.all_gather(part, axis), value)
    head = jax.tree.map(lambda part: part[0], pieces)
    tail = jax.tree.map(lambda part: part[1:], pieces)
    total, _ = lax.scan(lambda total, section: (join(total, section), None), head, tail)
    return total


def sinusoid(count, width):
    places = jnp.arange(count, dtype=jnp.float32)[:, None]
    freqs = jnp.exp(jnp.arange(width // 2, dtype=jnp.float32) * (-2.0 * math.log(10000.0) / width))
    angles = places * freqs[None, :]
    return jnp.concatenate([jnp.sin(angles), jnp.cos(angles)], axis=1)


def layer_norm(values, gain, shift):
    centre = jnp.mean(values, axis=-1, keepdims=True)
    offset = values - centre
    spread = jnp.mean(offset * offset, axis=-1, keepdims=True)
    inverse = lax.rsqrt(spread + norm_eps)
    normed = offset * inverse
    return (normed * gain + shift, (normed, inverse))


def norm_backward(grad, saved, gain):
    normed, inverse = saved
    scaled = grad * gain
    centred = scaled - jnp.mean(scaled, axis=-1, keepdims=True)
    result = inverse * (centred - normed * jnp.mean(scaled * normed, axis=-1, keepdims=True))
    return (result, jnp.stack([jnp.sum(grad * normed, axis=0), jnp.sum(grad, axis=0)]))


def gelu_exact(values):
    return jax.nn.gelu(values, approximate=False)


def gelu_back(hidden, grad):
    unused, pullback = jax.vjp(gelu_exact, hidden)
    return pullback(grad)[0]


def masked_scores(query, keyed, length):
    scale = query.shape[-1] ** (-0.5)
    scores = jnp.einsum("hqe,hke->hqk", query, keyed, preferred_element_type=jnp.float32) * scale
    visible = jnp.arange(keyed.shape[1]) < length
    return jnp.where(visible[None, None, :], scores, masked_score)


def fetch_forward(attn_part, ffn_part):
    return (
        lax.all_gather(attn_part, "mp", axis=1, tiled=True),
        lax.all_gather(ffn_part, "mp", axis=1, tiled=True),
    )


def fetch_backward(attn_part, ffn_part):
    return (
        lax.all_gather(attn_part, "mp", axis=1, tiled=True),
        lax.all_gather(ffn_part, "mp", axis=1, tiled=True),
    )


def reduce_layer(attn_grad, ffn_grad):
    return (
        lax.psum_scatter(attn_grad, "mp", scatter_dimension=1, tiled=True),
        lax.psum_scatter(ffn_grad, "mp", scatter_dimension=1, tiled=True),
    )


def ffn_forward(middle_b, ffn_w, unit_mask):
    hidden = jnp.einsum("td,fd->tf", middle_b, ffn_w[0], preferred_element_type=jnp.float32)
    active = (gelu_exact(hidden) * unit_mask[None, :]).astype(jnp.bfloat16)
    output = jnp.einsum("tf,fd->td", active, ffn_w[1], preferred_element_type=jnp.float32)
    return (hidden, active, output)


def ffn_backward(grad_out, middle_b, hidden, active, ffn_w, unit_mask):
    grad_active = jnp.einsum("td,fd->tf", grad_out, ffn_w[1], preferred_element_type=jnp.float32)
    grad_hidden = gelu_back(hidden, grad_active * unit_mask[None, :]).astype(jnp.bfloat16)
    up_grad = jnp.einsum("tf,td->fd", grad_hidden, middle_b, preferred_element_type=jnp.float32)
    down_grad = jnp.einsum("tf,td->fd", active, grad_out, preferred_element_type=jnp.float32)
    from_ffn = jnp.einsum("tf,fd->td", grad_hidden, ffn_w[0], preferred_element_type=jnp.float32)
    return (jnp.stack([up_grad, down_grad]), from_ffn)


def layer_forward(states, attn_w, ffn_w, pair, length, unit_mask):
    count = states.shape[0]
    inputs = states.astype(jnp.bfloat16)
    projected = jnp.einsum(
        "td,kde->kte", inputs, attn_w[:3], preferred_element_type=jnp.float32
    ).astype(jnp.bfloat16)
    heads = projected.reshape(3, count, HEADS, -1).transpose(0, 2, 1, 3)
    scores = masked_scores(heads[0], heads[1], length)
    peak = jnp.max(scores, axis=-1, keepdims=True)
    expo = jnp.exp(scores - peak)
    total = jnp.sum(expo, axis=-1, keepdims=True)
    log_total = peak + jnp.log(total)
    probs = (expo / total).astype(jnp.bfloat16)
    mixed = jnp.einsum("hqk,hke->hqe", probs, heads[2], preferred_element_type=jnp.float32)
    mixed = mixed.transpose(1, 0, 2).reshape(count, -1).astype(jnp.bfloat16)
    branch = jnp.dot(mixed, attn_w[3], preferred_element_type=jnp.float32)
    middle, norm_one = layer_norm(states + branch, pair[0, 0], pair[0, 1])
    middle_b = middle.astype(jnp.bfloat16)
    hidden, active, output = ffn_forward(middle_b, ffn_w, unit_mask)
    result, norm_two = layer_norm(middle + output, pair[1, 0], pair[1, 1])
    return (result, (inputs, heads, log_total, mixed, norm_one, middle_b, hidden, active, norm_two))


def layer_backward(grad, attn_w, ffn_w, pair, length, unit_mask, kept):
    inputs, heads, log_total, mixed, norm_one, middle_b, hidden, active, norm_two = kept
    count = inputs.shape[0]
    grad_two, pair_two = norm_backward(grad, norm_two, pair[1, 0])
    ffn_grad, from_ffn = ffn_backward(
        grad_two.astype(jnp.bfloat16), middle_b, hidden, active, ffn_w, unit_mask
    )
    grad_one, pair_one = norm_backward(grad_two + from_ffn, norm_one, pair[0, 0])
    grad_branch = grad_one.astype(jnp.bfloat16)
    output_grad = jnp.einsum("td,te->de", mixed, grad_branch, preferred_element_type=jnp.float32)
    grad_mixed = jnp.einsum("te,de->td", grad_branch, attn_w[3], preferred_element_type=jnp.float32)
    grad_mixed = grad_mixed.astype(jnp.bfloat16).reshape(count, HEADS, -1).transpose(1, 0, 2)
    scale = heads.shape[-1] ** (-0.5)
    probs = jnp.exp(masked_scores(heads[0], heads[1], length) - log_total)
    grad_values = jnp.einsum(
        "hqk,hqe->hke", probs.astype(jnp.bfloat16), grad_mixed, preferred_element_type=jnp.float32
    )
    grad_probs = jnp.einsum(
        "hqe,hke->hqk", grad_mixed, heads[2], preferred_element_type=jnp.float32
    )
    grad_scores = probs * (grad_probs - jnp.sum(grad_probs * probs, axis=-1, keepdims=True))
    grad_scores = grad_scores.astype(jnp.bfloat16)
    grad_query = (
        jnp.einsum("hqk,hke->hqe", grad_scores, heads[1], preferred_element_type=jnp.float32)
        * scale
    )
    grad_key = (
        jnp.einsum("hqk,hqe->hke", grad_scores, heads[0], preferred_element_type=jnp.float32)
        * scale
    )
    stacked = (
        jnp.stack([grad_query, grad_key, grad_values]).transpose(0, 2, 1, 3).reshape(3, count, -1)
    )
    stacked = stacked.astype(jnp.bfloat16)
    input_grad = jnp.einsum("td,kte->kde", inputs, stacked, preferred_element_type=jnp.float32)
    from_attn = jnp.einsum("kte,kde->td", stacked, attn_w[:3], preferred_element_type=jnp.float32)
    attn_grad = jnp.concatenate([input_grad, output_grad[None]], axis=0)
    return (grad_one + from_attn, attn_grad, ffn_grad, jnp.stack([pair_one, pair_two]))


def adamw(weight, moment_one, moment_two, grad, decay, rate):
    moment_one = beta_one * moment_one + (1.0 - beta_one) * grad
    moment_two = beta_two * moment_two + (1.0 - beta_two) * grad * grad
    fixed_one = moment_one / (1.0 - beta_one**STEP)
    fixed_two = moment_two / (1.0 - beta_two**STEP)
    weight = weight - rate * (fixed_one / (jnp.sqrt(fixed_two) + adam_eps) + decay * weight)
    return (moment_one, moment_two, weight)


def combine_vocab(first, second):
    peak = jnp.maximum(first[0], second[0])
    total = first[1] * jnp.exp(first[0] - peak) + second[1] * jnp.exp(second[0] - peak)
    return (peak, total, first[2] + second[2])


def local_general(
    tokens,
    lengths,
    places,
    targets,
    ramp,
    attn,
    attn_m,
    attn_v,
    ffn,
    ffn_m,
    ffn_v,
    table,
    table_m,
    table_v,
    out_table,
    out_m,
    out_v,
    gains,
    gains_m,
    gains_v,
):
    rank = lax.axis_index("mp")
    count = tokens.shape[2]
    flat_ids = tokens.reshape(-1)
    all_lengths = lengths.reshape(-1)
    length = lax.dynamic_index_in_dim(all_lengths, rank, keepdims=False)
    masks = jnp.minimum(ramp, RAMP).astype(jnp.float32) / RAMP
    unit_masks = [masks[depth] for depth in range(LAYERS)]
    looked = jnp.take(table, flat_ids, axis=0)
    embedded = lax.all_to_all(looked, "mp", split_axis=0, concat_axis=1, tiled=True)
    states, norm_zero = layer_norm(
        embedded + sinusoid(count, embedded.shape[1]), gains[0, 0], gains[0, 1]
    )
    kept_all = []
    weights_all = []
    for depth in range(LAYERS):
        attn_w, ffn_w = fetch_forward(
            attn[depth].astype(jnp.bfloat16), ffn[depth].astype(jnp.bfloat16)
        )
        states, kept = layer_forward(
            states, attn_w, ffn_w, gains[1 + 2 * depth : 3 + 2 * depth], length, unit_masks[depth]
        )
        kept_all.append(kept)
        weights_all.append(None)
    spots = places.reshape(-1)
    picked = jnp.take(states, spots, axis=0).astype(jnp.bfloat16)
    picked_all = lax.all_gather(picked, "mp", axis=0, tiled=True)
    out_b = out_table.astype(jnp.bfloat16)
    logits = jnp.einsum("rd,vd->rv", picked_all, out_b, preferred_element_type=jnp.float32)
    labels = targets.reshape(-1)
    columns = rank * out_table.shape[0] + jnp.arange(out_table.shape[0])
    hits = (labels[:, None] == columns[None, :]).astype(jnp.float32)
    peak = jnp.max(logits, axis=1)
    expsum = jnp.sum(jnp.exp(logits - peak[:, None]), axis=1)
    target_part = jnp.sum(hits * logits, axis=1)
    peak_all, expsum_all, target_all = merged((peak, expsum, target_part), "mp", combine_vocab)
    log_total = peak_all + jnp.log(expsum_all)
    slot_count = targets.shape[2]
    counted = jnp.maximum(1, all_lengths * slot_count // count)
    valid = (jnp.arange(slot_count)[None, :] < counted[:, None]).reshape(-1)
    loss_pair = jnp.stack(
        [
            jnp.sum(jnp.where(valid, log_total - target_all, 0.0)),
            jnp.sum(counted).astype(jnp.float32),
        ]
    )
    grad_logits = jnp.where(
        valid[:, None], jnp.exp(logits - log_total[:, None]) - hits, 0.0
    ).astype(jnp.bfloat16)
    out_grad = jnp.einsum("rv,rd->vd", grad_logits, picked_all, preferred_element_type=jnp.float32)
    picked_grad = lax.psum_scatter(
        jnp.dot(grad_logits, out_b, preferred_element_type=jnp.float32),
        "mp",
        scatter_dimension=0,
        tiled=True,
    )
    grad = jnp.zeros_like(states).at[spots].add(picked_grad)
    attn_parts = [None] * LAYERS
    ffn_parts = [None] * LAYERS
    pair_grads = [None] * LAYERS
    for depth in reversed(range(LAYERS)):
        attn_w, ffn_w = fetch_backward(
            attn[depth].astype(jnp.bfloat16), ffn[depth].astype(jnp.bfloat16)
        )
        grad, attn_grad, ffn_grad, pair_grad = layer_backward(
            grad,
            attn_w,
            ffn_w,
            gains[1 + 2 * depth : 3 + 2 * depth],
            length,
            unit_masks[depth],
            kept_all[depth],
        )
        attn_parts[depth], ffn_parts[depth] = reduce_layer(attn_grad, ffn_grad)
        pair_grads[depth] = pair_grad
    grad_sum, zero_grad = norm_backward(grad, norm_zero, gains[0, 0])
    returned = lax.all_to_all(grad_sum, "mp", split_axis=1, concat_axis=0, tiled=True)
    table_grad = jnp.zeros_like(table).at[flat_ids].add(returned)
    gains_grad = jnp.concatenate([zero_grad[None]] + pair_grads, axis=0)
    attn_sum, ffn_sum, table_sum, out_sum, gains_part, loss = lax.psum(
        (jnp.stack(attn_parts), jnp.stack(ffn_parts), table_grad, out_grad, gains_grad, loss_pair),
        "dp",
    )
    shard_squares = (
        jnp.sum(attn_sum * attn_sum)
        + jnp.sum(ffn_sum * ffn_sum)
        + jnp.sum(table_sum * table_sum)
        + jnp.sum(out_sum * out_sum)
    )
    square_total, gains_sum = lax.psum((shard_squares, gains_part), "mp")
    grad_norm = jnp.sqrt(square_total + jnp.sum(gains_sum * gains_sum))
    factor = clip_limit / jnp.maximum(grad_norm, clip_limit)
    attn_m_new, attn_v_new, attn_new = adamw(
        attn, attn_m, attn_v, attn_sum * factor, weight_decay, learn_rate
    )
    ffn_m_new, ffn_v_new, ffn_new = adamw(
        ffn, ffn_m, ffn_v, ffn_sum * factor, weight_decay, learn_rate
    )
    table_m_new, table_v_new, table_new = adamw(
        table, table_m, table_v, table_sum * factor, weight_decay, learn_rate
    )
    out_m_new, out_v_new, out_new = adamw(
        out_table, out_m, out_v, out_sum * factor, weight_decay, learn_rate
    )
    gains_m_new, gains_v_new, gains_new = adamw(
        gains, gains_m, gains_v, gains_sum * factor, 0.0, gain_rate
    )
    return (
        loss,
        grad_norm.reshape(1),
        attn_m_new,
        attn_v_new,
        attn_new,
        ffn_m_new,
        ffn_v_new,
        ffn_new,
        table_m_new,
        table_v_new,
        table_new,
        out_m_new,
        out_v_new,
        out_new,
        gains_m_new,
        gains_v_new,
        gains_new,
    )


def local(
    tokens,
    lengths,
    places,
    targets,
    ramp,
    attn,
    attn_m,
    attn_v,
    ffn,
    ffn_m,
    ffn_v,
    table,
    table_m,
    table_v,
    out_table,
    out_m,
    out_v,
    gains,
    gains_m,
    gains_v,
):
    n = tokens.shape[1]
    where = jnp.asarray(positions(tokens.shape[2], gains.shape[2]))
    attn_full, ffn_full, first, *kept, slope, act, grad, out_grad, losses = forward_call(
        n, tokens[0], lengths, places[0], targets[0], ramp, gains, table.T, where, out_table, attn, ffn
    )
    attn_sum, ffn_sum, table_turned, out_sum, loss, gains_sum, square = backward_call(
        n, tokens[0], lengths, losses, grad, first, gains, out_grad, kept, attn_full, ffn_full, slope, act, table
    )
    table_sum = table_turned.T
    ffn_sum = ffn_sum.astype(jnp.float32)
    grad_norm = jnp.sqrt(square[0, 0])
    factor = clip_limit / jnp.maximum(grad_norm, clip_limit)
    attn_m_new, attn_v_new, attn_new = adamw(
        attn, attn_m, attn_v, attn_sum * factor, weight_decay, learn_rate
    )
    ffn_m_new, ffn_v_new, ffn_new = adamw(
        ffn, ffn_m, ffn_v, ffn_sum * factor, weight_decay, learn_rate
    )
    table_m_new, table_v_new, table_new = adamw(
        table, table_m, table_v, table_sum * factor, weight_decay, learn_rate
    )
    out_m_new, out_v_new, out_new = adamw(
        out_table, out_m, out_v, out_sum * factor, weight_decay, learn_rate
    )
    gains_m_new, gains_v_new, gains_new = adamw(
        gains, gains_m, gains_v, gains_sum * factor, 0.0, gain_rate
    )
    return (
        loss[0, :2],
        grad_norm.reshape(1),
        attn_m_new,
        attn_v_new,
        attn_new,
        ffn_m_new,
        ffn_v_new,
        ffn_new,
        table_m_new,
        table_v_new,
        table_new,
        out_m_new,
        out_v_new,
        out_new,
        gains_m_new,
        gains_v_new,
        gains_new,
    )


def solution(mesh):
    in_specs = (
        P("dp", None, None),
        P("dp", None),
        P("dp", "mp", None),
        P("dp", None, None),
        P(),
        P(None, None, "mp", None),
        P(None, None, "mp", None),
        P(None, None, "mp", None),
        P(None, None, "mp", None),
        P(None, None, "mp", None),
        P(None, None, "mp", None),
        P(None, "mp"),
        P(None, "mp"),
        P(None, "mp"),
        P("mp", None),
        P("mp", None),
        P("mp", None),
        P(),
        P(),
        P(),
    )
    out_specs = (
        P(),
        P(),
        P(None, None, "mp", None),
        P(None, None, "mp", None),
        P(None, None, "mp", None),
        P(None, None, "mp", None),
        P(None, None, "mp", None),
        P(None, None, "mp", None),
        P(None, "mp"),
        P(None, "mp"),
        P(None, "mp"),
        P("mp", None),
        P("mp", None),
        P("mp", None),
        P(),
        P(),
        P(),
    )
    fits = mesh.shape['mp'] == 8 and mesh.shape['dp'] == 4
    chosen = local if fits else local_general
    return jax.shard_map(chosen, mesh=mesh, in_specs=in_specs, out_specs=out_specs, check_vma=False)
```
